32 devices in a mesh: dom: 8 (over y, x, core), rot: 4 (over z).
Axes of the slice: x: 2, y: 2, z: 4, core: 2. Of those that a mesh axis runs over, the one named last changes fastest.
Arguments:
- raw_images: bfloat16 [12288, 4096], P('dom'), may hold values from -200 to 200, as said below
- defocus_bin: int32 [12288], P('dom'), may hold values from 0 to 63
- dest_row: int32 [12288], P('dom'), may hold values from -1 to 6143, as said below
- ctf_table: float32 [64, 2048], replicated, may hold values from -1 to 1
- inv_noise: float32 [2048], replicated, may hold values from 0.4 to 4
- panels: bfloat16 [5760, 4096], P('rot', 'dom'), may hold values from -0.1796875 to 0.1796875
Outputs:
- class_sums: float32 [4096, 5760], P('dom', 'rot')
- bin_weights: float32 [64, 5760], P(None, 'rot')
- log_evidence: float32 [6144], P('dom')
The draws below stay inside these ranges and needn't reach their ends.
Inputs may be any that keep to these rules, and one draw needn't show every extreme that they name: `dest_row`: each row 0 to 6143 of the balanced layout is named by exactly one slot and -1 marks an empty slot. The slots of one device name at most 192 rows of any one block of 768 rows, and some device names exactly 192 rows of every block. `raw_images`: rows of empty slots are not read.
All inputs are finite; a program needn't handle non-finite values.
Results may differ from the reference program's by a relative error of at most 0.0095.
Values may be sent and summed in bfloat16 or wider, within the bound.
No kernel may reach another device: no remote copies, remote signals or barrier semaphores. Data moves between devices by JAX's collectives and lax.ppermute only.
A program may use at most 192 MiB of HBM per device.

```python
import math
import jax
import jax.numpy as jnp
from jax import lax

PIX = 2048
CLASSES = 16
ROTS = 360
NBIN = 64
P_DEV = 768
HOLD = 1536
SEND_CAP = 192
N_DOM = 8


def draw_raw_images(key, part):
    total_slots = N_DOM * HOLD
    columns = 2 * PIX
    base_key = jax.random.fold_in(key, 3)
    value_key = jax.random.fold_in(base_key, 0)
    drawn = jnp.clip(jax.random.normal(value_key, (total_slots, columns), jnp.float32), -6.0, 6.0)
    return drawn.astype(jnp.bfloat16)


def draw_dest_row(key, part):
    base_key = jax.random.fold_in(key, 7)
    pair_key, weight_key, busy_key, shuffle_key = jax.random.split(base_key, 4)
    owners = N_DOM
    weights = jax.random.randint(weight_key, (owners,), 1, 9)
    busiest = jax.random.randint(busy_key, (), 0, owners)
    pairings = jax.vmap(lambda sub_key: jax.random.permutation(sub_key, owners))(jax.random.split(pair_key, owners))
    left_pair = pairings[:, 0::2]
    right_pair = pairings[:, 1::2]
    portion = SEND_CAP * weights[left_pair] // (weights[left_pair] + weights[right_pair])
    portion = jnp.where(left_pair == busiest, SEND_CAP, jnp.where(right_pair == busiest, 0, portion))
    dest_index = jnp.broadcast_to(jnp.arange(owners)[:, None], left_pair.shape)
    counts = jnp.zeros((owners, owners), jnp.int32)
    counts = counts.at[left_pair, dest_index].set(portion).at[right_pair, dest_index].set(SEND_CAP - portion)
    before = jnp.cumsum(counts, axis=0) - counts
    cum_counts = jnp.cumsum(counts, axis=1)
    owner_load = cum_counts[:, -1]
    slot_ids = jnp.arange(HOLD, dtype=jnp.int32)
    target = jnp.sum((cum_counts[:, None, :] <= slot_ids[None, :, None]).astype(jnp.int32), axis=2)
    target = jnp.minimum(target, owners - 1)
    block_start = jnp.take_along_axis(cum_counts - counts, target, axis=1)
    offset = jnp.take_along_axis(before, target, axis=1)
    dest_rows = target * P_DEV + offset + slot_ids[None, :] - block_start
    is_live = slot_ids[None, :] < owner_load[:, None]
    dest_rows = jnp.where(is_live, dest_rows, -1)
    ranking = jax.random.randint(shuffle_key, (owners, HOLD), 0, 1 << 16) * HOLD + slot_ids[None, :]
    row_order = jnp.argsort(ranking, axis=1)
    dest_rows = jnp.take_along_axis(dest_rows, row_order, axis=1)
    return dest_rows.reshape(-1).astype(jnp.int32)


def plant(drawn, stream_key, least, top_value):
    extent = drawn.shape
    index_at = [jax.random.randint(jax.random.fold_in(stream_key, axis), (), 0, extent[axis]) for axis in range(len(extent))]
    drawn = drawn.at[tuple(index_at)].set(least)
    longest = extent.index(max(extent))
    index_at[longest] = (index_at[longest] + 1) % extent[longest]
    return drawn.at[tuple(index_at)].set(top_value)


def block_scale(rng, dims, pieces, least, top_value):
    factor_of, own = 1.0, jax.random.fold_in(rng, 6)
    for axis_at, parts in pieces:
        draws = jnp.exp(jax.random.uniform(jax.random.fold_in(own, axis_at), (parts,), jnp.float32, least / len(pieces), top_value / len(pieces)))
        factor_of = factor_of * jnp.repeat(draws, dims[axis_at] // parts).reshape([-1 if axis == axis_at else 1 for axis in range(len(dims))])
    return factor_of


def gaussian(key, shape, width, bound, cuts=(), kind=jnp.bfloat16):
    values = jax.random.normal(key, shape, jnp.float32) * width
    if len(cuts) > 0:
        values = block_scale(key, shape, cuts, -0.22, 0.18) * values
    return jnp.clip(values, min=-bound, max=bound).astype(kind)


def setup_inputs(seed: int = 0) -> dict:
    seeds = jax.random.split(jax.random.key(seed), 7)
    return {
        "raw_images": draw_raw_images(jax.random.fold_in(seeds[6], 71), 0),
        "defocus_bin": plant(jax.random.randint(seeds[1], (N_DOM * HOLD,), 0, NBIN), jax.random.fold_in(seeds[1], 1), 0, NBIN - 1).astype(jnp.int32),
        "dest_row": draw_dest_row(jax.random.fold_in(seeds[6], 71), 0),
        "ctf_table": jnp.clip(jax.random.uniform(seeds[3], (NBIN, PIX), jnp.float32, -1.0, 1.0), -1.0, 1.0),
        "inv_noise": jnp.clip(jnp.exp(jax.random.uniform(seeds[4], (PIX,), jnp.float32, math.log(0.4), math.log(4.0))), 0.4, 4.0),
        "panels": gaussian(seeds[5], (ROTS * CLASSES, 2 * PIX), 0.03, 0.1796875, ((0, 4), (1, 8))),
    }


def reference(raw_images, defocus_bin, dest_row, ctf_table, inv_noise, panels):
    total_rows = P_DEV * N_DOM
    slot_count = dest_row.shape[0]
    target = jnp.where(dest_row >= 0, dest_row, total_rows).astype(jnp.int32)
    row_order = jnp.zeros((total_rows,), jnp.int32).at[target].set(jnp.arange(slot_count, dtype=jnp.int32), mode="drop")
    gain_half = ctf_table * ctf_table * inv_noise[None, :]
    gain_full = jnp.concatenate([gain_half, gain_half], axis=1)
    panel_wide = panels.astype(jnp.float32)
    energy = jnp.dot(gain_full, (panel_wide * panel_wide).T, precision=lax.Precision.HIGHEST)
    bin_range = jnp.arange(NBIN, dtype=jnp.int32)

    def one_shard(running, shard_index):
        class_acc, bin_acc = running
        images = raw_images[shard_index]
        bin_ids = defocus_bin[shard_index]
        factor = ctf_table[bin_ids] * inv_noise[None, :]
        weighted = (images.astype(jnp.float32) * jnp.concatenate([factor, factor], axis=1)).astype(jnp.bfloat16)
        scores = jnp.dot(weighted, panels.T, preferred_element_type=jnp.float32) - 0.5 * energy[bin_ids]
        row_peak = jnp.max(scores, axis=1)
        shifted = jnp.exp(scores - row_peak[:, None])
        row_total = jnp.sum(shifted, axis=1)
        posterior = (shifted / row_total[:, None]).astype(jnp.bfloat16)
        shard_term = jnp.dot(weighted.T, posterior, preferred_element_type=jnp.float32).astype(jnp.bfloat16)
        shard_term = lax.optimization_barrier(shard_term)
        bin_table = (bin_ids[:, None] == bin_range[None, :]).astype(jnp.bfloat16)
        counts = jnp.dot(bin_table.T, posterior, preferred_element_type=jnp.float32)
        return (class_acc + shard_term.astype(jnp.float32), bin_acc + counts), row_peak + jnp.log(row_total)

    start_acc = (jnp.zeros((2 * PIX, ROTS * CLASSES), jnp.float32), jnp.zeros((NBIN, ROTS * CLASSES), jnp.float32))
    (class_sums, bin_weights), evidence = lax.scan(one_shard, start_acc, row_order.reshape(N_DOM, P_DEV))
    return class_sums, bin_weights, evidence.reshape(-1)
```

```python
import functools

import jax
import jax.numpy as jnp
from jax import lax
from jax.experimental import pallas as pl
from jax.experimental.pallas import tpu as pltpu
from jax.sharding import PartitionSpec as P

NN = (((1,), (0,)), ((), ()))
NT = (((1,), (1,)), ((), ()))
F32, BF16, I32 = jnp.float32, jnp.bfloat16, jnp.int32
VMEM_BYTES = 50 * 1024 * 1024


def mm(a, b, dims):
    return lax.dot_general(a, b, dims, preferred_element_type=F32)


def split3(x):
    hi = x.astype(BF16)
    rest = x - hi.astype(F32)
    mid = rest.astype(BF16)
    low = (rest - mid.astype(F32)).astype(BF16)
    return hi, mid, low


def call(body, grid, in_specs, out_specs, out_shape, scratch=(), alias=None, flops=0, moved=0):
    return pl.pallas_call(
        body,
        grid_spec=pltpu.PrefetchScalarGridSpec(
            num_scalar_prefetch=1,
            grid=grid,
            in_specs=in_specs,
            out_specs=out_specs,
            scratch_shapes=list(scratch),
        ),
        out_shape=out_shape,
        input_output_aliases=alias or {},
        compiler_params=pltpu.CompilerParams(vmem_limit_bytes=VMEM_BYTES),
        cost_estimate=pl.CostEstimate(flops=flops, bytes_accessed=moved, transcendentals=0),
    )


def sds(shape, dtype):
    return jax.ShapeDtypeStruct(shape, dtype)


def one_hot_rows(out_ref, wanted):
    rows, width = out_ref.shape
    step = 256 if rows % 256 == 0 else rows
    for start in range(0, rows, step):
        index = lax.broadcasted_iota(I32, (step, width), 0) + start
        out_ref[start : start + step, :] = jnp.where(index == wanted, 1.0, 0.0).astype(BF16)


def pack_body(dom, shard_rows, cap, meta, dest_ref, bin_ref, raw_ref, out_ref, code_ref, pick_ref):
    @pl.when(pl.program_id(0) == 0)
    def _():
        dest = dest_ref[...]
        hold = dest.shape[1]
        low = lax.broadcasted_iota(I32, (dom, hold), 0) * shard_rows
        inside = jnp.logical_and(dest >= low, dest < low + shard_rows)
        marks = jnp.where(inside, 1.0, 0.0)
        base = jnp.sum(jnp.where(inside, low, 0), axis=0, keepdims=True)
        local = dest - base
        lanes = 128
        before = (
            lax.broadcasted_iota(I32, (lanes, lanes), 0)
            < lax.broadcasted_iota(I32, (lanes, lanes), 1)
        )
        upper = jnp.where(before, 1.0, 0.0).astype(BF16)
        carry = jnp.zeros((dom, 1), F32)
        first_slot = lax.broadcasted_iota(I32, (dom, lanes), 0).astype(F32) * cap
        places = []
        for start in range(0, hold, lanes):
            part = marks[:, start : start + lanes]
            rank = mm(part.astype(BF16), upper, NN) + carry
            places.append(
                jnp.sum(jnp.where(part > 0, rank + first_slot + 1.0, 0.0), axis=0, keepdims=True)
            )
            carry = carry + jnp.sum(part, axis=1, keepdims=True)
        place = jnp.concatenate(places, axis=1).astype(I32) - 1
        one_hot_rows(pick_ref, place)
        which = lax.broadcasted_iota(I32, (8, hold), 0)
        digits = jnp.where(
            which == 0,
            local >> 4,
            jnp.where(which == 1, local & 15, jnp.where(which == 2, bin_ref[...], 1)),
        )
        digits = jnp.where(dest >= 0, digits, 0).astype(F32).astype(BF16)
        got = mm(digits, pick_ref[...], NT)
        code = got[0:1] * 1024.0 + got[1:2] * 64.0 + got[2:3] + got[3:4] - 1.0
        code_ref[...] = code.astype(I32)

    out_ref[...] = mm(pick_ref[...], raw_ref[...], NN).astype(BF16)


def pack(meta, raw_images, dest, bins, dom, width, block):
    hold, _ = raw_images.shape
    shard_rows = hold // 2
    cap = hold // dom
    slots = dom * cap
    steps = width // block
    body = functools.partial(pack_body, dom, shard_rows, cap)
    return call(
        body,
        (steps,),
        [
            pl.BlockSpec((1, hold), lambda j, m: (0, 0)),
            pl.BlockSpec((1, hold), lambda j, m: (0, 0)),
            pl.BlockSpec((hold, block), lambda j, m: (0, m[1] * steps + j)),
        ],
        [
            pl.BlockSpec((slots, block), lambda j, m: (0, j)),
            pl.BlockSpec((1, slots), lambda j, m: (0, 0)),
        ],
        [sds((slots, width), BF16), sds((1, slots), I32)],
        scratch=[pltpu.VMEM((slots, hold), BF16)],
        flops=2 * slots * hold * width,
        moved=4 * hold * width,
    )(meta, dest, bins, raw_images)


def unpack_body(bins, meta, code_ref, recv_ref, ctf_ref, inv_ref, out_ref, hot_ref, pick, wide):
    shard_rows = out_ref.shape[0]

    @pl.when(pl.program_id(0) == 0)
    def _():
        code = code_ref[...]
        one_hot_rows(pick, code >> 6)
        slot_bin = (code & 63).astype(F32).astype(BF16)
        slot_bins = jnp.broadcast_to(slot_bin, (8, slot_bin.shape[1]))
        down = mm(pick[...], slot_bins, NT)[:, 0:1].astype(I32)
        across = mm(slot_bins, pick[...], NT)[0:1].astype(I32)
        lane = lax.broadcasted_iota(I32, (shard_rows, 3 * bins), 1)
        wide[...] = jnp.where((lane & 63) == down, 1.0, 0.0).astype(BF16)
        row = lax.broadcasted_iota(I32, (3 * bins, shard_rows), 0)
        hot_ref[...] = jnp.where((row & 63) == across, 1.0, 0.0).astype(BF16)

    image = mm(pick[...], recv_ref[...], NN)
    table = jnp.concatenate(split3(ctf_ref[...] * inv_ref[...]), axis=0)
    factor = mm(wide[...], table, NN)
    out_ref[...] = (image * factor).astype(BF16)


def unpack(meta, code, recv, ctf, inv, block):
    slots, width = recv.shape
    shard_rows = slots // 2
    bins, pix = ctf.shape
    steps = width // block
    wrap = pix // block
    return call(
        functools.partial(unpack_body, bins),
        (steps,),
        [
            pl.BlockSpec((1, slots), lambda j, m: (0, 0)),
            pl.BlockSpec((slots, block), lambda j, m: (0, j)),
            pl.BlockSpec((bins, block), lambda j, m: (0, lax.rem(m[1] * steps + j, wrap))),
            pl.BlockSpec((1, block), lambda j, m: (0, lax.rem(m[1] * steps + j, wrap))),
        ],
        [
            pl.BlockSpec((shard_rows, block), lambda j, m: (0, j)),
            pl.BlockSpec((3 * bins, shard_rows), lambda j, m: (0, 0)),
        ],
        [sds((shard_rows, width), BF16), sds((3 * bins, shard_rows), BF16)],
        scratch=[
            pltpu.VMEM((shard_rows, slots), BF16),
            pltpu.VMEM((shard_rows, 3 * bins), BF16),
        ],
        flops=2 * slots * shard_rows * width,
        moved=2 * (slots + shard_rows) * width,
    )(meta, code, recv, ctf, inv)


def energy_body(bins, count, meta, *refs):
    pieces, (ctf_ref, inv_ref, panel_ref, extra_ref, total) = refs[:count], refs[count:]
    step = pl.program_id(0)

    @pl.when(step == 0)
    def _():
        total[...] = jnp.zeros_like(total)

    gain = ctf_ref[...] * ctf_ref[...] * inv_ref[...]
    gain3 = jnp.concatenate(split3(gain), axis=0)
    for index, piece in enumerate(pieces):

        @pl.when(step == index)
        def _():
            panel = piece[...]
            panel_ref[...] = panel
            wide = panel.astype(F32)
            square = wide * wide
            high = square.astype(BF16)
            low = (square - high.astype(F32)).astype(BF16)
            total[...] += mm(high, gain3, NT) + mm(low, gain3, NT)

    @pl.when(step == count - 1)
    def _():
        whole = total[:, :bins] + total[:, bins : 2 * bins] + total[:, 2 * bins :]
        extra_ref[...] = jnp.concatenate(split3(-0.5 * whole), axis=1)


def energy(meta, pieces, ctf, inv):
    count = len(pieces)
    rows, width = pieces[0].shape
    bins, pix = ctf.shape
    wrap = pix // width
    return call(
        functools.partial(energy_body, bins, count),
        (count,),
        [pl.BlockSpec((rows, width), lambda j, m: (0, 0))] * count
        + [
            pl.BlockSpec((bins, width), lambda j, m: (0, lax.rem(m[0] ^ j, wrap))),
            pl.BlockSpec((1, width), lambda j, m: (0, lax.rem(m[0] ^ j, wrap))),
        ],
        [
            pl.BlockSpec((rows, width), lambda j, m: (0, m[0] ^ j)),
            pl.BlockSpec((rows, 3 * bins), lambda j, m: (0, 0)),
        ],
        [sds((rows, count * width), BF16), sds((rows, 3 * bins), BF16)],
        scratch=[pltpu.VMEM((rows, 3 * bins), F32)],
        flops=2 * 4 * rows * bins * count * width * 3,
        moved=4 * rows * count * width,
    )(meta, *pieces, ctf, inv)


def score_body(first, last, meta, own_ref, sib_ref, panel_ref, *refs):
    if first:
        acc_out, full_ref = refs
    elif last:
        acc_ref, _, hot_own, hot_sib, extra_ref, shifted_ref, stat_ref, full_ref = refs
    else:
        acc_ref, _, acc_out, full_ref = refs
    half = pl.num_programs(0) // 2

    def tile(source, hot):
        block = source[...]
        full_ref[...] = block
        total = mm(panel_ref[...], block, NT)
        if not first:
            total = acc_ref[...] + total
        if not last:
            acc_out[...] = total
            return
        total = total + mm(extra_ref[...], hot[...], NN)
        peak = jnp.max(total, axis=0, keepdims=True)
        shifted = jnp.exp(total - peak)
        shifted_ref[...] = shifted
        mass = jnp.sum(shifted, axis=0, keepdims=True)
        which = lax.broadcasted_iota(I32, stat_ref.shape, 0)
        stat_ref[...] = jnp.where(which == 0, peak, mass)

    @pl.when(pl.program_id(0) < half)
    def _():
        tile(own_ref, hot_own if last else None)

    @pl.when(pl.program_id(0) >= half)
    def _():
        tile(sib_ref, hot_sib if last else None)


def score(meta, turn, turns, own, sib, panels, acc, full, hots=None, extra=None):
    rows, width = own.shape
    tile = 256
    half = rows // tile
    count = panels.shape[0]
    first, last = turn == 0, turn == turns - 1

    def share(m):
        return lax.rem(m[1] + turns - turn, turns)

    front = pl.BlockSpec((tile, width), lambda j, m: (jnp.minimum(j, half - 1), 0))
    back = pl.BlockSpec((tile, width), lambda j, m: (jnp.maximum(j - half, 0), 0))
    acc_spec = pl.BlockSpec((count, tile), lambda j, m: (0, j))
    full_spec = pl.BlockSpec((tile, width), lambda j, m: (j, share(m)))
    in_specs = [front, back, pl.BlockSpec((count, width), lambda j, m: (0, share(m)))]
    operands = [meta, own, sib, panels]
    alias = {}
    if not first:
        in_specs += [acc_spec, pl.BlockSpec(memory_space=pl.ANY)]
        operands += [acc, full]
        alias = {4: 0, 5: 2 if last else 1}
    out_specs = [acc_spec, full_spec]
    full_shape = sds((2 * rows, width * turns), BF16)
    out_shape = [sds((count, 2 * rows), F32), full_shape]
    if last:
        depth = extra.shape[1]
        in_specs += [
            pl.BlockSpec((depth, tile), lambda j, m: (0, jnp.minimum(j, half - 1))),
            pl.BlockSpec((depth, tile), lambda j, m: (0, jnp.maximum(j - half, 0))),
            pl.BlockSpec((count, depth), lambda j, m: (0, 0)),
        ]
        operands += [*hots, extra]
        out_specs = [acc_spec, pl.BlockSpec((8, tile), lambda j, m: (0, j)), full_spec]
        out_shape = [out_shape[0], sds((8, 2 * rows), F32), full_shape]
    return call(
        functools.partial(score_body, first, last),
        (2 * half,),
        in_specs,
        out_specs,
        out_shape,
        alias=alias,
        flops=2 * count * 2 * rows * width,
        moved=8 * count * 2 * rows + 8 * rows * width,
    )(*operands)


def merge_body(meta, mine_ref, other_ref, out_ref):
    rows = mine_ref.shape[1] // 2
    other = other_ref[...]
    other = jnp.concatenate([other[:, rows:], other[:, :rows]], axis=1)
    mine = mine_ref[...]
    peak = jnp.maximum(mine[0:1], other[0:1])
    mass = mine[1:2] * jnp.exp(mine[0:1] - peak) + other[1:2] * jnp.exp(other[0:1] - peak)
    which = lax.broadcasted_iota(I32, out_ref.shape, 0)
    out_ref[...] = jnp.where(which == 0, peak, mass)


def merge(meta, mine, other):
    spec = pl.BlockSpec(mine.shape, lambda j, m: (0, 0))
    return call(merge_body, (1,), [spec, spec], spec, sds(mine.shape, F32))(meta, mine, other)


def class_body(kind, meta, *refs):
    if kind == "first":
        shifted_ref, stat_ref, a_ref, b_ref, c_ref, d_ref, full_ref = refs[:7]
        out_ref, post_ref, log_ref = refs[7:]

        @pl.when(pl.program_id(0) == 0)
        def _():
            stats = [r[...] for r in (a_ref, b_ref, c_ref, d_ref)]
            peaks = [s[0:1] for s in stats]
            peak = jnp.maximum(
                jnp.maximum(peaks[0], peaks[1]), jnp.maximum(peaks[2], peaks[3])
            )
            parts = [s[1:2] * jnp.exp(p - peak) for s, p in zip(stats, peaks)]
            mass = (parts[0] + parts[1]) + (parts[2] + parts[3])
            factor = jnp.exp(stat_ref[0:1] - peak) / mass
            post_ref[...] = (shifted_ref[...] * factor).astype(BF16)
            log_ref[...] = (peak + jnp.log(mass))[:, : log_ref.shape[1]]

    elif kind == "mass":
        post_ref, hot_own, hot_sib, full_ref, out_ref, mass_ref = refs
        bins, columns = mass_ref.shape
        rows = hot_own.shape[1]

        @pl.when(pl.program_id(0) == 0)
        def _():
            mass_ref[...] = mm(hot_own[:bins, :], post_ref[:, :rows], NT) + mm(
                hot_sib[:bins, :], post_ref[:, rows:], NT
            )

    else:
        post_ref, full_ref, out_ref = refs
    out_ref[...] = mm(post_ref[...], full_ref[...], NN).astype(out_ref.dtype)


def class_sums_part(meta, kind, offset, steps, full, post=None, shifted=None, stats=None, hots=None, bins=0):
    rows, columns = full.shape
    width = columns // 8
    count = (shifted if post is None else post).shape[0]
    whole = lambda shape: pl.BlockSpec(shape, lambda j, m: (0, 0))
    full_spec = pl.BlockSpec((rows, width), lambda j, m: (0, m[offset + j]))
    out_spec = pl.BlockSpec((count, width), lambda j, m: (0, j))
    dtype = F32 if kind == "rest" else BF16
    out_shape = sds((count, steps * width), dtype)
    if kind == "first":
        operands = [shifted, *stats, full]
        in_specs = [whole(shifted.shape)] + [whole(stats[0].shape)] * 5 + [full_spec]
        out_specs = [out_spec, whole((count, rows)), whole((1, rows // 2))]
        out_shape = [out_shape, sds((count, rows), BF16), sds((1, rows // 2), F32)]
    elif kind == "mass":
        operands = [post, *hots, full]
        in_specs = [whole(post.shape), whole(hots[0].shape), whole(hots[1].shape), full_spec]
        out_specs = [out_spec, whole((bins, count))]
        out_shape = [out_shape, sds((bins, count), F32)]
    else:
        operands = [post, full]
        in_specs = [whole(post.shape), full_spec]
        out_specs = out_spec
    return call(
        functools.partial(class_body, kind),
        (steps,),
        in_specs,
        out_specs,
        out_shape,
        flops=2 * count * rows * width * steps,
        moved=2 * rows * width * steps + 4 * count * (rows + width * steps),
    )(meta, *operands)


def forward_body(meta, y_ref, x_ref, down_ref, left_ref, a_ref, b_ref):
    vertical = (y_ref[...] + down_ref[...].astype(F32)).astype(BF16)
    side = (x_ref[...] + left_ref[...].astype(F32)).astype(BF16)
    even = meta[0] % 2 == 0
    a_ref[...] = jnp.where(even, vertical, side)
    b_ref[...] = jnp.where(even, side, vertical)


def forward(meta, rest, got_x, got_y):
    count, columns = rest.shape
    width = columns // 4
    tile = count // 5
    at = lambda k: pl.BlockSpec((tile, width), lambda j, m: (j, k))
    shape = sds((count, width), BF16)
    return call(
        forward_body, (5,), [at(2), at(3), at(1), at(1)], [at(0), at(0)], [shape, shape]
    )(meta, rest, rest, got_x, got_y)


def settle_body(meta, first_ref, second_ref, down_ref, left_ref, keep_ref, give_ref):
    first = first_ref[...] + down_ref[...].astype(F32)
    second = second_ref[...] + left_ref[...].astype(F32)
    even = meta[0] % 2 == 0
    keep_ref[...] = jnp.where(even, first, second)
    give_ref[...] = jnp.where(even, second, first).astype(BF16)


def settle(meta, rest, got_x, got_y):
    count, columns = rest.shape
    width = columns // 4
    tile = count // 5
    at = lambda k: pl.BlockSpec((tile, width), lambda j, m: (j, k))
    return call(
        settle_body,
        (5,),
        [at(0), at(1), at(0), at(0)],
        [at(0), at(0)],
        [sds((count, width), F32), sds((count, width), BF16)],
    )(meta, rest, rest, got_x, got_y)


def finish_body(meta, keep_ref, a_ref, give_ref, b_ref, out_ref, tall):
    count = keep_ref.shape[0]
    core = meta[0] % 2
    mine = pl.multiple_of(core * count, 8)
    other = pl.multiple_of((1 - core) * count, 8)
    tall[pl.ds(mine, count), :] = keep_ref[...] + a_ref[...].astype(F32)
    tall[pl.ds(other, count), :] = give_ref[...].astype(F32) + b_ref[...].astype(F32)
    out_ref[...] = tall[...].T[:, : 2 * count]


def finish(meta, keep, got_a, got_self, got_b):
    count, width = keep.shape
    lanes = 128
    tall = -(-2 * count // lanes) * lanes
    spec = pl.BlockSpec((count, lanes), lambda j, m: (0, j))
    return call(
        finish_body,
        (width // lanes,),
        [spec] * 4,
        pl.BlockSpec((lanes, 2 * count), lambda j, m: (j, 0)),
        sds((width, 2 * count), F32),
        scratch=[pltpu.VMEM((tall, lanes), F32)],
    )(meta, keep, got_a, got_self, got_b)


def two_by_two(raw_images, defocus_bin, dest_row, ctf_table, inv_noise, panels):
    dom, turns = lax.axis_size("dom"), lax.axis_size("rot")
    device, plane = lax.axis_index("dom"), lax.axis_index("rot")
    bins = ctf_table.shape[0]
    hold, columns = raw_images.shape
    cap = hold // dom
    chip, core = device // 2, device % 2
    order = [(1, 0), (3, 0), (2, 1), (3, 1), (0, 0), (0, 1), (2, 0), (1, 1)]
    meta = jnp.stack(
        [device, plane] + [((chip ^ apart) * 2 + half) for apart, half in order]
    ).astype(I32)
    inv = inv_noise[None, :]

    def across(value, apart):
        return lax.ppermute(value, "dom", [(i, i ^ apart) for i in range(dom)])

    width = columns // turns
    packed, code = pack(meta, raw_images, dest_row[None, :], defocus_bin[None, :], dom, width, 256)
    got_code = lax.all_to_all(code.reshape(dom, cap), "dom", 0, 0, tiled=True)
    recv = lax.all_to_all(packed, "dom", 0, 0, tiled=True)

    count = panels.shape[0] // 2
    pieces = [None] * 8
    pieces[0] = lax.dynamic_slice_in_dim(panels, core * count, count, 0)
    pieces[1] = across(lax.dynamic_slice_in_dim(panels, (1 - core) * count, count, 0), 1)
    pieces[2], pieces[4] = across(pieces[0], 2), across(pieces[0], 4)
    pieces[3], pieces[5] = across(pieces[1], 2), across(pieces[1], 4)
    pieces[6], pieces[7] = across(pieces[2], 4), across(pieces[5], 2)
    panel_full, extra = energy(meta, pieces, ctf_table, inv)

    share, hot = unpack(meta, got_code.reshape(1, hold), recv, ctf_table, inv, 256)
    hots = (hot, across(hot, 1))
    acc = full = None
    for turn in range(turns):
        other = across(share, 1)
        if turn == turns - 1:
            shifted, stat, full = score(
                meta, turn, turns, share, other, panel_full, acc, full, hots, extra
            )
        else:
            acc, full = score(meta, turn, turns, share, other, panel_full, acc, full)
            share = lax.ppermute(share, "rot", [(i, (i + 1) % turns) for i in range(turns)])

    pair = merge(meta, stat, across(stat, 1))
    others = [
        lax.ppermute(pair, "rot", [(i, i ^ apart) for i in range(turns)]) for apart in (1, 2, 3)
    ]
    to_x, post, log_evidence = class_sums_part(
        meta, "first", 2, 2, full, shifted=shifted, stats=[stat, pair, *others]
    )
    got_x = across(to_x, 2)
    to_y, mass = class_sums_part(meta, "mass", 4, 2, full, post=post, hots=hots, bins=bins)
    got_y = across(to_y, 4)
    rest = class_sums_part(meta, "rest", 6, 4, full, post=post)
    mass = mass + across(mass, 2)
    mass = mass + across(mass, 4)
    mass_other = across(mass, 1)
    bin_weights = jnp.where(
        core == 0,
        jnp.concatenate([mass, mass_other], axis=1),
        jnp.concatenate([mass_other, mass], axis=1),
    )
    message_a, message_b = forward(meta, rest, got_x, got_y)
    got_a = lax.ppermute(message_a, "dom", [(i, i ^ (4 if i % 2 == 0 else 2)) for i in range(dom)])
    got_b = lax.ppermute(message_b, "dom", [(i, i ^ (3 if i % 2 == 0 else 5)) for i in range(dom)])
    keep, give = settle(meta, rest, got_x, got_y)
    got_self = across(give, 1)
    class_sums = finish(meta, keep, got_a, got_self, got_b)
    return class_sums, bin_weights, log_evidence.reshape(-1)


def energy_block(gain_block, panel_piece):
    widened = panel_piece.astype(jnp.float32)
    return lax.dot_general(
        gain_block, widened * widened, (((1,), (1,)), ((), ())), precision=lax.Precision.HIGHEST
    )


def on_device(raw_images, defocus_bin, dest_row, ctf_table, inv_noise, panels):
    dom_count = lax.axis_size("dom")
    bin_count = ctf_table.shape[0]
    columns = raw_images.shape[1]
    hold_rows = raw_images.shape[0]
    shard_rows = hold_rows // 2
    capacity = 2 * shard_rows // dom_count
    is_live = dest_row >= 0
    target = jnp.where(is_live, dest_row // shard_rows, dom_count)
    local_row = dest_row % shard_rows
    marks = (target[:, None] == jnp.arange(dom_count, dtype=jnp.int32)[None, :]).astype(jnp.int32)
    slot_rank = jnp.sum((jnp.cumsum(marks, axis=0) - marks) * marks, axis=1)
    row_code = jnp.where(is_live, local_row * bin_count + defocus_bin, -1)
    padded_images = jnp.concatenate([raw_images, jnp.zeros((1, columns), raw_images.dtype)], axis=0)
    padded_code = jnp.concatenate([row_code, jnp.full((1,), -1, jnp.int32)], axis=0)
    position = jnp.where(is_live, target * capacity + slot_rank, dom_count * capacity)
    slot_count = dom_count * capacity
    source = (
        jnp.full((slot_count,), hold_rows, jnp.int32)
        .at[position]
        .set(jnp.arange(hold_rows, dtype=jnp.int32), mode="drop")
    )
    send_images = padded_images[source].reshape(dom_count, capacity, columns)
    send_code = padded_code[source].reshape(dom_count, capacity)
    recv_images, recv_code = (
        lax.all_to_all(send_images, "dom", split_axis=0, concat_axis=0, tiled=True),
        lax.all_to_all(send_code, "dom", split_axis=0, concat_axis=0, tiled=True),
    )
    flat_images = recv_images.reshape(-1, columns)
    flat_code = recv_code.reshape(-1)
    arrived = flat_code >= 0
    row_of = jnp.where(arrived, flat_code // bin_count, shard_rows)
    row_order = (
        jnp.zeros((shard_rows,), jnp.int32)
        .at[row_of]
        .set(jnp.arange(flat_code.shape[0], dtype=jnp.int32), mode="drop")
    )
    images = flat_images[row_order]
    bin_ids = flat_code[row_order] % bin_count
    bin_table = (bin_ids[:, None] == jnp.arange(bin_count, dtype=jnp.int32)[None, :]).astype(
        jnp.float32
    )
    ctf_rows = jnp.dot(bin_table, ctf_table, precision=lax.Precision.HIGHEST)
    factor = ctf_rows * inv_noise[None, :]
    weighted = (images.astype(jnp.float32) * jnp.concatenate([factor, factor], axis=1)).astype(
        jnp.bfloat16
    )
    gain_half = ctf_table * ctf_table * inv_noise[None, :]
    gain_full = jnp.concatenate([gain_half, gain_half], axis=1)
    panel_piece = lax.all_gather(panels, "dom", axis=1, tiled=True)
    col_block = weighted
    cross_term = lax.dot_general(
        col_block, panel_piece, (((1,), (1,)), ((), ())), preferred_element_type=jnp.float32
    )
    energy = energy_block(gain_full, panel_piece)
    scores = cross_term - 0.5 * jnp.dot(bin_table, energy, precision=lax.Precision.HIGHEST)
    local_peak = jnp.max(scores, axis=1)
    row_peak = lax.pmax(local_peak, "rot")
    shifted = jnp.exp(scores - row_peak[:, None])
    row_total = lax.psum(jnp.sum(shifted, axis=1), "rot")
    posterior = (shifted / row_total[:, None]).astype(jnp.bfloat16)
    log_evidence = row_peak + jnp.log(row_total)
    col_block = weighted
    class_sums = lax.psum_scatter(
        lax.dot_general(
            col_block, posterior, (((0,), (0,)), ((), ())), preferred_element_type=jnp.float32
        ).astype(jnp.bfloat16),
        "dom",
        scatter_dimension=0,
        tiled=True,
    ).astype(jnp.float32)
    local_mass = lax.dot_general(
        bin_table.astype(jnp.bfloat16),
        posterior,
        (((0,), (0,)), ((), ())),
        preferred_element_type=jnp.float32,
    )
    bin_weights = lax.psum(local_mass.astype(jnp.bfloat16), "dom").astype(jnp.float32)
    return (class_sums, bin_weights, log_evidence)


def solution(mesh):
    small = mesh.shape["dom"] == 8 and mesh.shape["rot"] == 4
    return jax.shard_map(
        two_by_two if small else on_device,
        mesh=mesh,
        in_specs=(P("dom", None), P("dom"), P("dom"), P(), P(), P("rot", "dom")),
        out_specs=(P("dom", "rot"), P(None, "rot"), P("dom")),
        check_vma=False,
    )
```

```python
import functools

import jax
import jax.numpy as jnp
from jax import lax
from jax.experimental import pallas as pl
from jax.experimental.pallas import tpu as pltpu
from jax.sharding import PartitionSpec as P

NN = (((1,), (0,)), ((), ()))
NT = (((1,), (1,)), ((), ()))
F32, BF16, I32 = jnp.float32, jnp.bfloat16, jnp.int32
CODE = 128
VMEM_BYTES = 50 * 1024 * 1024


def mm(a, b, dims):
    return lax.dot_general(a, b, dims, preferred_element_type=F32)


def split3(x):
    hi = x.astype(BF16)
    rest = x - hi.astype(F32)
    mid = rest.astype(BF16)
    low = (rest - mid.astype(F32)).astype(BF16)
    return hi, mid, low


def call(body, grid, in_specs, out_specs, out_shape, scratch=(), alias=None, flops=0, moved=0):
    return pl.pallas_call(
        body,
        grid_spec=pltpu.PrefetchScalarGridSpec(
            num_scalar_prefetch=1,
            grid=grid,
            in_specs=in_specs,
            out_specs=out_specs,
            scratch_shapes=list(scratch),
        ),
        out_shape=out_shape,
        input_output_aliases=alias or {},
        compiler_params=pltpu.CompilerParams(vmem_limit_bytes=VMEM_BYTES),
        cost_estimate=pl.CostEstimate(flops=flops, bytes_accessed=moved, transcendentals=0),
    )


def sds(shape, dtype):
    return jax.ShapeDtypeStruct(shape, dtype)


def one_hot_rows(out_ref, wanted):
    rows, width = out_ref.shape
    step = 256 if rows % 256 == 0 else rows
    for start in range(0, rows, step):
        index = lax.broadcasted_iota(I32, (step, width), 0) + start
        out_ref[start : start + step, :] = jnp.where(index == wanted, 1.0, 0.0).astype(BF16)


def places_of(dest, shard_rows, cap, dom):
    hold = dest.shape[1]
    low = lax.broadcasted_iota(I32, (dom, hold), 0) * shard_rows
    inside = jnp.logical_and(dest >= low, dest < low + shard_rows)
    marks = jnp.where(inside, 1.0, 0.0)
    local = dest - jnp.sum(jnp.where(inside, low, 0), axis=0, keepdims=True)
    lanes = 128
    before = lax.broadcasted_iota(I32, (lanes, lanes), 0) < lax.broadcasted_iota(
        I32, (lanes, lanes), 1
    )
    upper = jnp.where(before, 1.0, 0.0).astype(BF16)
    carry = lax.broadcasted_iota(I32, (dom, 1), 0).astype(F32) * cap + 1.0
    found = []
    for start in range(0, hold, lanes):
        part = marks[:, start : start + lanes]
        rank = mm(part.astype(BF16), upper, NN) + carry
        found.append(jnp.sum(jnp.where(part > 0, rank, 0.0), axis=0, keepdims=True))
        carry = carry + jnp.sum(part, axis=1, keepdims=True)
    return jnp.concatenate(found, axis=1).astype(I32) - 1, local


def pack_first_body(dom, shard_rows, cap, meta, dest_ref, bin_ref, raw_ref, out_ref, place_ref, pick):
    dest = dest_ref[...]
    place, local = places_of(dest, shard_rows, cap, dom)
    place_ref[...] = place
    one_hot_rows(pick, place)
    which = lax.broadcasted_iota(I32, (CODE, dest.shape[1]), 0)
    digits = jnp.where(
        which == 0,
        local >> 4,
        jnp.where(which == 1, local & 15, jnp.where(which == 2, bin_ref[...], jnp.where(which == 3, 1, 0))),
    )
    digits = jnp.where(dest >= 0, digits, 0).astype(F32).astype(BF16)
    out_ref[:, :CODE] = mm(pick[...], digits, NT).astype(BF16)
    out_ref[:, CODE:] = mm(pick[...], raw_ref[...], NN).astype(BF16)


def pack_next_body(meta, place_ref, raw_ref, out_ref, pick):
    one_hot_rows(pick, place_ref[...])
    out_ref[...] = mm(pick[...], raw_ref[...], NN).astype(BF16)


def pack_first(meta, raw_images, dest, bins, dom, width, at):
    hold, _ = raw_images.shape
    cap = hold // dom
    slots = dom * cap
    row = pl.BlockSpec((1, hold), lambda j, m: (0, 0))
    return call(
        functools.partial(pack_first_body, dom, hold // 2, cap),
        (1,),
        [row, row, pl.BlockSpec((hold, width), lambda j, m: (0, at(m)))],
        [pl.BlockSpec((slots, CODE + width), lambda j, m: (0, 0)), row],
        [sds((slots, CODE + width), BF16), sds((1, hold), I32)],
        scratch=[pltpu.VMEM((slots, hold), BF16)],
        flops=2 * slots * hold * width,
        moved=4 * hold * width,
    )(meta, dest, bins, raw_images)


def pack_next(meta, raw_images, place, dom, width, at):
    hold, _ = raw_images.shape
    slots = dom * (hold // dom)
    return call(
        pack_next_body,
        (1,),
        [
            pl.BlockSpec((1, hold), lambda j, m: (0, 0)),
            pl.BlockSpec((hold, width), lambda j, m: (0, at(m))),
        ],
        pl.BlockSpec((slots, width), lambda j, m: (0, 0)),
        sds((slots, width), BF16),
        scratch=[pltpu.VMEM((slots, hold), BF16)],
        flops=2 * slots * hold * width,
        moved=4 * hold * width,
    )(meta, place, raw_images)


def weigh(pick, wide, recv, ctf_ref, inv_ref, out_ref):
    table = jnp.concatenate(split3(ctf_ref[...] * inv_ref[...]), axis=0)
    factor = mm(wide, table, NN)
    out_ref[...] = (mm(pick, recv, NN) * factor).astype(BF16)


def unpack_first_body(bins, meta, recv_ref, ctf_ref, inv_ref, out_ref, hot_ref, pick, wide):
    shard_rows = out_ref.shape[0]
    chosen = jnp.where(
        lax.broadcasted_iota(I32, (8, CODE), 0) == lax.broadcasted_iota(I32, (8, CODE), 1), 1.0, 0.0
    ).astype(BF16)
    got = mm(chosen, recv_ref[:, :CODE], NT)
    row = got[0:1] * 16.0 + got[1:2] + got[3:4] * 1024.0 - 1024.0
    one_hot_rows(pick, row.astype(I32))
    slot_bins = jnp.broadcast_to(got[2:3].astype(BF16), (8, got.shape[1]))
    down = mm(pick[...], slot_bins, NT)[:, 0:1].astype(I32)
    across = mm(slot_bins, pick[...], NT)[0:1].astype(I32)
    lane = lax.broadcasted_iota(I32, (shard_rows, 3 * bins), 1)
    wide[...] = jnp.where((lane & (bins - 1)) == down, 1.0, 0.0).astype(BF16)
    deep = lax.broadcasted_iota(I32, (3 * bins, shard_rows), 0)
    hot_ref[...] = jnp.where((deep & (bins - 1)) == across, 1.0, 0.0).astype(BF16)
    weigh(pick[...], wide[...], recv_ref[:, CODE:], ctf_ref, inv_ref, out_ref)


def unpack_next_body(meta, pick_ref, wide_ref, recv_ref, ctf_ref, inv_ref, out_ref):
    weigh(pick_ref[...], wide_ref[...], recv_ref[...], ctf_ref, inv_ref, out_ref)


def unpack_first(meta, recv, ctf, inv, at):
    slots, columns = recv.shape
    width = columns - CODE
    rows = slots // 2
    bins, pix = ctf.shape
    wrap = pix // width
    whole = lambda shape: pl.BlockSpec(shape, lambda j, m: (0, 0))
    shapes = [(rows, width), (3 * bins, rows), (rows, slots), (rows, 3 * bins)]
    return call(
        functools.partial(unpack_first_body, bins),
        (1,),
        [
            whole(recv.shape),
            pl.BlockSpec((bins, width), lambda j, m: (0, lax.rem(at(m), wrap))),
            pl.BlockSpec((1, width), lambda j, m: (0, lax.rem(at(m), wrap))),
        ],
        [whole(s) for s in shapes],
        [sds(s, BF16) for s in shapes],
        flops=2 * slots * rows * width,
        moved=2 * slots * columns,
    )(meta, recv, ctf, inv)


def unpack_next(meta, pick, wide, recv, ctf, inv, at):
    slots, width = recv.shape
    rows = slots // 2
    bins, pix = ctf.shape
    wrap = pix // width
    whole = lambda shape: pl.BlockSpec(shape, lambda j, m: (0, 0))
    return call(
        unpack_next_body,
        (1,),
        [
            whole(pick.shape),
            whole(wide.shape),
            whole(recv.shape),
            pl.BlockSpec((bins, width), lambda j, m: (0, lax.rem(at(m), wrap))),
            pl.BlockSpec((1, width), lambda j, m: (0, lax.rem(at(m), wrap))),
        ],
        whole((rows, width)),
        sds((rows, width), BF16),
        flops=2 * slots * rows * width,
        moved=2 * slots * width,
    )(meta, pick, wide, recv, ctf, inv)


def energy_body(bins, count, meta, *refs):
    pieces, (ctf_ref, inv_ref, panel_ref, extra_ref, total) = refs[:count], refs[count:]
    step = pl.program_id(0)

    @pl.when(step == 0)
    def _():
        total[...] = jnp.zeros_like(total)

    gain = ctf_ref[...] * ctf_ref[...] * inv_ref[...]
    gain3 = jnp.concatenate(split3(gain), axis=0)
    for index, piece in enumerate(pieces):

        @pl.when(step == index)
        def _():
            panel = piece[...]
            panel_ref[...] = panel
            wide = panel.astype(F32)
            square = wide * wide
            high = square.astype(BF16)
            low = (square - high.astype(F32)).astype(BF16)
            total[...] += mm(high, gain3, NT) + mm(low, gain3, NT)

    @pl.when(step == count - 1)
    def _():
        whole = total[:, :bins] + total[:, bins : 2 * bins] + total[:, 2 * bins :]
        extra_ref[...] = jnp.concatenate(split3(-0.5 * whole), axis=1)


def energy(meta, pieces, ctf, inv):
    count = len(pieces)
    rows, width = pieces[0].shape
    bins, pix = ctf.shape
    wrap = pix // width
    return call(
        functools.partial(energy_body, bins, count),
        (count,),
        [pl.BlockSpec((rows, width), lambda j, m: (0, 0))] * count
        + [
            pl.BlockSpec((bins, width), lambda j, m: (0, lax.rem(m[0] ^ j, wrap))),
            pl.BlockSpec((1, width), lambda j, m: (0, lax.rem(m[0] ^ j, wrap))),
        ],
        [
            pl.BlockSpec((rows, width), lambda j, m: (0, m[0] ^ j)),
            pl.BlockSpec((rows, 3 * bins), lambda j, m: (0, 0)),
        ],
        [sds((rows, count * width), BF16), sds((rows, 3 * bins), BF16)],
        scratch=[pltpu.VMEM((rows, 3 * bins), F32)],
        flops=2 * 4 * rows * bins * count * width * 3,
        moved=4 * rows * count * width,
    )(meta, *pieces, ctf, inv)


def score_body(first, last, meta, *refs):
    own, sib, panel_ref, refs = refs[:2], refs[2:4], refs[4], refs[5:]
    if first:
        acc_out, full_ref = refs
    elif last:
        acc_ref, _, hot_own, hot_sib, extra_ref, shifted_ref, stat_ref, full_ref = refs
    else:
        acc_ref, _, acc_out, full_ref = refs
    half = pl.num_programs(0) // 2

    def tile(sources, hot):
        block = jnp.concatenate([source[...] for source in sources], axis=1)
        full_ref[...] = block
        total = mm(panel_ref[...], block, NT)
        if not first:
            total = acc_ref[...] + total
        if not last:
            acc_out[...] = total
            return
        total = total + mm(extra_ref[...], hot[...], NN)
        peak = jnp.max(total, axis=0, keepdims=True)
        shifted = jnp.exp(total - peak)
        shifted_ref[...] = shifted
        mass = jnp.sum(shifted, axis=0, keepdims=True)
        which = lax.broadcasted_iota(I32, stat_ref.shape, 0)
        stat_ref[...] = jnp.where(which == 0, peak, mass)

    @pl.when(pl.program_id(0) < half)
    def _():
        tile(own, hot_own if last else None)

    @pl.when(pl.program_id(0) >= half)
    def _():
        tile(sib, hot_sib if last else None)


def score(meta, turn, turns, own, sib, panels, acc, full, hots=None, extra=None):
    rows, part = own[0].shape
    width = len(own) * part
    tile = 256
    half = rows // tile
    count = panels.shape[0]
    first, last = turn == 0, turn == turns - 1

    def share(m):
        return lax.rem(m[1] + turns - turn, turns)

    front = pl.BlockSpec((tile, part), lambda j, m: (jnp.minimum(j, half - 1), 0))
    back = pl.BlockSpec((tile, part), lambda j, m: (jnp.maximum(j - half, 0), 0))
    acc_spec = pl.BlockSpec((count, tile), lambda j, m: (0, j))
    full_spec = pl.BlockSpec((tile, width), lambda j, m: (j, share(m)))
    in_specs = [front, front, back, back]
    in_specs += [pl.BlockSpec((count, width), lambda j, m: (0, share(m)))]
    operands = [meta, *own, *sib, panels]
    alias = {}
    if not first:
        in_specs += [acc_spec, pl.BlockSpec(memory_space=pl.ANY)]
        operands += [acc, full]
        alias = {6: 0, 7: 2 if last else 1}
    out_specs = [acc_spec, full_spec]
    full_shape = sds((2 * rows, width * turns), BF16)
    out_shape = [sds((count, 2 * rows), F32), full_shape]
    if last:
        depth = extra.shape[1]
        in_specs += [
            pl.BlockSpec((depth, tile), lambda j, m: (0, jnp.minimum(j, half - 1))),
            pl.BlockSpec((depth, tile), lambda j, m: (0, jnp.maximum(j - half, 0))),
            pl.BlockSpec((count, depth), lambda j, m: (0, 0)),
        ]
        operands += [*hots, extra]
        out_specs = [acc_spec, pl.BlockSpec((8, tile), lambda j, m: (0, j)), full_spec]
        out_shape = [out_shape[0], sds((8, 2 * rows), F32), full_shape]
    return call(
        functools.partial(score_body, first, last),
        (2 * half,),
        in_specs,
        out_specs,
        out_shape,
        alias=alias,
        flops=2 * count * 2 * rows * width,
        moved=8 * count * 2 * rows + 8 * rows * width,
    )(*operands)


def merge_body(meta, mine_ref, other_ref, out_ref):
    rows = mine_ref.shape[1] // 2
    other = other_ref[...]
    other = jnp.concatenate([other[:, rows:], other[:, :rows]], axis=1)
    mine = mine_ref[...]
    peak = jnp.maximum(mine[0:1], other[0:1])
    mass = mine[1:2] * jnp.exp(mine[0:1] - peak) + other[1:2] * jnp.exp(other[0:1] - peak)
    which = lax.broadcasted_iota(I32, out_ref.shape, 0)
    out_ref[...] = jnp.where(which == 0, peak, mass)


def merge(meta, mine, other):
    spec = pl.BlockSpec(mine.shape, lambda j, m: (0, 0))
    return call(merge_body, (1,), [spec, spec], spec, sds(mine.shape, F32))(meta, mine, other)


def class_body(kind, steps, meta, *refs):
    if kind == "first":
        (shifted_ref, stat_ref), four, full_ref = refs[:2], refs[2:6], refs[6]
        outs, (post_ref, log_ref) = refs[7 : 7 + steps], refs[7 + steps :]

        @pl.when(pl.program_id(0) == 0)
        def _():
            stats = [ref[...] for ref in four]
            peaks = [s[0:1] for s in stats]
            peak = jnp.maximum(jnp.maximum(peaks[0], peaks[1]), jnp.maximum(peaks[2], peaks[3]))
            parts = [s[1:2] * jnp.exp(p - peak) for s, p in zip(stats, peaks)]
            mass = (parts[0] + parts[1]) + (parts[2] + parts[3])
            factor = jnp.exp(stat_ref[0:1] - peak) / mass
            post_ref[...] = (shifted_ref[...] * factor).astype(BF16)
            log_ref[...] = (peak + jnp.log(mass))[:, : log_ref.shape[1]]

    elif kind == "mass":
        post_ref, hot_own, hot_sib, full_ref = refs[:4]
        outs, mass_ref = refs[4 : 4 + steps], refs[4 + steps]
        bins, _ = mass_ref.shape
        rows = hot_own.shape[1]

        @pl.when(pl.program_id(0) == 0)
        def _():
            mass_ref[...] = mm(hot_own[:bins, :], post_ref[:, :rows], NT) + mm(
                hot_sib[:bins, :], post_ref[:, rows:], NT
            )

    else:
        (post_ref, full_ref), outs = refs[:2], refs[2:]
    for step, out_ref in enumerate(outs):

        @pl.when(pl.program_id(0) == step)
        def _():
            out_ref[...] = mm(post_ref[...], full_ref[...], NN).astype(out_ref.dtype)


def class_part(meta, kind, offset, steps, full, post=None, shifted=None, stats=None, hots=None, bins=0):
    rows, columns = full.shape
    width = columns // 8
    count = (shifted if post is None else post).shape[0]
    whole = lambda shape: pl.BlockSpec(shape, lambda j, m: (0, 0))
    full_spec = pl.BlockSpec((rows, width), lambda j, m: (0, m[offset + j]))
    out_specs = [whole((count, width))] * steps
    out_shape = [sds((count, width), F32 if kind == "rest" else BF16)] * steps
    if kind == "first":
        operands = [shifted, *stats, full]
        in_specs = [whole(shifted.shape)] + [whole(stats[0].shape)] * 5 + [full_spec]
        out_specs += [whole((count, rows)), whole((1, rows // 2))]
        out_shape += [sds((count, rows), BF16), sds((1, rows // 2), F32)]
    elif kind == "mass":
        operands = [post, *hots, full]
        in_specs = [whole(post.shape), whole(hots[0].shape), whole(hots[1].shape), full_spec]
        out_specs += [whole((bins, count))]
        out_shape += [sds((bins, count), F32)]
    else:
        operands = [post, full]
        in_specs = [whole(post.shape), full_spec]
    return call(
        functools.partial(class_body, kind, steps),
        (steps,),
        in_specs,
        out_specs,
        out_shape,
        flops=2 * count * rows * width * steps,
        moved=2 * rows * width * steps + 4 * count * (rows + width * steps),
    )(meta, *operands)


def forward_body(meta, a_sum, b_sum, down_ref, left_ref, a_ref, b_ref):
    even = meta[0] % 2 == 0
    down, left = down_ref[...].astype(F32), left_ref[...].astype(F32)
    a_ref[...] = (a_sum[...] + jnp.where(even, down, left)).astype(BF16)
    b_ref[...] = (b_sum[...] + jnp.where(even, left, down)).astype(BF16)


def forward(meta, a_sum, b_sum, got_x, got_y):
    shape = a_sum.shape
    spec = pl.BlockSpec((shape[0] // 5, shape[1]), lambda j, m: (j, 0))
    return call(forward_body, (5,), [spec] * 4, [spec] * 2, [sds(shape, BF16)] * 2)(
        meta, a_sum, b_sum, got_x, got_y
    )


def finish_body(meta, keep_ref, a_ref, c_ref, other_ref, b_ref, d_ref, out_ref):
    half = pl.num_programs(0) // 2
    wide = lambda ref: ref[...].astype(F32)

    @pl.when(pl.program_id(0) < half)
    def _():
        out_ref[...] = keep_ref[...] + wide(c_ref) + wide(a_ref)

    @pl.when(pl.program_id(0) >= half)
    def _():
        out_ref[...] = wide(other_ref) + wide(d_ref) + wide(b_ref)


def finish(meta, keep, got_a, got_c, got_self, got_b, got_d):
    count, width = keep.shape
    half = 5
    tile = count // half
    front = pl.BlockSpec((tile, width), lambda j, m: (jnp.minimum(j, half - 1), 0))
    back = pl.BlockSpec((tile, width), lambda j, m: (jnp.maximum(j - half, 0), 0))

    def place(j, m):
        core = lax.rem(m[0], 2)
        return jnp.where(j < half, core * half + j, (1 - core) * half + j - half), 0

    return call(
        finish_body,
        (2 * half,),
        [front] * 3 + [back] * 3,
        pl.BlockSpec((tile, width), place),
        sds((2 * count, width), F32),
    )(meta, keep, got_a, got_c, got_self, got_b, got_d)


def two_by_two(raw_images, defocus_bin, dest_row, ctf_table, inv_noise, panels):
    dom, turns = lax.axis_size("dom"), lax.axis_size("rot")
    device, plane = lax.axis_index("dom"), lax.axis_index("rot")
    bins = ctf_table.shape[0]
    columns = raw_images.shape[1]
    chip, core = device // 2, device % 2

    def block(apart, half):
        return (chip ^ apart) * 2 + half

    x_first, y_second = block(1, 0), block(2, 1)
    x_second, y_first = block(1, 1), block(2, 0)
    even = core == 0
    order = [
        device,
        plane,
        block(3, 0),
        block(3, 1),
        jnp.where(even, x_first, y_second),
        jnp.where(even, y_second, x_first),
        block(0, 1 - core),
        jnp.where(even, y_first, x_second),
        jnp.where(even, x_second, y_first),
        block(0, core),
    ]
    meta = jnp.stack(order).astype(I32)
    inv = inv_noise[None, :]

    def across(value, apart):
        return lax.ppermute(value, "dom", [(i, i ^ apart) for i in range(dom)])

    def by_core(value, when_even, when_odd):
        pairs = [(i, i ^ (when_odd if i % 2 else when_even)) for i in range(dom)]
        return lax.ppermute(value, "dom", pairs)

    def onward(value):
        return lax.ppermute(value, "rot", [(i, (i + 1) % turns) for i in range(turns)])

    width = columns // turns // 2
    dest, bin_row = dest_row[None, :], defocus_bin[None, :]
    send_a, place = pack_first(meta, raw_images, dest, bin_row, dom, width, lambda m: 2 * m[1])
    recv_a = lax.all_to_all(send_a, "dom", 0, 0, tiled=True)
    send_b = pack_next(meta, raw_images, place, dom, width, lambda m: 2 * m[1] + 1)
    recv_b = lax.all_to_all(send_b, "dom", 0, 0, tiled=True)

    count = panels.shape[0] // 2
    pieces = [None] * 8
    pieces[0] = lax.dynamic_slice_in_dim(panels, core * count, count, 0)
    pieces[1] = across(lax.dynamic_slice_in_dim(panels, (1 - core) * count, count, 0), 1)
    pieces[2], pieces[4] = across(pieces[0], 2), across(pieces[0], 4)
    pieces[3], pieces[5] = across(pieces[1], 2), across(pieces[1], 4)

    share_a, hot, pick, wide = unpack_first(meta, recv_a, ctf_table, inv, lambda m: 2 * m[1])
    share_b = unpack_next(meta, pick, wide, recv_b, ctf_table, inv, lambda m: 2 * m[1] + 1)
    hots = (hot, across(hot, 1))
    a1, b1 = onward(share_a), onward(share_b)
    a1, *pieces[2:6] = lax.optimization_barrier((a1, *pieces[2:6]))
    pieces[6], pieces[7] = across(pieces[2], 4), across(pieces[5], 2)
    a2, b2 = onward(a1), onward(b1)
    a2, *pieces[6:8] = lax.optimization_barrier((a2, *pieces[6:8]))
    panel_full, extra = energy(meta, pieces, ctf_table, inv)
    a3, b3 = onward(a2), onward(b2)

    own = [(share_a, share_b), (a1, b1), (a2, b2), (a3, b3)]
    acc = full = None
    for turn in range(turns - 1):
        sib = [across(value, 1) for value in own[turn]]
        acc, full = score(meta, turn, turns, own[turn], sib, panel_full, acc, full)
    sib = [across(value, 1) for value in own[-1]]
    shifted, stat, full = score(
        meta, turns - 1, turns, own[-1], sib, panel_full, acc, full, hots, extra
    )

    pair = merge(meta, stat, across(stat, 1))
    others = [
        lax.ppermute(pair, "rot", [(i, i ^ apart) for i in range(turns)]) for apart in (1, 2, 3)
    ]
    to_x, to_y, post, log_evidence = class_part(
        meta, "first", 2, 2, full, shifted=shifted, stats=[stat, pair, *others]
    )
    got_x, got_y = across(to_x, 2), across(to_y, 4)
    send_c, send_d, give, mass = class_part(
        meta, "mass", 4, 3, full, post=post, hots=hots, bins=bins
    )
    a_sum, b_sum, keep = class_part(meta, "rest", 7, 3, full, post=post)
    got_x, got_y, send_c, send_d = lax.optimization_barrier((got_x, got_y, send_c, send_d))
    got_c, got_d = by_core(send_c, 2, 4), by_core(send_d, 5, 3)
    message_a, message_b = forward(meta, a_sum, b_sum, got_x, got_y)
    got_a, got_b = by_core(message_a, 4, 2), by_core(message_b, 3, 5)
    got_self = across(give, 1)
    mass = mass + across(mass, 2)
    mass = mass + across(mass, 4)
    mass_other = across(mass, 1)
    bin_weights = jnp.where(
        even,
        jnp.concatenate([mass, mass_other], axis=1),
        jnp.concatenate([mass_other, mass], axis=1),
    )
    class_sums = finish(meta, keep, got_a, got_c, got_self, got_b, got_d).T
    return class_sums, bin_weights, log_evidence.reshape(-1)


def energy_block(gain_block, panel_piece):
    widened = panel_piece.astype(jnp.float32)
    return lax.dot_general(
        gain_block, widened * widened, (((1,), (1,)), ((), ())), precision=lax.Precision.HIGHEST
    )


def on_device(raw_images, defocus_bin, dest_row, ctf_table, inv_noise, panels):
    dom_count = lax.axis_size("dom")
    bin_count = ctf_table.shape[0]
    columns = raw_images.shape[1]
    hold_rows = raw_images.shape[0]
    shard_rows = hold_rows // 2
    capacity = 2 * shard_rows // dom_count
    is_live = dest_row >= 0
    target = jnp.where(is_live, dest_row // shard_rows, dom_count)
    local_row = dest_row % shard_rows
    marks = (target[:, None] == jnp.arange(dom_count, dtype=jnp.int32)[None, :]).astype(jnp.int32)
    slot_rank = jnp.sum((jnp.cumsum(marks, axis=0) - marks) * marks, axis=1)
    row_code = jnp.where(is_live, local_row * bin_count + defocus_bin, -1)
    padded_images = jnp.concatenate([raw_images, jnp.zeros((1, columns), raw_images.dtype)], axis=0)
    padded_code = jnp.concatenate([row_code, jnp.full((1,), -1, jnp.int32)], axis=0)
    position = jnp.where(is_live, target * capacity + slot_rank, dom_count * capacity)
    slot_count = dom_count * capacity
    source = (
        jnp.full((slot_count,), hold_rows, jnp.int32)
        .at[position]
        .set(jnp.arange(hold_rows, dtype=jnp.int32), mode="drop")
    )
    send_images = padded_images[source].reshape(dom_count, capacity, columns)
    send_code = padded_code[source].reshape(dom_count, capacity)
    recv_images, recv_code = (
        lax.all_to_all(send_images, "dom", split_axis=0, concat_axis=0, tiled=True),
        lax.all_to_all(send_code, "dom", split_axis=0, concat_axis=0, tiled=True),
    )
    flat_images = recv_images.reshape(-1, columns)
    flat_code = recv_code.reshape(-1)
    arrived = flat_code >= 0
    row_of = jnp.where(arrived, flat_code // bin_count, shard_rows)
    row_order = (
        jnp.zeros((shard_rows,), jnp.int32)
        .at[row_of]
        .set(jnp.arange(flat_code.shape[0], dtype=jnp.int32), mode="drop")
    )
    images = flat_images[row_order]
    bin_ids = flat_code[row_order] % bin_count
    bin_table = (bin_ids[:, None] == jnp.arange(bin_count, dtype=jnp.int32)[None, :]).astype(
        jnp.float32
    )
    ctf_rows = jnp.dot(bin_table, ctf_table, precision=lax.Precision.HIGHEST)
    factor = ctf_rows * inv_noise[None, :]
    weighted = (images.astype(jnp.float32) * jnp.concatenate([factor, factor], axis=1)).astype(
        jnp.bfloat16
    )
    gain_half = ctf_table * ctf_table * inv_noise[None, :]
    gain_full = jnp.concatenate([gain_half, gain_half], axis=1)
    panel_piece = lax.all_gather(panels, "dom", axis=1, tiled=True)
    col_block = weighted
    cross_term = lax.dot_general(
        col_block, panel_piece, (((1,), (1,)), ((), ())), preferred_element_type=jnp.float32
    )
    energy = energy_block(gain_full, panel_piece)
    scores = cross_term - 0.5 * jnp.dot(bin_table, energy, precision=lax.Precision.HIGHEST)
    local_peak = jnp.max(scores, axis=1)
    row_peak = lax.pmax(local_peak, "rot")
    shifted = jnp.exp(scores - row_peak[:, None])
    row_total = lax.psum(jnp.sum(shifted, axis=1), "rot")
    posterior = (shifted / row_total[:, None]).astype(jnp.bfloat16)
    log_evidence = row_peak + jnp.log(row_total)
    col_block = weighted
    class_sums = lax.psum_scatter(
        lax.dot_general(
            col_block, posterior, (((0,), (0,)), ((), ())), preferred_element_type=jnp.float32
        ).astype(jnp.bfloat16),
        "dom",
        scatter_dimension=0,
        tiled=True,
    ).astype(jnp.float32)
    local_mass = lax.dot_general(
        bin_table.astype(jnp.bfloat16),
        posterior,
        (((0,), (0,)), ((), ())),
        preferred_element_type=jnp.float32,
    )
    bin_weights = lax.psum(local_mass.astype(jnp.bfloat16), "dom").astype(jnp.float32)
    return (class_sums, bin_weights, log_evidence)


def solution(mesh):
    small = mesh.shape["dom"] == 8 and mesh.shape["rot"] == 4
    return jax.shard_map(
        two_by_two if small else on_device,
        mesh=mesh,
        in_specs=(P("dom", None), P("dom"), P("dom"), P(), P(), P("rot", "dom")),
        out_specs=(P("dom", "rot"), P(None, "rot"), P("dom")),
        check_vma=False,
    )
```

```python
import functools

import jax
import jax.numpy as jnp
from jax import lax
from jax.experimental import pallas as pl
from jax.experimental.pallas import tpu as pltpu
from jax.sharding import PartitionSpec as P

NN = (((1,), (0,)), ((), ()))
NT = (((1,), (1,)), ((), ()))
F32, BF16, I32 = jnp.float32, jnp.bfloat16, jnp.int32
CODE = 128
MIB = 1024 * 1024


def mm(a, b, dims):
    return lax.dot_general(a, b, dims, preferred_element_type=F32)


def split3(x):
    hi = x.astype(BF16)
    rest = x - hi.astype(F32)
    mid = rest.astype(BF16)
    low = (rest - mid.astype(F32)).astype(BF16)
    return hi, mid, low


def call(body, grid, in_specs, out_specs, out_shape, scratch=(), alias=None, flops=0, moved=0, room=24):
    return pl.pallas_call(
        body,
        grid_spec=pltpu.PrefetchScalarGridSpec(
            num_scalar_prefetch=1,
            grid=grid,
            in_specs=in_specs,
            out_specs=out_specs,
            scratch_shapes=list(scratch),
        ),
        out_shape=out_shape,
        input_output_aliases=alias or {},
        compiler_params=pltpu.CompilerParams(vmem_limit_bytes=room * MIB),
        cost_estimate=pl.CostEstimate(flops=flops, bytes_accessed=moved, transcendentals=0),
    )


def sds(shape, dtype):
    return jax.ShapeDtypeStruct(shape, dtype)


def one_hot_rows(out_ref, wanted):
    rows, width = out_ref.shape
    step = 256 if rows % 256 == 0 else rows
    for start in range(0, rows, step):
        index = lax.broadcasted_iota(I32, (step, width), 0) + start
        out_ref[start : start + step, :] = jnp.where(index == wanted, 1.0, 0.0).astype(BF16)


def places_of(dest, shard_rows, cap, dom, device):
    hold = dest.shape[1]
    low = lax.broadcasted_iota(I32, (dom, hold), 0) * shard_rows
    inside = jnp.logical_and(dest >= low, dest < low + shard_rows)
    marks = jnp.where(inside, 1.0, 0.0)
    local = dest - jnp.sum(jnp.where(inside, low, 0), axis=0, keepdims=True)
    lanes = 128
    before = lax.broadcasted_iota(I32, (lanes, lanes), 0) < lax.broadcasted_iota(
        I32, (lanes, lanes), 1
    )
    upper = jnp.where(before, 1.0, 0.0).astype(BF16)
    apart = lax.broadcasted_iota(I32, (dom, 1), 0) ^ device
    carry = apart.astype(F32) * cap + 1.0
    found = []
    for start in range(0, hold, lanes):
        part = marks[:, start : start + lanes]
        rank = mm(part.astype(BF16), upper, NN) + carry
        found.append(jnp.sum(jnp.where(part > 0, rank, 0.0), axis=0, keepdims=True))
        carry = carry + jnp.sum(part, axis=1, keepdims=True)
    return jnp.concatenate(found, axis=1).astype(I32) - 1, local


def pack_first_body(dom, shard_rows, cap, meta, dest_ref, bin_ref, raw_ref, *refs):
    outs, (place_ref, pick) = refs[:dom], refs[dom:]
    dest = dest_ref[...]
    place, local = places_of(dest, shard_rows, cap, dom, meta[0])
    place_ref[...] = place
    one_hot_rows(pick, place)
    which = lax.broadcasted_iota(I32, (CODE, dest.shape[1]), 0)
    digits = jnp.where(
        which == 0,
        local >> 4,
        jnp.where(which == 1, local & 15, jnp.where(which == 2, bin_ref[...], jnp.where(which == 3, 1, 0))),
    )
    digits = jnp.where(dest >= 0, digits, 0).astype(F32).astype(BF16)
    codes = mm(pick[...], digits, NT).astype(BF16)
    packed = mm(pick[...], raw_ref[...], NN).astype(BF16)
    for index, out_ref in enumerate(outs):
        out_ref[:, :CODE] = codes[index * cap : (index + 1) * cap]
        out_ref[:, CODE:] = packed[index * cap : (index + 1) * cap]


def pack_next_body(cap, meta, place_ref, raw_ref, *refs):
    outs, pick = refs[:-1], refs[-1]
    one_hot_rows(pick, place_ref[...])
    packed = mm(pick[...], raw_ref[...], NN).astype(BF16)
    for index, out_ref in enumerate(outs):
        out_ref[...] = packed[index * cap : (index + 1) * cap]


def pack_first(meta, raw_images, dest, bins, dom, width, at):
    hold, _ = raw_images.shape
    cap = hold // dom
    slots = dom * cap
    row = pl.BlockSpec((1, hold), lambda j, m: (0, 0))
    return call(
        functools.partial(pack_first_body, dom, hold // 2, cap),
        (1,),
        [row, row, pl.BlockSpec((hold, width), lambda j, m: (0, at(m)))],
        [pl.BlockSpec((cap, CODE + width), lambda j, m: (0, 0))] * dom + [row],
        [sds((cap, CODE + width), BF16)] * dom + [sds((1, hold), I32)],
        scratch=[pltpu.VMEM((slots, hold), BF16)],
        flops=2 * slots * hold * width,
        moved=4 * hold * width,
    )(meta, dest, bins, raw_images)


def pack_next(meta, raw_images, place, dom, width, at):
    hold, _ = raw_images.shape
    cap = hold // dom
    slots = dom * cap
    return call(
        functools.partial(pack_next_body, cap),
        (1,),
        [
            pl.BlockSpec((1, hold), lambda j, m: (0, 0)),
            pl.BlockSpec((hold, width), lambda j, m: (0, at(m))),
        ],
        [pl.BlockSpec((cap, width), lambda j, m: (0, 0))] * dom,
        [sds((cap, width), BF16)] * dom,
        scratch=[pltpu.VMEM((slots, hold), BF16)],
        flops=2 * slots * hold * width,
        moved=4 * hold * width,
    )(meta, place, raw_images)


def weigh(pick, wide, recv, ctf_ref, inv_ref, out_ref):
    table = jnp.concatenate(split3(ctf_ref[...] * inv_ref[...]), axis=0)
    factor = mm(wide, table, NN)
    out_ref[...] = (mm(pick, recv, NN) * factor).astype(BF16)


def gather(pieces, whole):
    rows = pieces[0].shape[0]
    for index, piece in enumerate(pieces):
        whole[index * rows : (index + 1) * rows, :] = piece[...]


def unpack_first_body(dom, bins, meta, *refs):
    recv_ref = refs[-1]
    gather(refs[:dom], recv_ref)
    ctf_ref, inv_ref, out_ref, hot_ref, pick, wide = refs[dom:-1]
    shard_rows = out_ref.shape[0]
    chosen = jnp.where(
        lax.broadcasted_iota(I32, (8, CODE), 0) == lax.broadcasted_iota(I32, (8, CODE), 1), 1.0, 0.0
    ).astype(BF16)
    got = mm(chosen, recv_ref[:, :CODE], NT)
    row = got[0:1] * 16.0 + got[1:2] + got[3:4] * 1024.0 - 1024.0
    one_hot_rows(pick, row.astype(I32))
    slot_bins = jnp.broadcast_to(got[2:3].astype(BF16), (8, got.shape[1]))
    down = mm(pick[...], slot_bins, NT)[:, 0:1].astype(I32)
    across = mm(slot_bins, pick[...], NT)[0:1].astype(I32)
    lane = lax.broadcasted_iota(I32, (shard_rows, 3 * bins), 1)
    wide[...] = jnp.where((lane & (bins - 1)) == down, 1.0, 0.0).astype(BF16)
    deep = lax.broadcasted_iota(I32, (3 * bins, shard_rows), 0)
    hot_ref[...] = jnp.where((deep & (bins - 1)) == across, 1.0, 0.0).astype(BF16)
    weigh(pick[...], wide[...], recv_ref[:, CODE:], ctf_ref, inv_ref, out_ref)


def unpack_next_body(dom, meta, *refs):
    recv_ref = refs[-1]
    gather(refs[:dom], recv_ref)
    pick_ref, wide_ref, ctf_ref, inv_ref, out_ref = refs[dom:-1]
    weigh(pick_ref[...], wide_ref[...], recv_ref[...], ctf_ref, inv_ref, out_ref)


def unpack_first(meta, recv, ctf, inv, at):
    cap, columns = recv[0].shape
    dom = len(recv)
    slots = dom * cap
    width = columns - CODE
    rows = slots // 2
    bins, pix = ctf.shape
    wrap = pix // width
    whole = lambda shape: pl.BlockSpec(shape, lambda j, m: (0, 0))
    shapes = [(rows, width), (3 * bins, rows), (rows, slots), (rows, 3 * bins)]
    return call(
        functools.partial(unpack_first_body, dom, bins),
        (1,),
        [whole(recv[0].shape)] * dom
        + [
            pl.BlockSpec((bins, width), lambda j, m: (0, lax.rem(at(m), wrap))),
            pl.BlockSpec((1, width), lambda j, m: (0, lax.rem(at(m), wrap))),
        ],
        [whole(s) for s in shapes],
        [sds(s, BF16) for s in shapes],
        scratch=[pltpu.VMEM((slots, columns), BF16)],
        flops=2 * slots * rows * width,
        moved=2 * slots * columns,
    )(meta, *recv, ctf, inv)


def unpack_next(meta, pick, wide, recv, ctf, inv, at):
    cap, width = recv[0].shape
    dom = len(recv)
    slots = dom * cap
    rows = slots // 2
    bins, pix = ctf.shape
    wrap = pix // width
    whole = lambda shape: pl.BlockSpec(shape, lambda j, m: (0, 0))
    return call(
        functools.partial(unpack_next_body, dom),
        (1,),
        [whole(recv[0].shape)] * dom
        + [
            whole(pick.shape),
            whole(wide.shape),
            pl.BlockSpec((bins, width), lambda j, m: (0, lax.rem(at(m), wrap))),
            pl.BlockSpec((1, width), lambda j, m: (0, lax.rem(at(m), wrap))),
        ],
        whole((rows, width)),
        sds((rows, width), BF16),
        scratch=[pltpu.VMEM((slots, width), BF16)],
        flops=2 * slots * rows * width,
        moved=2 * slots * width,
    )(meta, *recv, pick, wide, ctf, inv)


def energy_body(bins, count, meta, *refs):
    pieces, (ctf_ref, inv_ref, panel_ref, extra_ref, total) = refs[:count], refs[count:]
    step = pl.program_id(0)

    @pl.when(step == 0)
    def _():
        total[...] = jnp.zeros_like(total)

    gain = ctf_ref[...] * ctf_ref[...] * inv_ref[...]
    gain3 = jnp.concatenate(split3(gain), axis=0)
    for index, piece in enumerate(pieces):

        @pl.when(step == index)
        def _():
            panel = piece[...]
            panel_ref[...] = panel
            wide = panel.astype(F32)
            square = wide * wide
            high = square.astype(BF16)
            low = (square - high.astype(F32)).astype(BF16)
            total[...] += mm(high, gain3, NT) + mm(low, gain3, NT)

    @pl.when(step == count - 1)
    def _():
        whole = total[:, :bins] + total[:, bins : 2 * bins] + total[:, 2 * bins :]
        extra_ref[...] = jnp.concatenate(split3(-0.5 * whole), axis=1)


def energy(meta, pieces, ctf, inv):
    count = len(pieces)
    rows, width = pieces[0].shape
    bins, pix = ctf.shape
    wrap = pix // width
    return call(
        functools.partial(energy_body, bins, count),
        (count,),
        [pl.BlockSpec((rows, width), lambda j, m: (0, 0))] * count
        + [
            pl.BlockSpec((bins, width), lambda j, m: (0, lax.rem(m[0] ^ j, wrap))),
            pl.BlockSpec((1, width), lambda j, m: (0, lax.rem(m[0] ^ j, wrap))),
        ],
        [
            pl.BlockSpec((rows, width), lambda j, m: (0, m[0] ^ j)),
            pl.BlockSpec((rows, 3 * bins), lambda j, m: (0, 0)),
        ],
        [sds((rows, count * width), BF16), sds((rows, 3 * bins), BF16)],
        scratch=[pltpu.VMEM((rows, 3 * bins), F32)],
        flops=2 * 4 * rows * bins * count * width * 3,
        moved=4 * rows * count * width,
    )(meta, *pieces, ctf, inv)


def score_body(first, last, meta, *refs):
    own, sib, panel_ref, refs = refs[:2], refs[2:4], refs[4], refs[5:]
    if first:
        acc_out, full_ref = refs
    elif last:
        acc_ref, _, hot_own, hot_sib, extra_ref, shifted_ref, stat_ref, full_ref = refs
    else:
        acc_ref, _, acc_out, full_ref = refs
    half = pl.num_programs(0) // 2

    def tile(sources, hot):
        block = jnp.concatenate([source[...] for source in sources], axis=1)
        full_ref[...] = block
        total = mm(panel_ref[...], block, NT)
        if not first:
            total = acc_ref[...] + total
        if not last:
            acc_out[...] = total
            return
        total = total + mm(extra_ref[...], hot[...], NN)
        peak = jnp.max(total, axis=0, keepdims=True)
        shifted = jnp.exp(total - peak)
        shifted_ref[...] = shifted
        mass = jnp.sum(shifted, axis=0, keepdims=True)
        which = lax.broadcasted_iota(I32, stat_ref.shape, 0)
        stat_ref[...] = jnp.where(which == 0, peak, mass)

    @pl.when(pl.program_id(0) < half)
    def _():
        tile(own, hot_own if last else None)

    @pl.when(pl.program_id(0) >= half)
    def _():
        tile(sib, hot_sib if last else None)


def score(meta, turn, turns, own, sib, panels, acc, full, hots=None, extra=None):
    rows, part = own[0].shape
    width = len(own) * part
    tile = 256
    half = rows // tile
    count = panels.shape[0]
    first, last = turn == 0, turn == turns - 1

    def share(m):
        return lax.rem(m[1] + turns - turn, turns)

    front = pl.BlockSpec((tile, part), lambda j, m: (jnp.minimum(j, half - 1), 0))
    back = pl.BlockSpec((tile, part), lambda j, m: (jnp.maximum(j - half, 0), 0))
    acc_spec = pl.BlockSpec((count, tile), lambda j, m: (0, j))
    full_spec = pl.BlockSpec((tile, width), lambda j, m: (j, share(m)))
    in_specs = [front, front, back, back]
    in_specs += [pl.BlockSpec((count, width), lambda j, m: (0, share(m)))]
    operands = [meta, *own, *sib, panels]
    alias = {}
    if not first:
        in_specs += [acc_spec, pl.BlockSpec(memory_space=pl.ANY)]
        operands += [acc, full]
        alias = {6: 0, 7: 2 if last else 1}
    out_specs = [acc_spec, full_spec]
    full_shape = sds((2 * rows, width * turns), BF16)
    out_shape = [sds((count, 2 * rows), F32), full_shape]
    if last:
        depth = extra.shape[1]
        in_specs += [
            pl.BlockSpec((depth, tile), lambda j, m: (0, jnp.minimum(j, half - 1))),
            pl.BlockSpec((depth, tile), lambda j, m: (0, jnp.maximum(j - half, 0))),
            pl.BlockSpec((count, depth), lambda j, m: (0, 0)),
        ]
        operands += [*hots, extra]
        out_specs = [acc_spec, pl.BlockSpec((8, tile), lambda j, m: (0, j)), full_spec]
        out_shape = [out_shape[0], sds((8, 2 * rows), F32), full_shape]
    return call(
        functools.partial(score_body, first, last),
        (2 * half,),
        in_specs,
        out_specs,
        out_shape,
        alias=alias,
        flops=2 * count * 2 * rows * width,
        moved=8 * count * 2 * rows + 8 * rows * width,
    )(*operands)


def merge_body(meta, mine_ref, other_ref, out_ref):
    rows = mine_ref.shape[1] // 2
    other = other_ref[...]
    other = jnp.concatenate([other[:, rows:], other[:, :rows]], axis=1)
    mine = mine_ref[...]
    peak = jnp.maximum(mine[0:1], other[0:1])
    mass = mine[1:2] * jnp.exp(mine[0:1] - peak) + other[1:2] * jnp.exp(other[0:1] - peak)
    which = lax.broadcasted_iota(I32, out_ref.shape, 0)
    out_ref[...] = jnp.where(which == 0, peak, mass)


def merge(meta, mine, other):
    spec = pl.BlockSpec(mine.shape, lambda j, m: (0, 0))
    return call(merge_body, (1,), [spec, spec], spec, sds(mine.shape, F32))(meta, mine, other)


def class_body(kind, steps, meta, *refs):
    if kind == "first":
        (shifted_ref, stat_ref), four, full_ref = refs[:2], refs[2:6], refs[6]
        outs, (post_ref, log_ref) = refs[7 : 7 + steps], refs[7 + steps :]

        @pl.when(pl.program_id(0) == 0)
        def _():
            stats = [ref[...] for ref in four]
            peaks = [s[0:1] for s in stats]
            peak = jnp.maximum(jnp.maximum(peaks[0], peaks[1]), jnp.maximum(peaks[2], peaks[3]))
            parts = [s[1:2] * jnp.exp(p - peak) for s, p in zip(stats, peaks)]
            mass = (parts[0] + parts[1]) + (parts[2] + parts[3])
            factor = jnp.exp(stat_ref[0:1] - peak) / mass
            post_ref[...] = (shifted_ref[...] * factor).astype(BF16)
            log_ref[...] = (peak + jnp.log(mass))[:, : log_ref.shape[1]]

    elif kind == "mass":
        post_ref, hot_own, hot_sib, full_ref = refs[:4]
        outs, mass_ref = refs[4 : 4 + steps], refs[4 + steps]
        bins, _ = mass_ref.shape
        rows = hot_own.shape[1]

        @pl.when(pl.program_id(0) == 0)
        def _():
            mass_ref[...] = mm(hot_own[:bins, :], post_ref[:, :rows], NT) + mm(
                hot_sib[:bins, :], post_ref[:, rows:], NT
            )

    else:
        (post_ref, full_ref), outs = refs[:2], refs[2:]
    for step, out_ref in enumerate(outs):

        @pl.when(pl.program_id(0) == step)
        def _():
            out_ref[...] = mm(post_ref[...], full_ref[...], NN).astype(out_ref.dtype)


def class_part(meta, kind, offset, steps, full, post=None, shifted=None, stats=None, hots=None, bins=0):
    rows, columns = full.shape
    width = columns // 8
    count = (shifted if post is None else post).shape[0]
    whole = lambda shape: pl.BlockSpec(shape, lambda j, m: (0, 0))
    full_spec = pl.BlockSpec((rows, width), lambda j, m: (0, m[offset + j]))
    out_specs = [whole((count, width))] * steps
    out_shape = [sds((count, width), F32 if kind == "rest" else BF16)] * steps
    if kind == "first":
        operands = [shifted, *stats, full]
        in_specs = [whole(shifted.shape)] + [whole(stats[0].shape)] * 5 + [full_spec]
        out_specs += [whole((count, rows)), whole((1, rows // 2))]
        out_shape += [sds((count, rows), BF16), sds((1, rows // 2), F32)]
    elif kind == "mass":
        operands = [post, *hots, full]
        in_specs = [whole(post.shape), whole(hots[0].shape), whole(hots[1].shape), full_spec]
        out_specs += [whole((bins, count))]
        out_shape += [sds((bins, count), F32)]
    else:
        operands = [post, full]
        in_specs = [whole(post.shape), full_spec]
    return call(
        functools.partial(class_body, kind, steps),
        (steps,),
        in_specs,
        out_specs,
        out_shape,
        flops=2 * count * rows * width * steps,
        moved=2 * rows * width * steps + 4 * count * (rows + width * steps),
    )(meta, *operands)


def forward_body(meta, a_sum, b_sum, down_ref, left_ref, a_ref, b_ref):
    even = meta[0] % 2 == 0
    down, left = down_ref[...].astype(F32), left_ref[...].astype(F32)
    a_ref[...] = (a_sum[...] + jnp.where(even, down, left)).astype(BF16)
    b_ref[...] = (b_sum[...] + jnp.where(even, left, down)).astype(BF16)


def forward(meta, a_sum, b_sum, got_x, got_y):
    shape = a_sum.shape
    spec = pl.BlockSpec((shape[0] // 5, shape[1]), lambda j, m: (j, 0))
    return call(forward_body, (5,), [spec] * 4, [spec] * 2, [sds(shape, BF16)] * 2)(
        meta, a_sum, b_sum, got_x, got_y
    )


def finish_body(meta, keep_ref, a_ref, c_ref, other_ref, b_ref, d_ref, out_ref):
    half = pl.num_programs(0) // 2
    wide = lambda ref: ref[...].astype(F32)

    @pl.when(pl.program_id(0) < half)
    def _():
        out_ref[...] = keep_ref[...] + wide(c_ref) + wide(a_ref)

    @pl.when(pl.program_id(0) >= half)
    def _():
        out_ref[...] = wide(other_ref) + wide(d_ref) + wide(b_ref)


def finish(meta, keep, got_a, got_c, got_self, got_b, got_d):
    count, width = keep.shape
    half = 5
    tile = count // half
    front = pl.BlockSpec((tile, width), lambda j, m: (jnp.minimum(j, half - 1), 0))
    back = pl.BlockSpec((tile, width), lambda j, m: (jnp.maximum(j - half, 0), 0))

    def place(j, m):
        core = lax.rem(m[0], 2)
        return jnp.where(j < half, core * half + j, (1 - core) * half + j - half), 0

    return call(
        finish_body,
        (2 * half,),
        [front] * 3 + [back] * 3,
        pl.BlockSpec((tile, width), place),
        sds((2 * count, width), F32),
    )(meta, keep, got_a, got_c, got_self, got_b, got_d)


def two_by_two(raw_images, defocus_bin, dest_row, ctf_table, inv_noise, panels):
    dom, turns = lax.axis_size("dom"), lax.axis_size("rot")
    device, plane = lax.axis_index("dom"), lax.axis_index("rot")
    bins = ctf_table.shape[0]
    columns = raw_images.shape[1]
    chip, core = device // 2, device % 2

    def block(apart, half):
        return (chip ^ apart) * 2 + half

    x_first, y_second = block(1, 0), block(2, 1)
    x_second, y_first = block(1, 1), block(2, 0)
    even = core == 0
    order = [
        device,
        plane,
        block(3, 0),
        block(3, 1),
        jnp.where(even, x_first, y_second),
        jnp.where(even, y_second, x_first),
        block(0, 1 - core),
        jnp.where(even, y_first, x_second),
        jnp.where(even, x_second, y_first),
        block(0, core),
    ]
    meta = jnp.stack(order).astype(I32)
    inv = inv_noise[None, :]

    def across(value, apart):
        return lax.ppermute(value, "dom", [(i, i ^ apart) for i in range(dom)])

    def by_core(value, when_even, when_odd):
        pairs = [(i, i ^ (when_odd if i % 2 else when_even)) for i in range(dom)]
        return lax.ppermute(value, "dom", pairs)

    def onward(value):
        return lax.ppermute(value, "rot", [(i, (i + 1) % turns) for i in range(turns)])

    width = columns // turns // 2
    dest, bin_row = dest_row[None, :], defocus_bin[None, :]
    def exchange(blocks):
        got = [blocks[0]] + [None] * (dom - 1)
        for apart in (6, 7, 2, 4, 3, 5, 1):
            got[apart] = across(blocks[apart], apart)
        return got

    *send_a, place = pack_first(meta, raw_images, dest, bin_row, dom, width, lambda m: 2 * m[1])
    recv_a = exchange(send_a)
    send_b = pack_next(meta, raw_images, place, dom, width, lambda m: 2 * m[1] + 1)
    recv_b = exchange(send_b)

    count = panels.shape[0] // 2
    pieces = [None] * 8
    pieces[0] = lax.dynamic_slice_in_dim(panels, core * count, count, 0)
    pieces[1] = across(lax.dynamic_slice_in_dim(panels, (1 - core) * count, count, 0), 1)
    recv_a[1], *pieces[:2] = lax.optimization_barrier((recv_a[1], *pieces[:2]))
    pieces[2], pieces[4] = across(pieces[0], 2), across(pieces[0], 4)
    pieces[3], pieces[5] = across(pieces[1], 2), across(pieces[1], 4)

    share_a, hot, pick, wide = unpack_first(meta, recv_a, ctf_table, inv, lambda m: 2 * m[1])
    share_b = unpack_next(meta, pick, wide, recv_b, ctf_table, inv, lambda m: 2 * m[1] + 1)
    hots = (hot, across(hot, 1))
    a1, b1 = onward(share_a), onward(share_b)
    b1, *pieces[2:6] = lax.optimization_barrier((b1, *pieces[2:6]))
    pieces[6], pieces[7] = across(pieces[2], 4), across(pieces[5], 2)
    a2, b2 = onward(a1), onward(b1)
    panel_full, extra = energy(meta, pieces, ctf_table, inv)
    b2, panel_full, extra = lax.optimization_barrier((b2, panel_full, extra))
    a3, b3 = onward(a2), onward(b2)

    own = [(share_a, share_b), (a1, b1), (a2, b2), (a3, b3)]
    acc = full = None
    for turn in range(turns - 1):
        sib = [across(value, 1) for value in own[turn]]
        acc, full = score(meta, turn, turns, own[turn], sib, panel_full, acc, full)
    a3, b3, acc, full = lax.optimization_barrier((a3, b3, acc, full))
    own[-1] = (a3, b3)
    sib = [across(value, 1) for value in own[-1]]
    shifted, stat, full = score(
        meta, turns - 1, turns, own[-1], sib, panel_full, acc, full, hots, extra
    )

    pair = merge(meta, stat, across(stat, 1))
    others = [
        lax.ppermute(pair, "rot", [(i, i ^ apart) for i in range(turns)]) for apart in (1, 2, 3)
    ]
    to_x, to_y, post, log_evidence = class_part(
        meta, "first", 2, 2, full, shifted=shifted, stats=[stat, pair, *others]
    )
    got_x, got_y = across(to_x, 2), across(to_y, 4)
    send_c, send_d, give, mass = class_part(
        meta, "mass", 4, 3, full, post=post, hots=hots, bins=bins
    )
    a_sum, b_sum, keep = class_part(meta, "rest", 7, 3, full, post=post)
    got_x, got_y, send_c, send_d, a_sum, b_sum, keep = lax.optimization_barrier(
        (got_x, got_y, send_c, send_d, a_sum, b_sum, keep)
    )
    got_c, got_d = by_core(send_c, 2, 4), by_core(send_d, 5, 3)
    message_a, message_b = forward(meta, a_sum, b_sum, got_x, got_y)
    got_a, got_b = by_core(message_a, 4, 2), by_core(message_b, 3, 5)
    got_self = across(give, 1)
    mass = mass + across(mass, 2)
    mass = mass + across(mass, 4)
    mass_other = across(mass, 1)
    bin_weights = jnp.where(
        even,
        jnp.concatenate([mass, mass_other], axis=1),
        jnp.concatenate([mass_other, mass], axis=1),
    )
    class_sums = finish(meta, keep, got_a, got_c, got_self, got_b, got_d).T
    return class_sums, bin_weights, log_evidence.reshape(-1)


def energy_block(gain_block, panel_piece):
    widened = panel_piece.astype(jnp.float32)
    return lax.dot_general(
        gain_block, widened * widened, (((1,), (1,)), ((), ())), precision=lax.Precision.HIGHEST
    )


def on_device(raw_images, defocus_bin, dest_row, ctf_table, inv_noise, panels):
    dom_count = lax.axis_size("dom")
    bin_count = ctf_table.shape[0]
    columns = raw_images.shape[1]
    hold_rows = raw_images.shape[0]
    shard_rows = hold_rows // 2
    capacity = 2 * shard_rows // dom_count
    is_live = dest_row >= 0
    target = jnp.where(is_live, dest_row // shard_rows, dom_count)
    local_row = dest_row % shard_rows
    marks = (target[:, None] == jnp.arange(dom_count, dtype=jnp.int32)[None, :]).astype(jnp.int32)
    slot_rank = jnp.sum((jnp.cumsum(marks, axis=0) - marks) * marks, axis=1)
    row_code = jnp.where(is_live, local_row * bin_count + defocus_bin, -1)
    padded_images = jnp.concatenate([raw_images, jnp.zeros((1, columns), raw_images.dtype)], axis=0)
    padded_code = jnp.concatenate([row_code, jnp.full((1,), -1, jnp.int32)], axis=0)
    position = jnp.where(is_live, target * capacity + slot_rank, dom_count * capacity)
    slot_count = dom_count * capacity
    source = (
        jnp.full((slot_count,), hold_rows, jnp.int32)
        .at[position]
        .set(jnp.arange(hold_rows, dtype=jnp.int32), mode="drop")
    )
    send_images = padded_images[source].reshape(dom_count, capacity, columns)
    send_code = padded_code[source].reshape(dom_count, capacity)
    recv_images, recv_code = (
        lax.all_to_all(send_images, "dom", split_axis=0, concat_axis=0, tiled=True),
        lax.all_to_all(send_code, "dom", split_axis=0, concat_axis=0, tiled=True),
    )
    flat_images = recv_images.reshape(-1, columns)
    flat_code = recv_code.reshape(-1)
    arrived = flat_code >= 0
    row_of = jnp.where(arrived, flat_code // bin_count, shard_rows)
    row_order = (
        jnp.zeros((shard_rows,), jnp.int32)
        .at[row_of]
        .set(jnp.arange(flat_code.shape[0], dtype=jnp.int32), mode="drop")
    )
    images = flat_images[row_order]
    bin_ids = flat_code[row_order] % bin_count
    bin_table = (bin_ids[:, None] == jnp.arange(bin_count, dtype=jnp.int32)[None, :]).astype(
        jnp.float32
    )
    ctf_rows = jnp.dot(bin_table, ctf_table, precision=lax.Precision.HIGHEST)
    factor = ctf_rows * inv_noise[None, :]
    weighted = (images.astype(jnp.float32) * jnp.concatenate([factor, factor], axis=1)).astype(
        jnp.bfloat16
    )
    gain_half = ctf_table * ctf_table * inv_noise[None, :]
    gain_full = jnp.concatenate([gain_half, gain_half], axis=1)
    panel_piece = lax.all_gather(panels, "dom", axis=1, tiled=True)
    col_block = weighted
    cross_term = lax.dot_general(
        col_block, panel_piece, (((1,), (1,)), ((), ())), preferred_element_type=jnp.float32
    )
    energy = energy_block(gain_full, panel_piece)
    scores = cross_term - 0.5 * jnp.dot(bin_table, energy, precision=lax.Precision.HIGHEST)
    local_peak = jnp.max(scores, axis=1)
    row_peak = lax.pmax(local_peak, "rot")
    shifted = jnp.exp(scores - row_peak[:, None])
    row_total = lax.psum(jnp.sum(shifted, axis=1), "rot")
    posterior = (shifted / row_total[:, None]).astype(jnp.bfloat16)
    log_evidence = row_peak + jnp.log(row_total)
    col_block = weighted
    class_sums = lax.psum_scatter(
        lax.dot_general(
            col_block, posterior, (((0,), (0,)), ((), ())), preferred_element_type=jnp.float32
        ).astype(jnp.bfloat16),
        "dom",
        scatter_dimension=0,
        tiled=True,
    ).astype(jnp.float32)
    local_mass = lax.dot_general(
        bin_table.astype(jnp.bfloat16),
        posterior,
        (((0,), (0,)), ((), ())),
        preferred_element_type=jnp.float32,
    )
    bin_weights = lax.psum(local_mass.astype(jnp.bfloat16), "dom").astype(jnp.float32)
    return (class_sums, bin_weights, log_evidence)


def solution(mesh):
    small = mesh.shape["dom"] == 8 and mesh.shape["rot"] == 4
    return jax.shard_map(
        two_by_two if small else on_device,
        mesh=mesh,
        in_specs=(P("dom", None), P("dom"), P("dom"), P(), P(), P("rot", "dom")),
        out_specs=(P("dom", "rot"), P(None, "rot"), P("dom")),
        check_vma=False,
    )
```

```python
import functools

import jax
import jax.numpy as jnp
from jax import lax
from jax.experimental import pallas as pl
from jax.experimental.pallas import tpu as pltpu
from jax.sharding import PartitionSpec as P

NN = (((1,), (0,)), ((), ()))
NT = (((1,), (1,)), ((), ()))
F32, BF16, I32 = jnp.float32, jnp.bfloat16, jnp.int32
CODE = 128
MIB = 1024 * 1024


def mm(a, b, dims):
    return lax.dot_general(a, b, dims, preferred_element_type=F32)


def split3(x):
    hi = x.astype(BF16)
    rest = x - hi.astype(F32)
    mid = rest.astype(BF16)
    low = (rest - mid.astype(F32)).astype(BF16)
    return hi, mid, low


def call(body, grid, in_specs, out_specs, out_shape, scratch=(), alias=None, flops=0, moved=0, room=24):
    return pl.pallas_call(
        body,
        grid_spec=pltpu.PrefetchScalarGridSpec(
            num_scalar_prefetch=1,
            grid=grid,
            in_specs=in_specs,
            out_specs=out_specs,
            scratch_shapes=list(scratch),
        ),
        out_shape=out_shape,
        input_output_aliases=alias or {},
        compiler_params=pltpu.CompilerParams(vmem_limit_bytes=room * MIB),
        cost_estimate=pl.CostEstimate(
            flops=flops // 16, bytes_accessed=moved // 16, transcendentals=0
        ),
    )


def sds(shape, dtype):
    return jax.ShapeDtypeStruct(shape, dtype)


def one_hot_rows(out_ref, wanted):
    rows, width = out_ref.shape
    step = 256 if rows % 256 == 0 else rows
    for start in range(0, rows, step):
        index = lax.broadcasted_iota(I32, (step, width), 0) + start
        out_ref[start : start + step, :] = jnp.where(index == wanted, 1.0, 0.0).astype(BF16)


def places_of(dest, shard_rows, cap, dom, device):
    hold = dest.shape[1]
    low = lax.broadcasted_iota(I32, (dom, hold), 0) * shard_rows
    inside = jnp.logical_and(dest >= low, dest < low + shard_rows)
    marks = jnp.where(inside, 1.0, 0.0)
    local = dest - jnp.sum(jnp.where(inside, low, 0), axis=0, keepdims=True)
    lanes = 128
    before = lax.broadcasted_iota(I32, (lanes, lanes), 0) < lax.broadcasted_iota(
        I32, (lanes, lanes), 1
    )
    upper = jnp.where(before, 1.0, 0.0).astype(BF16)
    apart = lax.broadcasted_iota(I32, (dom, 1), 0) ^ device
    carry = apart.astype(F32) * cap + 1.0
    found = []
    for start in range(0, hold, lanes):
        part = marks[:, start : start + lanes]
        rank = mm(part.astype(BF16), upper, NN) + carry
        found.append(jnp.sum(jnp.where(part > 0, rank, 0.0), axis=0, keepdims=True))
        carry = carry + jnp.sum(part, axis=1, keepdims=True)
    return jnp.concatenate(found, axis=1).astype(I32) - 1, local


def pack_first_body(dom, shard_rows, cap, meta, dest_ref, bin_ref, raw_ref, *refs):
    outs, (place_ref, pick) = refs[:dom], refs[dom:]
    dest = dest_ref[...].reshape(1, dest_ref.shape[0])
    bins = bin_ref[...].reshape(1, dest_ref.shape[0])
    place, local = places_of(dest, shard_rows, cap, dom, meta[0])
    place_ref[...] = place
    one_hot_rows(pick, place)
    which = lax.broadcasted_iota(I32, (CODE, dest.shape[1]), 0)
    digits = jnp.where(
        which == 0,
        local >> 4,
        jnp.where(which == 1, local & 15, jnp.where(which == 2, bins, jnp.where(which == 3, 1, 0))),
    )
    digits = jnp.where(dest >= 0, digits, 0).astype(F32).astype(BF16)
    codes = mm(pick[...], digits, NT).astype(BF16)
    packed = mm(pick[...], raw_ref[...], NN).astype(BF16)
    for index, out_ref in enumerate(outs):
        out_ref[:, :CODE] = codes[index * cap : (index + 1) * cap]
        out_ref[:, CODE:] = packed[index * cap : (index + 1) * cap]


def pack_next_body(cap, meta, place_ref, raw_ref, *refs):
    outs, pick = refs[:-1], refs[-1]
    one_hot_rows(pick, place_ref[...])
    packed = mm(pick[...], raw_ref[...], NN).astype(BF16)
    for index, out_ref in enumerate(outs):
        out_ref[...] = packed[index * cap : (index + 1) * cap]


def pack_first(meta, raw_images, dest, bins, dom, width, at):
    hold, _ = raw_images.shape
    cap = hold // dom
    slots = dom * cap
    row = pl.BlockSpec((1, hold), lambda j, m: (0, 0))
    return call(
        functools.partial(pack_first_body, dom, hold // 2, cap),
        (1,),
        [
            pl.BlockSpec((hold,), lambda j, m: (0,)),
            pl.BlockSpec((hold,), lambda j, m: (0,)),
            pl.BlockSpec((hold, width), lambda j, m: (0, at(m))),
        ],
        [pl.BlockSpec((cap, CODE + width), lambda j, m: (0, 0))] * dom + [row],
        [sds((cap, CODE + width), BF16)] * dom + [sds((1, hold), I32)],
        scratch=[pltpu.VMEM((slots, hold), BF16)],
        room=54,
        flops=2 * slots * hold * width,
        moved=4 * hold * width,
    )(meta, dest, bins, raw_images)


def pack_next(meta, raw_images, place, dom, width, at):
    hold, _ = raw_images.shape
    cap = hold // dom
    slots = dom * cap
    return call(
        functools.partial(pack_next_body, cap),
        (1,),
        [
            pl.BlockSpec((1, hold), lambda j, m: (0, 0)),
            pl.BlockSpec((hold, width), lambda j, m: (0, at(m))),
        ],
        [pl.BlockSpec((cap, width), lambda j, m: (0, 0))] * dom,
        [sds((cap, width), BF16)] * dom,
        scratch=[pltpu.VMEM((slots, hold), BF16)],
        room=54,
        flops=2 * slots * hold * width,
        moved=4 * hold * width,
    )(meta, place, raw_images)


def weigh(pick, wide, recv, ctf_ref, inv_ref, out_ref):
    table = jnp.concatenate(split3(ctf_ref[...] * inv_ref[...]), axis=0)
    factor = mm(wide, table, NN)
    out_ref[...] = (mm(pick, recv, NN) * factor).astype(BF16)


def gather(pieces, whole):
    rows = pieces[0].shape[0]
    for index, piece in enumerate(pieces):
        whole[index * rows : (index + 1) * rows, :] = piece[...]


def unpack_first_body(dom, bins, meta, *refs):
    recv_ref = refs[-1]
    gather(refs[:dom], recv_ref)
    ctf_ref, inv_ref, out_ref, hot_ref, pick, wide = refs[dom:-1]
    shard_rows = out_ref.shape[0]
    chosen = jnp.where(
        lax.broadcasted_iota(I32, (8, CODE), 0) == lax.broadcasted_iota(I32, (8, CODE), 1), 1.0, 0.0
    ).astype(BF16)
    got = mm(chosen, recv_ref[:, :CODE], NT)
    row = got[0:1] * 16.0 + got[1:2] + got[3:4] * 1024.0 - 1024.0
    one_hot_rows(pick, row.astype(I32))
    slot_bins = jnp.broadcast_to(got[2:3].astype(BF16), (8, got.shape[1]))
    down = mm(pick[...], slot_bins, NT)[:, 0:1].astype(I32)
    across = mm(slot_bins, pick[...], NT)[0:1].astype(I32)
    lane = lax.broadcasted_iota(I32, (shard_rows, 3 * bins), 1)
    wide[...] = jnp.where((lane & (bins - 1)) == down, 1.0, 0.0).astype(BF16)
    deep = lax.broadcasted_iota(I32, (3 * bins, shard_rows), 0)
    hot_ref[...] = jnp.where((deep & (bins - 1)) == across, 1.0, 0.0).astype(BF16)
    weigh(pick[...], wide[...], recv_ref[:, CODE:], ctf_ref, inv_ref, out_ref)


def unpack_next_body(dom, meta, *refs):
    recv_ref = refs[-1]
    gather(refs[:dom], recv_ref)
    pick_ref, wide_ref, ctf_ref, inv_ref, out_ref = refs[dom:-1]
    weigh(pick_ref[...], wide_ref[...], recv_ref[...], ctf_ref, inv_ref, out_ref)


def unpack_first(meta, recv, ctf, inv, at):
    cap, columns = recv[0].shape
    dom = len(recv)
    slots = dom * cap
    width = columns - CODE
    rows = slots // 2
    bins, pix = ctf.shape
    wrap = pix // width
    whole = lambda shape: pl.BlockSpec(shape, lambda j, m: (0, 0))
    shapes = [(rows, width), (3 * bins, rows), (rows, slots), (rows, 3 * bins)]
    return call(
        functools.partial(unpack_first_body, dom, bins),
        (1,),
        [whole(recv[0].shape)] * dom
        + [
            pl.BlockSpec((bins, width), lambda j, m: (0, lax.rem(at(m), wrap))),
            pl.BlockSpec((1, width), lambda j, m: (0, lax.rem(at(m), wrap))),
        ],
        [whole(s) for s in shapes],
        [sds(s, BF16) for s in shapes],
        scratch=[pltpu.VMEM((slots, columns), BF16)],
        flops=2 * slots * rows * width,
        moved=2 * slots * columns,
    )(meta, *recv, ctf, inv)


def unpack_next(meta, pick, wide, recv, ctf, inv, at):
    cap, width = recv[0].shape
    dom = len(recv)
    slots = dom * cap
    rows = slots // 2
    bins, pix = ctf.shape
    wrap = pix // width
    whole = lambda shape: pl.BlockSpec(shape, lambda j, m: (0, 0))
    return call(
        functools.partial(unpack_next_body, dom),
        (1,),
        [whole(recv[0].shape)] * dom
        + [
            whole(pick.shape),
            whole(wide.shape),
            pl.BlockSpec((bins, width), lambda j, m: (0, lax.rem(at(m), wrap))),
            pl.BlockSpec((1, width), lambda j, m: (0, lax.rem(at(m), wrap))),
        ],
        whole((rows, width)),
        sds((rows, width), BF16),
        scratch=[pltpu.VMEM((slots, width), BF16)],
        flops=2 * slots * rows * width,
        moved=2 * slots * width,
    )(meta, *recv, pick, wide, ctf, inv)


def energy_body(bins, count, meta, *refs):
    pieces, (ctf_ref, inv_ref, panel_ref, extra_ref, total) = refs[:count], refs[count:]
    step = pl.program_id(0)

    @pl.when(step == 0)
    def _():
        total[...] = jnp.zeros_like(total)

    gain = ctf_ref[...] * ctf_ref[...] * inv_ref[...]
    gain3 = jnp.concatenate(split3(gain), axis=0)
    for index, piece in enumerate(pieces):

        @pl.when(step == index)
        def _():
            panel = piece[...]
            panel_ref[...] = panel
            wide = panel.astype(F32)
            square = wide * wide
            high = square.astype(BF16)
            low = (square - high.astype(F32)).astype(BF16)
            total[...] += mm(high, gain3, NT) + mm(low, gain3, NT)

    @pl.when(step == count - 1)
    def _():
        whole = total[:, :bins] + total[:, bins : 2 * bins] + total[:, 2 * bins :]
        extra_ref[...] = jnp.concatenate(split3(-0.5 * whole), axis=1)


def energy(meta, pieces, ctf, inv):
    count = len(pieces)
    rows, width = pieces[0].shape
    bins, pix = ctf.shape
    wrap = pix // width
    return call(
        functools.partial(energy_body, bins, count),
        (count,),
        [pl.BlockSpec((rows, width), lambda j, m: (0, 0))] * count
        + [
            pl.BlockSpec((bins, width), lambda j, m: (0, lax.rem(m[0] ^ j, wrap))),
            pl.BlockSpec((1, width), lambda j, m: (0, lax.rem(m[0] ^ j, wrap))),
        ],
        [
            pl.BlockSpec((rows, width), lambda j, m: (0, m[0] ^ j)),
            pl.BlockSpec((rows, 3 * bins), lambda j, m: (0, 0)),
        ],
        [sds((rows, count * width), BF16), sds((rows, 3 * bins), BF16)],
        scratch=[pltpu.VMEM((rows, 3 * bins), F32)],
        flops=2 * 4 * rows * bins * count * width * 3,
        moved=4 * rows * count * width,
    )(meta, *pieces, ctf, inv)


def score_body(parts, first, last, meta, *refs):
    own, sib, panel_ref, refs = refs[:parts], refs[parts : 2 * parts], refs[2 * parts], refs[2 * parts + 1 :]
    if first:
        acc_out, full_ref = refs
    elif last:
        acc_ref, _, hot_own, hot_sib, extra_ref, shifted_ref, stat_ref, full_ref = refs
    else:
        acc_ref, _, acc_out, full_ref = refs
    half = pl.num_programs(0) // 2

    def tile(sources, hot):
        block = jnp.concatenate([source[...] for source in sources], axis=1)
        full_ref[...] = block
        total = mm(panel_ref[...], block, NT)
        if not first:
            total = acc_ref[...] + total
        if not last:
            acc_out[...] = total
            return
        total = total + mm(extra_ref[...], hot[...], NN)
        peak = jnp.max(total, axis=0, keepdims=True)
        shifted = jnp.exp(total - peak)
        shifted_ref[...] = shifted
        mass = jnp.sum(shifted, axis=0, keepdims=True)
        which = lax.broadcasted_iota(I32, stat_ref.shape, 0)
        stat_ref[...] = jnp.where(which == 0, peak, mass)

    @pl.when(pl.program_id(0) < half)
    def _():
        tile(own, hot_own if last else None)

    @pl.when(pl.program_id(0) >= half)
    def _():
        tile(sib, hot_sib if last else None)


def score(meta, at, own, sib, panels, acc=None, full=None, hots=None, extra=None):
    rows, part = own[0].shape
    parts = len(own)
    width = parts * part
    tile = 256
    half = rows // tile
    count, columns = panels.shape
    first, last = acc is None, hots is not None
    front = pl.BlockSpec((tile, part), lambda j, m: (jnp.minimum(j, half - 1), 0))
    back = pl.BlockSpec((tile, part), lambda j, m: (jnp.maximum(j - half, 0), 0))
    acc_spec = pl.BlockSpec((count, tile), lambda j, m: (0, j))
    full_spec = pl.BlockSpec((tile, width), lambda j, m: (j, at(m)))
    in_specs = [front] * parts + [back] * parts
    in_specs += [pl.BlockSpec((count, width), lambda j, m: (0, at(m)))]
    operands = [meta, *own, *sib, panels]
    alias = {}
    if not first:
        in_specs += [acc_spec, pl.BlockSpec(memory_space=pl.ANY)]
        alias = {len(operands): 0, len(operands) + 1: 2 if last else 1}
        operands += [acc, full]
    out_specs = [acc_spec, full_spec]
    full_shape = sds((2 * rows, columns), BF16)
    out_shape = [sds((count, 2 * rows), F32), full_shape]
    if last:
        depth = extra.shape[1]
        in_specs += [
            pl.BlockSpec((depth, tile), lambda j, m: (0, jnp.minimum(j, half - 1))),
            pl.BlockSpec((depth, tile), lambda j, m: (0, jnp.maximum(j - half, 0))),
            pl.BlockSpec((count, depth), lambda j, m: (0, 0)),
        ]
        operands += [*hots, extra]
        out_specs = [acc_spec, pl.BlockSpec((8, tile), lambda j, m: (0, j)), full_spec]
        out_shape = [out_shape[0], sds((8, 2 * rows), F32), full_shape]
    return call(
        functools.partial(score_body, parts, first, last),
        (2 * half,),
        in_specs,
        out_specs,
        out_shape,
        alias=alias,
        room=16,
        flops=2 * count * 2 * rows * width,
        moved=8 * count * 2 * rows + 8 * rows * width,
    )(*operands)


def merge_body(meta, mine_ref, other_ref, out_ref):
    rows = mine_ref.shape[1] // 2
    other = other_ref[...]
    other = jnp.concatenate([other[:, rows:], other[:, :rows]], axis=1)
    mine = mine_ref[...]
    peak = jnp.maximum(mine[0:1], other[0:1])
    mass = mine[1:2] * jnp.exp(mine[0:1] - peak) + other[1:2] * jnp.exp(other[0:1] - peak)
    which = lax.broadcasted_iota(I32, out_ref.shape, 0)
    out_ref[...] = jnp.where(which == 0, peak, mass)


def merge(meta, mine, other):
    spec = pl.BlockSpec(mine.shape, lambda j, m: (0, 0))
    return call(merge_body, (1,), [spec, spec], spec, sds(mine.shape, F32), room=4)(meta, mine, other)


def class_body(kind, steps, meta, *refs):
    if kind == "first":
        (shifted_ref, stat_ref), four, full_ref = refs[:2], refs[2:6], refs[6]
        outs, (post_ref, log_ref) = refs[7 : 7 + steps], refs[7 + steps :]

        @pl.when(pl.program_id(0) == 0)
        def _():
            stats = [ref[...] for ref in four]
            peaks = [s[0:1] for s in stats]
            peak = jnp.maximum(jnp.maximum(peaks[0], peaks[1]), jnp.maximum(peaks[2], peaks[3]))
            parts = [s[1:2] * jnp.exp(p - peak) for s, p in zip(stats, peaks)]
            mass = (parts[0] + parts[1]) + (parts[2] + parts[3])
            factor = jnp.exp(stat_ref[0:1] - peak) / mass
            post_ref[...] = (shifted_ref[...] * factor).astype(BF16)
            log_ref[...] = (peak + jnp.log(mass))[:, : log_ref.shape[1]]

    elif kind == "mass":
        post_ref, hot_own, hot_sib, full_ref = refs[:4]
        outs, mass_ref = refs[4 : 4 + steps], refs[4 + steps]
        bins, _ = mass_ref.shape
        rows = hot_own.shape[1]

        @pl.when(pl.program_id(0) == 0)
        def _():
            mass_ref[...] = mm(hot_own[:bins, :], post_ref[:, :rows], NT) + mm(
                hot_sib[:bins, :], post_ref[:, rows:], NT
            )

    else:
        (post_ref, full_ref), outs = refs[:2], refs[2:]
    for step, out_ref in enumerate(outs):

        @pl.when(pl.program_id(0) == step)
        def _():
            out_ref[...] = mm(post_ref[...], full_ref[...], NN).astype(out_ref.dtype)


def class_part(meta, kind, offset, steps, full, post=None, shifted=None, stats=None, hots=None, bins=0):
    rows, columns = full.shape
    width = columns // 8
    count = (shifted if post is None else post).shape[0]
    whole = lambda shape: pl.BlockSpec(shape, lambda j, m: (0, 0))
    full_spec = pl.BlockSpec((rows, width), lambda j, m: (0, m[offset + j]))
    out_specs = [whole((count, width))] * steps
    out_shape = [sds((count, width), F32 if kind == "rest" else BF16)] * steps
    if kind == "first":
        operands = [shifted, *stats, full]
        in_specs = [whole(shifted.shape)] + [whole(stats[0].shape)] * 5 + [full_spec]
        out_specs += [whole((count, rows)), whole((1, rows // 2))]
        out_shape += [sds((count, rows), BF16), sds((1, rows // 2), F32)]
    elif kind == "mass":
        operands = [post, *hots, full]
        in_specs = [whole(post.shape), whole(hots[0].shape), whole(hots[1].shape), full_spec]
        out_specs += [whole((bins, count))]
        out_shape += [sds((bins, count), F32)]
    else:
        operands = [post, full]
        in_specs = [whole(post.shape), full_spec]
    return call(
        functools.partial(class_body, kind, steps),
        (steps,),
        in_specs,
        out_specs,
        out_shape,
        room=22 if kind == "first" else 18,
        flops=2 * count * rows * width * steps,
        moved=2 * rows * width * steps + 4 * count * (rows + width * steps),
    )(meta, *operands)


def forward_body(meta, a_sum, b_sum, down_ref, left_ref, a_ref, b_ref):
    even = meta[0] % 2 == 0
    down, left = down_ref[...].astype(F32), left_ref[...].astype(F32)
    a_ref[...] = (a_sum[...] + jnp.where(even, down, left)).astype(BF16)
    b_ref[...] = (b_sum[...] + jnp.where(even, left, down)).astype(BF16)


def forward(meta, a_sum, b_sum, got_x, got_y):
    shape = a_sum.shape
    spec = pl.BlockSpec((shape[0] // 5, shape[1]), lambda j, m: (j, 0))
    return call(forward_body, (5,), [spec] * 4, [spec] * 2, [sds(shape, BF16)] * 2, room=8)(
        meta, a_sum, b_sum, got_x, got_y
    )


def finish_body(meta, keep_ref, a_ref, c_ref, other_ref, b_ref, d_ref, out_ref):
    half = pl.num_programs(0) // 2
    wide = lambda ref: ref[...].astype(F32)

    @pl.when(pl.program_id(0) < half)
    def _():
        out_ref[...] = keep_ref[...] + wide(c_ref) + wide(a_ref)

    @pl.when(pl.program_id(0) >= half)
    def _():
        out_ref[...] = wide(other_ref) + wide(d_ref) + wide(b_ref)


def finish(meta, keep, got_a, got_c, got_self, got_b, got_d):
    count, width = keep.shape
    half = 3
    tile = count // half
    front = pl.BlockSpec((tile, width), lambda j, m: (jnp.minimum(j, half - 1), 0))
    back = pl.BlockSpec((tile, width), lambda j, m: (jnp.maximum(j - half, 0), 0))

    def place(j, m):
        core = lax.rem(m[0], 2)
        return jnp.where(j < half, core * half + j, (1 - core) * half + j - half), 0

    return call(
        finish_body,
        (2 * half,),
        [front] * 3 + [back] * 3,
        pl.BlockSpec((tile, width), place),
        sds((2 * count, width), F32),
        room=12,
    )(meta, keep, got_a, got_c, got_self, got_b, got_d)


def two_by_two(raw_images, defocus_bin, dest_row, ctf_table, inv_noise, panels):
    dom, turns = lax.axis_size("dom"), lax.axis_size("rot")
    device, plane = lax.axis_index("dom"), lax.axis_index("rot")
    bins = ctf_table.shape[0]
    columns = raw_images.shape[1]
    chip, core = device // 2, device % 2

    def block(apart, half):
        return (chip ^ apart) * 2 + half

    x_first, y_second = block(1, 0), block(2, 1)
    x_second, y_first = block(1, 1), block(2, 0)
    even = core == 0
    order = [
        device,
        plane,
        block(3, 0),
        block(3, 1),
        jnp.where(even, x_first, y_second),
        jnp.where(even, y_second, x_first),
        block(0, 1 - core),
        jnp.where(even, y_first, x_second),
        jnp.where(even, x_second, y_first),
        block(0, core),
    ]
    meta = jnp.stack(order).astype(I32)
    inv = inv_noise[None, :]

    def across(value, apart):
        return lax.ppermute(value, "dom", [(i, i ^ apart) for i in range(dom)])

    def by_core(value, when_even, when_odd):
        pairs = [(i, i ^ (when_odd if i % 2 else when_even)) for i in range(dom)]
        return lax.ppermute(value, "dom", pairs)

    def onward(value):
        return lax.ppermute(value, "rot", [(i, (i + 1) % turns) for i in range(turns)])

    width = columns // turns // 2
    def exchange(blocks):
        got = [blocks[0]] + [None] * (dom - 1)
        for apart in (6, 7, 2, 4, 3, 5, 1):
            got[apart] = across(blocks[apart], apart)
        return got

    *send_a, place = pack_first(meta, raw_images, dest_row, defocus_bin, dom, width, lambda m: 2 * m[1])
    recv_a = exchange(send_a)
    send_b = pack_next(meta, raw_images, place, dom, width, lambda m: 2 * m[1] + 1)
    together = lax.optimization_barrier

    count = panels.shape[0] // 2
    pieces = [None] * 8
    place, panels = together((place, panels))
    pieces[0] = lax.dynamic_slice_in_dim(panels, core * count, count, 0)
    pieces[1] = across(lax.dynamic_slice_in_dim(panels, (1 - core) * count, count, 0), 1)

    recv_a, send_b, pieces[:2] = together((recv_a, send_b, pieces[:2]))
    share_a, hot, pick, wide = unpack_first(meta, recv_a, ctf_table, inv, lambda m: 2 * m[1])
    share_a, send_b = together((share_a, send_b))
    a1, recv_b = onward(share_a), exchange(send_b)
    a1, recv_b, pieces[:2] = together((a1, recv_b, pieces[:2]))
    pieces[2], pieces[4] = across(pieces[0], 2), across(pieces[0], 4)
    pieces[3], pieces[5] = across(pieces[1], 2), across(pieces[1], 4)
    share_b = unpack_next(meta, pick, wide, recv_b, ctf_table, inv, lambda m: 2 * m[1] + 1)
    hots = (hot, across(hot, 1))
    a2, b1 = onward(a1), onward(share_b)
    a2, b1, pieces[2:6] = together((a2, b1, pieces[2:6]))
    pieces[6], pieces[7] = across(pieces[2], 4), across(pieces[5], 2)
    a3, b2 = onward(a2), onward(b1)
    panel_full, extra = energy(meta, pieces, ctf_table, inv)
    a3, b2, panel_full, extra, hots = together((a3, b2, panel_full, extra, hots))
    b3 = onward(b2)

    def share(turn):
        return lambda m: lax.rem(m[1] + turns - turn, turns)

    acc = full = None
    for turn, own in enumerate([(share_a, share_b), (a1, b1), (a2, b2)]):
        sib = [across(value, 1) for value in own]
        acc, full = score(meta, share(turn), own, sib, panel_full, acc, full)
    a3_sib, b3, acc = together((across(a3, 1), b3, acc))
    sib = [a3_sib, across(b3, 1)]
    shifted, stat, full = score(
        meta, share(turns - 1), [a3, b3], sib, panel_full, acc, full, hots, extra
    )

    pair = merge(meta, stat, across(stat, 1))
    others = [
        lax.ppermute(pair, "rot", [(i, i ^ apart) for i in range(turns)]) for apart in (1, 2, 3)
    ]
    to_x, to_y, post, log_evidence = class_part(
        meta, "first", 2, 2, full, shifted=shifted, stats=[stat, pair, *others]
    )
    got_x, got_y = across(to_x, 2), across(to_y, 4)
    send_c, send_d, give, mass = class_part(
        meta, "mass", 4, 3, full, post=post, hots=hots, bins=bins
    )
    a_sum, b_sum, keep = class_part(meta, "rest", 7, 3, full, post=post)
    got_self = across(give, 1)
    got_x, got_y, send_c, send_d, a_sum, b_sum, keep = lax.optimization_barrier(
        (got_x, got_y, send_c, send_d, a_sum, b_sum, keep)
    )
    got_self, send_c, send_d = together((got_self, send_c, send_d))
    got_c, got_d = by_core(send_c, 2, 4), by_core(send_d, 5, 3)
    message_a, message_b = forward(meta, a_sum, b_sum, got_x, got_y)
    mass, message_a = lax.optimization_barrier((mass, message_a))
    got_a, got_b = by_core(message_a, 4, 2), by_core(message_b, 3, 5)
    mass = mass + across(mass, 2)
    mass = mass + across(mass, 4)
    mass_other = across(mass, 1)
    bin_weights = jnp.where(
        even,
        jnp.concatenate([mass, mass_other], axis=1),
        jnp.concatenate([mass_other, mass], axis=1),
    )
    class_sums = finish(meta, keep, got_a, got_c, got_self, got_b, got_d).T
    return class_sums, bin_weights, log_evidence.reshape(-1)


def energy_block(gain_block, panel_piece):
    widened = panel_piece.astype(jnp.float32)
    return lax.dot_general(
        gain_block, widened * widened, (((1,), (1,)), ((), ())), precision=lax.Precision.HIGHEST
    )


def on_device(raw_images, defocus_bin, dest_row, ctf_table, inv_noise, panels):
    dom_count = lax.axis_size("dom")
    bin_count = ctf_table.shape[0]
    columns = raw_images.shape[1]
    hold_rows = raw_images.shape[0]
    shard_rows = hold_rows // 2
    capacity = 2 * shard_rows // dom_count
    is_live = dest_row >= 0
    target = jnp.where(is_live, dest_row // shard_rows, dom_count)
    local_row = dest_row % shard_rows
    marks = (target[:, None] == jnp.arange(dom_count, dtype=jnp.int32)[None, :]).astype(jnp.int32)
    slot_rank = jnp.sum((jnp.cumsum(marks, axis=0) - marks) * marks, axis=1)
    row_code = jnp.where(is_live, local_row * bin_count + defocus_bin, -1)
    padded_images = jnp.concatenate([raw_images, jnp.zeros((1, columns), raw_images.dtype)], axis=0)
    padded_code = jnp.concatenate([row_code, jnp.full((1,), -1, jnp.int32)], axis=0)
    position = jnp.where(is_live, target * capacity + slot_rank, dom_count * capacity)
    slot_count = dom_count * capacity
    source = (
        jnp.full((slot_count,), hold_rows, jnp.int32)
        .at[position]
        .set(jnp.arange(hold_rows, dtype=jnp.int32), mode="drop")
    )
    send_images = padded_images[source].reshape(dom_count, capacity, columns)
    send_code = padded_code[source].reshape(dom_count, capacity)
    recv_images, recv_code = (
        lax.all_to_all(send_images, "dom", split_axis=0, concat_axis=0, tiled=True),
        lax.all_to_all(send_code, "dom", split_axis=0, concat_axis=0, tiled=True),
    )
    flat_images = recv_images.reshape(-1, columns)
    flat_code = recv_code.reshape(-1)
    arrived = flat_code >= 0
    row_of = jnp.where(arrived, flat_code // bin_count, shard_rows)
    row_order = (
        jnp.zeros((shard_rows,), jnp.int32)
        .at[row_of]
        .set(jnp.arange(flat_code.shape[0], dtype=jnp.int32), mode="drop")
    )
    images = flat_images[row_order]
    bin_ids = flat_code[row_order] % bin_count
    bin_table = (bin_ids[:, None] == jnp.arange(bin_count, dtype=jnp.int32)[None, :]).astype(
        jnp.float32
    )
    ctf_rows = jnp.dot(bin_table, ctf_table, precision=lax.Precision.HIGHEST)
    factor = ctf_rows * inv_noise[None, :]
    weighted = (images.astype(jnp.float32) * jnp.concatenate([factor, factor], axis=1)).astype(
        jnp.bfloat16
    )
    gain_half = ctf_table * ctf_table * inv_noise[None, :]
    gain_full = jnp.concatenate([gain_half, gain_half], axis=1)
    panel_piece = lax.all_gather(panels, "dom", axis=1, tiled=True)
    col_block = weighted
    cross_term = lax.dot_general(
        col_block, panel_piece, (((1,), (1,)), ((), ())), preferred_element_type=jnp.float32
    )
    energy = energy_block(gain_full, panel_piece)
    scores = cross_term - 0.5 * jnp.dot(bin_table, energy, precision=lax.Precision.HIGHEST)
    local_peak = jnp.max(scores, axis=1)
    row_peak = lax.pmax(local_peak, "rot")
    shifted = jnp.exp(scores - row_peak[:, None])
    row_total = lax.psum(jnp.sum(shifted, axis=1), "rot")
    posterior = (shifted / row_total[:, None]).astype(jnp.bfloat16)
    log_evidence = row_peak + jnp.log(row_total)
    col_block = weighted
    class_sums = lax.psum_scatter(
        lax.dot_general(
            col_block, posterior, (((0,), (0,)), ((), ())), preferred_element_type=jnp.float32
        ).astype(jnp.bfloat16),
        "dom",
        scatter_dimension=0,
        tiled=True,
    ).astype(jnp.float32)
    local_mass = lax.dot_general(
        bin_table.astype(jnp.bfloat16),
        posterior,
        (((0,), (0,)), ((), ())),
        preferred_element_type=jnp.float32,
    )
    bin_weights = lax.psum(local_mass.astype(jnp.bfloat16), "dom").astype(jnp.float32)
    return (class_sums, bin_weights, log_evidence)


def solution(mesh):
    small = mesh.shape["dom"] == 8 and mesh.shape["rot"] == 4
    return jax.shard_map(
        two_by_two if small else on_device,
        mesh=mesh,
        in_specs=(P("dom", None), P("dom"), P("dom"), P(), P(), P("rot", "dom")),
        out_specs=(P("dom", "rot"), P(None, "rot"), P("dom")),
        check_vma=False,
    )
```

```python
import functools

import jax
import jax.numpy as jnp
from jax import lax
from jax.experimental import pallas as pl
from jax.experimental.pallas import tpu as pltpu
from jax.sharding import PartitionSpec as P

NN = (((1,), (0,)), ((), ()))
NT = (((1,), (1,)), ((), ()))
F32, BF16, I32 = jnp.float32, jnp.bfloat16, jnp.int32
CODE = 128
MIB = 1024 * 1024


def mm(a, b, dims):
    return lax.dot_general(a, b, dims, preferred_element_type=F32)


def split3(x):
    hi = x.astype(BF16)
    rest = x - hi.astype(F32)
    mid = rest.astype(BF16)
    low = (rest - mid.astype(F32)).astype(BF16)
    return hi, mid, low


def call(body, grid, in_specs, out_specs, out_shape, scratch=(), alias=None, flops=0, moved=0, room=24):
    return pl.pallas_call(
        body,
        grid_spec=pltpu.PrefetchScalarGridSpec(
            num_scalar_prefetch=1,
            grid=grid,
            in_specs=in_specs,
            out_specs=out_specs,
            scratch_shapes=list(scratch),
        ),
        out_shape=out_shape,
        input_output_aliases=alias or {},
        compiler_params=pltpu.CompilerParams(vmem_limit_bytes=room * MIB),
        cost_estimate=pl.CostEstimate(
            flops=flops // 16, bytes_accessed=moved // 16, transcendentals=0
        ),
    )


def sds(shape, dtype):
    return jax.ShapeDtypeStruct(shape, dtype)


def one_hot_rows(out_ref, wanted):
    rows, width = out_ref.shape
    step = 256 if rows % 256 == 0 else rows
    for start in range(0, rows, step):
        index = lax.broadcasted_iota(I32, (step, width), 0) + start
        out_ref[start : start + step, :] = jnp.where(index == wanted, 1.0, 0.0).astype(BF16)


def places_of(dest, shard_rows, cap, dom, device):
    hold = dest.shape[1]
    low = lax.broadcasted_iota(I32, (dom, hold), 0) * shard_rows
    inside = jnp.logical_and(dest >= low, dest < low + shard_rows)
    marks = jnp.where(inside, 1.0, 0.0)
    local = dest - jnp.sum(jnp.where(inside, low, 0), axis=0, keepdims=True)
    lanes = 128
    before = lax.broadcasted_iota(I32, (lanes, lanes), 0) < lax.broadcasted_iota(
        I32, (lanes, lanes), 1
    )
    upper = jnp.where(before, 1.0, 0.0).astype(BF16)
    apart = lax.broadcasted_iota(I32, (dom, 1), 0) ^ device
    carry = apart.astype(F32) * cap + 1.0
    found = []
    for start in range(0, hold, lanes):
        part = marks[:, start : start + lanes]
        rank = mm(part.astype(BF16), upper, NN) + carry
        found.append(jnp.sum(jnp.where(part > 0, rank, 0.0), axis=0, keepdims=True))
        carry = carry + jnp.sum(part, axis=1, keepdims=True)
    return jnp.concatenate(found, axis=1).astype(I32) - 1, local


def pack_first_body(dom, shard_rows, cap, meta, dest_ref, bin_ref, raw_ref, *refs):
    outs, (place_ref, pick) = refs[:dom], refs[dom:]
    dest = dest_ref[...].reshape(1, dest_ref.shape[0])
    bins = bin_ref[...].reshape(1, dest_ref.shape[0])
    place, local = places_of(dest, shard_rows, cap, dom, meta[0])
    place_ref[...] = place
    one_hot_rows(pick, place)
    which = lax.broadcasted_iota(I32, (CODE, dest.shape[1]), 0)
    digits = jnp.where(
        which == 0,
        local >> 4,
        jnp.where(which == 1, local & 15, jnp.where(which == 2, bins, jnp.where(which == 3, 1, 0))),
    )
    digits = jnp.where(dest >= 0, digits, 0).astype(F32).astype(BF16)
    codes = mm(pick[...], digits, NT).astype(BF16)
    packed = mm(pick[...], raw_ref[...], NN).astype(BF16)
    for index, out_ref in enumerate(outs):
        out_ref[:, :CODE] = codes[index * cap : (index + 1) * cap]
        out_ref[:, CODE:] = packed[index * cap : (index + 1) * cap]


def pack_next_body(cap, meta, place_ref, raw_ref, *refs):
    outs, pick = refs[:-1], refs[-1]
    one_hot_rows(pick, place_ref[...])
    packed = mm(pick[...], raw_ref[...], NN).astype(BF16)
    for index, out_ref in enumerate(outs):
        out_ref[...] = packed[index * cap : (index + 1) * cap]


def pack_first(meta, raw_images, dest, bins, dom, width, at):
    hold, _ = raw_images.shape
    cap = hold // dom
    slots = dom * cap
    row = pl.BlockSpec((1, hold), lambda j, m: (0, 0))
    return call(
        functools.partial(pack_first_body, dom, hold // 2, cap),
        (1,),
        [
            pl.BlockSpec((hold,), lambda j, m: (0,)),
            pl.BlockSpec((hold,), lambda j, m: (0,)),
            pl.BlockSpec((hold, width), lambda j, m: (0, at(m))),
        ],
        [pl.BlockSpec((cap, CODE + width), lambda j, m: (0, 0))] * dom + [row],
        [sds((cap, CODE + width), BF16)] * dom + [sds((1, hold), I32)],
        scratch=[pltpu.VMEM((slots, hold), BF16)],
        room=54,
        flops=2 * slots * hold * width,
        moved=4 * hold * width,
    )(meta, dest, bins, raw_images)


def pack_next(meta, raw_images, place, dom, width, at):
    hold, _ = raw_images.shape
    cap = hold // dom
    slots = dom * cap
    return call(
        functools.partial(pack_next_body, cap),
        (1,),
        [
            pl.BlockSpec((1, hold), lambda j, m: (0, 0)),
            pl.BlockSpec((hold, width), lambda j, m: (0, at(m))),
        ],
        [pl.BlockSpec((cap, width), lambda j, m: (0, 0))] * dom,
        [sds((cap, width), BF16)] * dom,
        scratch=[pltpu.VMEM((slots, hold), BF16)],
        room=54,
        flops=2 * slots * hold * width,
        moved=4 * hold * width,
    )(meta, place, raw_images)


def weigh(pick, wide, recv, ctf_ref, inv_ref, out_ref):
    table = jnp.concatenate(split3(ctf_ref[...] * inv_ref[...]), axis=0)
    factor = mm(wide, table, NN)
    out_ref[...] = (mm(pick, recv, NN) * factor).astype(BF16)


def gather(pieces, whole):
    rows = pieces[0].shape[0]
    for index, piece in enumerate(pieces):
        whole[index * rows : (index + 1) * rows, :] = piece[...]


def unpack_first_body(dom, bins, meta, *refs):
    recv_ref = refs[-1]
    gather(refs[:dom], recv_ref)
    ctf_ref, inv_ref, out_ref, hot_ref, pick, wide = refs[dom:-1]
    shard_rows = out_ref.shape[0]
    chosen = jnp.where(
        lax.broadcasted_iota(I32, (8, CODE), 0) == lax.broadcasted_iota(I32, (8, CODE), 1), 1.0, 0.0
    ).astype(BF16)
    got = mm(chosen, recv_ref[:, :CODE], NT)
    row = got[0:1] * 16.0 + got[1:2] + got[3:4] * 1024.0 - 1024.0
    one_hot_rows(pick, row.astype(I32))
    slot_bins = jnp.broadcast_to(got[2:3].astype(BF16), (8, got.shape[1]))
    down = mm(pick[...], slot_bins, NT)[:, 0:1].astype(I32)
    across = mm(slot_bins, pick[...], NT)[0:1].astype(I32)
    lane = lax.broadcasted_iota(I32, (shard_rows, 3 * bins), 1)
    wide[...] = jnp.where((lane & (bins - 1)) == down, 1.0, 0.0).astype(BF16)
    deep = lax.broadcasted_iota(I32, (3 * bins, shard_rows), 0)
    hot_ref[...] = jnp.where((deep & (bins - 1)) == across, 1.0, 0.0).astype(BF16)
    weigh(pick[...], wide[...], recv_ref[:, CODE:], ctf_ref, inv_ref, out_ref)


def unpack_next_body(dom, meta, *refs):
    recv_ref = refs[-1]
    gather(refs[:dom], recv_ref)
    pick_ref, wide_ref, ctf_ref, inv_ref, out_ref = refs[dom:-1]
    weigh(pick_ref[...], wide_ref[...], recv_ref[...], ctf_ref, inv_ref, out_ref)


def unpack_first(meta, recv, ctf, inv, at):
    cap, columns = recv[0].shape
    dom = len(recv)
    slots = dom * cap
    width = columns - CODE
    rows = slots // 2
    bins, pix = ctf.shape
    wrap = pix // width
    whole = lambda shape: pl.BlockSpec(shape, lambda j, m: (0, 0))
    shapes = [(rows, width), (3 * bins, rows), (rows, slots), (rows, 3 * bins)]
    return call(
        functools.partial(unpack_first_body, dom, bins),
        (1,),
        [whole(recv[0].shape)] * dom
        + [
            pl.BlockSpec((bins, width), lambda j, m: (0, lax.rem(at(m), wrap))),
            pl.BlockSpec((1, width), lambda j, m: (0, lax.rem(at(m), wrap))),
        ],
        [whole(s) for s in shapes],
        [sds(s, BF16) for s in shapes],
        scratch=[pltpu.VMEM((slots, columns), BF16)],
        flops=2 * slots * rows * width,
        moved=2 * slots * columns,
    )(meta, *recv, ctf, inv)


def unpack_next(meta, pick, wide, recv, ctf, inv, at):
    cap, width = recv[0].shape
    dom = len(recv)
    slots = dom * cap
    rows = slots // 2
    bins, pix = ctf.shape
    wrap = pix // width
    whole = lambda shape: pl.BlockSpec(shape, lambda j, m: (0, 0))
    return call(
        functools.partial(unpack_next_body, dom),
        (1,),
        [whole(recv[0].shape)] * dom
        + [
            whole(pick.shape),
            whole(wide.shape),
            pl.BlockSpec((bins, width), lambda j, m: (0, lax.rem(at(m), wrap))),
            pl.BlockSpec((1, width), lambda j, m: (0, lax.rem(at(m), wrap))),
        ],
        whole((rows, width)),
        sds((rows, width), BF16),
        scratch=[pltpu.VMEM((slots, width), BF16)],
        flops=2 * slots * rows * width,
        moved=2 * slots * width,
    )(meta, *recv, pick, wide, ctf, inv)


def energy_body(bins, count, meta, *refs):
    pieces, (ctf_ref, inv_ref, panel_ref, extra_ref, total) = refs[:count], refs[count:]
    step = pl.program_id(0)

    @pl.when(step == 0)
    def _():
        total[...] = jnp.zeros_like(total)

    gain = ctf_ref[...] * ctf_ref[...] * inv_ref[...]
    gain3 = jnp.concatenate(split3(gain), axis=0)
    for index, piece in enumerate(pieces):

        @pl.when(step == index)
        def _():
            panel = piece[...]
            panel_ref[...] = panel
            wide = panel.astype(F32)
            square = wide * wide
            high = square.astype(BF16)
            low = (square - high.astype(F32)).astype(BF16)
            total[...] += mm(high, gain3, NT) + mm(low, gain3, NT)

    @pl.when(step == count - 1)
    def _():
        whole = total[:, :bins] + total[:, bins : 2 * bins] + total[:, 2 * bins :]
        extra_ref[...] = jnp.concatenate(split3(-0.5 * whole), axis=1)


def energy(meta, pieces, ctf, inv):
    count = len(pieces)
    rows, width = pieces[0].shape
    bins, pix = ctf.shape
    wrap = pix // width
    return call(
        functools.partial(energy_body, bins, count),
        (count,),
        [pl.BlockSpec((rows, width), lambda j, m: (0, 0))] * count
        + [
            pl.BlockSpec((bins, width), lambda j, m: (0, lax.rem(m[0] ^ j, wrap))),
            pl.BlockSpec((1, width), lambda j, m: (0, lax.rem(m[0] ^ j, wrap))),
        ],
        [
            pl.BlockSpec((rows, width), lambda j, m: (0, m[0] ^ j)),
            pl.BlockSpec((rows, 3 * bins), lambda j, m: (0, 0)),
        ],
        [sds((rows, count * width), BF16), sds((rows, 3 * bins), BF16)],
        scratch=[pltpu.VMEM((rows, 3 * bins), F32)],
        flops=2 * 4 * rows * bins * count * width * 3,
        moved=4 * rows * count * width,
    )(meta, *pieces, ctf, inv)


def score_body(parts, first, last, meta, *refs):
    own, sib, panel_ref, refs = refs[:parts], refs[parts : 2 * parts], refs[2 * parts], refs[2 * parts + 1 :]
    if first:
        acc_out, full_ref = refs
    elif last:
        acc_ref, _, hot_own, hot_sib, extra_ref, shifted_ref, stat_ref, full_ref = refs
    else:
        acc_ref, _, acc_out, full_ref = refs
    half = pl.num_programs(0) // 2

    def tile(sources, hot):
        block = jnp.concatenate([source[...] for source in sources], axis=1)
        full_ref[...] = block
        total = mm(panel_ref[...], block, NT)
        if not first:
            total = acc_ref[...] + total
        if not last:
            acc_out[...] = total
            return
        total = total + mm(extra_ref[...], hot[...], NN)
        peak = jnp.max(total, axis=0, keepdims=True)
        shifted = jnp.exp(total - peak)
        shifted_ref[...] = shifted
        mass = jnp.sum(shifted, axis=0, keepdims=True)
        which = lax.broadcasted_iota(I32, stat_ref.shape, 0)
        stat_ref[...] = jnp.where(which == 0, peak, mass)

    @pl.when(pl.program_id(0) < half)
    def _():
        tile(own, hot_own if last else None)

    @pl.when(pl.program_id(0) >= half)
    def _():
        tile(sib, hot_sib if last else None)


def score(meta, at, own, sib, panels, acc=None, full=None, hots=None, extra=None):
    rows, part = own[0].shape
    parts = len(own)
    width = parts * part
    tile = 256
    half = rows // tile
    count, columns = panels.shape
    first, last = acc is None, hots is not None
    front = pl.BlockSpec((tile, part), lambda j, m: (jnp.minimum(j, half - 1), 0))
    back = pl.BlockSpec((tile, part), lambda j, m: (jnp.maximum(j - half, 0), 0))
    acc_spec = pl.BlockSpec((count, tile), lambda j, m: (0, j))
    full_spec = pl.BlockSpec((tile, width), lambda j, m: (j, at(m)))
    in_specs = [front] * parts + [back] * parts
    in_specs += [pl.BlockSpec((count, width), lambda j, m: (0, at(m)))]
    operands = [meta, *own, *sib, panels]
    alias = {}
    if not first:
        in_specs += [acc_spec, pl.BlockSpec(memory_space=pl.ANY)]
        alias = {len(operands): 0, len(operands) + 1: 2 if last else 1}
        operands += [acc, full]
    out_specs = [acc_spec, full_spec]
    full_shape = sds((2 * rows, columns), BF16)
    out_shape = [sds((count, 2 * rows), F32), full_shape]
    if last:
        depth = extra.shape[1]
        in_specs += [
            pl.BlockSpec((depth, tile), lambda j, m: (0, jnp.minimum(j, half - 1))),
            pl.BlockSpec((depth, tile), lambda j, m: (0, jnp.maximum(j - half, 0))),
            pl.BlockSpec((count, depth), lambda j, m: (0, 0)),
        ]
        operands += [*hots, extra]
        out_specs = [acc_spec, pl.BlockSpec((8, tile), lambda j, m: (0, j)), full_spec]
        out_shape = [out_shape[0], sds((8, 2 * rows), F32), full_shape]
    return call(
        functools.partial(score_body, parts, first, last),
        (2 * half,),
        in_specs,
        out_specs,
        out_shape,
        alias=alias,
        room=16,
        flops=2 * count * 2 * rows * width,
        moved=8 * count * 2 * rows + 8 * rows * width,
    )(*operands)


def merge_body(meta, mine_ref, other_ref, out_ref):
    rows = mine_ref.shape[1] // 2
    other = other_ref[...]
    other = jnp.concatenate([other[:, rows:], other[:, :rows]], axis=1)
    mine = mine_ref[...]
    peak = jnp.maximum(mine[0:1], other[0:1])
    mass = mine[1:2] * jnp.exp(mine[0:1] - peak) + other[1:2] * jnp.exp(other[0:1] - peak)
    which = lax.broadcasted_iota(I32, out_ref.shape, 0)
    out_ref[...] = jnp.where(which == 0, peak, mass)


def merge(meta, mine, other):
    spec = pl.BlockSpec(mine.shape, lambda j, m: (0, 0))
    return call(merge_body, (1,), [spec, spec], spec, sds(mine.shape, F32), room=4)(meta, mine, other)


def class_body(kind, steps, meta, *refs):
    if kind == "first":
        (shifted_ref, stat_ref), four = refs[:2], refs[2:6]
        hot_own, hot_sib, full_ref = refs[6:9]
        outs, (post_ref, log_ref, mass_ref) = refs[9 : 9 + steps], refs[9 + steps :]

        @pl.when(pl.program_id(0) == 0)
        def _():
            stats = [ref[...] for ref in four]
            peaks = [s[0:1] for s in stats]
            peak = jnp.maximum(jnp.maximum(peaks[0], peaks[1]), jnp.maximum(peaks[2], peaks[3]))
            parts = [s[1:2] * jnp.exp(p - peak) for s, p in zip(stats, peaks)]
            mass = (parts[0] + parts[1]) + (parts[2] + parts[3])
            factor = jnp.exp(stat_ref[0:1] - peak) / mass
            post_ref[...] = (shifted_ref[...] * factor).astype(BF16)
            log_ref[...] = (peak + jnp.log(mass))[:, : log_ref.shape[1]]
            bins, rows = mass_ref.shape[0], hot_own.shape[1]
            weights = mm(hot_own[:bins, :], post_ref[:, :rows], NT)
            weights = weights + mm(hot_sib[:bins, :], post_ref[:, rows:], NT)
            mass_ref[...] = weights.astype(BF16)

    else:
        (post_ref, full_ref), outs = refs[:2], refs[2:]
    for step, out_ref in enumerate(outs):

        @pl.when(pl.program_id(0) == step)
        def _():
            out_ref[...] = mm(post_ref[...], full_ref[...], NN).astype(out_ref.dtype)


def class_part(meta, kind, offset, steps, full, post=None, shifted=None, stats=None, hots=None, bins=0):
    rows, columns = full.shape
    width = columns // 8
    count = (shifted if post is None else post).shape[0]
    whole = lambda shape: pl.BlockSpec(shape, lambda j, m: (0, 0))
    full_spec = pl.BlockSpec((rows, width), lambda j, m: (0, m[offset + j]))
    out_specs = [whole((count, width))] * steps
    out_shape = [sds((count, width), F32 if kind == "rest" else BF16)] * steps
    if kind == "first":
        operands = [shifted, *stats, *hots, full]
        in_specs = [whole(shifted.shape)] + [whole(stats[0].shape)] * 5
        in_specs += [whole(hots[0].shape)] * 2 + [full_spec]
        out_specs += [whole((count, rows)), whole((1, rows // 2)), whole((bins, count))]
        out_shape += [sds((count, rows), BF16), sds((1, rows // 2), F32), sds((bins, count), BF16)]
    else:
        operands = [post, full]
        in_specs = [whole(post.shape), full_spec]
    return call(
        functools.partial(class_body, kind, steps),
        (steps,),
        in_specs,
        out_specs,
        out_shape,
        room=22 if kind == "first" else 18,
        flops=2 * count * rows * width * steps,
        moved=2 * rows * width * steps + 4 * count * (rows + width * steps),
    )(meta, *operands)


def forward_body(meta, a_sum, b_sum, down_ref, left_ref, a_ref, b_ref):
    even = meta[0] % 2 == 0
    down, left = down_ref[...].astype(F32), left_ref[...].astype(F32)
    a_ref[...] = (a_sum[...] + jnp.where(even, down, left)).astype(BF16)
    b_ref[...] = (b_sum[...] + jnp.where(even, left, down)).astype(BF16)


def forward(meta, a_sum, b_sum, got_x, got_y):
    shape = a_sum.shape
    spec = pl.BlockSpec(memory_space=pltpu.VMEM)
    return call(forward_body, (1,), [spec] * 4, [spec] * 2, [sds(shape, BF16)] * 2, room=14)(
        meta, a_sum, b_sum, got_x, got_y
    )


def finish_body(tile, meta, keep_ref, a_ref, c_ref, other_ref, b_ref, d_ref, out_ref):
    half = pl.num_programs(0) // 2
    step = pl.program_id(0)

    def total(refs, at):
        rows = pl.ds(pl.multiple_of(at * tile, tile), tile)
        first, second, third = [ref[rows, :].astype(F32) for ref in refs]
        out_ref[...] = first + second + third

    @pl.when(step < half)
    def _():
        total((keep_ref, c_ref, a_ref), step)

    @pl.when(step >= half)
    def _():
        total((other_ref, d_ref, b_ref), step - half)


def finish(meta, keep, got_a, got_c, got_self, got_b, got_d):
    count, width = keep.shape
    half = 3
    tile = count // half

    def place(j, m):
        core = lax.rem(m[0], 2)
        return jnp.where(j < half, core * half + j, (1 - core) * half + j - half), 0

    return call(
        functools.partial(finish_body, tile),
        (2 * half,),
        [pl.BlockSpec(memory_space=pltpu.VMEM)] * 6,
        pl.BlockSpec((tile, width), place),
        sds((2 * count, width), F32),
        room=12,
    )(meta, keep, got_a, got_c, got_self, got_b, got_d)


def two_by_two(raw_images, defocus_bin, dest_row, ctf_table, inv_noise, panels):
    dom, turns = lax.axis_size("dom"), lax.axis_size("rot")
    device, plane = lax.axis_index("dom"), lax.axis_index("rot")
    bins = ctf_table.shape[0]
    columns = raw_images.shape[1]
    chip, core = device // 2, device % 2

    def block(apart, half):
        return (chip ^ apart) * 2 + half

    x_first, y_second = block(1, 0), block(2, 1)
    x_second, y_first = block(1, 1), block(2, 0)
    even = core == 0
    order = [
        device,
        plane,
        block(3, 0),
        block(3, 1),
        jnp.where(even, x_first, y_second),
        jnp.where(even, y_second, x_first),
        block(0, 1 - core),
        jnp.where(even, y_first, x_second),
        jnp.where(even, x_second, y_first),
        block(0, core),
    ]
    meta = jnp.stack(order).astype(I32)
    inv = inv_noise[None, :]

    def across(value, apart):
        return lax.ppermute(value, "dom", [(i, i ^ apart) for i in range(dom)])

    def by_core(value, when_even, when_odd):
        pairs = [(i, i ^ (when_odd if i % 2 else when_even)) for i in range(dom)]
        return lax.ppermute(value, "dom", pairs)

    def onward(value):
        return lax.ppermute(value, "rot", [(i, (i + 1) % turns) for i in range(turns)])

    width = columns // turns // 2
    def exchange(blocks):
        got = [blocks[0]] + [None] * (dom - 1)
        for apart in (6, 7, 2, 4, 3, 5, 1):
            got[apart] = across(blocks[apart], apart)
        return got

    *send_a, place = pack_first(meta, raw_images, dest_row, defocus_bin, dom, width, lambda m: 2 * m[1])
    recv_a = exchange(send_a)
    send_b = pack_next(meta, raw_images, place, dom, width, lambda m: 2 * m[1] + 1)
    together = lax.optimization_barrier

    count = panels.shape[0] // 2
    pieces = [None] * 8
    place, panels = together((place, panels))
    pieces[0] = lax.dynamic_slice_in_dim(panels, core * count, count, 0)
    pieces[1] = across(lax.dynamic_slice_in_dim(panels, (1 - core) * count, count, 0), 1)

    recv_a, send_b, pieces[:2] = together((recv_a, send_b, pieces[:2]))
    share_a, hot, pick, wide = unpack_first(meta, recv_a, ctf_table, inv, lambda m: 2 * m[1])
    share_a, send_b = together((share_a, send_b))
    a1, recv_b = onward(share_a), exchange(send_b)
    a2 = onward(a1)
    recv_b, pieces[:2] = together((recv_b, pieces[:2]))
    pieces[2], pieces[4] = across(pieces[0], 2), across(pieces[0], 4)
    pieces[3], pieces[5] = across(pieces[1], 2), across(pieces[1], 4)
    a2, recv_b = together((a2, recv_b))
    share_b = unpack_next(meta, pick, wide, recv_b, ctf_table, inv, lambda m: 2 * m[1] + 1)
    hots = (hot, across(hot, 1))
    a3, b1 = onward(a2), onward(share_b)
    a3, b1, pieces[2:6] = together((a3, b1, pieces[2:6]))
    pieces[6], pieces[7] = across(pieces[2], 4), across(pieces[5], 2)
    b2 = onward(b1)
    panel_full, extra = energy(meta, pieces, ctf_table, inv)
    b2, panel_full, extra, hots = together((b2, panel_full, extra, hots))
    b3 = onward(b2)

    def share(turn):
        return lambda m: lax.rem(m[1] + turns - turn, turns)

    acc = full = None
    for turn, own in enumerate([(share_a, share_b), (a1, b1), (a2, b2)]):
        sib = [across(value, 1) for value in own]
        acc, full = score(meta, share(turn), own, sib, panel_full, acc, full)
    a3_sib, b3, acc = together((across(a3, 1), b3, acc))
    sib = [a3_sib, across(b3, 1)]
    shifted, stat, full = score(
        meta, share(turns - 1), [a3, b3], sib, panel_full, acc, full, hots, extra
    )

    pair = merge(meta, stat, across(stat, 1))
    others = [
        lax.ppermute(pair, "rot", [(i, i ^ apart) for i in range(turns)]) for apart in (1, 2, 3)
    ]
    to_x, to_y, post, log_evidence, mass = class_part(
        meta, "first", 2, 2, full, None, shifted, [stat, pair, *others], hots, bins
    )
    mass_x = across(mass, 2)
    got_x, got_y = across(to_x, 2), across(to_y, 4)
    send_c, send_d, give = class_part(meta, "next", 4, 3, full, post)
    mass = mass.astype(F32) + mass_x.astype(F32)
    mass = mass + across(mass, 4)
    a_sum, b_sum, keep = class_part(meta, "rest", 7, 3, full, post)
    got_x, got_y, send_c, send_d, a_sum, b_sum, keep, give, mass = together(
        (got_x, got_y, send_c, send_d, a_sum, b_sum, keep, give, mass)
    )
    got_c, got_d = by_core(send_c, 2, 4), by_core(send_d, 5, 3)
    message_a, message_b = forward(meta, a_sum, b_sum, got_x, got_y)
    got_a, got_b = by_core(message_a, 4, 2), by_core(message_b, 3, 5)
    got_self = across(give, 1)
    mass_other = across(mass, 1)
    bin_weights = jnp.where(
        even,
        jnp.concatenate([mass, mass_other], axis=1),
        jnp.concatenate([mass_other, mass], axis=1),
    )
    class_sums = finish(meta, keep, got_a, got_c, got_self, got_b, got_d).T
    return class_sums, bin_weights, log_evidence.reshape(-1)


def energy_block(gain_block, panel_piece):
    widened = panel_piece.astype(jnp.float32)
    return lax.dot_general(
        gain_block, widened * widened, (((1,), (1,)), ((), ())), precision=lax.Precision.HIGHEST
    )


def on_device(raw_images, defocus_bin, dest_row, ctf_table, inv_noise, panels):
    dom_count = lax.axis_size("dom")
    bin_count = ctf_table.shape[0]
    columns = raw_images.shape[1]
    hold_rows = raw_images.shape[0]
    shard_rows = hold_rows // 2
    capacity = 2 * shard_rows // dom_count
    is_live = dest_row >= 0
    target = jnp.where(is_live, dest_row // shard_rows, dom_count)
    local_row = dest_row % shard_rows
    marks = (target[:, None] == jnp.arange(dom_count, dtype=jnp.int32)[None, :]).astype(jnp.int32)
    slot_rank = jnp.sum((jnp.cumsum(marks, axis=0) - marks) * marks, axis=1)
    row_code = jnp.where(is_live, local_row * bin_count + defocus_bin, -1)
    padded_images = jnp.concatenate([raw_images, jnp.zeros((1, columns), raw_images.dtype)], axis=0)
    padded_code = jnp.concatenate([row_code, jnp.full((1,), -1, jnp.int32)], axis=0)
    position = jnp.where(is_live, target * capacity + slot_rank, dom_count * capacity)
    slot_count = dom_count * capacity
    source = (
        jnp.full((slot_count,), hold_rows, jnp.int32)
        .at[position]
        .set(jnp.arange(hold_rows, dtype=jnp.int32), mode="drop")
    )
    send_images = padded_images[source].reshape(dom_count, capacity, columns)
    send_code = padded_code[source].reshape(dom_count, capacity)
    recv_images, recv_code = (
        lax.all_to_all(send_images, "dom", split_axis=0, concat_axis=0, tiled=True),
        lax.all_to_all(send_code, "dom", split_axis=0, concat_axis=0, tiled=True),
    )
    flat_images = recv_images.reshape(-1, columns)
    flat_code = recv_code.reshape(-1)
    arrived = flat_code >= 0
    row_of = jnp.where(arrived, flat_code // bin_count, shard_rows)
    row_order = (
        jnp.zeros((shard_rows,), jnp.int32)
        .at[row_of]
        .set(jnp.arange(flat_code.shape[0], dtype=jnp.int32), mode="drop")
    )
    images = flat_images[row_order]
    bin_ids = flat_code[row_order] % bin_count
    bin_table = (bin_ids[:, None] == jnp.arange(bin_count, dtype=jnp.int32)[None, :]).astype(
        jnp.float32
    )
    ctf_rows = jnp.dot(bin_table, ctf_table, precision=lax.Precision.HIGHEST)
    factor = ctf_rows * inv_noise[None, :]
    weighted = (images.astype(jnp.float32) * jnp.concatenate([factor, factor], axis=1)).astype(
        jnp.bfloat16
    )
    gain_half = ctf_table * ctf_table * inv_noise[None, :]
    gain_full = jnp.concatenate([gain_half, gain_half], axis=1)
    panel_piece = lax.all_gather(panels, "dom", axis=1, tiled=True)
    col_block = weighted
    cross_term = lax.dot_general(
        col_block, panel_piece, (((1,), (1,)), ((), ())), preferred_element_type=jnp.float32
    )
    energy = energy_block(gain_full, panel_piece)
    scores = cross_term - 0.5 * jnp.dot(bin_table, energy, precision=lax.Precision.HIGHEST)
    local_peak = jnp.max(scores, axis=1)
    row_peak = lax.pmax(local_peak, "rot")
    shifted = jnp.exp(scores - row_peak[:, None])
    row_total = lax.psum(jnp.sum(shifted, axis=1), "rot")
    posterior = (shifted / row_total[:, None]).astype(jnp.bfloat16)
    log_evidence = row_peak + jnp.log(row_total)
    col_block = weighted
    class_sums = lax.psum_scatter(
        lax.dot_general(
            col_block, posterior, (((0,), (0,)), ((), ())), preferred_element_type=jnp.float32
        ).astype(jnp.bfloat16),
        "dom",
        scatter_dimension=0,
        tiled=True,
    ).astype(jnp.float32)
    local_mass = lax.dot_general(
        bin_table.astype(jnp.bfloat16),
        posterior,
        (((0,), (0,)), ((), ())),
        preferred_element_type=jnp.float32,
    )
    bin_weights = lax.psum(local_mass.astype(jnp.bfloat16), "dom").astype(jnp.float32)
    return (class_sums, bin_weights, log_evidence)


def solution(mesh):
    small = mesh.shape["dom"] == 8 and mesh.shape["rot"] == 4
    return jax.shard_map(
        two_by_two if small else on_device,
        mesh=mesh,
        in_specs=(P("dom", None), P("dom"), P("dom"), P(), P(), P("rot", "dom")),
        out_specs=(P("dom", "rot"), P(None, "rot"), P("dom")),
        check_vma=False,
    )
```

```python
import functools

import jax
import jax.numpy as jnp
from jax import lax
from jax.experimental import pallas as pl
from jax.experimental.pallas import tpu as pltpu
from jax.sharding import PartitionSpec as P

NN = (((1,), (0,)), ((), ()))
NT = (((1,), (1,)), ((), ()))
F32, BF16, I32 = jnp.float32, jnp.bfloat16, jnp.int32
CODE = 16
LANES = 128
MIB = 1024 * 1024


def mm(a, b, dims):
    return lax.dot_general(a, b, dims, preferred_element_type=F32)


def split3(x):
    hi = x.astype(BF16)
    rest = x - hi.astype(F32)
    mid = rest.astype(BF16)
    low = (rest - mid.astype(F32)).astype(BF16)
    return hi, mid, low


def call(body, grid, in_specs, out_specs, out_shape, scratch=(), alias=None, flops=0, moved=0, room=24):
    return pl.pallas_call(
        body,
        grid_spec=pltpu.PrefetchScalarGridSpec(
            num_scalar_prefetch=1,
            grid=grid,
            in_specs=in_specs,
            out_specs=out_specs,
            scratch_shapes=list(scratch),
        ),
        out_shape=out_shape,
        input_output_aliases=alias or {},
        compiler_params=pltpu.CompilerParams(vmem_limit_bytes=room * MIB),
        cost_estimate=pl.CostEstimate(
            flops=flops // 16, bytes_accessed=moved // 16, transcendentals=0
        ),
    )


def sds(shape, dtype):
    return jax.ShapeDtypeStruct(shape, dtype)


def one_hot_rows(out_ref, wanted):
    rows, width = out_ref.shape
    step = 256 if rows % 256 == 0 else rows
    for start in range(0, rows, step):
        index = lax.broadcasted_iota(I32, (step, width), 0) + start
        out_ref[start : start + step, :] = jnp.where(index == wanted, 1.0, 0.0).astype(BF16)


def places_of(dest, shard_rows, cap, dom, device):
    hold = dest.shape[1]
    low = lax.broadcasted_iota(I32, (dom, hold), 0) * shard_rows
    inside = jnp.logical_and(dest >= low, dest < low + shard_rows)
    marks = jnp.where(inside, 1.0, 0.0)
    local = dest - jnp.sum(jnp.where(inside, low, 0), axis=0, keepdims=True)
    lanes = 128
    before = lax.broadcasted_iota(I32, (lanes, lanes), 0) < lax.broadcasted_iota(
        I32, (lanes, lanes), 1
    )
    upper = jnp.where(before, 1.0, 0.0).astype(BF16)
    apart = lax.broadcasted_iota(I32, (dom, 1), 0) ^ device
    carry = apart.astype(F32) * cap + 1.0
    found = []
    for start in range(0, hold, lanes):
        part = marks[:, start : start + lanes]
        rank = mm(part.astype(BF16), upper, NN) + carry
        found.append(jnp.sum(jnp.where(part > 0, rank, 0.0), axis=0, keepdims=True))
        carry = carry + jnp.sum(part, axis=1, keepdims=True)
    return jnp.concatenate(found, axis=1).astype(I32) - 1, local


def joined(refs):
    return jnp.concatenate([ref[...] for ref in refs], axis=1)


def pack_first_body(dom, shard_rows, cap, meta, dest_ref, bin_ref, *refs):
    raw, outs, (place_ref, pick) = refs[: -dom - 2], refs[-dom - 2 : -2], refs[-2:]
    dest = dest_ref[...].reshape(1, dest_ref.shape[0])
    bins = bin_ref[...].reshape(1, dest_ref.shape[0])
    place, local = places_of(dest, shard_rows, cap, dom, meta[0])
    place_ref[...] = place
    one_hot_rows(pick, place)
    which = lax.broadcasted_iota(I32, (CODE, dest.shape[1]), 0)
    digits = jnp.where(
        which == 0,
        local >> 4,
        jnp.where(which == 1, local & 15, jnp.where(which == 2, bins, jnp.where(which == 3, 1, 0))),
    )
    digits = jnp.where(dest >= 0, digits, 0).astype(F32).astype(BF16)
    codes = mm(digits, pick[...], NT)
    packed = mm(pick[...], joined(raw), NN).astype(BF16)
    for index, out_ref in enumerate(outs):
        block = slice(index * cap, (index + 1) * cap)
        out_ref[:cap, :] = packed[block]
        out_ref[cap:, :] = jnp.zeros((CODE, out_ref.shape[1]), BF16)
        out_ref[cap:, :cap] = codes[:, block].astype(BF16)


def pack_next_body(cap, dom, meta, place_ref, *refs):
    raw, outs, pick = refs[: -dom - 1], refs[-dom - 1 : -1], refs[-1]
    one_hot_rows(pick, place_ref[...])
    packed = mm(pick[...], joined(raw), NN).astype(BF16)
    for index, out_ref in enumerate(outs):
        out_ref[...] = packed[index * cap : (index + 1) * cap]


def raw_specs(hold, share, chunk):
    first, width = chunk
    at = lambda k: lambda j, m: (0, m[1] * (share // LANES) + first // LANES + k)
    return [pl.BlockSpec((hold, LANES), at(k)) for k in range(width // LANES)]


def pack_first(meta, raw_images, dest, bins, dom, share, chunk):
    hold, _ = raw_images.shape
    width = chunk[1]
    cap = hold // dom
    slots = dom * cap
    specs = raw_specs(hold, share, chunk)
    return call(
        functools.partial(pack_first_body, dom, hold // 2, cap),
        (1,),
        [pl.BlockSpec((hold,), lambda j, m: (0,))] * 2 + specs,
        [pl.BlockSpec((cap + CODE, width), lambda j, m: (0, 0))] * dom
        + [pl.BlockSpec((1, hold), lambda j, m: (0, 0))],
        [sds((cap + CODE, width), BF16)] * dom + [sds((1, hold), I32)],
        scratch=[pltpu.VMEM((slots, hold), BF16)],
        room=51,
        flops=2 * slots * hold * width,
        moved=4 * hold * width,
    )(meta, dest, bins, *[raw_images] * len(specs))


def pack_next(meta, raw_images, place, dom, share, chunk):
    hold, _ = raw_images.shape
    width = chunk[1]
    cap = hold // dom
    slots = dom * cap
    specs = raw_specs(hold, share, chunk)
    return call(
        functools.partial(pack_next_body, cap, dom),
        (1,),
        [pl.BlockSpec((1, hold), lambda j, m: (0, 0))] + specs,
        [pl.BlockSpec((cap, width), lambda j, m: (0, 0))] * dom,
        [sds((cap, width), BF16)] * dom,
        scratch=[pltpu.VMEM((slots, hold), BF16)],
        room=51,
        flops=2 * slots * hold * width,
        moved=4 * hold * width,
    )(meta, place, *[raw_images] * len(specs))


def weigh(first, share, pick, wide, recv, meta, ctf_ref, inv_ref, out_ref):
    width = out_ref.shape[1]
    start = lax.rem(meta[1] * share, ctf_ref.shape[1]) + first
    columns = pl.ds(pl.multiple_of(start, LANES), width)
    table = jnp.concatenate(split3(ctf_ref[:, columns] * inv_ref[:, columns]), axis=0)
    out_ref[...] = (mm(pick, recv, NN) * mm(wide, table, NN)).astype(BF16)


def gather(pieces, whole, rows):
    for index, piece in enumerate(pieces):
        whole[index * rows : (index + 1) * rows, :] = piece[:rows, :]


def unpack_first_body(dom, bins, share, first, meta, *refs):
    pieces, recv_ref = refs[:dom], refs[-1]
    cap = pieces[0].shape[0] - CODE
    gather(pieces, recv_ref, cap)
    ctf_ref, inv_ref, out_ref, hot_ref, pick, wide = refs[dom:-1]
    shard_rows = out_ref.shape[0]
    got = jnp.concatenate([piece[cap:, :cap].astype(F32) for piece in pieces], axis=1)
    row = got[0:1] * 16.0 + got[1:2] + got[3:4] * 1024.0 - 1024.0
    one_hot_rows(pick, row.astype(I32))
    slot_bins = jnp.broadcast_to(got[2:3].astype(BF16), (8, got.shape[1]))
    down = mm(pick[...], slot_bins, NT)[:, 0:1].astype(I32)
    across = mm(slot_bins, pick[...], NT)[0:1].astype(I32)
    lane = lax.broadcasted_iota(I32, (shard_rows, 3 * bins), 1)
    wide[...] = jnp.where((lane & (bins - 1)) == down, 1.0, 0.0).astype(BF16)
    deep = lax.broadcasted_iota(I32, (3 * bins, shard_rows), 0)
    hot_ref[...] = jnp.where((deep & (bins - 1)) == across, 1.0, 0.0).astype(BF16)
    weigh(first, share, pick[...], wide[...], recv_ref[...], meta, ctf_ref, inv_ref, out_ref)


def unpack_next_body(dom, share, first, meta, *refs):
    recv_ref = refs[-1]
    gather(refs[:dom], recv_ref, refs[0].shape[0])
    pick_ref, wide_ref, ctf_ref, inv_ref, out_ref = refs[dom:-1]
    weigh(first, share, pick_ref[...], wide_ref[...], recv_ref[...], meta, ctf_ref, inv_ref, out_ref)


def unpack_first(meta, recv, ctf, inv, share, chunk):
    first, width = chunk
    dom = len(recv)
    slots = dom * (recv[0].shape[0] - CODE)
    rows = slots // 2
    bins, pix = ctf.shape
    whole = lambda shape: pl.BlockSpec(shape, lambda j, m: (0, 0))
    shapes = [(rows, width), (3 * bins, rows), (rows, slots), (rows, 3 * bins)]
    return call(
        functools.partial(unpack_first_body, dom, bins, share, first),
        (1,),
        [whole(recv[0].shape)] * dom + [whole(ctf.shape), whole(inv.shape)],
        [whole(s) for s in shapes],
        [sds(s, BF16) for s in shapes],
        scratch=[pltpu.VMEM((slots, width), BF16)],
        room=28,
        flops=2 * slots * rows * width,
        moved=2 * slots * width,
    )(meta, *recv, ctf, inv)


def unpack_next(meta, pick, wide, recv, ctf, inv, share, chunk):
    first, width = chunk
    dom = len(recv)
    slots = dom * recv[0].shape[0]
    rows = slots // 2
    whole = lambda shape: pl.BlockSpec(shape, lambda j, m: (0, 0))
    return call(
        functools.partial(unpack_next_body, dom, share, first),
        (1,),
        [whole(recv[0].shape)] * dom
        + [whole(pick.shape), whole(wide.shape), whole(ctf.shape), whole(inv.shape)],
        whole((rows, width)),
        sds((rows, width), BF16),
        scratch=[pltpu.VMEM((slots, width), BF16)],
        flops=2 * slots * rows * width,
        moved=2 * slots * width,
    )(meta, *recv, pick, wide, ctf, inv)


def energy_body(bins, count, meta, *refs):
    pieces, (ctf_ref, inv_ref, panel_ref, extra_ref, total) = refs[:-5], refs[-5:]
    width = panel_ref.shape[1]
    blocks = []
    for piece in pieces:
        for start in range(0, piece.shape[1], width):
            blocks.append((piece, start))
    step = pl.program_id(0)

    @pl.when(step == 0)
    def _():
        total[...] = jnp.zeros_like(total)

    gain = ctf_ref[...] * ctf_ref[...] * inv_ref[...]
    gain3 = jnp.concatenate(split3(gain), axis=0)
    for index, (piece, start) in enumerate(blocks):

        @pl.when(step == index)
        def _():
            panel = piece[:, start : start + width]
            panel_ref[...] = panel
            wide = panel.astype(F32)
            square = wide * wide
            high = square.astype(BF16)
            low = (square - high.astype(F32)).astype(BF16)
            total[...] += mm(high, gain3, NT) + mm(low, gain3, NT)

    @pl.when(step == count - 1)
    def _():
        whole = total[:, :bins] + total[:, bins : 2 * bins] + total[:, 2 * bins :]
        extra_ref[...] = jnp.concatenate(split3(-0.5 * whole), axis=1)


def energy(meta, pieces, ctf, inv):
    rows, width = pieces[-1].shape
    count = sum(piece.shape[1] for piece in pieces) // width
    bins, pix = ctf.shape
    wrap = pix // width
    return call(
        functools.partial(energy_body, bins, count),
        (count,),
        [pl.BlockSpec(piece.shape, lambda j, m: (0, 0)) for piece in pieces]
        + [
            pl.BlockSpec((bins, width), lambda j, m: (0, lax.rem(m[0] ^ j, wrap))),
            pl.BlockSpec((1, width), lambda j, m: (0, lax.rem(m[0] ^ j, wrap))),
        ],
        [
            pl.BlockSpec((rows, width), lambda j, m: (0, m[0] ^ j)),
            pl.BlockSpec((rows, 3 * bins), lambda j, m: (0, 0)),
        ],
        [sds((rows, count * width), BF16), sds((rows, 3 * bins), BF16)],
        scratch=[pltpu.VMEM((rows, 3 * bins), F32)],
        flops=2 * 4 * rows * bins * count * width * 3,
        moved=4 * rows * count * width,
    )(meta, *pieces, ctf, inv)


def score_body(parts, used, first, last, meta, *refs):
    own, sib, panel_ref, refs = (
        refs[:parts],
        refs[parts : 2 * parts],
        refs[2 * parts],
        refs[2 * parts + 1 :],
    )
    if first:
        acc_out, full_ref = refs
    elif last:
        acc_ref, _, hot_own, hot_sib, extra_ref, shifted_ref, stat_ref, full_ref = refs
    elif used is None:
        acc_ref, _, acc_out, full_ref = refs
    else:
        acc_ref, acc_out = refs
    half = pl.num_programs(0) // 2

    def tile(sources, hot):
        block = jnp.concatenate([source[...] for source in sources], axis=1)
        if used is None or last:
            full_ref[...] = block
        if last:
            block = block[:, used[0] : used[0] + used[1]]
        panel = panel_ref[...] if used is None else panel_ref[:, used[0] : used[0] + used[1]]
        total = mm(panel, block, NT)
        if not first:
            total = acc_ref[...] + total
        if not last:
            acc_out[...] = total
            return
        total = total + mm(extra_ref[...], hot[...], NN)
        peak = jnp.max(total, axis=0, keepdims=True)
        shifted = jnp.exp(total - peak)
        shifted_ref[...] = shifted
        mass = jnp.sum(shifted, axis=0, keepdims=True)
        which = lax.broadcasted_iota(I32, stat_ref.shape, 0)
        stat_ref[...] = jnp.where(which == 0, peak, mass)

    @pl.when(pl.program_id(0) < half)
    def _():
        tile(own, hot_own if last else None)

    @pl.when(pl.program_id(0) >= half)
    def _():
        tile(sib, hot_sib if last else None)


def score(meta, at, own, sib, panels, width, acc=None, full=None, hots=None, extra=None, used=None):
    rows = own[0].shape[0]
    parts = len(own)
    tile = 256
    half = rows // tile
    count, columns = panels.shape
    first, last = acc is None, hots is not None
    store = used is None or last
    fronts = [pl.BlockSpec((tile, v.shape[1]), lambda j, m: (jnp.minimum(j, half - 1), 0)) for v in own]
    backs = [pl.BlockSpec((tile, v.shape[1]), lambda j, m: (jnp.maximum(j - half, 0), 0)) for v in own]
    acc_spec = pl.BlockSpec((count, tile), lambda j, m: (0, j))
    full_spec = pl.BlockSpec((tile, width), lambda j, m: (j, at(m)))
    in_specs = fronts + backs + [pl.BlockSpec((count, width), lambda j, m: (0, at(m)))]
    operands = [meta, *own, *sib, panels]
    alias = {}
    if not first:
        in_specs += [acc_spec]
        alias = {len(operands): 0}
        operands += [acc]
        if store:
            in_specs += [pl.BlockSpec(memory_space=pl.ANY)]
            alias[len(operands)] = 2 if last else 1
            operands += [full]
    full_shape = sds((2 * rows, columns), BF16)
    acc_shape = sds((count, 2 * rows), F32)
    out_specs, out_shape = [acc_spec, full_spec], [acc_shape, full_shape]
    if last:
        depth = extra.shape[1]
        in_specs += [
            pl.BlockSpec((depth, tile), lambda j, m: (0, jnp.minimum(j, half - 1))),
            pl.BlockSpec((depth, tile), lambda j, m: (0, jnp.maximum(j - half, 0))),
            pl.BlockSpec((count, depth), lambda j, m: (0, 0)),
        ]
        operands += [*hots, extra]
        out_specs = [acc_spec, pl.BlockSpec((8, tile), lambda j, m: (0, j)), full_spec]
        out_shape = [acc_shape, sds((8, 2 * rows), F32), full_shape]
    elif not store:
        out_specs, out_shape = acc_spec, acc_shape
    return call(
        functools.partial(score_body, parts, used, first, last),
        (2 * half,),
        in_specs,
        out_specs,
        out_shape,
        alias=alias,
        room=16,
        flops=2 * count * 2 * rows * width,
        moved=8 * count * 2 * rows + 8 * rows * width,
    )(*operands)


def merge_body(turned, meta, mine_ref, other_ref, out_ref):
    rows = mine_ref.shape[1] // 2
    other = other_ref[...]
    if turned:
        other = jnp.concatenate([other[:, rows:], other[:, :rows]], axis=1)
    mine = mine_ref[...]
    peak = jnp.maximum(mine[0:1], other[0:1])
    mass = mine[1:2] * jnp.exp(mine[0:1] - peak) + other[1:2] * jnp.exp(other[0:1] - peak)
    which = lax.broadcasted_iota(I32, out_ref.shape, 0)
    out_ref[...] = jnp.where(which == 0, peak, mass)


def merge(meta, mine, other, turned=False):
    spec = pl.BlockSpec(mine.shape, lambda j, m: (0, 0))
    return call(functools.partial(merge_body, turned), (1,), [spec, spec], spec, sds(mine.shape, F32), room=4)(meta, mine, other)


def class_body(kind, steps, meta, *refs):
    if kind == "first":
        shifted_ref, stat_ref, all_ref, hot_own, hot_sib, full_ref = refs[:6]
        outs, (post_ref, log_ref, mass_ref) = refs[6 : 6 + steps], refs[6 + steps :]

        @pl.when(pl.program_id(0) == 0)
        def _():
            peak, mass = all_ref[0:1], all_ref[1:2]
            factor = jnp.exp(stat_ref[0:1] - peak) / mass
            post_ref[...] = (shifted_ref[...] * factor).astype(BF16)
            log_ref[...] = (peak + jnp.log(mass))[:, : log_ref.shape[1]]
            bins, rows = mass_ref.shape[0], hot_own.shape[1]
            weights = mm(hot_own[:bins, :], post_ref[:, :rows], NT)
            weights = weights + mm(hot_sib[:bins, :], post_ref[:, rows:], NT)
            mass_ref[...] = weights.astype(BF16)

    else:
        (post_ref, full_ref), outs = refs[:2], refs[2:]
    for step, out_ref in enumerate(outs):

        @pl.when(pl.program_id(0) == step)
        def _():
            out_ref[...] = mm(post_ref[...], full_ref[...], NN).astype(out_ref.dtype)


def class_part(meta, kind, offset, steps, full, post=None, shifted=None, stats=None, hots=None, bins=0):
    rows, columns = full.shape
    width = columns // 8
    count = (shifted if post is None else post).shape[0]
    whole = lambda shape: pl.BlockSpec(shape, lambda j, m: (0, 0))
    full_spec = pl.BlockSpec((rows, width), lambda j, m: (0, m[offset + j]))
    out_specs = [whole((count, width))] * steps
    out_shape = [sds((count, width), F32 if kind == "rest" else BF16)] * steps
    if kind == "first":
        operands = [shifted, *stats, *hots, full]
        in_specs = [whole(shifted.shape)] + [whole(stats[0].shape)] * 2
        in_specs += [whole(hots[0].shape)] * 2 + [full_spec]
        out_specs += [whole((count, rows)), whole((1, rows // 2)), whole((bins, count))]
        out_shape += [sds((count, rows), BF16), sds((1, rows // 2), F32), sds((bins, count), BF16)]
    else:
        operands = [post, full]
        in_specs = [whole(post.shape), full_spec]
    return call(
        functools.partial(class_body, kind, steps),
        (steps,),
        in_specs,
        out_specs,
        out_shape,
        room=22 if kind == "first" else 18,
        flops=2 * count * rows * width * steps,
        moved=2 * rows * width * steps + 4 * count * (rows + width * steps),
    )(meta, *operands)


def forward_body(meta, a_sum, b_sum, down_ref, left_ref, a_ref, b_ref):
    even = meta[0] % 2 == 0
    down, left = down_ref[...].astype(F32), left_ref[...].astype(F32)
    a_ref[...] = (a_sum[...] + jnp.where(even, down, left)).astype(BF16)
    b_ref[...] = (b_sum[...] + jnp.where(even, left, down)).astype(BF16)


def forward(meta, a_sum, b_sum, got_x, got_y):
    shape = a_sum.shape
    spec = pl.BlockSpec(memory_space=pltpu.VMEM)
    return call(forward_body, (1,), [spec] * 4, [spec] * 2, [sds(shape, BF16)] * 2, room=14)(
        meta, a_sum, b_sum, got_x, got_y
    )


def finish_body(tile, meta, keep_ref, a_ref, c_ref, other_ref, b_ref, d_ref, out_ref):
    half = pl.num_programs(0) // 2
    step = pl.program_id(0)

    def total(refs, at):
        rows = pl.ds(pl.multiple_of(at * tile, tile), tile)
        first, second, third = [ref[rows, :].astype(F32) for ref in refs]
        out_ref[...] = first + second + third

    @pl.when(step < half)
    def _():
        total((keep_ref, c_ref, a_ref), step)

    @pl.when(step >= half)
    def _():
        total((other_ref, d_ref, b_ref), step - half)


def finish(meta, keep, got_a, got_c, got_self, got_b, got_d):
    count, width = keep.shape
    half = 3
    tile = count // half

    def place(j, m):
        core = lax.rem(m[0], 2)
        return jnp.where(j < half, core * half + j, (1 - core) * half + j - half), 0

    return call(
        functools.partial(finish_body, tile),
        (2 * half,),
        [pl.BlockSpec(memory_space=pltpu.VMEM)] * 6,
        pl.BlockSpec((tile, width), place),
        sds((2 * count, width), F32),
        room=12,
    )(meta, keep, got_a, got_c, got_self, got_b, got_d)


def two_by_two(raw_images, defocus_bin, dest_row, ctf_table, inv_noise, panels):
    dom, turns = lax.axis_size("dom"), lax.axis_size("rot")
    device, plane = lax.axis_index("dom"), lax.axis_index("rot")
    bins = ctf_table.shape[0]
    columns = raw_images.shape[1]
    chip, core = device // 2, device % 2

    def block(apart, half):
        return (chip ^ apart) * 2 + half

    x_first, y_second = block(1, 0), block(2, 1)
    x_second, y_first = block(1, 1), block(2, 0)
    even = core == 0
    order = [
        device,
        plane,
        block(3, 0),
        block(3, 1),
        jnp.where(even, x_first, y_second),
        jnp.where(even, y_second, x_first),
        block(0, 1 - core),
        jnp.where(even, y_first, x_second),
        jnp.where(even, x_second, y_first),
        block(0, core),
    ]
    meta = jnp.stack(order).astype(I32)
    inv = inv_noise[None, :]

    def across(value, apart):
        return lax.ppermute(value, "dom", [(i, i ^ apart) for i in range(dom)])

    def by_core(value, when_even, when_odd):
        pairs = [(i, i ^ (when_odd if i % 2 else when_even)) for i in range(dom)]
        return lax.ppermute(value, "dom", pairs)

    def onward(value):
        return lax.ppermute(value, "rot", [(i, (i + 1) % turns) for i in range(turns)])

    width = columns // turns
    cut = width * 5 // 8
    chunk_a, chunk_b = (0, cut), (cut, width - cut)

    def exchange(blocks):
        got = [blocks[0]] + [None] * (dom - 1)
        for apart in (6, 7, 2, 4, 3, 5, 1):
            got[apart] = across(blocks[apart], apart)
        return got

    *send_a, place = pack_first(meta, raw_images, dest_row, defocus_bin, dom, width, chunk_a)
    recv_a = exchange(send_a)
    send_b = pack_next(meta, raw_images, place, dom, width, chunk_b)
    together = lax.optimization_barrier

    count = panels.shape[0] // 2
    place, panels = together((place, panels))
    mine = lax.dynamic_slice_in_dim(panels, core * count, count, 0)
    other = across(lax.dynamic_slice_in_dim(panels, (1 - core) * count, count, 0), 1)
    near = jnp.concatenate([mine, other], axis=1)

    recv_a, send_b, near = together((recv_a, send_b, near))
    share_a, hot, pick, wide = unpack_first(meta, recv_a, ctf_table, inv, width, chunk_a)
    share_a, send_b = together((share_a, send_b))
    a1, recv_b = onward(share_a), exchange(send_b)
    a1, recv_b, near = together((a1, recv_b, near))
    by_x, by_y = across(near, 2), across(near, 4)
    share_b = unpack_next(meta, pick, wide, recv_b, ctf_table, inv, width, chunk_b)
    hots = (hot, across(hot, 1))
    a2, b1 = onward(a1), onward(share_b)
    a2, b1, by_x, by_y = together((a2, b1, by_x, by_y))
    piece = near.shape[1] // 2
    far_y, far_x = across(by_x[:, :piece], 4), across(by_y[:, piece:], 2)
    a3, b2 = onward(a2), onward(b1)
    panel_full, extra = energy(meta, [near, by_x, by_y, far_y, far_x], ctf_table, inv)
    a3, b2, panel_full, extra, hots = together((a3, b2, panel_full, extra, hots))
    b3 = onward(b2)

    def share(turn):
        return lambda m: lax.rem(m[1] + turns - turn, turns)

    acc = full = None
    for turn, own in enumerate([(share_a, share_b), (a1, b1), (a2, b2)]):
        sib = [across(value, 1) for value in own]
        acc, full = score(meta, share(turn), own, sib, panel_full, width, acc, full)
    final = share(turns - 1)
    a3_sib = across(a3, 1)
    acc = score(meta, final, [a3], [a3_sib], panel_full, width, acc, used=chunk_a)
    b3, acc = together((b3, acc))
    shifted, stat, full = score(
        meta,
        final,
        [a3, b3],
        [a3_sib, across(b3, 1)],
        panel_full,
        width,
        acc,
        full,
        hots,
        extra,
        chunk_b,
    )

    total = merge(meta, stat, across(stat, 1), turned=True)
    for apart in (1, 2):
        pairs = [(i, i ^ apart) for i in range(turns)]
        total = merge(meta, total, lax.ppermute(total, "rot", pairs))
    to_x, to_y, post, log_evidence, mass = class_part(
        meta, "first", 2, 2, full, None, shifted, [stat, total], hots, bins
    )
    mass_x = across(mass, 2)
    got_x, got_y = across(to_x, 2), across(to_y, 4)
    send_c, send_d, give = class_part(meta, "next", 4, 3, full, post)
    mass = mass.astype(F32) + mass_x.astype(F32)
    mass = mass + across(mass, 4)
    a_sum, b_sum, keep = class_part(meta, "rest", 7, 3, full, post)
    got_x, got_y, send_c, send_d, a_sum, b_sum, keep, give, mass = together(
        (got_x, got_y, send_c, send_d, a_sum, b_sum, keep, give, mass)
    )
    got_c, got_d = by_core(send_c, 2, 4), by_core(send_d, 5, 3)
    message_a, message_b = forward(meta, a_sum, b_sum, got_x, got_y)
    got_a, got_b = by_core(message_a, 4, 2), by_core(message_b, 3, 5)
    got_self = across(give, 1)
    mass_other = across(mass, 1)
    bin_weights = jnp.where(
        even,
        jnp.concatenate([mass, mass_other], axis=1),
        jnp.concatenate([mass_other, mass], axis=1),
    )
    class_sums = finish(meta, keep, got_a, got_c, got_self, got_b, got_d).T
    return class_sums, bin_weights, log_evidence.reshape(-1)


def energy_block(gain_block, panel_piece):
    widened = panel_piece.astype(jnp.float32)
    return lax.dot_general(
        gain_block, widened * widened, (((1,), (1,)), ((), ())), precision=lax.Precision.HIGHEST
    )


def on_device(raw_images, defocus_bin, dest_row, ctf_table, inv_noise, panels):
    dom_count = lax.axis_size("dom")
    bin_count = ctf_table.shape[0]
    columns = raw_images.shape[1]
    hold_rows = raw_images.shape[0]
    shard_rows = hold_rows // 2
    capacity = 2 * shard_rows // dom_count
    is_live = dest_row >= 0
    target = jnp.where(is_live, dest_row // shard_rows, dom_count)
    local_row = dest_row % shard_rows
    marks = (target[:, None] == jnp.arange(dom_count, dtype=jnp.int32)[None, :]).astype(jnp.int32)
    slot_rank = jnp.sum((jnp.cumsum(marks, axis=0) - marks) * marks, axis=1)
    row_code = jnp.where(is_live, local_row * bin_count + defocus_bin, -1)
    padded_images = jnp.concatenate([raw_images, jnp.zeros((1, columns), raw_images.dtype)], axis=0)
    padded_code = jnp.concatenate([row_code, jnp.full((1,), -1, jnp.int32)], axis=0)
    position = jnp.where(is_live, target * capacity + slot_rank, dom_count * capacity)
    slot_count = dom_count * capacity
    source = (
        jnp.full((slot_count,), hold_rows, jnp.int32)
        .at[position]
        .set(jnp.arange(hold_rows, dtype=jnp.int32), mode="drop")
    )
    send_images = padded_images[source].reshape(dom_count, capacity, columns)
    send_code = padded_code[source].reshape(dom_count, capacity)
    recv_images, recv_code = (
        lax.all_to_all(send_images, "dom", split_axis=0, concat_axis=0, tiled=True),
        lax.all_to_all(send_code, "dom", split_axis=0, concat_axis=0, tiled=True),
    )
    flat_images = recv_images.reshape(-1, columns)
    flat_code = recv_code.reshape(-1)
    arrived = flat_code >= 0
    row_of = jnp.where(arrived, flat_code // bin_count, shard_rows)
    row_order = (
        jnp.zeros((shard_rows,), jnp.int32)
        .at[row_of]
        .set(jnp.arange(flat_code.shape[0], dtype=jnp.int32), mode="drop")
    )
    images = flat_images[row_order]
    bin_ids = flat_code[row_order] % bin_count
    bin_table = (bin_ids[:, None] == jnp.arange(bin_count, dtype=jnp.int32)[None, :]).astype(
        jnp.float32
    )
    ctf_rows = jnp.dot(bin_table, ctf_table, precision=lax.Precision.HIGHEST)
    factor = ctf_rows * inv_noise[None, :]
    weighted = (images.astype(jnp.float32) * jnp.concatenate([factor, factor], axis=1)).astype(
        jnp.bfloat16
    )
    gain_half = ctf_table * ctf_table * inv_noise[None, :]
    gain_full = jnp.concatenate([gain_half, gain_half], axis=1)
    panel_piece = lax.all_gather(panels, "dom", axis=1, tiled=True)
    col_block = weighted
    cross_term = lax.dot_general(
        col_block, panel_piece, (((1,), (1,)), ((), ())), preferred_element_type=jnp.float32
    )
    energy = energy_block(gain_full, panel_piece)
    scores = cross_term - 0.5 * jnp.dot(bin_table, energy, precision=lax.Precision.HIGHEST)
    local_peak = jnp.max(scores, axis=1)
    row_peak = lax.pmax(local_peak, "rot")
    shifted = jnp.exp(scores - row_peak[:, None])
    row_total = lax.psum(jnp.sum(shifted, axis=1), "rot")
    posterior = (shifted / row_total[:, None]).astype(jnp.bfloat16)
    log_evidence = row_peak + jnp.log(row_total)
    col_block = weighted
    class_sums = lax.psum_scatter(
        lax.dot_general(
            col_block, posterior, (((0,), (0,)), ((), ())), preferred_element_type=jnp.float32
        ).astype(jnp.bfloat16),
        "dom",
        scatter_dimension=0,
        tiled=True,
    ).astype(jnp.float32)
    local_mass = lax.dot_general(
        bin_table.astype(jnp.bfloat16),
        posterior,
        (((0,), (0,)), ((), ())),
        preferred_element_type=jnp.float32,
    )
    bin_weights = lax.psum(local_mass.astype(jnp.bfloat16), "dom").astype(jnp.float32)
    return (class_sums, bin_weights, log_evidence)


def solution(mesh):
    small = mesh.shape["dom"] == 8 and mesh.shape["rot"] == 4
    return jax.shard_map(
        two_by_two if small else on_device,
        mesh=mesh,
        in_specs=(P("dom", None), P("dom"), P("dom"), P(), P(), P("rot", "dom")),
        out_specs=(P("dom", "rot"), P(None, "rot"), P("dom")),
        check_vma=False,
    )
```

```python
import functools

import jax
import jax.numpy as jnp
from jax import lax
from jax.experimental import pallas as pl
from jax.experimental.pallas import tpu as pltpu
from jax.sharding import PartitionSpec as P

NN = (((1,), (0,)), ((), ()))
NT = (((1,), (1,)), ((), ()))
F32, BF16, I32 = jnp.float32, jnp.bfloat16, jnp.int32
CODE = 16
LANES = 128
MIB = 1024 * 1024


def mm(a, b, dims):
    return lax.dot_general(a, b, dims, preferred_element_type=F32)


def split3(x):
    hi = x.astype(BF16)
    rest = x - hi.astype(F32)
    mid = rest.astype(BF16)
    low = (rest - mid.astype(F32)).astype(BF16)
    return hi, mid, low


def call(body, grid, in_specs, out_specs, out_shape, scratch=(), alias=None, flops=0, moved=0, room=24):
    return pl.pallas_call(
        body,
        grid_spec=pltpu.PrefetchScalarGridSpec(
            num_scalar_prefetch=1,
            grid=grid,
            in_specs=in_specs,
            out_specs=out_specs,
            scratch_shapes=list(scratch),
        ),
        out_shape=out_shape,
        input_output_aliases=alias or {},
        compiler_params=pltpu.CompilerParams(vmem_limit_bytes=room * MIB),
        cost_estimate=pl.CostEstimate(
            flops=flops // 16, bytes_accessed=moved // 16, transcendentals=0
        ),
    )


def sds(shape, dtype):
    return jax.ShapeDtypeStruct(shape, dtype)


def one_hot_rows(out_ref, wanted):
    rows, width = out_ref.shape
    step = 256 if rows % 256 == 0 else rows
    for start in range(0, rows, step):
        index = lax.broadcasted_iota(I32, (step, width), 0) + start
        out_ref[start : start + step, :] = jnp.where(index == wanted, 1.0, 0.0).astype(BF16)


def places_of(dest, shard_rows, cap, dom, device):
    hold = dest.shape[1]
    low = lax.broadcasted_iota(I32, (dom, hold), 0) * shard_rows
    inside = jnp.logical_and(dest >= low, dest < low + shard_rows)
    marks = jnp.where(inside, 1.0, 0.0)
    local = dest - jnp.sum(jnp.where(inside, low, 0), axis=0, keepdims=True)
    lanes = 128
    before = lax.broadcasted_iota(I32, (lanes, lanes), 0) < lax.broadcasted_iota(
        I32, (lanes, lanes), 1
    )
    upper = jnp.where(before, 1.0, 0.0).astype(BF16)
    apart = lax.broadcasted_iota(I32, (dom, 1), 0) ^ device
    carry = apart.astype(F32) * cap + 1.0
    found = []
    for start in range(0, hold, lanes):
        part = marks[:, start : start + lanes]
        rank = mm(part.astype(BF16), upper, NN) + carry
        found.append(jnp.sum(jnp.where(part > 0, rank, 0.0), axis=0, keepdims=True))
        carry = carry + jnp.sum(part, axis=1, keepdims=True)
    return jnp.concatenate(found, axis=1).astype(I32) - 1, local


def joined(refs):
    return jnp.concatenate([ref[...] for ref in refs], axis=1)


def pack_first_body(dom, shard_rows, cap, meta, dest_ref, bin_ref, *refs):
    raw, outs, (place_ref, pick) = refs[: -dom - 2], refs[-dom - 2 : -2], refs[-2:]
    dest = dest_ref[...].reshape(1, dest_ref.shape[0])
    bins = bin_ref[...].reshape(1, dest_ref.shape[0])
    place, local = places_of(dest, shard_rows, cap, dom, meta[0])
    place_ref[...] = place
    one_hot_rows(pick, place)
    which = lax.broadcasted_iota(I32, (CODE, dest.shape[1]), 0)
    digits = jnp.where(
        which == 0,
        local >> 4,
        jnp.where(which == 1, local & 15, jnp.where(which == 2, bins, jnp.where(which == 3, 1, 0))),
    )
    digits = jnp.where(dest >= 0, digits, 0).astype(F32).astype(BF16)
    codes = mm(digits, pick[...], NT)
    packed = mm(pick[...], joined(raw), NN).astype(BF16)
    for index, out_ref in enumerate(outs):
        block = slice(index * cap, (index + 1) * cap)
        out_ref[:cap, :] = packed[block]
        out_ref[cap:, :] = jnp.zeros((CODE, out_ref.shape[1]), BF16)
        out_ref[cap:, :cap] = codes[:, block].astype(BF16)


def pack_next_body(cap, dom, meta, place_ref, *refs):
    raw, outs, pick = refs[: -dom - 1], refs[-dom - 1 : -1], refs[-1]
    one_hot_rows(pick, place_ref[...])
    packed = mm(pick[...], joined(raw), NN).astype(BF16)
    for index, out_ref in enumerate(outs):
        out_ref[...] = packed[index * cap : (index + 1) * cap]


def raw_specs(hold, share, chunk):
    first, width = chunk
    at = lambda k: lambda j, m: (0, m[1] * (share // LANES) + first // LANES + k)
    return [pl.BlockSpec((hold, LANES), at(k)) for k in range(width // LANES)]


def pack_first(meta, raw_images, dest, bins, dom, share, chunk):
    hold, _ = raw_images.shape
    width = chunk[1]
    cap = hold // dom
    slots = dom * cap
    specs = raw_specs(hold, share, chunk)
    return call(
        functools.partial(pack_first_body, dom, hold // 2, cap),
        (1,),
        [pl.BlockSpec((hold,), lambda j, m: (0,))] * 2 + specs,
        [pl.BlockSpec((cap + CODE, width), lambda j, m: (0, 0))] * dom
        + [pl.BlockSpec((1, hold), lambda j, m: (0, 0))],
        [sds((cap + CODE, width), BF16)] * dom + [sds((1, hold), I32)],
        scratch=[pltpu.VMEM((slots, hold), BF16)],
        room=51,
        flops=2 * slots * hold * width,
        moved=4 * hold * width,
    )(meta, dest, bins, *[raw_images] * len(specs))


def pack_next(meta, raw_images, place, dom, share, chunk):
    hold, _ = raw_images.shape
    width = chunk[1]
    cap = hold // dom
    slots = dom * cap
    specs = raw_specs(hold, share, chunk)
    return call(
        functools.partial(pack_next_body, cap, dom),
        (1,),
        [pl.BlockSpec((1, hold), lambda j, m: (0, 0))] + specs,
        [pl.BlockSpec((cap, width), lambda j, m: (0, 0))] * dom,
        [sds((cap, width), BF16)] * dom,
        scratch=[pltpu.VMEM((slots, hold), BF16)],
        room=51,
        flops=2 * slots * hold * width,
        moved=4 * hold * width,
    )(meta, place, *[raw_images] * len(specs))


def weigh(first, share, pick, wide, recv, meta, ctf_ref, inv_ref, out_ref):
    width = out_ref.shape[1]
    start = lax.rem(meta[1] * share, ctf_ref.shape[1]) + first
    columns = pl.ds(pl.multiple_of(start, LANES), width)
    table = jnp.concatenate(split3(ctf_ref[:, columns] * inv_ref[:, columns]), axis=0)
    out_ref[...] = (mm(pick, recv, NN) * mm(wide, table, NN)).astype(BF16)


def gather(pieces, whole, rows):
    for index, piece in enumerate(pieces):
        whole[index * rows : (index + 1) * rows, :] = piece[:rows, :]


def unpack_first_body(dom, bins, share, first, meta, *refs):
    pieces, recv_ref = refs[:dom], refs[-1]
    cap = pieces[0].shape[0] - CODE
    gather(pieces, recv_ref, cap)
    ctf_ref, inv_ref, out_ref, hot_ref, pick, wide = refs[dom:-1]
    shard_rows = out_ref.shape[0]
    got = jnp.concatenate([piece[cap:, :cap].astype(F32) for piece in pieces], axis=1)
    row = got[0:1] * 16.0 + got[1:2] + got[3:4] * 1024.0 - 1024.0
    one_hot_rows(pick, row.astype(I32))
    slot_bins = jnp.broadcast_to(got[2:3].astype(BF16), (8, got.shape[1]))
    down = mm(pick[...], slot_bins, NT)[:, 0:1].astype(I32)
    across = mm(slot_bins, pick[...], NT)[0:1].astype(I32)
    lane = lax.broadcasted_iota(I32, (shard_rows, 3 * bins), 1)
    wide[...] = jnp.where((lane & (bins - 1)) == down, 1.0, 0.0).astype(BF16)
    deep = lax.broadcasted_iota(I32, (3 * bins, shard_rows), 0)
    hot_ref[...] = jnp.where((deep & (bins - 1)) == across, 1.0, 0.0).astype(BF16)
    weigh(first, share, pick[...], wide[...], recv_ref[...], meta, ctf_ref, inv_ref, out_ref)


def unpack_next_body(dom, share, first, meta, *refs):
    recv_ref = refs[-1]
    gather(refs[:dom], recv_ref, refs[0].shape[0])
    pick_ref, wide_ref, ctf_ref, inv_ref, out_ref = refs[dom:-1]
    weigh(first, share, pick_ref[...], wide_ref[...], recv_ref[...], meta, ctf_ref, inv_ref, out_ref)


def unpack_first(meta, recv, ctf, inv, share, chunk):
    first, width = chunk
    dom = len(recv)
    slots = dom * (recv[0].shape[0] - CODE)
    rows = slots // 2
    bins, pix = ctf.shape
    whole = lambda shape: pl.BlockSpec(shape, lambda j, m: (0, 0))
    shapes = [(rows, width), (3 * bins, rows), (rows, slots), (rows, 3 * bins)]
    return call(
        functools.partial(unpack_first_body, dom, bins, share, first),
        (1,),
        [whole(recv[0].shape)] * dom + [whole(ctf.shape), whole(inv.shape)],
        [whole(s) for s in shapes],
        [sds(s, BF16) for s in shapes],
        scratch=[pltpu.VMEM((slots, width), BF16)],
        room=28,
        flops=2 * slots * rows * width,
        moved=2 * slots * width,
    )(meta, *recv, ctf, inv)


def unpack_next(meta, pick, wide, recv, ctf, inv, share, chunk):
    first, width = chunk
    dom = len(recv)
    slots = dom * recv[0].shape[0]
    rows = slots // 2
    whole = lambda shape: pl.BlockSpec(shape, lambda j, m: (0, 0))
    return call(
        functools.partial(unpack_next_body, dom, share, first),
        (1,),
        [whole(recv[0].shape)] * dom
        + [whole(pick.shape), whole(wide.shape), whole(ctf.shape), whole(inv.shape)],
        whole((rows, width)),
        sds((rows, width), BF16),
        scratch=[pltpu.VMEM((slots, width), BF16)],
        flops=2 * slots * rows * width,
        moved=2 * slots * width,
    )(meta, *recv, pick, wide, ctf, inv)


def energy_body(bins, count, meta, *refs):
    pieces, (ctf_ref, inv_ref, panel_ref, extra_ref, total) = refs[:-5], refs[-5:]
    width = panel_ref.shape[1]
    blocks = []
    for piece in pieces:
        for start in range(0, piece.shape[1], width):
            blocks.append((piece, start))
    step = pl.program_id(0)

    @pl.when(step == 0)
    def _():
        total[...] = jnp.zeros_like(total)

    gain = ctf_ref[...] * ctf_ref[...] * inv_ref[...]
    gain3 = jnp.concatenate(split3(gain), axis=0)
    for index, (piece, start) in enumerate(blocks):

        @pl.when(step == index)
        def _():
            panel = piece[:, start : start + width]
            panel_ref[...] = panel
            wide = panel.astype(F32)
            square = wide * wide
            high = square.astype(BF16)
            low = (square - high.astype(F32)).astype(BF16)
            total[...] += mm(high, gain3, NT) + mm(low, gain3, NT)

    @pl.when(step == count - 1)
    def _():
        whole = total[:, :bins] + total[:, bins : 2 * bins] + total[:, 2 * bins :]
        extra_ref[...] = jnp.concatenate(split3(-0.5 * whole), axis=1)


def energy(meta, pieces, ctf, inv):
    rows, width = pieces[-1].shape
    count = sum(piece.shape[1] for piece in pieces) // width
    bins, pix = ctf.shape
    wrap = pix // width
    return call(
        functools.partial(energy_body, bins, count),
        (count,),
        [pl.BlockSpec(piece.shape, lambda j, m: (0, 0)) for piece in pieces]
        + [
            pl.BlockSpec((bins, width), lambda j, m: (0, lax.rem(m[0] ^ j, wrap))),
            pl.BlockSpec((1, width), lambda j, m: (0, lax.rem(m[0] ^ j, wrap))),
        ],
        [
            pl.BlockSpec((rows, width), lambda j, m: (0, m[0] ^ j)),
            pl.BlockSpec((rows, 3 * bins), lambda j, m: (0, 0)),
        ],
        [sds((rows, count * width), BF16), sds((rows, 3 * bins), BF16)],
        scratch=[pltpu.VMEM((rows, 3 * bins), F32)],
        flops=2 * 4 * rows * bins * count * width * 3,
        moved=4 * rows * count * width,
    )(meta, *pieces, ctf, inv)


def score_body(parts, used, first, last, meta, *refs):
    own, sib, panel_ref, refs = (
        refs[:parts],
        refs[parts : 2 * parts],
        refs[2 * parts],
        refs[2 * parts + 1 :],
    )
    if first:
        acc_out, full_ref = refs
    elif last:
        acc_ref, _, hot_own, hot_sib, extra_ref, shifted_ref, stat_ref, full_ref = refs
    elif used is None:
        acc_ref, _, acc_out, full_ref = refs
    else:
        acc_ref, acc_out = refs
    half = pl.num_programs(0) // 2

    def tile(sources, hot):
        block = jnp.concatenate([source[...] for source in sources], axis=1)
        if used is None or last:
            full_ref[...] = block
        if last:
            block = block[:, used[0] : used[0] + used[1]]
        panel = panel_ref[...] if used is None else panel_ref[:, used[0] : used[0] + used[1]]
        total = mm(panel, block, NT)
        if not first:
            total = acc_ref[...] + total
        if not last:
            acc_out[...] = total
            return
        total = total + mm(extra_ref[...], hot[...], NN)
        peak = jnp.max(total, axis=0, keepdims=True)
        shifted = jnp.exp(total - peak)
        shifted_ref[...] = shifted
        mass = jnp.sum(shifted, axis=0, keepdims=True)
        which = lax.broadcasted_iota(I32, stat_ref.shape, 0)
        stat_ref[...] = jnp.where(which == 0, peak, mass)

    @pl.when(pl.program_id(0) < half)
    def _():
        tile(own, hot_own if last else None)

    @pl.when(pl.program_id(0) >= half)
    def _():
        tile(sib, hot_sib if last else None)


def score(meta, at, own, sib, panels, width, acc=None, full=None, hots=None, extra=None, used=None):
    rows = own[0].shape[0]
    parts = len(own)
    tile = 256
    half = rows // tile
    count, columns = panels.shape
    first, last = acc is None, hots is not None
    store = used is None or last
    fronts = [pl.BlockSpec((tile, v.shape[1]), lambda j, m: (jnp.minimum(j, half - 1), 0)) for v in own]
    backs = [pl.BlockSpec((tile, v.shape[1]), lambda j, m: (jnp.maximum(j - half, 0), 0)) for v in own]
    acc_spec = pl.BlockSpec((count, tile), lambda j, m: (0, j))
    full_spec = pl.BlockSpec((tile, width), lambda j, m: (j, at(m)))
    in_specs = fronts + backs + [pl.BlockSpec((count, width), lambda j, m: (0, at(m)))]
    operands = [meta, *own, *sib, panels]
    alias = {}
    if not first:
        in_specs += [acc_spec]
        alias = {len(operands): 0}
        operands += [acc]
        if store:
            in_specs += [pl.BlockSpec(memory_space=pl.ANY)]
            alias[len(operands)] = 2 if last else 1
            operands += [full]
    full_shape = sds((2 * rows, columns), BF16)
    acc_shape = sds((count, 2 * rows), F32)
    out_specs, out_shape = [acc_spec, full_spec], [acc_shape, full_shape]
    if last:
        depth = extra.shape[1]
        in_specs += [
            pl.BlockSpec((depth, tile), lambda j, m: (0, jnp.minimum(j, half - 1))),
            pl.BlockSpec((depth, tile), lambda j, m: (0, jnp.maximum(j - half, 0))),
            pl.BlockSpec((count, depth), lambda j, m: (0, 0)),
        ]
        operands += [*hots, extra]
        out_specs = [acc_spec, pl.BlockSpec((8, tile), lambda j, m: (0, j)), full_spec]
        out_shape = [acc_shape, sds((8, 2 * rows), F32), full_shape]
    elif not store:
        out_specs, out_shape = acc_spec, acc_shape
    return call(
        functools.partial(score_body, parts, used, first, last),
        (2 * half,),
        in_specs,
        out_specs,
        out_shape,
        alias=alias,
        room=16,
        flops=2 * count * 2 * rows * width,
        moved=8 * count * 2 * rows + 8 * rows * width,
    )(*operands)


def merge_body(meta, mine_ref, other_ref, out_ref):
    rows = mine_ref.shape[1] // 2
    other = other_ref[...]
    other = jnp.concatenate([other[:, rows:], other[:, :rows]], axis=1)
    mine = mine_ref[...]
    peak = jnp.maximum(mine[0:1], other[0:1])
    mass = mine[1:2] * jnp.exp(mine[0:1] - peak) + other[1:2] * jnp.exp(other[0:1] - peak)
    which = lax.broadcasted_iota(I32, out_ref.shape, 0)
    out_ref[...] = jnp.where(which == 0, peak, mass)


def add_body(meta, mine_ref, other_ref, out_ref):
    out_ref[...] = (mine_ref[...].astype(F32) + other_ref[...].astype(F32)).astype(BF16)


def pairwise(body, meta, mine, other):
    spec = pl.BlockSpec(mine.shape, lambda j, m: (0, 0))
    return call(body, (1,), [spec, spec], spec, sds(mine.shape, mine.dtype), room=4)(
        meta, mine, other
    )


merge = functools.partial(pairwise, merge_body)
add_pair = functools.partial(pairwise, add_body)


def class_body(kind, steps, meta, *refs):
    if kind == "first":
        (shifted_ref, stat_ref), four = refs[:2], refs[2:6]
        hot_own, hot_sib, full_ref = refs[6:9]
        outs, (post_ref, log_ref, mass_ref) = refs[9 : 9 + steps], refs[9 + steps :]

        @pl.when(pl.program_id(0) == 0)
        def _():
            stats = [ref[...] for ref in four]
            peaks = [s[0:1] for s in stats]
            peak = jnp.maximum(jnp.maximum(peaks[0], peaks[1]), jnp.maximum(peaks[2], peaks[3]))
            parts = [s[1:2] * jnp.exp(p - peak) for s, p in zip(stats, peaks)]
            mass = (parts[0] + parts[1]) + (parts[2] + parts[3])
            factor = jnp.exp(stat_ref[0:1] - peak) / mass
            post_ref[...] = (shifted_ref[...] * factor).astype(BF16)
            log_ref[...] = (peak + jnp.log(mass))[:, : log_ref.shape[1]]
            bins, rows = mass_ref.shape[0], hot_own.shape[1]
            weights = mm(hot_own[:bins, :], post_ref[:, :rows], NT)
            weights = weights + mm(hot_sib[:bins, :], post_ref[:, rows:], NT)
            mass_ref[...] = weights.astype(BF16)

    else:
        (post_ref, full_ref), outs = refs[:2], refs[2:]
    for step, out_ref in enumerate(outs):

        @pl.when(pl.program_id(0) == step)
        def _():
            out_ref[...] = mm(post_ref[...], full_ref[...], NN).astype(out_ref.dtype)


def class_part(meta, kind, offset, steps, full, post=None, shifted=None, stats=None, hots=None, bins=0):
    rows, columns = full.shape
    width = columns // 8
    count = (shifted if post is None else post).shape[0]
    whole = lambda shape: pl.BlockSpec(shape, lambda j, m: (0, 0))
    full_spec = pl.BlockSpec((rows, width), lambda j, m: (0, m[offset + j]))
    out_specs = [whole((count, width))] * steps
    out_shape = [sds((count, width), F32 if kind == "rest" else BF16)] * steps
    if kind == "first":
        operands = [shifted, *stats, *hots, full]
        in_specs = [whole(shifted.shape)] + [whole(stats[0].shape)] * 5
        in_specs += [whole(hots[0].shape)] * 2 + [full_spec]
        out_specs += [whole((count, rows)), whole((1, rows // 2)), whole((bins, count))]
        out_shape += [sds((count, rows), BF16), sds((1, rows // 2), F32), sds((bins, count), BF16)]
    else:
        operands = [post, full]
        in_specs = [whole(post.shape), full_spec]
    return call(
        functools.partial(class_body, kind, steps),
        (steps,),
        in_specs,
        out_specs,
        out_shape,
        room=22 if kind == "first" else 18,
        flops=2 * count * rows * width * steps,
        moved=2 * rows * width * steps + 4 * count * (rows + width * steps),
    )(meta, *operands)


def two_by_two(raw_images, defocus_bin, dest_row, ctf_table, inv_noise, panels):
    dom, turns = lax.axis_size("dom"), lax.axis_size("rot")
    device, plane = lax.axis_index("dom"), lax.axis_index("rot")
    bins = ctf_table.shape[0]
    columns = raw_images.shape[1]
    chip, core = device // 2, device % 2

    def block(apart, half):
        return (chip ^ apart) * 2 + half

    x_first, y_second = block(1, 0), block(2, 1)
    x_second, y_first = block(1, 1), block(2, 0)
    even = core == 0
    order = [
        device,
        plane,
        block(3, 0),
        block(3, 1),
        jnp.where(even, x_first, y_second),
        jnp.where(even, y_second, x_first),
        block(0, 1 - core),
        jnp.where(even, y_first, x_second),
        jnp.where(even, x_second, y_first),
        block(0, core),
    ]
    meta = jnp.stack(order).astype(I32)
    inv = inv_noise[None, :]

    def across(value, apart):
        return lax.ppermute(value, "dom", [(i, i ^ apart) for i in range(dom)])

    def by_core(value, when_even, when_odd):
        pairs = [(i, i ^ (when_odd if i % 2 else when_even)) for i in range(dom)]
        return lax.ppermute(value, "dom", pairs)

    def onward(value):
        return lax.ppermute(value, "rot", [(i, (i + 1) % turns) for i in range(turns)])

    width = columns // turns
    cut = width * 5 // 8
    chunk_a, chunk_b = (0, cut), (cut, width - cut)

    def exchange(blocks):
        got = [blocks[0]] + [None] * (dom - 1)
        for apart in (6, 7, 2, 4, 3, 5, 1):
            got[apart] = across(blocks[apart], apart)
        return got

    *send_a, place = pack_first(meta, raw_images, dest_row, defocus_bin, dom, width, chunk_a)
    recv_a = exchange(send_a)
    send_b = pack_next(meta, raw_images, place, dom, width, chunk_b)
    together = lax.optimization_barrier

    count = panels.shape[0] // 2
    mine = lax.dynamic_slice_in_dim(panels, core * count, count, 0)
    other = lax.dynamic_slice_in_dim(across(panels, 1), core * count, count, 0)
    near = jnp.concatenate([mine, other], axis=1)

    recv_a, send_b, near = together((recv_a, send_b, near))
    share_a, hot, pick, wide = unpack_first(meta, recv_a, ctf_table, inv, width, chunk_a)
    share_a, send_b = together((share_a, send_b))
    a1, recv_b = onward(share_a), exchange(send_b)
    a1, recv_b, near = together((a1, recv_b, near))
    by_x, by_y = across(near, 2), across(near, 4)
    share_b = unpack_next(meta, pick, wide, recv_b, ctf_table, inv, width, chunk_b)
    a2, b1 = onward(a1), onward(share_b)
    sib0, sib1, hots = [across(share_a, 1), across(share_b, 1)], [across(a1, 1)], [hot, across(hot, 1)]
    a2, b1, by_x, by_y, sib0, sib1, hots = together((a2, b1, by_x, by_y, sib0, sib1, hots))
    sib1 = sib1 + [across(b1, 1)]
    piece = near.shape[1] // 2
    far_y, far_x = across(by_x[:, :piece], 4), across(by_y[:, piece:], 2)
    a3, b2 = onward(a2), onward(b1)
    panel_full, extra = energy(meta, [near, by_x, by_y, far_y, far_x], ctf_table, inv)

    def share(turn):
        return lambda m: lax.rem(m[1] + turns - turn, turns)

    acc, full = score(meta, share(0), [share_a, share_b], sib0, panel_full, width)
    acc, full = score(meta, share(1), [a1, b1], sib1, panel_full, width, acc, full)
    a3, b2, acc, full = together((a3, b2, acc, full))
    b3 = onward(b2)
    sib2 = [across(a2, 1), across(b2, 1)]
    acc, full = score(meta, share(2), [a2, b2], sib2, panel_full, width, acc, full)
    final = share(turns - 1)
    a3_sib = across(a3, 1)
    acc = score(meta, final, [a3], [a3_sib], panel_full, width, acc, used=chunk_a)
    b3, acc = together((b3, acc))
    shifted, stat, full = score(
        meta,
        final,
        [a3, b3],
        [a3_sib, across(b3, 1)],
        panel_full,
        width,
        acc,
        full,
        hots,
        extra,
        chunk_b,
    )

    pair = merge(meta, stat, across(stat, 1))
    others = [
        lax.ppermute(pair, "rot", [(i, i ^ apart) for i in range(turns)]) for apart in (1, 2, 3)
    ]
    to_x, to_y, post, log_evidence, mass = class_part(
        meta, "first", 2, 2, full, None, shifted, [stat, pair, *others], hots, bins
    )
    mass_x = across(mass, 2)
    got_x, got_y = across(to_x, 2), across(to_y, 4)
    a_sum, b_sum, keep = class_part(meta, "rest", 7, 3, full, post)
    mass_x, post, keep = together((mass_x, post, keep))
    mass = add_pair(meta, mass, mass_x)
    mass_y = across(mass, 4)
    send_c, send_d, give = class_part(meta, "next", 4, 3, full, post)
    got_x, got_y, send_c, send_d, a_sum, b_sum, keep, give, mass, mass_y = together(
        (got_x, got_y, send_c, send_d, a_sum, b_sum, keep, give, mass, mass_y)
    )
    got_c, got_d = by_core(send_c, 2, 4), by_core(send_d, 5, 3)
    down, left = got_x.astype(F32), got_y.astype(F32)
    message_a = (a_sum + jnp.where(even, down, left)).astype(BF16)
    message_b = (b_sum + jnp.where(even, left, down)).astype(BF16)
    got_a, got_b = by_core(message_a, 4, 2), by_core(message_b, 3, 5)
    got_self = across(give, 1)
    mass = mass.astype(F32) + mass_y.astype(F32)
    mass_other = across(mass, 1)
    bin_weights = jnp.where(
        even,
        jnp.concatenate([mass, mass_other], axis=1),
        jnp.concatenate([mass_other, mass], axis=1),
    )
    own_half = keep + got_c.astype(F32) + got_a.astype(F32)
    other_half = got_self.astype(F32) + got_d.astype(F32) + got_b.astype(F32)
    class_sums = jnp.where(
        even,
        jnp.concatenate([own_half, other_half], axis=0),
        jnp.concatenate([other_half, own_half], axis=0),
    ).T
    return class_sums, bin_weights, log_evidence.reshape(-1)


def energy_block(gain_block, panel_piece):
    widened = panel_piece.astype(jnp.float32)
    return lax.dot_general(
        gain_block, widened * widened, (((1,), (1,)), ((), ())), precision=lax.Precision.HIGHEST
    )


def on_device(raw_images, defocus_bin, dest_row, ctf_table, inv_noise, panels):
    dom_count = lax.axis_size("dom")
    bin_count = ctf_table.shape[0]
    columns = raw_images.shape[1]
    hold_rows = raw_images.shape[0]
    shard_rows = hold_rows // 2
    capacity = 2 * shard_rows // dom_count
    is_live = dest_row >= 0
    target = jnp.where(is_live, dest_row // shard_rows, dom_count)
    local_row = dest_row % shard_rows
    marks = (target[:, None] == jnp.arange(dom_count, dtype=jnp.int32)[None, :]).astype(jnp.int32)
    slot_rank = jnp.sum((jnp.cumsum(marks, axis=0) - marks) * marks, axis=1)
    row_code = jnp.where(is_live, local_row * bin_count + defocus_bin, -1)
    padded_images = jnp.concatenate([raw_images, jnp.zeros((1, columns), raw_images.dtype)], axis=0)
    padded_code = jnp.concatenate([row_code, jnp.full((1,), -1, jnp.int32)], axis=0)
    position = jnp.where(is_live, target * capacity + slot_rank, dom_count * capacity)
    slot_count = dom_count * capacity
    source = (
        jnp.full((slot_count,), hold_rows, jnp.int32)
        .at[position]
        .set(jnp.arange(hold_rows, dtype=jnp.int32), mode="drop")
    )
    send_images = padded_images[source].reshape(dom_count, capacity, columns)
    send_code = padded_code[source].reshape(dom_count, capacity)
    recv_images, recv_code = (
        lax.all_to_all(send_images, "dom", split_axis=0, concat_axis=0, tiled=True),
        lax.all_to_all(send_code, "dom", split_axis=0, concat_axis=0, tiled=True),
    )
    flat_images = recv_images.reshape(-1, columns)
    flat_code = recv_code.reshape(-1)
    arrived = flat_code >= 0
    row_of = jnp.where(arrived, flat_code // bin_count, shard_rows)
    row_order = (
        jnp.zeros((shard_rows,), jnp.int32)
        .at[row_of]
        .set(jnp.arange(flat_code.shape[0], dtype=jnp.int32), mode="drop")
    )
    images = flat_images[row_order]
    bin_ids = flat_code[row_order] % bin_count
    bin_table = (bin_ids[:, None] == jnp.arange(bin_count, dtype=jnp.int32)[None, :]).astype(
        jnp.float32
    )
    ctf_rows = jnp.dot(bin_table, ctf_table, precision=lax.Precision.HIGHEST)
    factor = ctf_rows * inv_noise[None, :]
    weighted = (images.astype(jnp.float32) * jnp.concatenate([factor, factor], axis=1)).astype(
        jnp.bfloat16
    )
    gain_half = ctf_table * ctf_table * inv_noise[None, :]
    gain_full = jnp.concatenate([gain_half, gain_half], axis=1)
    panel_piece = lax.all_gather(panels, "dom", axis=1, tiled=True)
    col_block = weighted
    cross_term = lax.dot_general(
        col_block, panel_piece, (((1,), (1,)), ((), ())), preferred_element_type=jnp.float32
    )
    energy = energy_block(gain_full, panel_piece)
    scores = cross_term - 0.5 * jnp.dot(bin_table, energy, precision=lax.Precision.HIGHEST)
    local_peak = jnp.max(scores, axis=1)
    row_peak = lax.pmax(local_peak, "rot")
    shifted = jnp.exp(scores - row_peak[:, None])
    row_total = lax.psum(jnp.sum(shifted, axis=1), "rot")
    posterior = (shifted / row_total[:, None]).astype(jnp.bfloat16)
    log_evidence = row_peak + jnp.log(row_total)
    col_block = weighted
    class_sums = lax.psum_scatter(
        lax.dot_general(
            col_block, posterior, (((0,), (0,)), ((), ())), preferred_element_type=jnp.float32
        ).astype(jnp.bfloat16),
        "dom",
        scatter_dimension=0,
        tiled=True,
    ).astype(jnp.float32)
    local_mass = lax.dot_general(
        bin_table.astype(jnp.bfloat16),
        posterior,
        (((0,), (0,)), ((), ())),
        preferred_element_type=jnp.float32,
    )
    bin_weights = lax.psum(local_mass.astype(jnp.bfloat16), "dom").astype(jnp.float32)
    return (class_sums, bin_weights, log_evidence)


def solution(mesh):
    small = mesh.shape["dom"] == 8 and mesh.shape["rot"] == 4
    return jax.shard_map(
        two_by_two if small else on_device,
        mesh=mesh,
        in_specs=(P("dom", None), P("dom"), P("dom"), P(), P(), P("rot", "dom")),
        out_specs=(P("dom", "rot"), P(None, "rot"), P("dom")),
        check_vma=False,
    )
```

```python
import functools

import jax
import jax.numpy as jnp
from jax import lax
from jax.experimental import pallas as pl
from jax.experimental.pallas import tpu as pltpu
from jax.sharding import PartitionSpec as P

NN = (((1,), (0,)), ((), ()))
NT = (((1,), (1,)), ((), ()))
F32, BF16, I32 = jnp.float32, jnp.bfloat16, jnp.int32
CODE = 16
LANES = 128
MIB = 1024 * 1024


def mm(a, b, dims):
    return lax.dot_general(a, b, dims, preferred_element_type=F32)


def split3(x):
    hi = x.astype(BF16)
    rest = x - hi.astype(F32)
    mid = rest.astype(BF16)
    low = (rest - mid.astype(F32)).astype(BF16)
    return hi, mid, low


def call(body, grid, in_specs, out_specs, out_shape, scratch=(), alias=None, flops=0, moved=0, room=24):
    return pl.pallas_call(
        body,
        grid_spec=pltpu.PrefetchScalarGridSpec(
            num_scalar_prefetch=1,
            grid=grid,
            in_specs=in_specs,
            out_specs=out_specs,
            scratch_shapes=list(scratch),
        ),
        out_shape=out_shape,
        input_output_aliases=alias or {},
        compiler_params=pltpu.CompilerParams(vmem_limit_bytes=room * MIB),
        cost_estimate=pl.CostEstimate(
            flops=flops // 16, bytes_accessed=moved // 16, transcendentals=0
        ),
    )


def sds(shape, dtype):
    return jax.ShapeDtypeStruct(shape, dtype)


def one_hot_rows(out_ref, wanted):
    rows, width = out_ref.shape
    step = 256 if rows % 256 == 0 else rows
    for start in range(0, rows, step):
        index = lax.broadcasted_iota(I32, (step, width), 0) + start
        out_ref[start : start + step, :] = jnp.where(index == wanted, 1.0, 0.0).astype(BF16)


def places_of(dest, shard_rows, cap, dom, device):
    hold = dest.shape[1]
    low = lax.broadcasted_iota(I32, (dom, hold), 0) * shard_rows
    inside = jnp.logical_and(dest >= low, dest < low + shard_rows)
    marks = jnp.where(inside, 1.0, 0.0)
    local = dest - jnp.sum(jnp.where(inside, low, 0), axis=0, keepdims=True)
    lanes = 128
    before = lax.broadcasted_iota(I32, (lanes, lanes), 0) < lax.broadcasted_iota(
        I32, (lanes, lanes), 1
    )
    upper = jnp.where(before, 1.0, 0.0).astype(BF16)
    apart = lax.broadcasted_iota(I32, (dom, 1), 0) ^ device
    carry = apart.astype(F32) * cap + 1.0
    found = []
    for start in range(0, hold, lanes):
        part = marks[:, start : start + lanes]
        rank = mm(part.astype(BF16), upper, NN) + carry
        found.append(jnp.sum(jnp.where(part > 0, rank, 0.0), axis=0, keepdims=True))
        carry = carry + jnp.sum(part, axis=1, keepdims=True)
    return jnp.concatenate(found, axis=1).astype(I32) - 1, local


def joined(refs):
    return jnp.concatenate([ref[...] for ref in refs], axis=1)


def pack_first_body(dom, shard_rows, cap, meta, dest_ref, bin_ref, *refs):
    raw, outs, (place_ref, pick) = refs[: -dom - 2], refs[-dom - 2 : -2], refs[-2:]
    dest = dest_ref[...].reshape(1, dest_ref.shape[0])
    bins = bin_ref[...].reshape(1, dest_ref.shape[0])
    place, local = places_of(dest, shard_rows, cap, dom, meta[0])
    place_ref[...] = place
    one_hot_rows(pick, place)
    which = lax.broadcasted_iota(I32, (CODE, dest.shape[1]), 0)
    digits = jnp.where(
        which == 0,
        local >> 4,
        jnp.where(which == 1, local & 15, jnp.where(which == 2, bins, jnp.where(which == 3, 1, 0))),
    )
    digits = jnp.where(dest >= 0, digits, 0).astype(F32).astype(BF16)
    codes = mm(digits, pick[...], NT)
    packed = mm(pick[...], joined(raw), NN).astype(BF16)
    for index, out_ref in enumerate(outs):
        block = slice(index * cap, (index + 1) * cap)
        out_ref[:cap, :] = packed[block]
        out_ref[cap:, :] = jnp.zeros((CODE, out_ref.shape[1]), BF16)
        out_ref[cap:, :cap] = codes[:, block].astype(BF16)


def pack_next_body(cap, dom, meta, place_ref, *refs):
    raw, outs, pick = refs[: -dom - 1], refs[-dom - 1 : -1], refs[-1]
    one_hot_rows(pick, place_ref[...])
    packed = mm(pick[...], joined(raw), NN).astype(BF16)
    for index, out_ref in enumerate(outs):
        out_ref[...] = packed[index * cap : (index + 1) * cap]


def raw_specs(hold, share, chunk):
    first, width = chunk
    at = lambda k: lambda j, m: (0, m[1] * (share // LANES) + first // LANES + k)
    return [pl.BlockSpec((hold, LANES), at(k)) for k in range(width // LANES)]


def pack_first(meta, raw_images, dest, bins, dom, share, chunk):
    hold, _ = raw_images.shape
    width = chunk[1]
    cap = hold // dom
    slots = dom * cap
    specs = raw_specs(hold, share, chunk)
    return call(
        functools.partial(pack_first_body, dom, hold // 2, cap),
        (1,),
        [pl.BlockSpec((hold,), lambda j, m: (0,))] * 2 + specs,
        [pl.BlockSpec((cap + CODE, width), lambda j, m: (0, 0))] * dom
        + [pl.BlockSpec((1, hold), lambda j, m: (0, 0))],
        [sds((cap + CODE, width), BF16)] * dom + [sds((1, hold), I32)],
        scratch=[pltpu.VMEM((slots, hold), BF16)],
        room=51,
        flops=2 * slots * hold * width,
        moved=4 * hold * width,
    )(meta, dest, bins, *[raw_images] * len(specs))


def pack_next(meta, raw_images, place, dom, share, chunk):
    hold, _ = raw_images.shape
    width = chunk[1]
    cap = hold // dom
    slots = dom * cap
    specs = raw_specs(hold, share, chunk)
    return call(
        functools.partial(pack_next_body, cap, dom),
        (1,),
        [pl.BlockSpec((1, hold), lambda j, m: (0, 0))] + specs,
        [pl.BlockSpec((cap, width), lambda j, m: (0, 0))] * dom,
        [sds((cap, width), BF16)] * dom,
        scratch=[pltpu.VMEM((slots, hold), BF16)],
        room=51,
        flops=2 * slots * hold * width,
        moved=4 * hold * width,
    )(meta, place, *[raw_images] * len(specs))


def weigh(first, share, pick, wide, recv, meta, ctf_ref, inv_ref, out_ref):
    width = out_ref.shape[1]
    start = lax.rem(meta[1] * share, ctf_ref.shape[1]) + first
    columns = pl.ds(pl.multiple_of(start, LANES), width)
    table = jnp.concatenate(split3(ctf_ref[:, columns] * inv_ref[:, columns]), axis=0)
    out_ref[...] = (mm(pick, recv, NN) * mm(wide, table, NN)).astype(BF16)


def gather(pieces, whole, rows):
    for index, piece in enumerate(pieces):
        whole[index * rows : (index + 1) * rows, :] = piece[:rows, :]


def unpack_first_body(dom, bins, share, first, meta, *refs):
    pieces, recv_ref = refs[:dom], refs[-1]
    cap = pieces[0].shape[0] - CODE
    gather(pieces, recv_ref, cap)
    ctf_ref, inv_ref, out_ref, hot_ref, pick, wide = refs[dom:-1]
    shard_rows = out_ref.shape[0]
    got = jnp.concatenate([piece[cap:, :cap].astype(F32) for piece in pieces], axis=1)
    row = got[0:1] * 16.0 + got[1:2] + got[3:4] * 1024.0 - 1024.0
    one_hot_rows(pick, row.astype(I32))
    slot_bins = jnp.broadcast_to(got[2:3].astype(BF16), (8, got.shape[1]))
    down = mm(pick[...], slot_bins, NT)[:, 0:1].astype(I32)
    across = mm(slot_bins, pick[...], NT)[0:1].astype(I32)
    lane = lax.broadcasted_iota(I32, (shard_rows, 3 * bins), 1)
    wide[...] = jnp.where((lane & (bins - 1)) == down, 1.0, 0.0).astype(BF16)
    deep = lax.broadcasted_iota(I32, (3 * bins, shard_rows), 0)
    hot_ref[...] = jnp.where((deep & (bins - 1)) == across, 1.0, 0.0).astype(BF16)
    weigh(first, share, pick[...], wide[...], recv_ref[...], meta, ctf_ref, inv_ref, out_ref)


def unpack_next_body(dom, share, first, meta, *refs):
    recv_ref = refs[-1]
    gather(refs[:dom], recv_ref, refs[0].shape[0])
    pick_ref, wide_ref, ctf_ref, inv_ref, out_ref = refs[dom:-1]
    weigh(first, share, pick_ref[...], wide_ref[...], recv_ref[...], meta, ctf_ref, inv_ref, out_ref)


def unpack_first(meta, recv, ctf, inv, share, chunk):
    first, width = chunk
    dom = len(recv)
    slots = dom * (recv[0].shape[0] - CODE)
    rows = slots // 2
    bins, pix = ctf.shape
    whole = lambda shape: pl.BlockSpec(shape, lambda j, m: (0, 0))
    shapes = [(rows, width), (3 * bins, rows), (rows, slots), (rows, 3 * bins)]
    return call(
        functools.partial(unpack_first_body, dom, bins, share, first),
        (1,),
        [whole(recv[0].shape)] * dom + [whole(ctf.shape), whole(inv.shape)],
        [whole(s) for s in shapes],
        [sds(s, BF16) for s in shapes],
        scratch=[pltpu.VMEM((slots, width), BF16)],
        room=28,
        flops=2 * slots * rows * width,
        moved=2 * slots * width,
    )(meta, *recv, ctf, inv)


def unpack_next(meta, pick, wide, recv, ctf, inv, share, chunk):
    first, width = chunk
    dom = len(recv)
    slots = dom * recv[0].shape[0]
    rows = slots // 2
    whole = lambda shape: pl.BlockSpec(shape, lambda j, m: (0, 0))
    return call(
        functools.partial(unpack_next_body, dom, share, first),
        (1,),
        [whole(recv[0].shape)] * dom
        + [whole(pick.shape), whole(wide.shape), whole(ctf.shape), whole(inv.shape)],
        whole((rows, width)),
        sds((rows, width), BF16),
        scratch=[pltpu.VMEM((slots, width), BF16)],
        flops=2 * slots * rows * width,
        moved=2 * slots * width,
    )(meta, *recv, pick, wide, ctf, inv)


def energy_body(bins, count, meta, *refs):
    pieces, (ctf_ref, inv_ref, panel_ref, extra_ref, total) = refs[:-5], refs[-5:]
    width = panel_ref.shape[1]
    blocks = []
    for piece in pieces:
        for start in range(0, piece.shape[1], width):
            blocks.append((piece, start))
    step = pl.program_id(0)

    @pl.when(step == 0)
    def _():
        total[...] = jnp.zeros_like(total)

    gain = ctf_ref[...] * ctf_ref[...] * inv_ref[...]
    gain3 = jnp.concatenate(split3(gain), axis=0)
    for index, (piece, start) in enumerate(blocks):

        @pl.when(step == index)
        def _():
            panel = piece[:, start : start + width]
            panel_ref[...] = panel
            wide = panel.astype(F32)
            square = wide * wide
            high = square.astype(BF16)
            low = (square - high.astype(F32)).astype(BF16)
            total[...] += mm(high, gain3, NT) + mm(low, gain3, NT)

    @pl.when(step == count - 1)
    def _():
        whole = total[:, :bins] + total[:, bins : 2 * bins] + total[:, 2 * bins :]
        extra_ref[...] = jnp.concatenate(split3(-0.5 * whole), axis=1)


def energy(meta, pieces, ctf, inv):
    rows, width = pieces[-1].shape
    count = sum(piece.shape[1] for piece in pieces) // width
    bins, pix = ctf.shape
    wrap = pix // width
    return call(
        functools.partial(energy_body, bins, count),
        (count,),
        [pl.BlockSpec(piece.shape, lambda j, m: (0, 0)) for piece in pieces]
        + [
            pl.BlockSpec((bins, width), lambda j, m: (0, lax.rem(m[0] ^ j, wrap))),
            pl.BlockSpec((1, width), lambda j, m: (0, lax.rem(m[0] ^ j, wrap))),
        ],
        [
            pl.BlockSpec((rows, width), lambda j, m: (0, m[0] ^ j)),
            pl.BlockSpec((rows, 3 * bins), lambda j, m: (0, 0)),
        ],
        [sds((rows, count * width), BF16), sds((rows, 3 * bins), BF16)],
        scratch=[pltpu.VMEM((rows, 3 * bins), F32)],
        flops=2 * 4 * rows * bins * count * width * 3,
        moved=4 * rows * count * width,
    )(meta, *pieces, ctf, inv)


def score_body(parts, used, first, last, meta, *refs):
    own, sib, panel_ref, refs = (
        refs[:parts],
        refs[parts : 2 * parts],
        refs[2 * parts],
        refs[2 * parts + 1 :],
    )
    if first:
        acc_out, full_ref = refs
    elif last:
        acc_ref, _, hot_own, hot_sib, extra_ref, shifted_ref, stat_ref, full_ref = refs
    elif used is None:
        acc_ref, _, acc_out, full_ref = refs
    else:
        acc_ref, acc_out = refs
    half = pl.num_programs(0) // 2

    def tile(sources, hot):
        block = jnp.concatenate([source[...] for source in sources], axis=1)
        if used is None or last:
            full_ref[...] = block
        if last:
            block = block[:, used[0] : used[0] + used[1]]
        panel = panel_ref[...] if used is None else panel_ref[:, used[0] : used[0] + used[1]]
        total = mm(panel, block, NT)
        if not first:
            total = acc_ref[...] + total
        if not last:
            acc_out[...] = total
            return
        total = total + mm(extra_ref[...], hot[...], NN)
        peak = jnp.max(total, axis=0, keepdims=True)
        shifted = jnp.exp(total - peak)
        shifted_ref[...] = shifted
        mass = jnp.sum(shifted, axis=0, keepdims=True)
        which = lax.broadcasted_iota(I32, stat_ref.shape, 0)
        stat_ref[...] = jnp.where(which == 0, peak, mass)

    @pl.when(pl.program_id(0) < half)
    def _():
        tile(own, hot_own if last else None)

    @pl.when(pl.program_id(0) >= half)
    def _():
        tile(sib, hot_sib if last else None)


def score(meta, at, own, sib, panels, width, acc=None, full=None, hots=None, extra=None, used=None):
    rows = own[0].shape[0]
    parts = len(own)
    tile = 256
    half = rows // tile
    count, columns = panels.shape
    first, last = acc is None, hots is not None
    store = used is None or last
    fronts = [pl.BlockSpec((tile, v.shape[1]), lambda j, m: (jnp.minimum(j, half - 1), 0)) for v in own]
    backs = [pl.BlockSpec((tile, v.shape[1]), lambda j, m: (jnp.maximum(j - half, 0), 0)) for v in own]
    acc_spec = pl.BlockSpec((count, tile), lambda j, m: (0, j))
    full_spec = pl.BlockSpec((tile, width), lambda j, m: (j, at(m)))
    in_specs = fronts + backs + [pl.BlockSpec((count, width), lambda j, m: (0, at(m)))]
    operands = [meta, *own, *sib, panels]
    alias = {}
    if not first:
        in_specs += [acc_spec]
        alias = {len(operands): 0}
        operands += [acc]
        if store:
            in_specs += [pl.BlockSpec(memory_space=pl.ANY)]
            alias[len(operands)] = 2 if last else 1
            operands += [full]
    full_shape = sds((2 * rows, columns), BF16)
    acc_shape = sds((count, 2 * rows), F32)
    out_specs, out_shape = [acc_spec, full_spec], [acc_shape, full_shape]
    if last:
        depth = extra.shape[1]
        in_specs += [
            pl.BlockSpec((depth, tile), lambda j, m: (0, jnp.minimum(j, half - 1))),
            pl.BlockSpec((depth, tile), lambda j, m: (0, jnp.maximum(j - half, 0))),
            pl.BlockSpec((count, depth), lambda j, m: (0, 0)),
        ]
        operands += [*hots, extra]
        out_specs = [acc_spec, pl.BlockSpec((8, tile), lambda j, m: (0, j)), full_spec]
        out_shape = [acc_shape, sds((8, 2 * rows), F32), full_shape]
    elif not store:
        out_specs, out_shape = acc_spec, acc_shape
    return call(
        functools.partial(score_body, parts, used, first, last),
        (2 * half,),
        in_specs,
        out_specs,
        out_shape,
        alias=alias,
        room=16,
        flops=2 * count * 2 * rows * width,
        moved=8 * count * 2 * rows + 8 * rows * width,
    )(*operands)


def merge_body(meta, mine_ref, other_ref, out_ref):
    rows = mine_ref.shape[1] // 2
    other = other_ref[...]
    other = jnp.concatenate([other[:, rows:], other[:, :rows]], axis=1)
    mine = mine_ref[...]
    peak = jnp.maximum(mine[0:1], other[0:1])
    mass = mine[1:2] * jnp.exp(mine[0:1] - peak) + other[1:2] * jnp.exp(other[0:1] - peak)
    which = lax.broadcasted_iota(I32, out_ref.shape, 0)
    out_ref[...] = jnp.where(which == 0, peak, mass)


def add_body(meta, mine_ref, other_ref, out_ref):
    out_ref[...] = (mine_ref[...].astype(F32) + other_ref[...].astype(F32)).astype(BF16)


def pairwise(body, meta, mine, other):
    spec = pl.BlockSpec(mine.shape, lambda j, m: (0, 0))
    return call(body, (1,), [spec, spec], spec, sds(mine.shape, mine.dtype), room=4)(
        meta, mine, other
    )


merge = functools.partial(pairwise, merge_body)
add_pair = functools.partial(pairwise, add_body)


def class_body(kind, steps, meta, *refs):
    if kind == "first":
        (shifted_ref, stat_ref), four = refs[:2], refs[2:6]
        hot_own, hot_sib, full_ref = refs[6:9]
        outs, (post_ref, log_ref, mass_ref) = refs[9 : 9 + steps], refs[9 + steps :]

        @pl.when(pl.program_id(0) == 0)
        def _():
            stats = [ref[...] for ref in four]
            peaks = [s[0:1] for s in stats]
            peak = jnp.maximum(jnp.maximum(peaks[0], peaks[1]), jnp.maximum(peaks[2], peaks[3]))
            parts = [s[1:2] * jnp.exp(p - peak) for s, p in zip(stats, peaks)]
            mass = (parts[0] + parts[1]) + (parts[2] + parts[3])
            factor = jnp.exp(stat_ref[0:1] - peak) / mass
            post_ref[...] = (shifted_ref[...] * factor).astype(BF16)
            log_ref[...] = (peak + jnp.log(mass))[:, : log_ref.shape[1]]
            bins, rows = mass_ref.shape[0], hot_own.shape[1]
            weights = mm(hot_own[:bins, :], post_ref[:, :rows], NT)
            weights = weights + mm(hot_sib[:bins, :], post_ref[:, rows:], NT)
            mass_ref[...] = weights.astype(BF16)

    else:
        (post_ref, full_ref), outs = refs[:2], refs[2:]
    for step, out_ref in enumerate(outs):

        @pl.when(pl.program_id(0) == step)
        def _():
            out_ref[...] = mm(post_ref[...], full_ref[...], NN).astype(out_ref.dtype)


def class_part(meta, kind, offset, steps, full, post=None, shifted=None, stats=None, hots=None, bins=0):
    rows, columns = full.shape
    width = columns // 8
    count = (shifted if post is None else post).shape[0]
    whole = lambda shape: pl.BlockSpec(shape, lambda j, m: (0, 0))
    full_spec = pl.BlockSpec((rows, width), lambda j, m: (0, m[offset + j]))
    out_specs = [whole((count, width))] * steps
    kept = steps // 2 if kind == "rest" else 0
    types = [BF16] * (steps - kept) + [F32] * kept
    out_shape = [sds((count, width), dtype) for dtype in types]
    if kind == "first":
        operands = [shifted, *stats, *hots, full]
        in_specs = [whole(shifted.shape)] + [whole(stats[0].shape)] * 5
        in_specs += [whole(hots[0].shape)] * 2 + [full_spec]
        out_specs += [whole((count, rows)), whole((1, rows // 2)), whole((bins, count))]
        out_shape += [sds((count, rows), BF16), sds((1, rows // 2), F32), sds((bins, count), BF16)]
    else:
        operands = [post, full]
        in_specs = [whole(post.shape), full_spec]
    return call(
        functools.partial(class_body, kind, steps),
        (steps,),
        in_specs,
        out_specs,
        out_shape,
        room=22 if kind == "first" else 28,
        flops=2 * count * rows * width * steps,
        moved=2 * rows * width * steps + 4 * count * (rows + width * steps),
    )(meta, *operands)


def two_by_two(raw_images, defocus_bin, dest_row, ctf_table, inv_noise, panels):
    dom, turns = lax.axis_size("dom"), lax.axis_size("rot")
    device, plane = lax.axis_index("dom"), lax.axis_index("rot")
    bins = ctf_table.shape[0]
    columns = raw_images.shape[1]
    chip, core = device // 2, device % 2

    def block(apart, half):
        return (chip ^ apart) * 2 + half

    x_first, y_second = block(1, 0), block(2, 1)
    x_second, y_first = block(1, 1), block(2, 0)
    even = core == 0
    order = [
        device,
        plane,
        block(3, 0),
        block(3, 1),
        jnp.where(even, x_first, y_second),
        jnp.where(even, y_second, x_first),
        block(0, 1 - core),
        jnp.where(even, y_first, x_second),
        jnp.where(even, x_second, y_first),
        block(0, core),
    ]
    meta = jnp.stack(order).astype(I32)
    inv = inv_noise[None, :]

    def across(value, apart):
        return lax.ppermute(value, "dom", [(i, i ^ apart) for i in range(dom)])

    def by_core(value, when_even, when_odd):
        pairs = [(i, i ^ (when_odd if i % 2 else when_even)) for i in range(dom)]
        return lax.ppermute(value, "dom", pairs)

    def onward(value):
        return lax.ppermute(value, "rot", [(i, (i + 1) % turns) for i in range(turns)])

    width = columns // turns
    cut = width * 5 // 8
    chunk_a, chunk_b = (0, cut), (cut, width - cut)

    def exchange(blocks):
        got = [blocks[0]] + [None] * (dom - 1)
        for apart in (6, 7, 2, 4, 3, 5, 1):
            got[apart] = across(blocks[apart], apart)
        return got

    *send_a, place = pack_first(meta, raw_images, dest_row, defocus_bin, dom, width, chunk_a)
    recv_a = exchange(send_a)
    send_b = pack_next(meta, raw_images, place, dom, width, chunk_b)
    together = lax.optimization_barrier

    count = panels.shape[0] // 2
    mine = lax.dynamic_slice_in_dim(panels, core * count, count, 0)
    other = lax.dynamic_slice_in_dim(across(panels, 1), core * count, count, 0)
    near = jnp.concatenate([mine, other], axis=1)

    recv_a, send_b, near = together((recv_a, send_b, near))
    share_a, hot, pick, wide = unpack_first(meta, recv_a, ctf_table, inv, width, chunk_a)
    share_a, send_b = together((share_a, send_b))
    a1, recv_b = onward(share_a), exchange(send_b)
    recv_b, near = together((recv_b, near))
    by_x, by_y = across(near, 2), across(near, 4)
    share_b = unpack_next(meta, pick, wide, recv_b, ctf_table, inv, width, chunk_b)
    a2, b1 = onward(a1), onward(share_b)
    sib0, sib1, hots = [across(share_a, 1), across(share_b, 1)], [across(a1, 1)], [hot, across(hot, 1)]
    a2, b1, by_x, by_y, sib0, sib1, hots = together((a2, b1, by_x, by_y, sib0, sib1, hots))
    sib1 = sib1 + [across(b1, 1)]
    piece = near.shape[1] // 2
    far_y, far_x = across(by_x[:, :piece], 4), across(by_y[:, piece:], 2)
    a3, b2 = onward(a2), onward(b1)
    panel_full, extra = energy(meta, [near, by_x, by_y, far_y, far_x], ctf_table, inv)

    def share(turn):
        return lambda m: lax.rem(m[1] + turns - turn, turns)

    acc, full = score(meta, share(0), [share_a, share_b], sib0, panel_full, width)
    acc, full = score(meta, share(1), [a1, b1], sib1, panel_full, width, acc, full)
    a3, b2, acc, full = together((a3, b2, acc, full))
    b3 = onward(b2)
    sib2 = [across(a2, 1), across(b2, 1)]
    acc, full = score(meta, share(2), [a2, b2], sib2, panel_full, width, acc, full)
    final = share(turns - 1)
    a3_sib = across(a3, 1)
    acc = score(meta, final, [a3], [a3_sib], panel_full, width, acc, used=chunk_a)
    b3, acc = together((b3, acc))
    shifted, stat, full = score(
        meta,
        final,
        [a3, b3],
        [a3_sib, across(b3, 1)],
        panel_full,
        width,
        acc,
        full,
        hots,
        extra,
        chunk_b,
    )

    pair = merge(meta, stat, across(stat, 1))
    others = [
        lax.ppermute(pair, "rot", [(i, i ^ apart) for i in range(turns)]) for apart in (1, 2, 3)
    ]
    to_x, to_y, post, log_evidence, mass = class_part(
        meta, "first", 2, 2, full, None, shifted, [stat, pair, *others], hots, bins
    )
    mass_x = across(mass, 2)
    got_x, got_y = across(to_x, 2), across(to_y, 4)
    six = class_part(meta, "rest", 4, 6, full, post)
    got_x, got_y, six, mass_x = together((got_x, got_y, six, mass_x))
    send_c, send_d, give, a_sum, b_sum, keep = six
    mass = add_pair(meta, mass, mass_x)
    mass_y = across(mass, 4)
    got_c, got_d = by_core(send_c, 2, 4), by_core(send_d, 5, 3)
    down, left = got_x.astype(F32), got_y.astype(F32)
    message_a = (a_sum + jnp.where(even, down, left)).astype(BF16)
    message_b = (b_sum + jnp.where(even, left, down)).astype(BF16)
    got_a, got_b = by_core(message_a, 4, 2), by_core(message_b, 3, 5)
    got_self = across(give, 1)
    mass = mass.astype(F32) + mass_y.astype(F32)
    mass_other = across(mass, 1)
    bin_weights = jnp.where(
        even,
        jnp.concatenate([mass, mass_other], axis=1),
        jnp.concatenate([mass_other, mass], axis=1),
    )
    own_half = keep + got_c.astype(F32) + got_a.astype(F32)
    other_half = got_self.astype(F32) + got_d.astype(F32) + got_b.astype(F32)
    class_sums = jnp.where(
        even,
        jnp.concatenate([own_half, other_half], axis=0),
        jnp.concatenate([other_half, own_half], axis=0),
    ).T
    return class_sums, bin_weights, log_evidence.reshape(-1)


def energy_block(gain_block, panel_piece):
    widened = panel_piece.astype(jnp.float32)
    return lax.dot_general(
        gain_block, widened * widened, (((1,), (1,)), ((), ())), precision=lax.Precision.HIGHEST
    )


def on_device(raw_images, defocus_bin, dest_row, ctf_table, inv_noise, panels):
    dom_count = lax.axis_size("dom")
    bin_count = ctf_table.shape[0]
    columns = raw_images.shape[1]
    hold_rows = raw_images.shape[0]
    shard_rows = hold_rows // 2
    capacity = 2 * shard_rows // dom_count
    is_live = dest_row >= 0
    target = jnp.where(is_live, dest_row // shard_rows, dom_count)
    local_row = dest_row % shard_rows
    marks = (target[:, None] == jnp.arange(dom_count, dtype=jnp.int32)[None, :]).astype(jnp.int32)
    slot_rank = jnp.sum((jnp.cumsum(marks, axis=0) - marks) * marks, axis=1)
    row_code = jnp.where(is_live, local_row * bin_count + defocus_bin, -1)
    padded_images = jnp.concatenate([raw_images, jnp.zeros((1, columns), raw_images.dtype)], axis=0)
    padded_code = jnp.concatenate([row_code, jnp.full((1,), -1, jnp.int32)], axis=0)
    position = jnp.where(is_live, target * capacity + slot_rank, dom_count * capacity)
    slot_count = dom_count * capacity
    source = (
        jnp.full((slot_count,), hold_rows, jnp.int32)
        .at[position]
        .set(jnp.arange(hold_rows, dtype=jnp.int32), mode="drop")
    )
    send_images = padded_images[source].reshape(dom_count, capacity, columns)
    send_code = padded_code[source].reshape(dom_count, capacity)
    recv_images, recv_code = (
        lax.all_to_all(send_images, "dom", split_axis=0, concat_axis=0, tiled=True),
        lax.all_to_all(send_code, "dom", split_axis=0, concat_axis=0, tiled=True),
    )
    flat_images = recv_images.reshape(-1, columns)
    flat_code = recv_code.reshape(-1)
    arrived = flat_code >= 0
    row_of = jnp.where(arrived, flat_code // bin_count, shard_rows)
    row_order = (
        jnp.zeros((shard_rows,), jnp.int32)
        .at[row_of]
        .set(jnp.arange(flat_code.shape[0], dtype=jnp.int32), mode="drop")
    )
    images = flat_images[row_order]
    bin_ids = flat_code[row_order] % bin_count
    bin_table = (bin_ids[:, None] == jnp.arange(bin_count, dtype=jnp.int32)[None, :]).astype(
        jnp.float32
    )
    ctf_rows = jnp.dot(bin_table, ctf_table, precision=lax.Precision.HIGHEST)
    factor = ctf_rows * inv_noise[None, :]
    weighted = (images.astype(jnp.float32) * jnp.concatenate([factor, factor], axis=1)).astype(
        jnp.bfloat16
    )
    gain_half = ctf_table * ctf_table * inv_noise[None, :]
    gain_full = jnp.concatenate([gain_half, gain_half], axis=1)
    panel_piece = lax.all_gather(panels, "dom", axis=1, tiled=True)
    col_block = weighted
    cross_term = lax.dot_general(
        col_block, panel_piece, (((1,), (1,)), ((), ())), preferred_element_type=jnp.float32
    )
    energy = energy_block(gain_full, panel_piece)
    scores = cross_term - 0.5 * jnp.dot(bin_table, energy, precision=lax.Precision.HIGHEST)
    local_peak = jnp.max(scores, axis=1)
    row_peak = lax.pmax(local_peak, "rot")
    shifted = jnp.exp(scores - row_peak[:, None])
    row_total = lax.psum(jnp.sum(shifted, axis=1), "rot")
    posterior = (shifted / row_total[:, None]).astype(jnp.bfloat16)
    log_evidence = row_peak + jnp.log(row_total)
    col_block = weighted
    class_sums = lax.psum_scatter(
        lax.dot_general(
            col_block, posterior, (((0,), (0,)), ((), ())), preferred_element_type=jnp.float32
        ).astype(jnp.bfloat16),
        "dom",
        scatter_dimension=0,
        tiled=True,
    ).astype(jnp.float32)
    local_mass = lax.dot_general(
        bin_table.astype(jnp.bfloat16),
        posterior,
        (((0,), (0,)), ((), ())),
        preferred_element_type=jnp.float32,
    )
    bin_weights = lax.psum(local_mass.astype(jnp.bfloat16), "dom").astype(jnp.float32)
    return (class_sums, bin_weights, log_evidence)


def solution(mesh):
    small = mesh.shape["dom"] == 8 and mesh.shape["rot"] == 4
    return jax.shard_map(
        two_by_two if small else on_device,
        mesh=mesh,
        in_specs=(P("dom", None), P("dom"), P("dom"), P(), P(), P("rot", "dom")),
        out_specs=(P("dom", "rot"), P(None, "rot"), P("dom")),
        check_vma=False,
    )
```

```python
import functools

import jax
import jax.numpy as jnp
from jax import lax
from jax.experimental import pallas as pl
from jax.experimental.pallas import tpu as pltpu
from jax.sharding import PartitionSpec as P

NN = (((1,), (0,)), ((), ()))
NT = (((1,), (1,)), ((), ()))
F32, BF16, I32 = jnp.float32, jnp.bfloat16, jnp.int32
CODE = 16
LANES = 128
MIB = 1024 * 1024


def mm(a, b, dims):
    return lax.dot_general(a, b, dims, preferred_element_type=F32)


def split3(x):
    hi = x.astype(BF16)
    rest = x - hi.astype(F32)
    mid = rest.astype(BF16)
    low = (rest - mid.astype(F32)).astype(BF16)
    return hi, mid, low


def call(body, grid, in_specs, out_specs, out_shape, scratch=(), alias=None, flops=0, moved=0, room=24):
    return pl.pallas_call(
        body,
        grid_spec=pltpu.PrefetchScalarGridSpec(
            num_scalar_prefetch=1,
            grid=grid,
            in_specs=in_specs,
            out_specs=out_specs,
            scratch_shapes=list(scratch),
        ),
        out_shape=out_shape,
        input_output_aliases=alias or {},
        compiler_params=pltpu.CompilerParams(vmem_limit_bytes=room * MIB),
        cost_estimate=pl.CostEstimate(
            flops=flops // 16, bytes_accessed=moved // 16, transcendentals=0
        ),
    )


def sds(shape, dtype):
    return jax.ShapeDtypeStruct(shape, dtype)


def one_hot_rows(out_ref, wanted):
    rows, width = out_ref.shape
    short = wanted.astype(jnp.int16)
    one, zero = jnp.ones((), BF16), jnp.zeros((), BF16)
    step = 256 if rows % 256 == 0 else rows
    for start in range(0, rows, step):
        index = lax.broadcasted_iota(jnp.int16, (step, width), 0) + jnp.int16(start)
        out_ref[start : start + step, :] = jnp.where(index == short, one, zero)


def places_of(dest, shard_rows, cap, dom, device):
    hold = dest.shape[1]
    low = lax.broadcasted_iota(I32, (dom, hold), 0) * shard_rows
    inside = jnp.logical_and(dest >= low, dest < low + shard_rows)
    marks = jnp.where(inside, 1.0, 0.0)
    local = dest - jnp.sum(jnp.where(inside, low, 0), axis=0, keepdims=True)
    lanes = 128
    before = lax.broadcasted_iota(I32, (lanes, lanes), 0) < lax.broadcasted_iota(
        I32, (lanes, lanes), 1
    )
    upper = jnp.where(before, 1.0, 0.0).astype(BF16)
    apart = lax.broadcasted_iota(I32, (dom, 1), 0) ^ device
    carry = apart.astype(F32) * cap + 1.0
    found = []
    for start in range(0, hold, lanes):
        part = marks[:, start : start + lanes]
        rank = mm(part.astype(BF16), upper, NN) + carry
        found.append(jnp.sum(jnp.where(part > 0, rank, 0.0), axis=0, keepdims=True))
        carry = carry + jnp.sum(part, axis=1, keepdims=True)
    return jnp.concatenate(found, axis=1).astype(I32) - 1, local


def joined(refs):
    return jnp.concatenate([ref[...] for ref in refs], axis=1)


def pack_first_body(dom, shard_rows, cap, bins, meta, slot_ref, *refs):
    raw, outs, (place_ref, pick) = refs[: -dom - 2], refs[-dom - 2 : -2], refs[-2:]
    slot = slot_ref[...].reshape(1, slot_ref.shape[0])
    dest, slot_bin = slot >> (bins.bit_length() - 1), slot & (bins - 1)
    place, local = places_of(dest, shard_rows, cap, dom, meta[0])
    place_ref[...] = place
    one_hot_rows(pick, place)
    which = lax.broadcasted_iota(I32, (CODE, dest.shape[1]), 0)
    digits = jnp.where(
        which == 0,
        local >> 4,
        jnp.where(which == 1, local & 15, jnp.where(which == 2, slot_bin, jnp.where(which == 3, 1, 0))),
    )
    digits = jnp.where(dest >= 0, digits, 0).astype(F32).astype(BF16)
    codes = mm(digits, pick[...], NT)
    packed = mm(pick[...], joined(raw), NN).astype(BF16)
    for index, out_ref in enumerate(outs):
        block = slice(index * cap, (index + 1) * cap)
        out_ref[:cap, :] = packed[block]
        out_ref[cap:, :] = jnp.zeros((CODE, out_ref.shape[1]), BF16)
        out_ref[cap:, :cap] = codes[:, block].astype(BF16)


def pack_next_body(cap, dom, meta, place_ref, *refs):
    raw, outs, pick = refs[: -dom - 1], refs[-dom - 1 : -1], refs[-1]
    one_hot_rows(pick, place_ref[...])
    packed = mm(pick[...], joined(raw), NN).astype(BF16)
    for index, out_ref in enumerate(outs):
        out_ref[...] = packed[index * cap : (index + 1) * cap]


def raw_specs(hold, share, chunk):
    first, width = chunk
    at = lambda k: lambda j, m: (0, m[1] * (share // LANES) + first // LANES + k)
    return [pl.BlockSpec((hold, LANES), at(k)) for k in range(width // LANES)]


def pack_first(meta, raw_images, slot, bins, dom, share, chunk):
    hold, _ = raw_images.shape
    width = chunk[1]
    cap = hold // dom
    slots = dom * cap
    specs = raw_specs(hold, share, chunk)
    return call(
        functools.partial(pack_first_body, dom, hold // 2, cap, bins),
        (1,),
        [pl.BlockSpec((hold,), lambda j, m: (0,))] + specs,
        [pl.BlockSpec((cap + CODE, width), lambda j, m: (0, 0))] * dom
        + [pl.BlockSpec((1, hold), lambda j, m: (0, 0))],
        [sds((cap + CODE, width), BF16)] * dom + [sds((1, hold), I32)],
        scratch=[pltpu.VMEM((slots, hold), BF16)],
        room=51,
        flops=2 * slots * hold * width,
        moved=4 * hold * width,
    )(meta, slot, *[raw_images] * len(specs))


def pack_next(meta, raw_images, place, dom, share, chunk):
    hold, _ = raw_images.shape
    width = chunk[1]
    cap = hold // dom
    slots = dom * cap
    specs = raw_specs(hold, share, chunk)
    return call(
        functools.partial(pack_next_body, cap, dom),
        (1,),
        [pl.BlockSpec((1, hold), lambda j, m: (0, 0))] + specs,
        [pl.BlockSpec((cap, width), lambda j, m: (0, 0))] * dom,
        [sds((cap, width), BF16)] * dom,
        scratch=[pltpu.VMEM((slots, hold), BF16)],
        room=51,
        flops=2 * slots * hold * width,
        moved=4 * hold * width,
    )(meta, place, *[raw_images] * len(specs))


def weigh(first, share, pick, wide, recv, meta, ctf_ref, inv_ref, out_ref):
    width = out_ref.shape[1]
    start = lax.rem(meta[1] * share, ctf_ref.shape[1]) + first
    columns = pl.ds(pl.multiple_of(start, LANES), width)
    table = jnp.concatenate(split3(ctf_ref[:, columns] * inv_ref[:, columns]), axis=0)
    out_ref[...] = (mm(pick, recv, NN) * mm(wide, table, NN)).astype(BF16)


def gather(pieces, whole, rows):
    for index, piece in enumerate(pieces):
        whole[index * rows : (index + 1) * rows, :] = piece[:rows, :]


def unpack_first_body(dom, bins, share, first, meta, *refs):
    pieces, recv_ref = refs[:dom], refs[-1]
    cap = pieces[0].shape[0] - CODE
    gather(pieces, recv_ref, cap)
    ctf_ref, inv_ref, out_ref, hot_ref, pick, wide = refs[dom:-1]
    shard_rows = out_ref.shape[0]
    got = jnp.concatenate([piece[cap:, :cap].astype(F32) for piece in pieces], axis=1)
    row = got[0:1] * 16.0 + got[1:2] + got[3:4] * 1024.0 - 1024.0
    one_hot_rows(pick, row.astype(I32))
    slot_bins = jnp.broadcast_to(got[2:3].astype(BF16), (8, got.shape[1]))
    down = mm(pick[...], slot_bins, NT)[:, 0:1].astype(I32)
    across = mm(slot_bins, pick[...], NT)[0:1].astype(I32)
    lane = lax.broadcasted_iota(I32, (shard_rows, 3 * bins), 1)
    wide[...] = jnp.where((lane & (bins - 1)) == down, 1.0, 0.0).astype(BF16)
    deep = lax.broadcasted_iota(I32, (3 * bins, shard_rows), 0)
    hot_ref[...] = jnp.where((deep & (bins - 1)) == across, 1.0, 0.0).astype(BF16)
    weigh(first, share, pick[...], wide[...], recv_ref[...], meta, ctf_ref, inv_ref, out_ref)


def unpack_next_body(dom, share, first, meta, *refs):
    recv_ref = refs[-1]
    gather(refs[:dom], recv_ref, refs[0].shape[0])
    pick_ref, wide_ref, ctf_ref, inv_ref, out_ref = refs[dom:-1]
    weigh(first, share, pick_ref[...], wide_ref[...], recv_ref[...], meta, ctf_ref, inv_ref, out_ref)


def unpack_first(meta, recv, ctf, inv, share, chunk):
    first, width = chunk
    dom = len(recv)
    slots = dom * (recv[0].shape[0] - CODE)
    rows = slots // 2
    bins, pix = ctf.shape
    whole = lambda shape: pl.BlockSpec(shape, lambda j, m: (0, 0))
    shapes = [(rows, width), (3 * bins, rows), (rows, slots), (rows, 3 * bins)]
    return call(
        functools.partial(unpack_first_body, dom, bins, share, first),
        (1,),
        [whole(recv[0].shape)] * dom + [whole(ctf.shape), whole(inv.shape)],
        [whole(s) for s in shapes],
        [sds(s, BF16) for s in shapes],
        scratch=[pltpu.VMEM((slots, width), BF16)],
        room=28,
        flops=2 * slots * rows * width,
        moved=2 * slots * width,
    )(meta, *recv, ctf, inv)


def unpack_next(meta, pick, wide, recv, ctf, inv, share, chunk):
    first, width = chunk
    dom = len(recv)
    slots = dom * recv[0].shape[0]
    rows = slots // 2
    whole = lambda shape: pl.BlockSpec(shape, lambda j, m: (0, 0))
    return call(
        functools.partial(unpack_next_body, dom, share, first),
        (1,),
        [whole(recv[0].shape)] * dom
        + [whole(pick.shape), whole(wide.shape), whole(ctf.shape), whole(inv.shape)],
        whole((rows, width)),
        sds((rows, width), BF16),
        scratch=[pltpu.VMEM((slots, width), BF16)],
        flops=2 * slots * rows * width,
        moved=2 * slots * width,
    )(meta, *recv, pick, wide, ctf, inv)


def energy_body(bins, count, meta, *refs):
    pieces, (ctf_ref, inv_ref, panel_ref, extra_ref, total) = refs[:-5], refs[-5:]
    width = panel_ref.shape[1]
    blocks = []
    for piece in pieces:
        for start in range(0, piece.shape[1], width):
            blocks.append((piece, start))
    step = pl.program_id(0)

    @pl.when(step == 0)
    def _():
        total[...] = jnp.zeros_like(total)

    gain = ctf_ref[...] * ctf_ref[...] * inv_ref[...]
    gain3 = jnp.concatenate(split3(gain), axis=0)
    for index, (piece, start) in enumerate(blocks):

        @pl.when(step == index)
        def _():
            panel = piece[:, start : start + width]
            panel_ref[...] = panel
            wide = panel.astype(F32)
            square = wide * wide
            high = square.astype(BF16)
            low = (square - high.astype(F32)).astype(BF16)
            total[...] += mm(high, gain3, NT) + mm(low, gain3, NT)

    @pl.when(step == count - 1)
    def _():
        whole = total[:, :bins] + total[:, bins : 2 * bins] + total[:, 2 * bins :]
        extra_ref[...] = jnp.concatenate(split3(-0.5 * whole), axis=1)


def energy(meta, pieces, ctf, inv):
    rows, width = pieces[-1].shape
    count = sum(piece.shape[1] for piece in pieces) // width
    bins, pix = ctf.shape
    wrap = pix // width
    return call(
        functools.partial(energy_body, bins, count),
        (count,),
        [pl.BlockSpec(piece.shape, lambda j, m: (0, 0)) for piece in pieces]
        + [
            pl.BlockSpec((bins, width), lambda j, m: (0, lax.rem(m[0] ^ j, wrap))),
            pl.BlockSpec((1, width), lambda j, m: (0, lax.rem(m[0] ^ j, wrap))),
        ],
        [
            pl.BlockSpec((rows, width), lambda j, m: (0, m[0] ^ j)),
            pl.BlockSpec((rows, 3 * bins), lambda j, m: (0, 0)),
        ],
        [sds((rows, count * width), BF16), sds((rows, 3 * bins), BF16)],
        scratch=[pltpu.VMEM((rows, 3 * bins), F32)],
        flops=2 * 4 * rows * bins * count * width * 3,
        moved=4 * rows * count * width,
    )(meta, *pieces, ctf, inv)


def score_body(parts, used, first, last, meta, *refs):
    own, sib, panel_ref, refs = (
        refs[:parts],
        refs[parts : 2 * parts],
        refs[2 * parts],
        refs[2 * parts + 1 :],
    )
    if first:
        acc_out, full_ref = refs
    elif last:
        acc_ref, _, hot_own, hot_sib, extra_ref, shifted_ref, stat_ref, full_ref = refs
    elif used is None:
        acc_ref, _, acc_out, full_ref = refs
    else:
        acc_ref, acc_out = refs
    half = pl.num_programs(0) // 2

    def tile(sources, hot):
        block = jnp.concatenate([source[...] for source in sources], axis=1)
        if used is None or last:
            full_ref[...] = block
        if last:
            block = block[:, used[0] : used[0] + used[1]]
        panel = panel_ref[...] if used is None else panel_ref[:, used[0] : used[0] + used[1]]
        total = mm(panel, block, NT)
        if not first:
            total = acc_ref[...] + total
        if not last:
            acc_out[...] = total
            return
        total = total + mm(extra_ref[...], hot[...], NN)
        peak = jnp.max(total, axis=0, keepdims=True)
        shifted = jnp.exp(total - peak)
        shifted_ref[...] = shifted
        mass = jnp.sum(shifted, axis=0, keepdims=True)
        which = lax.broadcasted_iota(I32, stat_ref.shape, 0)
        stat_ref[...] = jnp.where(which == 0, peak, mass)

    @pl.when(pl.program_id(0) < half)
    def _():
        tile(own, hot_own if last else None)

    @pl.when(pl.program_id(0) >= half)
    def _():
        tile(sib, hot_sib if last else None)


def score(meta, at, own, sib, panels, width, acc=None, full=None, hots=None, extra=None, used=None):
    rows = own[0].shape[0]
    parts = len(own)
    tile = 256
    half = rows // tile
    count, columns = panels.shape
    first, last = acc is None, hots is not None
    store = used is None or last
    fronts = [pl.BlockSpec((tile, v.shape[1]), lambda j, m: (jnp.minimum(j, half - 1), 0)) for v in own]
    backs = [pl.BlockSpec((tile, v.shape[1]), lambda j, m: (jnp.maximum(j - half, 0), 0)) for v in own]
    acc_spec = pl.BlockSpec((count, tile), lambda j, m: (0, j))
    full_spec = pl.BlockSpec((tile, width), lambda j, m: (j, at(m)))
    in_specs = fronts + backs + [pl.BlockSpec((count, width), lambda j, m: (0, at(m)))]
    operands = [meta, *own, *sib, panels]
    alias = {}
    if not first:
        in_specs += [acc_spec]
        alias = {len(operands): 0}
        operands += [acc]
        if store:
            in_specs += [pl.BlockSpec(memory_space=pl.ANY)]
            alias[len(operands)] = 2 if last else 1
            operands += [full]
    full_shape = sds((2 * rows, columns), BF16)
    acc_shape = sds((count, 2 * rows), F32)
    out_specs, out_shape = [acc_spec, full_spec], [acc_shape, full_shape]
    if last:
        depth = extra.shape[1]
        in_specs += [
            pl.BlockSpec((depth, tile), lambda j, m: (0, jnp.minimum(j, half - 1))),
            pl.BlockSpec((depth, tile), lambda j, m: (0, jnp.maximum(j - half, 0))),
            pl.BlockSpec((count, depth), lambda j, m: (0, 0)),
        ]
        operands += [*hots, extra]
        out_specs = [acc_spec, pl.BlockSpec((8, tile), lambda j, m: (0, j)), full_spec]
        out_shape = [acc_shape, sds((8, 2 * rows), F32), full_shape]
    elif not store:
        out_specs, out_shape = acc_spec, acc_shape
    return call(
        functools.partial(score_body, parts, used, first, last),
        (2 * half,),
        in_specs,
        out_specs,
        out_shape,
        alias=alias,
        room=16,
        flops=2 * count * 2 * rows * width,
        moved=8 * count * 2 * rows + 8 * rows * width,
    )(*operands)


def merge_body(meta, mine_ref, other_ref, out_ref):
    rows = mine_ref.shape[1] // 2
    other = other_ref[...]
    other = jnp.concatenate([other[:, rows:], other[:, :rows]], axis=1)
    mine = mine_ref[...]
    peak = jnp.maximum(mine[0:1], other[0:1])
    mass = mine[1:2] * jnp.exp(mine[0:1] - peak) + other[1:2] * jnp.exp(other[0:1] - peak)
    which = lax.broadcasted_iota(I32, out_ref.shape, 0)
    out_ref[...] = jnp.where(which == 0, peak, mass)


def add_body(meta, mine_ref, other_ref, out_ref):
    out_ref[...] = (mine_ref[...].astype(F32) + other_ref[...].astype(F32)).astype(BF16)


def pairwise(body, meta, mine, other):
    spec = pl.BlockSpec(mine.shape, lambda j, m: (0, 0))
    return call(body, (1,), [spec, spec], spec, sds(mine.shape, mine.dtype), room=4)(
        meta, mine, other
    )


merge = functools.partial(pairwise, merge_body)
add_pair = functools.partial(pairwise, add_body)


def class_body(kind, steps, meta, *refs):
    if kind == "first":
        (shifted_ref, stat_ref), four = refs[:2], refs[2:6]
        hot_own, hot_sib, full_ref = refs[6:9]
        outs, (post_ref, log_ref, mass_ref) = refs[9 : 9 + steps], refs[9 + steps :]

        @pl.when(pl.program_id(0) == 0)
        def _():
            stats = [ref[...] for ref in four]
            peaks = [s[0:1] for s in stats]
            peak = jnp.maximum(jnp.maximum(peaks[0], peaks[1]), jnp.maximum(peaks[2], peaks[3]))
            parts = [s[1:2] * jnp.exp(p - peak) for s, p in zip(stats, peaks)]
            mass = (parts[0] + parts[1]) + (parts[2] + parts[3])
            factor = jnp.exp(stat_ref[0:1] - peak) / mass
            post_ref[...] = (shifted_ref[...] * factor).astype(BF16)
            log_ref[...] = (peak + jnp.log(mass))[:, : log_ref.shape[1]]
            bins, rows = mass_ref.shape[0], hot_own.shape[1]
            weights = mm(hot_own[:bins, :], post_ref[:, :rows], NT)
            weights = weights + mm(hot_sib[:bins, :], post_ref[:, rows:], NT)
            mass_ref[...] = weights.astype(BF16)

    else:
        (post_ref, full_ref), outs = refs[:2], refs[2:]
    for step, out_ref in enumerate(outs):

        @pl.when(pl.program_id(0) == step)
        def _():
            out_ref[...] = mm(post_ref[...], full_ref[...], NN).astype(out_ref.dtype)


def class_part(meta, kind, offset, steps, full, post=None, shifted=None, stats=None, hots=None, bins=0):
    rows, columns = full.shape
    width = columns // 8
    count = (shifted if post is None else post).shape[0]
    whole = lambda shape: pl.BlockSpec(shape, lambda j, m: (0, 0))
    full_spec = pl.BlockSpec((rows, width), lambda j, m: (0, m[offset + j]))
    out_specs = [whole((count, width))] * steps
    kept = steps // 2 if kind == "rest" else 0
    types = [BF16] * (steps - kept) + [F32] * kept
    out_shape = [sds((count, width), dtype) for dtype in types]
    if kind == "first":
        operands = [shifted, *stats, *hots, full]
        in_specs = [whole(shifted.shape)] + [whole(stats[0].shape)] * 5
        in_specs += [whole(hots[0].shape)] * 2 + [full_spec]
        out_specs += [whole((count, rows)), whole((1, rows // 2)), whole((bins, count))]
        out_shape += [sds((count, rows), BF16), sds((1, rows // 2), F32), sds((bins, count), BF16)]
    else:
        operands = [post, full]
        in_specs = [whole(post.shape), full_spec]
    return call(
        functools.partial(class_body, kind, steps),
        (steps,),
        in_specs,
        out_specs,
        out_shape,
        room=22 if kind == "first" else 28,
        flops=2 * count * rows * width * steps,
        moved=2 * rows * width * steps + 4 * count * (rows + width * steps),
    )(meta, *operands)


def own_half_body(tile, meta, keep_ref, c_ref, a_ref, out_ref):
    rows = pl.ds(pl.multiple_of(pl.program_id(0) * tile, tile), tile)
    out_ref[...] = keep_ref[rows, :] + c_ref[rows, :].astype(F32) + a_ref[rows, :].astype(F32)


def own_half(meta, keep, got_c, got_a):
    count, width = keep.shape
    parts = 3
    tile = count // parts
    return call(
        functools.partial(own_half_body, tile),
        (parts,),
        [pl.BlockSpec(memory_space=pltpu.VMEM)] * 3,
        pl.BlockSpec((tile, width), lambda j, m: (lax.rem(m[0], 2) * parts + j, 0)),
        sds((2 * count, width), F32),
        room=8,
    )(meta, keep, got_c, got_a)


def two_by_two(raw_images, defocus_bin, dest_row, ctf_table, inv_noise, panels):
    dom, turns = lax.axis_size("dom"), lax.axis_size("rot")
    device, plane = lax.axis_index("dom"), lax.axis_index("rot")
    bins = ctf_table.shape[0]
    columns = raw_images.shape[1]
    chip, core = device // 2, device % 2

    def block(apart, half):
        return (chip ^ apart) * 2 + half

    x_first, y_second = block(1, 0), block(2, 1)
    x_second, y_first = block(1, 1), block(2, 0)
    even = core == 0
    order = [
        device,
        plane,
        block(3, 0),
        block(3, 1),
        jnp.where(even, x_first, y_second),
        jnp.where(even, y_second, x_first),
        block(0, 1 - core),
        jnp.where(even, y_first, x_second),
        jnp.where(even, x_second, y_first),
        block(0, core),
    ]
    meta = jnp.stack(order).astype(I32)
    inv = inv_noise[None, :]

    def across(value, apart):
        return lax.ppermute(value, "dom", [(i, i ^ apart) for i in range(dom)])

    def by_core(value, when_even, when_odd):
        pairs = [(i, i ^ (when_odd if i % 2 else when_even)) for i in range(dom)]
        return lax.ppermute(value, "dom", pairs)

    def onward(value):
        return lax.ppermute(value, "rot", [(i, (i + 1) % turns) for i in range(turns)])

    width = columns // turns
    cut = width * 5 // 8
    chunk_a, chunk_b = (0, cut), (cut, width - cut)

    def exchange(blocks):
        far_first = [across(blocks[apart], apart) for apart in (6, 7, 4, 2, 5, 3, 1)]
        return far_first + [blocks[0]]

    slot = jnp.where(dest_row >= 0, dest_row * bins + defocus_bin, -1)
    *send_a, place = pack_first(meta, raw_images, slot, bins, dom, width, chunk_a)
    recv_a = exchange(send_a)
    swapped, place = lax.optimization_barrier((across(panels, 1), place))
    send_b = pack_next(meta, raw_images, place, dom, width, chunk_b)
    together = lax.optimization_barrier

    count = panels.shape[0] // 2
    mine = lax.dynamic_slice_in_dim(panels, core * count, count, 0)
    other = lax.dynamic_slice_in_dim(swapped, core * count, count, 0)
    near = jnp.concatenate([mine, other], axis=1)

    recv_a, send_b, near = together((recv_a, send_b, near))
    share_a, hot, pick, wide = unpack_first(meta, recv_a, ctf_table, inv, width, chunk_a)
    share_a, send_b = together((share_a, send_b))
    a1, recv_b = onward(share_a), exchange(send_b)
    recv_b, near = together((recv_b, near))
    by_x, by_y = across(near, 2), across(near, 4)
    share_b = unpack_next(meta, pick, wide, recv_b, ctf_table, inv, width, chunk_b)
    a2, b1 = onward(a1), onward(share_b)
    sib0, sib1, hots = [across(share_a, 1), across(share_b, 1)], [across(a1, 1)], [hot, across(hot, 1)]
    a2, b1, by_x, by_y, sib0, sib1, hots = together((a2, b1, by_x, by_y, sib0, sib1, hots))
    sib1 = sib1 + [across(b1, 1)]
    piece = near.shape[1] // 2
    far_y, far_x = across(by_x[:, :piece], 4), across(by_y[:, piece:], 2)
    a3, b2 = onward(a2), onward(b1)
    panel_full, extra = energy(meta, [near, by_x, by_y, far_y, far_x], ctf_table, inv)

    def share(turn):
        return lambda m: lax.rem(m[1] + turns - turn, turns)

    acc, full = score(meta, share(0), [share_a, share_b], sib0, panel_full, width)
    acc, full = score(meta, share(1), [a1, b1], sib1, panel_full, width, acc, full)
    a3, b2, acc, full = together((a3, b2, acc, full))
    b3 = onward(b2)
    sib2 = [across(a2, 1), across(b2, 1)]
    acc, full = score(meta, share(2), [a2, b2], sib2, panel_full, width, acc, full)
    final = share(turns - 1)
    a3_sib = across(a3, 1)
    acc = score(meta, final, [a3], [a3_sib], panel_full, width, acc, used=chunk_a)
    b3, acc = together((b3, acc))
    shifted, stat, full = score(
        meta,
        final,
        [a3, b3],
        [a3_sib, across(b3, 1)],
        panel_full,
        width,
        acc,
        full,
        hots,
        extra,
        chunk_b,
    )

    pair = merge(meta, stat, across(stat, 1))
    others = [
        lax.ppermute(pair, "rot", [(i, i ^ apart) for i in range(turns)]) for apart in (1, 2, 3)
    ]
    to_x, to_y, post, log_evidence, mass = class_part(
        meta, "first", 2, 2, full, None, shifted, [stat, pair, *others], hots, bins
    )
    mass_x = across(mass, 2)
    got_x, got_y = across(to_x, 2), across(to_y, 4)
    six = class_part(meta, "rest", 4, 6, full, post)
    got_x, got_y, six, mass_x = together((got_x, got_y, six, mass_x))
    send_c, send_d, give, a_sum, b_sum, keep = six
    mass = add_pair(meta, mass, mass_x)
    mass_y = across(mass, 4)
    got_c, got_d = by_core(send_c, 2, 4), by_core(send_d, 5, 3)
    down, left = got_x.astype(F32), got_y.astype(F32)
    message_a = (a_sum + jnp.where(even, down, left)).astype(BF16)
    message_b = (b_sum + jnp.where(even, left, down)).astype(BF16)
    got_a, got_b = by_core(message_a, 4, 2), by_core(message_b, 3, 5)
    got_self = across(give, 1)
    mass = mass.astype(F32) + mass_y.astype(F32)
    mass_other = across(mass, 1)
    bin_weights = jnp.where(
        even,
        jnp.concatenate([mass, mass_other], axis=1),
        jnp.concatenate([mass_other, mass], axis=1),
    )
    sums = own_half(meta, keep, got_c, got_a)
    other_half = got_self.astype(F32) + got_d.astype(F32) + got_b.astype(F32)
    class_sums = lax.dynamic_update_slice_in_dim(sums, other_half, (1 - core) * count, 0).T
    return class_sums, bin_weights, log_evidence.reshape(-1)


def energy_block(gain_block, panel_piece):
    widened = panel_piece.astype(jnp.float32)
    return lax.dot_general(
        gain_block, widened * widened, (((1,), (1,)), ((), ())), precision=lax.Precision.HIGHEST
    )


def on_device(raw_images, defocus_bin, dest_row, ctf_table, inv_noise, panels):
    dom_count = lax.axis_size("dom")
    bin_count = ctf_table.shape[0]
    columns = raw_images.shape[1]
    hold_rows = raw_images.shape[0]
    shard_rows = hold_rows // 2
    capacity = 2 * shard_rows // dom_count
    is_live = dest_row >= 0
    target = jnp.where(is_live, dest_row // shard_rows, dom_count)
    local_row = dest_row % shard_rows
    marks = (target[:, None] == jnp.arange(dom_count, dtype=jnp.int32)[None, :]).astype(jnp.int32)
    slot_rank = jnp.sum((jnp.cumsum(marks, axis=0) - marks) * marks, axis=1)
    row_code = jnp.where(is_live, local_row * bin_count + defocus_bin, -1)
    padded_images = jnp.concatenate([raw_images, jnp.zeros((1, columns), raw_images.dtype)], axis=0)
    padded_code = jnp.concatenate([row_code, jnp.full((1,), -1, jnp.int32)], axis=0)
    position = jnp.where(is_live, target * capacity + slot_rank, dom_count * capacity)
    slot_count = dom_count * capacity
    source = (
        jnp.full((slot_count,), hold_rows, jnp.int32)
        .at[position]
        .set(jnp.arange(hold_rows, dtype=jnp.int32), mode="drop")
    )
    send_images = padded_images[source].reshape(dom_count, capacity, columns)
    send_code = padded_code[source].reshape(dom_count, capacity)
    recv_images, recv_code = (
        lax.all_to_all(send_images, "dom", split_axis=0, concat_axis=0, tiled=True),
        lax.all_to_all(send_code, "dom", split_axis=0, concat_axis=0, tiled=True),
    )
    flat_images = recv_images.reshape(-1, columns)
    flat_code = recv_code.reshape(-1)
    arrived = flat_code >= 0
    row_of = jnp.where(arrived, flat_code // bin_count, shard_rows)
    row_order = (
        jnp.zeros((shard_rows,), jnp.int32)
        .at[row_of]
        .set(jnp.arange(flat_code.shape[0], dtype=jnp.int32), mode="drop")
    )
    images = flat_images[row_order]
    bin_ids = flat_code[row_order] % bin_count
    bin_table = (bin_ids[:, None] == jnp.arange(bin_count, dtype=jnp.int32)[None, :]).astype(
        jnp.float32
    )
    ctf_rows = jnp.dot(bin_table, ctf_table, precision=lax.Precision.HIGHEST)
    factor = ctf_rows * inv_noise[None, :]
    weighted = (images.astype(jnp.float32) * jnp.concatenate([factor, factor], axis=1)).astype(
        jnp.bfloat16
    )
    gain_half = ctf_table * ctf_table * inv_noise[None, :]
    gain_full = jnp.concatenate([gain_half, gain_half], axis=1)
    panel_piece = lax.all_gather(panels, "dom", axis=1, tiled=True)
    col_block = weighted
    cross_term = lax.dot_general(
        col_block, panel_piece, (((1,), (1,)), ((), ())), preferred_element_type=jnp.float32
    )
    energy = energy_block(gain_full, panel_piece)
    scores = cross_term - 0.5 * jnp.dot(bin_table, energy, precision=lax.Precision.HIGHEST)
    local_peak = jnp.max(scores, axis=1)
    row_peak = lax.pmax(local_peak, "rot")
    shifted = jnp.exp(scores - row_peak[:, None])
    row_total = lax.psum(jnp.sum(shifted, axis=1), "rot")
    posterior = (shifted / row_total[:, None]).astype(jnp.bfloat16)
    log_evidence = row_peak + jnp.log(row_total)
    col_block = weighted
    class_sums = lax.psum_scatter(
        lax.dot_general(
            col_block, posterior, (((0,), (0,)), ((), ())), preferred_element_type=jnp.float32
        ).astype(jnp.bfloat16),
        "dom",
        scatter_dimension=0,
        tiled=True,
    ).astype(jnp.float32)
    local_mass = lax.dot_general(
        bin_table.astype(jnp.bfloat16),
        posterior,
        (((0,), (0,)), ((), ())),
        preferred_element_type=jnp.float32,
    )
    bin_weights = lax.psum(local_mass.astype(jnp.bfloat16), "dom").astype(jnp.float32)
    return (class_sums, bin_weights, log_evidence)


def solution(mesh):
    small = mesh.shape["dom"] == 8 and mesh.shape["rot"] == 4
    return jax.shard_map(
        two_by_two if small else on_device,
        mesh=mesh,
        in_specs=(P("dom", None), P("dom"), P("dom"), P(), P(), P("rot", "dom")),
        out_specs=(P("dom", "rot"), P(None, "rot"), P("dom")),
        check_vma=False,
    )
```

```python
import functools

import jax
import jax.numpy as jnp
from jax import lax
from jax.experimental import pallas as pl
from jax.experimental.pallas import tpu as pltpu
from jax.sharding import PartitionSpec as P

NN = (((1,), (0,)), ((), ()))
NT = (((1,), (1,)), ((), ()))
F32, BF16, I32 = jnp.float32, jnp.bfloat16, jnp.int32
CODE = 16
LANES = 128
MIB = 1024 * 1024


def mm(a, b, dims):
    return lax.dot_general(a, b, dims, preferred_element_type=F32)


def split3(x):
    hi = x.astype(BF16)
    rest = x - hi.astype(F32)
    mid = rest.astype(BF16)
    low = (rest - mid.astype(F32)).astype(BF16)
    return hi, mid, low


def call(body, grid, in_specs, out_specs, out_shape, scratch=(), alias=None, flops=0, moved=0, room=24):
    return pl.pallas_call(
        body,
        grid_spec=pltpu.PrefetchScalarGridSpec(
            num_scalar_prefetch=1,
            grid=grid,
            in_specs=in_specs,
            out_specs=out_specs,
            scratch_shapes=list(scratch),
        ),
        out_shape=out_shape,
        input_output_aliases=alias or {},
        compiler_params=pltpu.CompilerParams(vmem_limit_bytes=room * MIB),
        cost_estimate=pl.CostEstimate(
            flops=flops // 16, bytes_accessed=moved // 16, transcendentals=0
        ),
    )


def sds(shape, dtype):
    return jax.ShapeDtypeStruct(shape, dtype)


def one_hot_rows(out_ref, wanted):
    rows, width = out_ref.shape
    short = wanted.astype(jnp.int16)
    one, zero = jnp.ones((), BF16), jnp.zeros((), BF16)
    step = 256 if rows % 256 == 0 else rows
    for start in range(0, rows, step):
        index = lax.broadcasted_iota(jnp.int16, (step, width), 0) + jnp.int16(start)
        out_ref[start : start + step, :] = jnp.where(index == short, one, zero)


def places_of(dest, shard_rows, cap, dom, device):
    hold = dest.shape[1]
    low = lax.broadcasted_iota(I32, (dom, hold), 0) * shard_rows
    inside = jnp.logical_and(dest >= low, dest < low + shard_rows)
    marks = jnp.where(inside, 1.0, 0.0)
    local = dest - jnp.sum(jnp.where(inside, low, 0), axis=0, keepdims=True)
    lanes = 128
    before = lax.broadcasted_iota(I32, (lanes, lanes), 0) < lax.broadcasted_iota(
        I32, (lanes, lanes), 1
    )
    upper = jnp.where(before, 1.0, 0.0).astype(BF16)
    apart = lax.broadcasted_iota(I32, (dom, 1), 0) ^ device
    carry = apart.astype(F32) * cap + 1.0
    found = []
    for start in range(0, hold, lanes):
        part = marks[:, start : start + lanes]
        rank = mm(part.astype(BF16), upper, NN) + carry
        found.append(jnp.sum(jnp.where(part > 0, rank, 0.0), axis=0, keepdims=True))
        carry = carry + jnp.sum(part, axis=1, keepdims=True)
    return jnp.concatenate(found, axis=1).astype(I32) - 1, local


def joined(refs):
    return jnp.concatenate([ref[...] for ref in refs], axis=1)


def pack_first_body(dom, shard_rows, cap, bins, meta, slot_ref, *refs):
    raw, outs, (place_ref, pick) = refs[: -dom - 2], refs[-dom - 2 : -2], refs[-2:]
    slot = slot_ref[...].reshape(1, slot_ref.shape[0])
    dest, slot_bin = slot >> (bins.bit_length() - 1), slot & (bins - 1)
    place, local = places_of(dest, shard_rows, cap, dom, meta[0])
    place_ref[...] = place
    one_hot_rows(pick, place)
    which = lax.broadcasted_iota(I32, (CODE, dest.shape[1]), 0)
    digits = jnp.where(
        which == 0,
        local >> 4,
        jnp.where(which == 1, local & 15, jnp.where(which == 2, slot_bin, jnp.where(which == 3, 1, 0))),
    )
    digits = jnp.where(dest >= 0, digits, 0).astype(F32).astype(BF16)
    codes = mm(digits, pick[...], NT)
    packed = mm(pick[...], joined(raw), NN).astype(BF16)
    for index, out_ref in enumerate(outs):
        block = slice(index * cap, (index + 1) * cap)
        out_ref[:cap, :] = packed[block]
        out_ref[cap:, :] = jnp.zeros((CODE, out_ref.shape[1]), BF16)
        out_ref[cap:, :cap] = codes[:, block].astype(BF16)


def pack_next_body(cap, dom, meta, place_ref, *refs):
    raw, outs, pick = refs[: -dom - 1], refs[-dom - 1 : -1], refs[-1]
    one_hot_rows(pick, place_ref[...])
    packed = mm(pick[...], joined(raw), NN).astype(BF16)
    for index, out_ref in enumerate(outs):
        out_ref[...] = packed[index * cap : (index + 1) * cap]


def raw_specs(hold, share, chunk):
    first, width = chunk
    at = lambda k: lambda j, m: (0, m[1] * (share // LANES) + first // LANES + k)
    return [pl.BlockSpec((hold, LANES), at(k)) for k in range(width // LANES)]


def pack_first(meta, raw_images, slot, bins, dom, share, chunk):
    hold, _ = raw_images.shape
    width = chunk[1]
    cap = hold // dom
    slots = dom * cap
    specs = raw_specs(hold, share, chunk)
    return call(
        functools.partial(pack_first_body, dom, hold // 2, cap, bins),
        (1,),
        [pl.BlockSpec((hold,), lambda j, m: (0,))] + specs,
        [pl.BlockSpec((cap + CODE, width), lambda j, m: (0, 0))] * dom
        + [pl.BlockSpec((1, hold), lambda j, m: (0, 0))],
        [sds((cap + CODE, width), BF16)] * dom + [sds((1, hold), I32)],
        scratch=[pltpu.VMEM((slots, hold), BF16)],
        room=51,
        flops=2 * slots * hold * width,
        moved=4 * hold * width,
    )(meta, slot, *[raw_images] * len(specs))


def pack_next(meta, raw_images, place, dom, share, chunk):
    hold, _ = raw_images.shape
    width = chunk[1]
    cap = hold // dom
    slots = dom * cap
    specs = raw_specs(hold, share, chunk)
    return call(
        functools.partial(pack_next_body, cap, dom),
        (1,),
        [pl.BlockSpec((1, hold), lambda j, m: (0, 0))] + specs,
        [pl.BlockSpec((cap, width), lambda j, m: (0, 0))] * dom,
        [sds((cap, width), BF16)] * dom,
        scratch=[pltpu.VMEM((slots, hold), BF16)],
        room=51,
        flops=2 * slots * hold * width,
        moved=4 * hold * width,
    )(meta, place, *[raw_images] * len(specs))


def weigh(first, share, pick, wide, recv, meta, ctf_ref, inv_ref, out_ref):
    width = out_ref.shape[1]
    start = lax.rem(meta[1] * share, ctf_ref.shape[1]) + first
    columns = pl.ds(pl.multiple_of(start, LANES), width)
    table = jnp.concatenate(split3(ctf_ref[:, columns] * inv_ref[:, columns]), axis=0)
    out_ref[...] = (mm(pick, recv, NN) * mm(wide, table, NN)).astype(BF16)


def gather(pieces, whole, rows):
    for index, piece in enumerate(pieces):
        whole[index * rows : (index + 1) * rows, :] = piece[:rows, :]


def unpack_first_body(dom, bins, share, first, meta, *refs):
    pieces, recv_ref = refs[:dom], refs[-1]
    cap = pieces[0].shape[0] - CODE
    gather(pieces, recv_ref, cap)
    ctf_ref, inv_ref, out_ref, hot_ref, pick, wide = refs[dom:-1]
    shard_rows = out_ref.shape[0]
    got = jnp.concatenate([piece[cap:, :cap].astype(F32) for piece in pieces], axis=1)
    row = got[0:1] * 16.0 + got[1:2] + got[3:4] * 1024.0 - 1024.0
    one_hot_rows(pick, row.astype(I32))
    slot_bins = jnp.broadcast_to(got[2:3].astype(BF16), (8, got.shape[1]))
    down = mm(pick[...], slot_bins, NT)[:, 0:1].astype(I32)
    across = mm(slot_bins, pick[...], NT)[0:1].astype(I32)
    lane = lax.broadcasted_iota(I32, (shard_rows, 3 * bins), 1)
    wide[...] = jnp.where((lane & (bins - 1)) == down, 1.0, 0.0).astype(BF16)
    deep = lax.broadcasted_iota(I32, (3 * bins, shard_rows), 0)
    hot_ref[...] = jnp.where((deep & (bins - 1)) == across, 1.0, 0.0).astype(BF16)
    weigh(first, share, pick[...], wide[...], recv_ref[...], meta, ctf_ref, inv_ref, out_ref)


def unpack_next_body(dom, share, first, meta, *refs):
    recv_ref = refs[-1]
    gather(refs[:dom], recv_ref, refs[0].shape[0])
    pick_ref, wide_ref, ctf_ref, inv_ref, out_ref = refs[dom:-1]
    weigh(first, share, pick_ref[...], wide_ref[...], recv_ref[...], meta, ctf_ref, inv_ref, out_ref)


def unpack_first(meta, recv, ctf, inv, share, chunk):
    first, width = chunk
    dom = len(recv)
    slots = dom * (recv[0].shape[0] - CODE)
    rows = slots // 2
    bins, pix = ctf.shape
    whole = lambda shape: pl.BlockSpec(shape, lambda j, m: (0, 0))
    shapes = [(rows, width), (3 * bins, rows), (rows, slots), (rows, 3 * bins)]
    return call(
        functools.partial(unpack_first_body, dom, bins, share, first),
        (1,),
        [whole(recv[0].shape)] * dom + [whole(ctf.shape), whole(inv.shape)],
        [whole(s) for s in shapes],
        [sds(s, BF16) for s in shapes],
        scratch=[pltpu.VMEM((slots, width), BF16)],
        room=28,
        flops=2 * slots * rows * width,
        moved=2 * slots * width,
    )(meta, *recv, ctf, inv)


def unpack_next(meta, pick, wide, recv, ctf, inv, share, chunk):
    first, width = chunk
    dom = len(recv)
    slots = dom * recv[0].shape[0]
    rows = slots // 2
    whole = lambda shape: pl.BlockSpec(shape, lambda j, m: (0, 0))
    return call(
        functools.partial(unpack_next_body, dom, share, first),
        (1,),
        [whole(recv[0].shape)] * dom
        + [whole(pick.shape), whole(wide.shape), whole(ctf.shape), whole(inv.shape)],
        whole((rows, width)),
        sds((rows, width), BF16),
        scratch=[pltpu.VMEM((slots, width), BF16)],
        room=28,
        flops=2 * slots * rows * width,
        moved=2 * slots * width,
    )(meta, *recv, pick, wide, ctf, inv)


def energy_body(bins, count, meta, *refs):
    pieces, (ctf_ref, inv_ref, panel_ref, extra_ref, total) = refs[:-5], refs[-5:]
    width = panel_ref.shape[1]
    blocks = []
    for piece in pieces:
        for start in range(0, piece.shape[1], width):
            blocks.append((piece, start))
    step = pl.program_id(0)

    @pl.when(step == 0)
    def _():
        total[...] = jnp.zeros_like(total)

    gain = ctf_ref[...] * ctf_ref[...] * inv_ref[...]
    gain3 = jnp.concatenate(split3(gain), axis=0)
    for index, (piece, start) in enumerate(blocks):

        @pl.when(step == index)
        def _():
            panel = piece[:, start : start + width]
            panel_ref[...] = panel
            wide = panel.astype(F32)
            square = wide * wide
            high = square.astype(BF16)
            low = (square - high.astype(F32)).astype(BF16)
            total[...] += mm(high, gain3, NT) + mm(low, gain3, NT)

    @pl.when(step == count - 1)
    def _():
        whole = total[:, :bins] + total[:, bins : 2 * bins] + total[:, 2 * bins :]
        extra_ref[...] = jnp.concatenate(split3(-0.5 * whole), axis=1)


def energy(meta, pieces, ctf, inv):
    rows, width = pieces[-1].shape
    count = sum(piece.shape[1] for piece in pieces) // width
    bins, pix = ctf.shape
    wrap = pix // width
    return call(
        functools.partial(energy_body, bins, count),
        (count,),
        [pl.BlockSpec(piece.shape, lambda j, m: (0, 0)) for piece in pieces]
        + [
            pl.BlockSpec((bins, width), lambda j, m: (0, lax.rem(m[0] ^ j, wrap))),
            pl.BlockSpec((1, width), lambda j, m: (0, lax.rem(m[0] ^ j, wrap))),
        ],
        [
            pl.BlockSpec((rows, width), lambda j, m: (0, m[0] ^ j)),
            pl.BlockSpec((rows, 3 * bins), lambda j, m: (0, 0)),
        ],
        [sds((rows, count * width), BF16), sds((rows, 3 * bins), BF16)],
        scratch=[pltpu.VMEM((rows, 3 * bins), F32)],
        flops=2 * 4 * rows * bins * count * width * 3,
        moved=4 * rows * count * width,
    )(meta, *pieces, ctf, inv)


def score_body(parts, used, first, last, meta, *refs):
    own, sib, panel_ref, refs = (
        refs[:parts],
        refs[parts : 2 * parts],
        refs[2 * parts],
        refs[2 * parts + 1 :],
    )
    if first:
        acc_out, full_ref = refs
    elif last:
        acc_ref, _, hot_own, hot_sib, extra_ref, shifted_ref, stat_ref, full_ref = refs
    elif used is None:
        acc_ref, _, acc_out, full_ref = refs
    else:
        acc_ref, acc_out = refs
    half = pl.num_programs(0) // 2

    def tile(sources, hot):
        block = jnp.concatenate([source[...] for source in sources], axis=1)
        if used is None or last:
            full_ref[...] = block
        if last:
            block = block[:, used[0] : used[0] + used[1]]
        panel = panel_ref[...] if used is None else panel_ref[:, used[0] : used[0] + used[1]]
        total = mm(panel, block, NT)
        if not first:
            total = acc_ref[...] + total
        if not last:
            acc_out[...] = total
            return
        total = total + mm(extra_ref[...], hot[...], NN)
        peak = jnp.max(total, axis=0, keepdims=True)
        shifted = jnp.exp(total - peak)
        shifted_ref[...] = shifted
        mass = jnp.sum(shifted, axis=0, keepdims=True)
        which = lax.broadcasted_iota(I32, stat_ref.shape, 0)
        stat_ref[...] = jnp.where(which == 0, peak, mass)

    @pl.when(pl.program_id(0) < half)
    def _():
        tile(own, hot_own if last else None)

    @pl.when(pl.program_id(0) >= half)
    def _():
        tile(sib, hot_sib if last else None)


def score(meta, at, own, sib, panels, width, acc=None, full=None, hots=None, extra=None, used=None):
    rows = own[0].shape[0]
    parts = len(own)
    tile = 256
    half = rows // tile
    count, columns = panels.shape
    first, last = acc is None, hots is not None
    store = used is None or last
    fronts = [pl.BlockSpec((tile, v.shape[1]), lambda j, m: (jnp.minimum(j, half - 1), 0)) for v in own]
    backs = [pl.BlockSpec((tile, v.shape[1]), lambda j, m: (jnp.maximum(j - half, 0), 0)) for v in own]
    acc_spec = pl.BlockSpec((count, tile), lambda j, m: (0, j))
    full_spec = pl.BlockSpec((tile, width), lambda j, m: (j, at(m)))
    in_specs = fronts + backs + [pl.BlockSpec((count, width), lambda j, m: (0, at(m)))]
    operands = [meta, *own, *sib, panels]
    alias = {}
    if not first:
        in_specs += [acc_spec]
        alias = {len(operands): 0}
        operands += [acc]
        if store:
            in_specs += [pl.BlockSpec(memory_space=pl.ANY)]
            alias[len(operands)] = 2 if last else 1
            operands += [full]
    full_shape = sds((2 * rows, columns), BF16)
    acc_shape = sds((count, 2 * rows), F32)
    out_specs, out_shape = [acc_spec, full_spec], [acc_shape, full_shape]
    if last:
        depth = extra.shape[1]
        in_specs += [
            pl.BlockSpec((depth, tile), lambda j, m: (0, jnp.minimum(j, half - 1))),
            pl.BlockSpec((depth, tile), lambda j, m: (0, jnp.maximum(j - half, 0))),
            pl.BlockSpec((count, depth), lambda j, m: (0, 0)),
        ]
        operands += [*hots, extra]
        out_specs = [acc_spec, pl.BlockSpec((8, tile), lambda j, m: (0, j)), full_spec]
        out_shape = [acc_shape, sds((8, 2 * rows), F32), full_shape]
    elif not store:
        out_specs, out_shape = acc_spec, acc_shape
    return call(
        functools.partial(score_body, parts, used, first, last),
        (2 * half,),
        in_specs,
        out_specs,
        out_shape,
        alias=alias,
        room=16,
        flops=2 * count * 2 * rows * width,
        moved=8 * count * 2 * rows + 8 * rows * width,
    )(*operands)


def merge_body(meta, mine_ref, other_ref, out_ref):
    rows = mine_ref.shape[1] // 2
    other = other_ref[...]
    other = jnp.concatenate([other[:, rows:], other[:, :rows]], axis=1)
    mine = mine_ref[...]
    peak = jnp.maximum(mine[0:1], other[0:1])
    mass = mine[1:2] * jnp.exp(mine[0:1] - peak) + other[1:2] * jnp.exp(other[0:1] - peak)
    which = lax.broadcasted_iota(I32, out_ref.shape, 0)
    out_ref[...] = jnp.where(which == 0, peak, mass)


def add_body(meta, mine_ref, other_ref, out_ref):
    out_ref[...] = (mine_ref[...].astype(F32) + other_ref[...].astype(F32)).astype(BF16)


def pairwise(body, meta, mine, other):
    spec = pl.BlockSpec(mine.shape, lambda j, m: (0, 0))
    return call(body, (1,), [spec, spec], spec, sds(mine.shape, mine.dtype), room=4)(
        meta, mine, other
    )


merge = functools.partial(pairwise, merge_body)
add_pair = functools.partial(pairwise, add_body)


def class_body(kind, steps, meta, *refs):
    if kind == "first":
        (shifted_ref, stat_ref), four = refs[:2], refs[2:6]
        hot_own, hot_sib, full_ref = refs[6:9]
        outs, (post_ref, log_ref, mass_ref) = refs[9 : 9 + steps], refs[9 + steps :]

        @pl.when(pl.program_id(0) == 0)
        def _():
            stats = [ref[...] for ref in four]
            peaks = [s[0:1] for s in stats]
            peak = jnp.maximum(jnp.maximum(peaks[0], peaks[1]), jnp.maximum(peaks[2], peaks[3]))
            parts = [s[1:2] * jnp.exp(p - peak) for s, p in zip(stats, peaks)]
            mass = (parts[0] + parts[1]) + (parts[2] + parts[3])
            factor = jnp.exp(stat_ref[0:1] - peak) / mass
            post_ref[...] = (shifted_ref[...] * factor).astype(BF16)
            log_ref[...] = (peak + jnp.log(mass))[:, : log_ref.shape[1]]
            bins, rows = mass_ref.shape[0], hot_own.shape[1]
            weights = mm(hot_own[:bins, :], post_ref[:, :rows], NT)
            weights = weights + mm(hot_sib[:bins, :], post_ref[:, rows:], NT)
            mass_ref[...] = weights.astype(BF16)

    else:
        (post_ref, full_ref), outs = refs[:2], refs[2:]
    for step, out_ref in enumerate(outs):

        @pl.when(pl.program_id(0) == step)
        def _():
            out_ref[...] = mm(post_ref[...], full_ref[...], NN).astype(out_ref.dtype)


def class_part(meta, kind, offset, steps, full, post=None, shifted=None, stats=None, hots=None, bins=0):
    rows, columns = full.shape
    width = columns // 8
    count = (shifted if post is None else post).shape[0]
    whole = lambda shape: pl.BlockSpec(shape, lambda j, m: (0, 0))
    full_spec = pl.BlockSpec((rows, width), lambda j, m: (0, m[offset + j]))
    out_specs = [whole((count, width))] * steps
    kept = steps // 2 if kind == "rest" else 0
    types = [BF16] * (steps - kept) + [F32] * kept
    out_shape = [sds((count, width), dtype) for dtype in types]
    if kind == "first":
        operands = [shifted, *stats, *hots, full]
        in_specs = [whole(shifted.shape)] + [whole(stats[0].shape)] * 5
        in_specs += [whole(hots[0].shape)] * 2 + [full_spec]
        out_specs += [whole((count, rows)), whole((1, rows // 2)), whole((bins, count))]
        out_shape += [sds((count, rows), BF16), sds((1, rows // 2), F32), sds((bins, count), BF16)]
    else:
        operands = [post, full]
        in_specs = [whole(post.shape), full_spec]
    return call(
        functools.partial(class_body, kind, steps),
        (steps,),
        in_specs,
        out_specs,
        out_shape,
        room=22 if kind == "first" else 28,
        flops=2 * count * rows * width * steps,
        moved=2 * rows * width * steps + 4 * count * (rows + width * steps),
    )(meta, *operands)


def own_half_body(tile, meta, keep_ref, c_ref, a_ref, out_ref):
    rows = pl.ds(pl.multiple_of(pl.program_id(0) * tile, tile), tile)
    out_ref[...] = keep_ref[rows, :] + c_ref[rows, :].astype(F32) + a_ref[rows, :].astype(F32)


def own_half(meta, keep, got_c, got_a):
    count, width = keep.shape
    parts = 3
    tile = count // parts
    return call(
        functools.partial(own_half_body, tile),
        (parts,),
        [pl.BlockSpec(memory_space=pltpu.VMEM)] * 3,
        pl.BlockSpec((tile, width), lambda j, m: (lax.rem(m[0], 2) * parts + j, 0)),
        sds((2 * count, width), F32),
        room=8,
    )(meta, keep, got_c, got_a)


def two_by_two(raw_images, defocus_bin, dest_row, ctf_table, inv_noise, panels):
    dom, turns = lax.axis_size("dom"), lax.axis_size("rot")
    device, plane = lax.axis_index("dom"), lax.axis_index("rot")
    bins = ctf_table.shape[0]
    columns = raw_images.shape[1]
    chip, core = device // 2, device % 2

    def block(apart, half):
        return (chip ^ apart) * 2 + half

    x_first, y_second = block(1, 0), block(2, 1)
    x_second, y_first = block(1, 1), block(2, 0)
    even = core == 0
    order = [
        device,
        plane,
        block(3, 0),
        block(3, 1),
        jnp.where(even, x_first, y_second),
        jnp.where(even, y_second, x_first),
        block(0, 1 - core),
        jnp.where(even, y_first, x_second),
        jnp.where(even, x_second, y_first),
        block(0, core),
    ]
    meta = jnp.stack(order).astype(I32)
    inv = inv_noise[None, :]

    def across(value, apart):
        return lax.ppermute(value, "dom", [(i, i ^ apart) for i in range(dom)])

    def by_core(value, when_even, when_odd):
        pairs = [(i, i ^ (when_odd if i % 2 else when_even)) for i in range(dom)]
        return lax.ppermute(value, "dom", pairs)

    def onward(value):
        return lax.ppermute(value, "rot", [(i, (i + 1) % turns) for i in range(turns)])

    width = columns // turns
    cut = width * 3 // 8
    chunk_a, chunk_b = (0, cut), (cut, width - cut)

    def exchange(blocks):
        far_first = [across(blocks[apart], apart) for apart in (6, 7, 4, 2, 5, 3, 1)]
        return far_first + [blocks[0]]

    slot = jnp.where(dest_row >= 0, dest_row * bins + defocus_bin, -1)
    *send_a, place = pack_first(meta, raw_images, slot, bins, dom, width, chunk_a)
    recv_a = exchange(send_a)
    swapped, place = lax.optimization_barrier((across(panels, 1), place))
    send_b = pack_next(meta, raw_images, place, dom, width, chunk_b)
    together = lax.optimization_barrier

    count = panels.shape[0] // 2
    mine = lax.dynamic_slice_in_dim(panels, core * count, count, 0)
    other = lax.dynamic_slice_in_dim(swapped, core * count, count, 0)
    near = jnp.concatenate([mine, other], axis=1)

    recv_a, send_b, near = together((recv_a, send_b, near))
    share_a, hot, pick, wide = unpack_first(meta, recv_a, ctf_table, inv, width, chunk_a)
    share_a, send_b = together((share_a, send_b))
    a1, recv_b = onward(share_a), exchange(send_b)
    a1, recv_b[:2] = together((a1, recv_b[:2]))
    a2 = onward(a1)
    share_b = unpack_next(meta, pick, wide, recv_b, ctf_table, inv, width, chunk_b)
    a2, share_b, near = together((a2, share_b, near))
    by_x, by_y = across(near, 2), across(near, 4)
    a3, b1 = onward(a2), onward(share_b)
    sib0, sib1, hots = [across(share_a, 1), across(share_b, 1)], [across(a1, 1)], [hot, across(hot, 1)]
    a3, b1, by_x, by_y, sib0, sib1, hots = together((a3, b1, by_x, by_y, sib0, sib1, hots))
    sib1, sib2 = sib1 + [across(b1, 1)], [across(a2, 1)]
    piece = near.shape[1] // 2
    far_y, far_x = across(by_x[:, :piece], 4), across(by_y[:, piece:], 2)
    b2 = onward(b1)
    panel_full, extra = energy(meta, [near, by_x, by_y, far_y, far_x], ctf_table, inv)
    b2, panel_full, extra, sib1, sib2 = together((b2, panel_full, extra, sib1, sib2))
    b3 = onward(b2)
    sib2 = sib2 + [across(b2, 1)]

    def share(turn):
        return lambda m: lax.rem(m[1] + turns - turn, turns)

    acc, full = score(meta, share(0), [share_a, share_b], sib0, panel_full, width)
    acc, full = score(meta, share(1), [a1, b1], sib1, panel_full, width, acc, full)
    acc, full = score(meta, share(2), [a2, b2], sib2, panel_full, width, acc, full)
    final = share(turns - 1)
    a3_sib = across(a3, 1)
    acc = score(meta, final, [a3], [a3_sib], panel_full, width, acc, used=chunk_a)
    b3, acc = together((b3, acc))
    shifted, stat, full = score(
        meta,
        final,
        [a3, b3],
        [a3_sib, across(b3, 1)],
        panel_full,
        width,
        acc,
        full,
        hots,
        extra,
        chunk_b,
    )

    pair = merge(meta, stat, across(stat, 1))
    others = [
        lax.ppermute(pair, "rot", [(i, i ^ apart) for i in range(turns)]) for apart in (1, 2, 3)
    ]
    to_x, to_y, post, log_evidence, mass = class_part(
        meta, "first", 2, 2, full, None, shifted, [stat, pair, *others], hots, bins
    )
    mass_x = across(mass, 2)
    got_x, got_y = across(to_x, 2), across(to_y, 4)
    six = class_part(meta, "rest", 4, 6, full, post)
    got_x, got_y, six, mass_x = together((got_x, got_y, six, mass_x))
    send_c, send_d, give, a_sum, b_sum, keep = six
    mass = add_pair(meta, mass, mass_x)
    mass_y = across(mass, 4)
    got_c, got_d = by_core(send_c, 2, 4), by_core(send_d, 5, 3)
    down, left = got_x.astype(F32), got_y.astype(F32)
    message_a = (a_sum + jnp.where(even, down, left)).astype(BF16)
    message_b = (b_sum + jnp.where(even, left, down)).astype(BF16)
    got_a, got_b = by_core(message_a, 4, 2), by_core(message_b, 3, 5)
    got_self = across(give, 1)
    mass_y, got_a, got_c = together((mass_y, got_a, got_c))
    mass = mass.astype(F32) + mass_y.astype(F32)
    mass_other = across(mass, 1)
    bin_weights = jnp.where(
        even,
        jnp.concatenate([mass, mass_other], axis=1),
        jnp.concatenate([mass_other, mass], axis=1),
    )
    sums = own_half(meta, keep, got_c, got_a)
    bin_weights, got_b = together((bin_weights, got_b))
    other_half = got_self.astype(F32) + got_d.astype(F32) + got_b.astype(F32)
    class_sums = lax.dynamic_update_slice_in_dim(sums, other_half, (1 - core) * count, 0).T
    return class_sums, bin_weights, log_evidence.reshape(-1)


def energy_block(gain_block, panel_piece):
    widened = panel_piece.astype(jnp.float32)
    return lax.dot_general(
        gain_block, widened * widened, (((1,), (1,)), ((), ())), precision=lax.Precision.HIGHEST
    )


def on_device(raw_images, defocus_bin, dest_row, ctf_table, inv_noise, panels):
    dom_count = lax.axis_size("dom")
    bin_count = ctf_table.shape[0]
    columns = raw_images.shape[1]
    hold_rows = raw_images.shape[0]
    shard_rows = hold_rows // 2
    capacity = 2 * shard_rows // dom_count
    is_live = dest_row >= 0
    target = jnp.where(is_live, dest_row // shard_rows, dom_count)
    local_row = dest_row % shard_rows
    marks = (target[:, None] == jnp.arange(dom_count, dtype=jnp.int32)[None, :]).astype(jnp.int32)
    slot_rank = jnp.sum((jnp.cumsum(marks, axis=0) - marks) * marks, axis=1)
    row_code = jnp.where(is_live, local_row * bin_count + defocus_bin, -1)
    padded_images = jnp.concatenate([raw_images, jnp.zeros((1, columns), raw_images.dtype)], axis=0)
    padded_code = jnp.concatenate([row_code, jnp.full((1,), -1, jnp.int32)], axis=0)
    position = jnp.where(is_live, target * capacity + slot_rank, dom_count * capacity)
    slot_count = dom_count * capacity
    source = (
        jnp.full((slot_count,), hold_rows, jnp.int32)
        .at[position]
        .set(jnp.arange(hold_rows, dtype=jnp.int32), mode="drop")
    )
    send_images = padded_images[source].reshape(dom_count, capacity, columns)
    send_code = padded_code[source].reshape(dom_count, capacity)
    recv_images, recv_code = (
        lax.all_to_all(send_images, "dom", split_axis=0, concat_axis=0, tiled=True),
        lax.all_to_all(send_code, "dom", split_axis=0, concat_axis=0, tiled=True),
    )
    flat_images = recv_images.reshape(-1, columns)
    flat_code = recv_code.reshape(-1)
    arrived = flat_code >= 0
    row_of = jnp.where(arrived, flat_code // bin_count, shard_rows)
    row_order = (
        jnp.zeros((shard_rows,), jnp.int32)
        .at[row_of]
        .set(jnp.arange(flat_code.shape[0], dtype=jnp.int32), mode="drop")
    )
    images = flat_images[row_order]
    bin_ids = flat_code[row_order] % bin_count
    bin_table = (bin_ids[:, None] == jnp.arange(bin_count, dtype=jnp.int32)[None, :]).astype(
        jnp.float32
    )
    ctf_rows = jnp.dot(bin_table, ctf_table, precision=lax.Precision.HIGHEST)
    factor = ctf_rows * inv_noise[None, :]
    weighted = (images.astype(jnp.float32) * jnp.concatenate([factor, factor], axis=1)).astype(
        jnp.bfloat16
    )
    gain_half = ctf_table * ctf_table * inv_noise[None, :]
    gain_full = jnp.concatenate([gain_half, gain_half], axis=1)
    panel_piece = lax.all_gather(panels, "dom", axis=1, tiled=True)
    col_block = weighted
    cross_term = lax.dot_general(
        col_block, panel_piece, (((1,), (1,)), ((), ())), preferred_element_type=jnp.float32
    )
    energy = energy_block(gain_full, panel_piece)
    scores = cross_term - 0.5 * jnp.dot(bin_table, energy, precision=lax.Precision.HIGHEST)
    local_peak = jnp.max(scores, axis=1)
    row_peak = lax.pmax(local_peak, "rot")
    shifted = jnp.exp(scores - row_peak[:, None])
    row_total = lax.psum(jnp.sum(shifted, axis=1), "rot")
    posterior = (shifted / row_total[:, None]).astype(jnp.bfloat16)
    log_evidence = row_peak + jnp.log(row_total)
    col_block = weighted
    class_sums = lax.psum_scatter(
        lax.dot_general(
            col_block, posterior, (((0,), (0,)), ((), ())), preferred_element_type=jnp.float32
        ).astype(jnp.bfloat16),
        "dom",
        scatter_dimension=0,
        tiled=True,
    ).astype(jnp.float32)
    local_mass = lax.dot_general(
        bin_table.astype(jnp.bfloat16),
        posterior,
        (((0,), (0,)), ((), ())),
        preferred_element_type=jnp.float32,
    )
    bin_weights = lax.psum(local_mass.astype(jnp.bfloat16), "dom").astype(jnp.float32)
    return (class_sums, bin_weights, log_evidence)


def solution(mesh):
    small = mesh.shape["dom"] == 8 and mesh.shape["rot"] == 4
    return jax.shard_map(
        two_by_two if small else on_device,
        mesh=mesh,
        in_specs=(P("dom", None), P("dom"), P("dom"), P(), P(), P("rot", "dom")),
        out_specs=(P("dom", "rot"), P(None, "rot"), P("dom")),
        check_vma=False,
    )
```

```python
import functools

import jax
import jax.numpy as jnp
from jax import lax
from jax.experimental import pallas as pl
from jax.experimental.pallas import tpu as pltpu
from jax.sharding import PartitionSpec as P

NN = (((1,), (0,)), ((), ()))
NT = (((1,), (1,)), ((), ()))
F32, BF16, I32 = jnp.float32, jnp.bfloat16, jnp.int32
CODE = 16
LANES = 128
MIB = 1024 * 1024


def mm(a, b, dims):
    return lax.dot_general(a, b, dims, preferred_element_type=F32)


def split3(x):
    hi = x.astype(BF16)
    rest = x - hi.astype(F32)
    mid = rest.astype(BF16)
    low = (rest - mid.astype(F32)).astype(BF16)
    return hi, mid, low


def call(body, grid, in_specs, out_specs, out_shape, scratch=(), alias=None, flops=0, moved=0, room=24):
    return pl.pallas_call(
        body,
        grid_spec=pltpu.PrefetchScalarGridSpec(
            num_scalar_prefetch=1,
            grid=grid,
            in_specs=in_specs,
            out_specs=out_specs,
            scratch_shapes=list(scratch),
        ),
        out_shape=out_shape,
        input_output_aliases=alias or {},
        compiler_params=pltpu.CompilerParams(vmem_limit_bytes=room * MIB),
        cost_estimate=pl.CostEstimate(
            flops=flops // 16, bytes_accessed=moved // 16, transcendentals=0
        ),
    )


def sds(shape, dtype):
    return jax.ShapeDtypeStruct(shape, dtype)


def one_hot_rows(out_ref, wanted):
    rows, width = out_ref.shape
    short = wanted.astype(jnp.int16)
    one, zero = jnp.ones((), BF16), jnp.zeros((), BF16)
    step = 256 if rows % 256 == 0 else rows
    for start in range(0, rows, step):
        index = lax.broadcasted_iota(jnp.int16, (step, width), 0) + jnp.int16(start)
        out_ref[start : start + step, :] = jnp.where(index == short, one, zero)


def places_of(dest, shard_rows, cap, dom, device):
    hold = dest.shape[1]
    low = lax.broadcasted_iota(I32, (dom, hold), 0) * shard_rows
    inside = jnp.logical_and(dest >= low, dest < low + shard_rows)
    marks = jnp.where(inside, 1.0, 0.0)
    local = dest - jnp.sum(jnp.where(inside, low, 0), axis=0, keepdims=True)
    lanes = 128
    before = lax.broadcasted_iota(I32, (lanes, lanes), 0) < lax.broadcasted_iota(
        I32, (lanes, lanes), 1
    )
    upper = jnp.where(before, 1.0, 0.0).astype(BF16)
    apart = lax.broadcasted_iota(I32, (dom, 1), 0) ^ device
    carry = apart.astype(F32) * cap + 1.0
    found = []
    for start in range(0, hold, lanes):
        part = marks[:, start : start + lanes]
        rank = mm(part.astype(BF16), upper, NN) + carry
        found.append(jnp.sum(jnp.where(part > 0, rank, 0.0), axis=0, keepdims=True))
        carry = carry + jnp.sum(part, axis=1, keepdims=True)
    return jnp.concatenate(found, axis=1).astype(I32) - 1, local


def joined(refs):
    return jnp.concatenate([ref[...] for ref in refs], axis=1)


def pack_first_body(dom, shard_rows, cap, bins, meta, slot_ref, *refs):
    raw, outs, (place_ref, pick) = refs[: -dom - 2], refs[-dom - 2 : -2], refs[-2:]
    slot = slot_ref[...].reshape(1, slot_ref.shape[0])
    dest, slot_bin = slot >> (bins.bit_length() - 1), slot & (bins - 1)
    place, local = places_of(dest, shard_rows, cap, dom, meta[0])
    place_ref[...] = place
    one_hot_rows(pick, place)
    which = lax.broadcasted_iota(I32, (CODE, dest.shape[1]), 0)
    digits = jnp.where(
        which == 0,
        local >> 4,
        jnp.where(which == 1, local & 15, jnp.where(which == 2, slot_bin, jnp.where(which == 3, 1, 0))),
    )
    digits = jnp.where(dest >= 0, digits, 0).astype(F32).astype(BF16)
    codes = mm(digits, pick[...], NT)
    packed = mm(pick[...], joined(raw), NN).astype(BF16)
    for index, out_ref in enumerate(outs):
        block = slice(index * cap, (index + 1) * cap)
        out_ref[:cap, :] = packed[block]
        out_ref[cap:, :] = jnp.zeros((CODE, out_ref.shape[1]), BF16)
        out_ref[cap:, :cap] = codes[:, block].astype(BF16)


def pack_next_body(cap, dom, meta, place_ref, *refs):
    raw, outs, pick = refs[: -dom - 1], refs[-dom - 1 : -1], refs[-1]
    one_hot_rows(pick, place_ref[...])
    packed = mm(pick[...], joined(raw), NN).astype(BF16)
    for index, out_ref in enumerate(outs):
        out_ref[...] = packed[index * cap : (index + 1) * cap]


def raw_specs(hold, share, chunk):
    first, width = chunk
    at = lambda k: lambda j, m: (0, m[1] * (share // LANES) + first // LANES + k)
    return [pl.BlockSpec((hold, LANES), at(k)) for k in range(width // LANES)]


def pack_first(meta, raw_images, slot, bins, dom, share, chunk):
    hold, _ = raw_images.shape
    width = chunk[1]
    cap = hold // dom
    slots = dom * cap
    specs = raw_specs(hold, share, chunk)
    return call(
        functools.partial(pack_first_body, dom, hold // 2, cap, bins),
        (1,),
        [pl.BlockSpec((hold,), lambda j, m: (0,))] + specs,
        [pl.BlockSpec((cap + CODE, width), lambda j, m: (0, 0))] * dom
        + [pl.BlockSpec((1, hold), lambda j, m: (0, 0))],
        [sds((cap + CODE, width), BF16)] * dom + [sds((1, hold), I32)],
        scratch=[pltpu.VMEM((slots, hold), BF16)],
        room=51,
        flops=2 * slots * hold * width,
        moved=4 * hold * width,
    )(meta, slot, *[raw_images] * len(specs))


def pack_next(meta, raw_images, place, dom, share, chunk):
    hold, _ = raw_images.shape
    width = chunk[1]
    cap = hold // dom
    slots = dom * cap
    specs = raw_specs(hold, share, chunk)
    return call(
        functools.partial(pack_next_body, cap, dom),
        (1,),
        [pl.BlockSpec((1, hold), lambda j, m: (0, 0))] + specs,
        [pl.BlockSpec((cap, width), lambda j, m: (0, 0))] * dom,
        [sds((cap, width), BF16)] * dom,
        scratch=[pltpu.VMEM((slots, hold), BF16)],
        room=51,
        flops=2 * slots * hold * width,
        moved=4 * hold * width,
    )(meta, place, *[raw_images] * len(specs))


def weigh(first, share, pick, wide, recv, meta, ctf_ref, inv_ref, out_ref):
    width = out_ref.shape[1]
    start = lax.rem(meta[1] * share, ctf_ref.shape[1]) + first
    columns = pl.ds(pl.multiple_of(start, LANES), width)
    table = jnp.concatenate(split3(ctf_ref[:, columns] * inv_ref[:, columns]), axis=0)
    out_ref[...] = (mm(pick, recv, NN) * mm(wide, table, NN)).astype(BF16)


def gather(pieces, whole, rows):
    for index, piece in enumerate(pieces):
        whole[index * rows : (index + 1) * rows, :] = piece[:rows, :]


def unpack_first_body(dom, bins, share, first, meta, *refs):
    pieces, recv_ref = refs[:dom], refs[-1]
    cap = pieces[0].shape[0] - CODE
    gather(pieces, recv_ref, cap)
    ctf_ref, inv_ref, out_ref, hot_ref, pick, wide = refs[dom:-1]
    shard_rows = out_ref.shape[0]
    got = jnp.concatenate([piece[cap:, :cap].astype(F32) for piece in pieces], axis=1)
    row = got[0:1] * 16.0 + got[1:2] + got[3:4] * 1024.0 - 1024.0
    one_hot_rows(pick, row.astype(I32))
    slot_bins = jnp.broadcast_to(got[2:3].astype(BF16), (8, got.shape[1]))
    down = mm(pick[...], slot_bins, NT)[:, 0:1].astype(I32)
    across = mm(slot_bins, pick[...], NT)[0:1].astype(I32)
    lane = lax.broadcasted_iota(I32, (shard_rows, 3 * bins), 1)
    wide[...] = jnp.where((lane & (bins - 1)) == down, 1.0, 0.0).astype(BF16)
    deep = lax.broadcasted_iota(I32, (3 * bins, shard_rows), 0)
    hot_ref[...] = jnp.where((deep & (bins - 1)) == across, 1.0, 0.0).astype(BF16)
    weigh(first, share, pick[...], wide[...], recv_ref[...], meta, ctf_ref, inv_ref, out_ref)


def unpack_next_body(dom, share, first, meta, *refs):
    recv_ref = refs[-1]
    gather(refs[:dom], recv_ref, refs[0].shape[0])
    pick_ref, wide_ref, ctf_ref, inv_ref, out_ref = refs[dom:-1]
    weigh(first, share, pick_ref[...], wide_ref[...], recv_ref[...], meta, ctf_ref, inv_ref, out_ref)


def unpack_first(meta, recv, ctf, inv, share, chunk):
    first, width = chunk
    dom = len(recv)
    slots = dom * (recv[0].shape[0] - CODE)
    rows = slots // 2
    bins, pix = ctf.shape
    whole = lambda shape: pl.BlockSpec(shape, lambda j, m: (0, 0))
    shapes = [(rows, width), (3 * bins, rows), (rows, slots), (rows, 3 * bins)]
    return call(
        functools.partial(unpack_first_body, dom, bins, share, first),
        (1,),
        [whole(recv[0].shape)] * dom + [whole(ctf.shape), whole(inv.shape)],
        [whole(s) for s in shapes],
        [sds(s, BF16) for s in shapes],
        scratch=[pltpu.VMEM((slots, width), BF16)],
        room=28,
        flops=2 * slots * rows * width,
        moved=2 * slots * width,
    )(meta, *recv, ctf, inv)


def unpack_next(meta, pick, wide, recv, ctf, inv, share, chunk):
    first, width = chunk
    dom = len(recv)
    slots = dom * recv[0].shape[0]
    rows = slots // 2
    whole = lambda shape: pl.BlockSpec(shape, lambda j, m: (0, 0))
    return call(
        functools.partial(unpack_next_body, dom, share, first),
        (1,),
        [whole(recv[0].shape)] * dom
        + [whole(pick.shape), whole(wide.shape), whole(ctf.shape), whole(inv.shape)],
        whole((rows, width)),
        sds((rows, width), BF16),
        scratch=[pltpu.VMEM((slots, width), BF16)],
        room=28,
        flops=2 * slots * rows * width,
        moved=2 * slots * width,
    )(meta, *recv, pick, wide, ctf, inv)


def energy_body(bins, count, meta, *refs):
    pieces, (ctf_ref, inv_ref, panel_ref, extra_ref, total) = refs[:-5], refs[-5:]
    width = panel_ref.shape[1]
    blocks = []
    for piece in pieces:
        for start in range(0, piece.shape[1], width):
            blocks.append((piece, start))
    step = pl.program_id(0)

    @pl.when(step == 0)
    def _():
        total[...] = jnp.zeros_like(total)

    gain = ctf_ref[...] * ctf_ref[...] * inv_ref[...]
    gain3 = jnp.concatenate(split3(gain), axis=0)
    for index, (piece, start) in enumerate(blocks):

        @pl.when(step == index)
        def _():
            panel = piece[:, start : start + width]
            panel_ref[...] = panel
            wide = panel.astype(F32)
            square = wide * wide
            high = square.astype(BF16)
            low = (square - high.astype(F32)).astype(BF16)
            total[...] += mm(high, gain3, NT) + mm(low, gain3, NT)

    @pl.when(step == count - 1)
    def _():
        whole = total[:, :bins] + total[:, bins : 2 * bins] + total[:, 2 * bins :]
        extra_ref[...] = jnp.concatenate(split3(-0.5 * whole), axis=1)


def energy(meta, pieces, ctf, inv):
    rows, width = pieces[-1].shape
    count = sum(piece.shape[1] for piece in pieces) // width
    bins, pix = ctf.shape
    wrap = pix // width
    return call(
        functools.partial(energy_body, bins, count),
        (count,),
        [pl.BlockSpec(piece.shape, lambda j, m: (0, 0)) for piece in pieces]
        + [
            pl.BlockSpec((bins, width), lambda j, m: (0, lax.rem(m[0] ^ j, wrap))),
            pl.BlockSpec((1, width), lambda j, m: (0, lax.rem(m[0] ^ j, wrap))),
        ],
        [
            pl.BlockSpec((rows, width), lambda j, m: (0, m[0] ^ j)),
            pl.BlockSpec((rows, 3 * bins), lambda j, m: (0, 0)),
        ],
        [sds((rows, count * width), BF16), sds((rows, 3 * bins), BF16)],
        scratch=[pltpu.VMEM((rows, 3 * bins), F32)],
        flops=2 * 4 * rows * bins * count * width * 3,
        moved=4 * rows * count * width,
    )(meta, *pieces, ctf, inv)


def score_body(parts, used, first, last, meta, *refs):
    own, sib, panel_ref, refs = (
        refs[:parts],
        refs[parts : 2 * parts],
        refs[2 * parts],
        refs[2 * parts + 1 :],
    )
    if first:
        acc_out, full_ref = refs
    elif last:
        acc_ref, _, hot_own, hot_sib, extra_ref, shifted_ref, stat_ref, full_ref = refs
    elif used is None:
        acc_ref, _, acc_out, full_ref = refs
    else:
        acc_ref, acc_out = refs
    half = pl.num_programs(0) // 2

    def tile(sources, hot):
        block = jnp.concatenate([source[...] for source in sources], axis=1)
        if used is None or last:
            full_ref[...] = block
        if last:
            block = block[:, used[0] : used[0] + used[1]]
        panel = panel_ref[...] if used is None else panel_ref[:, used[0] : used[0] + used[1]]
        total = mm(panel, block, NT)
        if not first:
            total = acc_ref[...] + total
        if not last:
            acc_out[...] = total
            return
        total = total + mm(extra_ref[...], hot[...], NN)
        peak = jnp.max(total, axis=0, keepdims=True)
        shifted = jnp.exp(total - peak)
        shifted_ref[...] = shifted
        mass = jnp.sum(shifted, axis=0, keepdims=True)
        which = lax.broadcasted_iota(I32, stat_ref.shape, 0)
        stat_ref[...] = jnp.where(which == 0, peak, mass)

    @pl.when(pl.program_id(0) < half)
    def _():
        tile(own, hot_own if last else None)

    @pl.when(pl.program_id(0) >= half)
    def _():
        tile(sib, hot_sib if last else None)


def score(meta, at, own, sib, panels, width, acc=None, full=None, hots=None, extra=None, used=None):
    rows = own[0].shape[0]
    parts = len(own)
    tile = 256
    half = rows // tile
    count, columns = panels.shape
    first, last = acc is None, hots is not None
    store = used is None or last
    fronts = [pl.BlockSpec((tile, v.shape[1]), lambda j, m: (jnp.minimum(j, half - 1), 0)) for v in own]
    backs = [pl.BlockSpec((tile, v.shape[1]), lambda j, m: (jnp.maximum(j - half, 0), 0)) for v in own]
    acc_spec = pl.BlockSpec((count, tile), lambda j, m: (0, j))
    full_spec = pl.BlockSpec((tile, width), lambda j, m: (j, at(m)))
    in_specs = fronts + backs + [pl.BlockSpec((count, width), lambda j, m: (0, at(m)))]
    operands = [meta, *own, *sib, panels]
    alias = {}
    if not first:
        in_specs += [acc_spec]
        alias = {len(operands): 0}
        operands += [acc]
        if store:
            in_specs += [pl.BlockSpec(memory_space=pl.ANY)]
            alias[len(operands)] = 2 if last else 1
            operands += [full]
    full_shape = sds((2 * rows, columns), BF16)
    acc_shape = sds((count, 2 * rows), F32)
    out_specs, out_shape = [acc_spec, full_spec], [acc_shape, full_shape]
    if last:
        depth = extra.shape[1]
        in_specs += [
            pl.BlockSpec((depth, tile), lambda j, m: (0, jnp.minimum(j, half - 1))),
            pl.BlockSpec((depth, tile), lambda j, m: (0, jnp.maximum(j - half, 0))),
            pl.BlockSpec((count, depth), lambda j, m: (0, 0)),
        ]
        operands += [*hots, extra]
        out_specs = [acc_spec, pl.BlockSpec((8, tile), lambda j, m: (0, j)), full_spec]
        out_shape = [acc_shape, sds((8, 2 * rows), F32), full_shape]
    elif not store:
        out_specs, out_shape = acc_spec, acc_shape
    return call(
        functools.partial(score_body, parts, used, first, last),
        (2 * half,),
        in_specs,
        out_specs,
        out_shape,
        alias=alias,
        room=16,
        flops=2 * count * 2 * rows * width,
        moved=8 * count * 2 * rows + 8 * rows * width,
    )(*operands)


def merge_body(meta, mine_ref, other_ref, out_ref):
    rows = mine_ref.shape[1] // 2
    other = other_ref[...]
    other = jnp.concatenate([other[:, rows:], other[:, :rows]], axis=1)
    mine = mine_ref[...]
    peak = jnp.maximum(mine[0:1], other[0:1])
    mass = mine[1:2] * jnp.exp(mine[0:1] - peak) + other[1:2] * jnp.exp(other[0:1] - peak)
    which = lax.broadcasted_iota(I32, out_ref.shape, 0)
    out_ref[...] = jnp.where(which == 0, peak, mass)


def add_body(meta, mine_ref, other_ref, out_ref):
    out_ref[...] = (mine_ref[...].astype(F32) + other_ref[...].astype(F32)).astype(BF16)


def pairwise(body, meta, mine, other):
    spec = pl.BlockSpec(mine.shape, lambda j, m: (0, 0))
    return call(body, (1,), [spec, spec], spec, sds(mine.shape, mine.dtype), room=4)(
        meta, mine, other
    )


merge = functools.partial(pairwise, merge_body)
add_pair = functools.partial(pairwise, add_body)


def class_body(kind, steps, meta, *refs):
    if kind == "first":
        (shifted_ref, stat_ref), four = refs[:2], refs[2:6]
        hot_own, hot_sib, full_ref = refs[6:9]
        outs, (post_ref, log_ref, mass_ref) = refs[9 : 9 + steps], refs[9 + steps :]

        @pl.when(pl.program_id(0) == 0)
        def _():
            stats = [ref[...] for ref in four]
            peaks = [s[0:1] for s in stats]
            peak = jnp.maximum(jnp.maximum(peaks[0], peaks[1]), jnp.maximum(peaks[2], peaks[3]))
            parts = [s[1:2] * jnp.exp(p - peak) for s, p in zip(stats, peaks)]
            mass = (parts[0] + parts[1]) + (parts[2] + parts[3])
            factor = jnp.exp(stat_ref[0:1] - peak) / mass
            post_ref[...] = (shifted_ref[...] * factor).astype(BF16)
            log_ref[...] = (peak + jnp.log(mass))[:, : log_ref.shape[1]]
            bins, rows = mass_ref.shape[0], hot_own.shape[1]
            weights = mm(hot_own[:bins, :], post_ref[:, :rows], NT)
            weights = weights + mm(hot_sib[:bins, :], post_ref[:, rows:], NT)
            mass_ref[...] = weights.astype(BF16)

    else:
        (post_ref, full_ref), outs = refs[:2], refs[2:]
    for step, out_ref in enumerate(outs):

        @pl.when(pl.program_id(0) == step)
        def _():
            out_ref[...] = mm(post_ref[...], full_ref[...], NN).astype(out_ref.dtype)


def class_part(meta, kind, offset, steps, full, post=None, shifted=None, stats=None, hots=None, bins=0):
    rows, columns = full.shape
    width = columns // 8
    count = (shifted if post is None else post).shape[0]
    whole = lambda shape: pl.BlockSpec(shape, lambda j, m: (0, 0))
    full_spec = pl.BlockSpec((rows, width), lambda j, m: (0, m[offset + j]))
    out_specs = [whole((count, width))] * steps
    kept = steps // 2 if kind == "rest" else 0
    types = [BF16] * (steps - kept) + [F32] * kept
    out_shape = [sds((count, width), dtype) for dtype in types]
    if kind == "first":
        operands = [shifted, *stats, *hots, full]
        in_specs = [whole(shifted.shape)] + [whole(stats[0].shape)] * 5
        in_specs += [whole(hots[0].shape)] * 2 + [full_spec]
        out_specs += [whole((count, rows)), whole((1, rows // 2)), whole((bins, count))]
        out_shape += [sds((count, rows), BF16), sds((1, rows // 2), F32), sds((bins, count), BF16)]
    else:
        operands = [post, full]
        in_specs = [whole(post.shape), full_spec]
    return call(
        functools.partial(class_body, kind, steps),
        (steps,),
        in_specs,
        out_specs,
        out_shape,
        room=22 if kind == "first" else 28,
        flops=2 * count * rows * width * steps,
        moved=2 * rows * width * steps + 4 * count * (rows + width * steps),
    )(meta, *operands)


def own_half_body(tile, meta, keep_ref, c_ref, a_ref, out_ref):
    rows = pl.ds(pl.multiple_of(pl.program_id(0) * tile, tile), tile)
    out_ref[...] = keep_ref[rows, :] + c_ref[rows, :].astype(F32) + a_ref[rows, :].astype(F32)


def own_half(meta, keep, got_c, got_a):
    count, width = keep.shape
    parts = 3
    tile = count // parts
    return call(
        functools.partial(own_half_body, tile),
        (parts,),
        [pl.BlockSpec(memory_space=pltpu.VMEM)] * 3,
        pl.BlockSpec((tile, width), lambda j, m: (lax.rem(m[0], 2) * parts + j, 0)),
        sds((2 * count, width), F32),
        room=8,
    )(meta, keep, got_c, got_a)


def two_by_two(raw_images, defocus_bin, dest_row, ctf_table, inv_noise, panels):
    dom, turns = lax.axis_size("dom"), lax.axis_size("rot")
    device, plane = lax.axis_index("dom"), lax.axis_index("rot")
    bins = ctf_table.shape[0]
    columns = raw_images.shape[1]
    chip, core = device // 2, device % 2

    def block(apart, half):
        return (chip ^ apart) * 2 + half

    x_first, y_second = block(1, 0), block(2, 1)
    x_second, y_first = block(1, 1), block(2, 0)
    even = core == 0
    order = [
        device,
        plane,
        block(3, 0),
        block(3, 1),
        jnp.where(even, x_first, y_second),
        jnp.where(even, y_second, x_first),
        block(0, 1 - core),
        jnp.where(even, y_first, x_second),
        jnp.where(even, x_second, y_first),
        block(0, core),
    ]
    meta = jnp.stack(order).astype(I32)
    inv = inv_noise[None, :]

    def across(value, apart):
        return lax.ppermute(value, "dom", [(i, i ^ apart) for i in range(dom)])

    def by_core(value, when_even, when_odd):
        pairs = [(i, i ^ (when_odd if i % 2 else when_even)) for i in range(dom)]
        return lax.ppermute(value, "dom", pairs)

    def onward(value):
        return lax.ppermute(value, "rot", [(i, (i + 1) % turns) for i in range(turns)])

    width = columns // turns
    cut = width * 3 // 8
    chunk_a, chunk_b = (0, cut), (cut, width - cut)

    def exchange(blocks):
        far_first = [across(blocks[apart], apart) for apart in (6, 7, 4, 2, 5, 3, 1)]
        return far_first + [blocks[0]]

    slot = jnp.where(dest_row >= 0, dest_row * bins + defocus_bin, -1)
    *send_a, place = pack_first(meta, raw_images, slot, bins, dom, width, chunk_a)
    recv_a = exchange(send_a)
    swapped, place = lax.optimization_barrier((across(panels, 1), place))
    send_b = pack_next(meta, raw_images, place, dom, width, chunk_b)
    together = lax.optimization_barrier

    count = panels.shape[0] // 2
    mine = lax.dynamic_slice_in_dim(panels, core * count, count, 0)
    other = lax.dynamic_slice_in_dim(swapped, core * count, count, 0)
    near = jnp.concatenate([mine, other], axis=1)

    recv_a, send_b, near = together((recv_a, send_b, near))
    share_a, hot, pick, wide = unpack_first(meta, recv_a, ctf_table, inv, width, chunk_a)
    share_a, send_b = together((share_a, send_b))
    a1, recv_b = onward(share_a), exchange(send_b)
    a1, recv_b[:2] = together((a1, recv_b[:2]))
    a2 = onward(a1)
    share_b = unpack_next(meta, pick, wide, recv_b, ctf_table, inv, width, chunk_b)
    a2, share_b, near = together((a2, share_b, near))
    by_x, by_y = across(near, 2), across(near, 4)
    a3, b1 = onward(a2), onward(share_b)
    sib0, hots = [across(share_a, 1), across(share_b, 1)], [hot, across(hot, 1)]
    sib1, sib2 = [across(a1, 1), across(b1, 1)], [across(a2, 1)]
    piece = near.shape[1] // 2
    far_y, far_x = across(by_x[:, :piece], 4), across(by_y[:, piece:], 2)
    b2 = onward(b1)
    panel_full, extra = energy(meta, [near, by_x, by_y, far_y, far_x], ctf_table, inv)
    a3, b2, panel_full, hots = together((a3, b2, panel_full, hots))
    b3 = onward(b2)
    sib2 = sib2 + [across(b2, 1)]

    def share(turn):
        return lambda m: lax.rem(m[1] + turns - turn, turns)

    acc, full = score(meta, share(0), [share_a, share_b], sib0, panel_full, width)
    acc, full = score(meta, share(1), [a1, b1], sib1, panel_full, width, acc, full)
    acc, full = score(meta, share(2), [a2, b2], sib2, panel_full, width, acc, full)
    final = share(turns - 1)
    a3_sib = across(a3, 1)
    acc = score(meta, final, [a3], [a3_sib], panel_full, width, acc, used=chunk_a)
    b3, acc = together((b3, acc))
    shifted, stat, full = score(
        meta,
        final,
        [a3, b3],
        [a3_sib, across(b3, 1)],
        panel_full,
        width,
        acc,
        full,
        hots,
        extra,
        chunk_b,
    )

    pair = merge(meta, stat, across(stat, 1))
    others = [
        lax.ppermute(pair, "rot", [(i, i ^ apart) for i in range(turns)]) for apart in (1, 2, 3)
    ]
    to_x, to_y, post, log_evidence, mass = class_part(
        meta, "first", 2, 2, full, None, shifted, [stat, pair, *others], hots, bins
    )
    mass_x = across(mass, 2)
    got_x, got_y = across(to_x, 2), across(to_y, 4)
    six = class_part(meta, "rest", 4, 6, full, post)
    got_x, got_y, six, mass_x = together((got_x, got_y, six, mass_x))
    send_c, send_d, give, a_sum, b_sum, keep = six
    mass = add_pair(meta, mass, mass_x)
    mass_y = across(mass, 4)
    got_c, got_d = by_core(send_c, 2, 4), by_core(send_d, 5, 3)
    down, left = got_x.astype(F32), got_y.astype(F32)
    message_a = (a_sum + jnp.where(even, down, left)).astype(BF16)
    message_b = (b_sum + jnp.where(even, left, down)).astype(BF16)
    got_a, got_b = by_core(message_a, 4, 2), by_core(message_b, 3, 5)
    got_self = across(give, 1)
    mass_y, got_a, got_c = together((mass_y, got_a, got_c))
    mass = mass.astype(F32) + mass_y.astype(F32)
    mass_other = across(mass, 1)
    bin_weights = jnp.where(
        even,
        jnp.concatenate([mass, mass_other], axis=1),
        jnp.concatenate([mass_other, mass], axis=1),
    )
    sums = own_half(meta, keep, got_c, got_a)
    bin_weights, got_b = together((bin_weights, got_b))
    other_half = got_self.astype(F32) + got_d.astype(F32) + got_b.astype(F32)
    class_sums = lax.dynamic_update_slice_in_dim(sums, other_half, (1 - core) * count, 0).T
    return class_sums, bin_weights, log_evidence.reshape(-1)


def energy_block(gain_block, panel_piece):
    widened = panel_piece.astype(jnp.float32)
    return lax.dot_general(
        gain_block, widened * widened, (((1,), (1,)), ((), ())), precision=lax.Precision.HIGHEST
    )


def on_device(raw_images, defocus_bin, dest_row, ctf_table, inv_noise, panels):
    dom_count = lax.axis_size("dom")
    bin_count = ctf_table.shape[0]
    columns = raw_images.shape[1]
    hold_rows = raw_images.shape[0]
    shard_rows = hold_rows // 2
    capacity = 2 * shard_rows // dom_count
    is_live = dest_row >= 0
    target = jnp.where(is_live, dest_row // shard_rows, dom_count)
    local_row = dest_row % shard_rows
    marks = (target[:, None] == jnp.arange(dom_count, dtype=jnp.int32)[None, :]).astype(jnp.int32)
    slot_rank = jnp.sum((jnp.cumsum(marks, axis=0) - marks) * marks, axis=1)
    row_code = jnp.where(is_live, local_row * bin_count + defocus_bin, -1)
    padded_images = jnp.concatenate([raw_images, jnp.zeros((1, columns), raw_images.dtype)], axis=0)
    padded_code = jnp.concatenate([row_code, jnp.full((1,), -1, jnp.int32)], axis=0)
    position = jnp.where(is_live, target * capacity + slot_rank, dom_count * capacity)
    slot_count = dom_count * capacity
    source = (
        jnp.full((slot_count,), hold_rows, jnp.int32)
        .at[position]
        .set(jnp.arange(hold_rows, dtype=jnp.int32), mode="drop")
    )
    send_images = padded_images[source].reshape(dom_count, capacity, columns)
    send_code = padded_code[source].reshape(dom_count, capacity)
    recv_images, recv_code = (
        lax.all_to_all(send_images, "dom", split_axis=0, concat_axis=0, tiled=True),
        lax.all_to_all(send_code, "dom", split_axis=0, concat_axis=0, tiled=True),
    )
    flat_images = recv_images.reshape(-1, columns)
    flat_code = recv_code.reshape(-1)
    arrived = flat_code >= 0
    row_of = jnp.where(arrived, flat_code // bin_count, shard_rows)
    row_order = (
        jnp.zeros((shard_rows,), jnp.int32)
        .at[row_of]
        .set(jnp.arange(flat_code.shape[0], dtype=jnp.int32), mode="drop")
    )
    images = flat_images[row_order]
    bin_ids = flat_code[row_order] % bin_count
    bin_table = (bin_ids[:, None] == jnp.arange(bin_count, dtype=jnp.int32)[None, :]).astype(
        jnp.float32
    )
    ctf_rows = jnp.dot(bin_table, ctf_table, precision=lax.Precision.HIGHEST)
    factor = ctf_rows * inv_noise[None, :]
    weighted = (images.astype(jnp.float32) * jnp.concatenate([factor, factor], axis=1)).astype(
        jnp.bfloat16
    )
    gain_half = ctf_table * ctf_table * inv_noise[None, :]
    gain_full = jnp.concatenate([gain_half, gain_half], axis=1)
    panel_piece = lax.all_gather(panels, "dom", axis=1, tiled=True)
    col_block = weighted
    cross_term = lax.dot_general(
        col_block, panel_piece, (((1,), (1,)), ((), ())), preferred_element_type=jnp.float32
    )
    energy = energy_block(gain_full, panel_piece)
    scores = cross_term - 0.5 * jnp.dot(bin_table, energy, precision=lax.Precision.HIGHEST)
    local_peak = jnp.max(scores, axis=1)
    row_peak = lax.pmax(local_peak, "rot")
    shifted = jnp.exp(scores - row_peak[:, None])
    row_total = lax.psum(jnp.sum(shifted, axis=1), "rot")
    posterior = (shifted / row_total[:, None]).astype(jnp.bfloat16)
    log_evidence = row_peak + jnp.log(row_total)
    col_block = weighted
    class_sums = lax.psum_scatter(
        lax.dot_general(
            col_block, posterior, (((0,), (0,)), ((), ())), preferred_element_type=jnp.float32
        ).astype(jnp.bfloat16),
        "dom",
        scatter_dimension=0,
        tiled=True,
    ).astype(jnp.float32)
    local_mass = lax.dot_general(
        bin_table.astype(jnp.bfloat16),
        posterior,
        (((0,), (0,)), ((), ())),
        preferred_element_type=jnp.float32,
    )
    bin_weights = lax.psum(local_mass.astype(jnp.bfloat16), "dom").astype(jnp.float32)
    return (class_sums, bin_weights, log_evidence)


def solution(mesh):
    small = mesh.shape["dom"] == 8 and mesh.shape["rot"] == 4
    return jax.shard_map(
        two_by_two if small else on_device,
        mesh=mesh,
        in_specs=(P("dom", None), P("dom"), P("dom"), P(), P(), P("rot", "dom")),
        out_specs=(P("dom", "rot"), P(None, "rot"), P("dom")),
        check_vma=False,
    )
```

```python
import functools

import jax
import jax.numpy as jnp
from jax import lax
from jax.experimental import pallas as pl
from jax.experimental.pallas import tpu as pltpu
from jax.sharding import PartitionSpec as P

NN = (((1,), (0,)), ((), ()))
NT = (((1,), (1,)), ((), ()))
F32, BF16, I32 = jnp.float32, jnp.bfloat16, jnp.int32
CODE = 16
LANES = 128
MIB = 1024 * 1024


def mm(a, b, dims):
    return lax.dot_general(a, b, dims, preferred_element_type=F32)


def split3(x):
    hi = x.astype(BF16)
    rest = x - hi.astype(F32)
    mid = rest.astype(BF16)
    low = (rest - mid.astype(F32)).astype(BF16)
    return hi, mid, low


def call(body, grid, in_specs, out_specs, out_shape, scratch=(), alias=None, flops=0, moved=0, room=24):
    return pl.pallas_call(
        body,
        grid_spec=pltpu.PrefetchScalarGridSpec(
            num_scalar_prefetch=1,
            grid=grid,
            in_specs=in_specs,
            out_specs=out_specs,
            scratch_shapes=list(scratch),
        ),
        out_shape=out_shape,
        input_output_aliases=alias or {},
        compiler_params=pltpu.CompilerParams(vmem_limit_bytes=room * MIB),
        cost_estimate=pl.CostEstimate(
            flops=flops // 16, bytes_accessed=moved // 16, transcendentals=0
        ),
    )


def sds(shape, dtype):
    return jax.ShapeDtypeStruct(shape, dtype)


def one_hot_rows(out_ref, wanted):
    rows, width = out_ref.shape
    short = wanted.astype(jnp.int16)
    one, zero = jnp.ones((), BF16), jnp.zeros((), BF16)
    step = 256 if rows % 256 == 0 else rows
    for start in range(0, rows, step):
        index = lax.broadcasted_iota(jnp.int16, (step, width), 0) + jnp.int16(start)
        out_ref[start : start + step, :] = jnp.where(index == short, one, zero)


def places_of(dest, shard_rows, cap, dom, device):
    hold = dest.shape[1]
    low = lax.broadcasted_iota(I32, (dom, hold), 0) * shard_rows
    inside = jnp.logical_and(dest >= low, dest < low + shard_rows)
    marks = jnp.where(inside, 1.0, 0.0)
    local = dest - jnp.sum(jnp.where(inside, low, 0), axis=0, keepdims=True)
    lanes = 128
    before = lax.broadcasted_iota(I32, (lanes, lanes), 0) < lax.broadcasted_iota(
        I32, (lanes, lanes), 1
    )
    upper = jnp.where(before, 1.0, 0.0).astype(BF16)
    apart = lax.broadcasted_iota(I32, (dom, 1), 0) ^ device
    carry = apart.astype(F32) * cap + 1.0
    found = []
    for start in range(0, hold, lanes):
        part = marks[:, start : start + lanes]
        rank = mm(part.astype(BF16), upper, NN) + carry
        found.append(jnp.sum(jnp.where(part > 0, rank, 0.0), axis=0, keepdims=True))
        carry = carry + jnp.sum(part, axis=1, keepdims=True)
    return jnp.concatenate(found, axis=1).astype(I32) - 1, local


def joined(refs):
    return jnp.concatenate([ref[...] for ref in refs], axis=1)


def pack_first_body(dom, shard_rows, cap, bins, meta, slot_ref, *refs):
    raw, outs, (place_ref, pick) = refs[: -dom - 2], refs[-dom - 2 : -2], refs[-2:]
    slot = slot_ref[...].reshape(1, slot_ref.shape[0])
    dest, slot_bin = slot >> (bins.bit_length() - 1), slot & (bins - 1)
    place, local = places_of(dest, shard_rows, cap, dom, meta[0])
    place_ref[...] = place
    one_hot_rows(pick, place)
    which = lax.broadcasted_iota(I32, (CODE, dest.shape[1]), 0)
    digits = jnp.where(
        which == 0,
        local >> 4,
        jnp.where(which == 1, local & 15, jnp.where(which == 2, slot_bin, jnp.where(which == 3, 1, 0))),
    )
    digits = jnp.where(dest >= 0, digits, 0).astype(F32).astype(BF16)
    codes = mm(digits, pick[...], NT)
    packed = mm(pick[...], joined(raw), NN).astype(BF16)
    for index, out_ref in enumerate(outs):
        block = slice(index * cap, (index + 1) * cap)
        out_ref[:cap, :] = packed[block]
        out_ref[cap:, :] = jnp.zeros((CODE, out_ref.shape[1]), BF16)
        out_ref[cap:, :cap] = codes[:, block].astype(BF16)


def pack_next_body(cap, dom, meta, place_ref, *refs):
    raw, outs, pick = refs[: -dom - 1], refs[-dom - 1 : -1], refs[-1]
    one_hot_rows(pick, place_ref[...])
    packed = mm(pick[...], joined(raw), NN).astype(BF16)
    for index, out_ref in enumerate(outs):
        out_ref[...] = packed[index * cap : (index + 1) * cap]


def raw_specs(hold, share, chunk):
    first, width = chunk
    at = lambda k: lambda j, m: (0, m[1] * (share // LANES) + first // LANES + k)
    return [pl.BlockSpec((hold, LANES), at(k)) for k in range(width // LANES)]


def pack_first(meta, raw_images, slot, bins, dom, share, chunk):
    hold, _ = raw_images.shape
    width = chunk[1]
    cap = hold // dom
    slots = dom * cap
    specs = raw_specs(hold, share, chunk)
    return call(
        functools.partial(pack_first_body, dom, hold // 2, cap, bins),
        (1,),
        [pl.BlockSpec((hold,), lambda j, m: (0,))] + specs,
        [pl.BlockSpec((cap + CODE, width), lambda j, m: (0, 0))] * dom
        + [pl.BlockSpec((1, hold), lambda j, m: (0, 0))],
        [sds((cap + CODE, width), BF16)] * dom + [sds((1, hold), I32)],
        scratch=[pltpu.VMEM((slots, hold), BF16)],
        room=51,
        flops=2 * slots * hold * width,
        moved=4 * hold * width,
    )(meta, slot, *[raw_images] * len(specs))


def pack_next(meta, raw_images, place, dom, share, chunk):
    hold, _ = raw_images.shape
    width = chunk[1]
    cap = hold // dom
    slots = dom * cap
    specs = raw_specs(hold, share, chunk)
    return call(
        functools.partial(pack_next_body, cap, dom),
        (1,),
        [pl.BlockSpec((1, hold), lambda j, m: (0, 0))] + specs,
        [pl.BlockSpec((cap, width), lambda j, m: (0, 0))] * dom,
        [sds((cap, width), BF16)] * dom,
        scratch=[pltpu.VMEM((slots, hold), BF16)],
        room=51,
        flops=2 * slots * hold * width,
        moved=4 * hold * width,
    )(meta, place, *[raw_images] * len(specs))


def weigh(first, share, pick, wide, recv, meta, ctf_ref, inv_ref, out_ref):
    width = out_ref.shape[1]
    start = lax.rem(meta[1] * share, ctf_ref.shape[1]) + first
    columns = pl.ds(pl.multiple_of(start, LANES), width)
    table = jnp.concatenate(split3(ctf_ref[:, columns] * inv_ref[:, columns]), axis=0)
    out_ref[...] = (mm(pick, recv, NN) * mm(wide, table, NN)).astype(BF16)


def gather(pieces, whole, rows):
    for index, piece in enumerate(pieces):
        whole[index * rows : (index + 1) * rows, :] = piece[:rows, :]


def unpack_first_body(dom, bins, share, first, meta, *refs):
    pieces, recv_ref = refs[:dom], refs[-1]
    cap = pieces[0].shape[0] - CODE
    gather(pieces, recv_ref, cap)
    ctf_ref, inv_ref, out_ref, hot_ref, pick, wide = refs[dom:-1]
    shard_rows = out_ref.shape[0]
    got = jnp.concatenate([piece[cap:, :cap].astype(F32) for piece in pieces], axis=1)
    row = got[0:1] * 16.0 + got[1:2] + got[3:4] * 1024.0 - 1024.0
    one_hot_rows(pick, row.astype(I32))
    slot_bins = jnp.broadcast_to(got[2:3].astype(BF16), (8, got.shape[1]))
    down = mm(pick[...], slot_bins, NT)[:, 0:1].astype(I32)
    across = mm(slot_bins, pick[...], NT)[0:1].astype(I32)
    lane = lax.broadcasted_iota(I32, (shard_rows, 3 * bins), 1)
    wide[...] = jnp.where((lane & (bins - 1)) == down, 1.0, 0.0).astype(BF16)
    deep = lax.broadcasted_iota(I32, (3 * bins, shard_rows), 0)
    hot_ref[...] = jnp.where((deep & (bins - 1)) == across, 1.0, 0.0).astype(BF16)
    weigh(first, share, pick[...], wide[...], recv_ref[...], meta, ctf_ref, inv_ref, out_ref)


def unpack_next_body(dom, share, first, meta, *refs):
    recv_ref = refs[-1]
    gather(refs[:dom], recv_ref, refs[0].shape[0])
    pick_ref, wide_ref, ctf_ref, inv_ref, out_ref = refs[dom:-1]
    weigh(first, share, pick_ref[...], wide_ref[...], recv_ref[...], meta, ctf_ref, inv_ref, out_ref)


def unpack_first(meta, recv, ctf, inv, share, chunk):
    first, width = chunk
    dom = len(recv)
    slots = dom * (recv[0].shape[0] - CODE)
    rows = slots // 2
    bins, pix = ctf.shape
    whole = lambda shape: pl.BlockSpec(shape, lambda j, m: (0, 0))
    shapes = [(rows, width), (3 * bins, rows), (rows, slots), (rows, 3 * bins)]
    return call(
        functools.partial(unpack_first_body, dom, bins, share, first),
        (1,),
        [whole(recv[0].shape)] * dom + [whole(ctf.shape), whole(inv.shape)],
        [whole(s) for s in shapes],
        [sds(s, BF16) for s in shapes],
        scratch=[pltpu.VMEM((slots, width), BF16)],
        room=28,
        flops=2 * slots * rows * width,
        moved=2 * slots * width,
    )(meta, *recv, ctf, inv)


def unpack_next(meta, pick, wide, recv, ctf, inv, share, chunk):
    first, width = chunk
    dom = len(recv)
    slots = dom * recv[0].shape[0]
    rows = slots // 2
    whole = lambda shape: pl.BlockSpec(shape, lambda j, m: (0, 0))
    return call(
        functools.partial(unpack_next_body, dom, share, first),
        (1,),
        [whole(recv[0].shape)] * dom
        + [whole(pick.shape), whole(wide.shape), whole(ctf.shape), whole(inv.shape)],
        whole((rows, width)),
        sds((rows, width), BF16),
        scratch=[pltpu.VMEM((slots, width), BF16)],
        room=28,
        flops=2 * slots * rows * width,
        moved=2 * slots * width,
    )(meta, *recv, pick, wide, ctf, inv)


def energy_body(bins, count, meta, *refs):
    pieces, (ctf_ref, inv_ref, panel_ref, extra_ref, total) = refs[:-5], refs[-5:]
    width = panel_ref.shape[1]
    blocks = []
    for piece in pieces:
        for start in range(0, piece.shape[1], width):
            blocks.append((piece, start))
    step = pl.program_id(0)

    @pl.when(step == 0)
    def _():
        total[...] = jnp.zeros_like(total)

    gain = ctf_ref[...] * ctf_ref[...] * inv_ref[...]
    gain3 = jnp.concatenate(split3(gain), axis=0)
    for index, (piece, start) in enumerate(blocks):

        @pl.when(step == index)
        def _():
            panel = piece[:, start : start + width]
            panel_ref[...] = panel
            wide = panel.astype(F32)
            square = wide * wide
            high = square.astype(BF16)
            low = (square - high.astype(F32)).astype(BF16)
            total[...] += mm(high, gain3, NT) + mm(low, gain3, NT)

    @pl.when(step == count - 1)
    def _():
        whole = total[:, :bins] + total[:, bins : 2 * bins] + total[:, 2 * bins :]
        extra_ref[...] = jnp.concatenate(split3(-0.5 * whole), axis=1)


def energy(meta, pieces, ctf, inv):
    rows, width = pieces[-1].shape
    count = sum(piece.shape[1] for piece in pieces) // width
    bins, pix = ctf.shape
    wrap = pix // width
    return call(
        functools.partial(energy_body, bins, count),
        (count,),
        [pl.BlockSpec(piece.shape, lambda j, m: (0, 0)) for piece in pieces]
        + [
            pl.BlockSpec((bins, width), lambda j, m: (0, lax.rem(m[0] ^ j, wrap))),
            pl.BlockSpec((1, width), lambda j, m: (0, lax.rem(m[0] ^ j, wrap))),
        ],
        [
            pl.BlockSpec((rows, width), lambda j, m: (0, m[0] ^ j)),
            pl.BlockSpec((rows, 3 * bins), lambda j, m: (0, 0)),
        ],
        [sds((rows, count * width), BF16), sds((rows, 3 * bins), BF16)],
        scratch=[pltpu.VMEM((rows, 3 * bins), F32)],
        flops=2 * 4 * rows * bins * count * width * 3,
        moved=4 * rows * count * width,
    )(meta, *pieces, ctf, inv)


def score_body(parts, used, first, last, meta, *refs):
    own, sib, panel_ref, refs = (
        refs[:parts],
        refs[parts : 2 * parts],
        refs[2 * parts],
        refs[2 * parts + 1 :],
    )
    if first:
        acc_out, full_ref = refs
    elif last:
        acc_ref, _, hot_own, hot_sib, extra_ref, shifted_ref, stat_ref, full_ref = refs
    elif used is None:
        acc_ref, _, acc_out, full_ref = refs
    else:
        acc_ref, acc_out = refs
    half = pl.num_programs(0) // 2

    def tile(sources, hot):
        block = jnp.concatenate([source[...] for source in sources], axis=1)
        if used is None or last:
            full_ref[...] = block
        if last:
            block = block[:, used[0] : used[0] + used[1]]
        panel = panel_ref[...] if used is None else panel_ref[:, used[0] : used[0] + used[1]]
        total = mm(panel, block, NT)
        if not first:
            total = acc_ref[...] + total
        if not last:
            acc_out[...] = total
            return
        total = total + mm(extra_ref[...], hot[...], NN)
        peak = jnp.max(total, axis=0, keepdims=True)
        shifted = jnp.exp(total - peak)
        shifted_ref[...] = shifted
        mass = jnp.sum(shifted, axis=0, keepdims=True)
        which = lax.broadcasted_iota(I32, stat_ref.shape, 0)
        stat_ref[...] = jnp.where(which == 0, peak, mass)

    @pl.when(pl.program_id(0) < half)
    def _():
        tile(own, hot_own if last else None)

    @pl.when(pl.program_id(0) >= half)
    def _():
        tile(sib, hot_sib if last else None)


def score(meta, at, own, sib, panels, width, acc=None, full=None, hots=None, extra=None, used=None):
    rows = own[0].shape[0]
    parts = len(own)
    tile = 256
    half = rows // tile
    count, columns = panels.shape
    first, last = acc is None, hots is not None
    store = used is None or last
    fronts = [pl.BlockSpec((tile, v.shape[1]), lambda j, m: (jnp.minimum(j, half - 1), 0)) for v in own]
    backs = [pl.BlockSpec((tile, v.shape[1]), lambda j, m: (jnp.maximum(j - half, 0), 0)) for v in own]
    acc_spec = pl.BlockSpec((count, tile), lambda j, m: (0, j))
    full_spec = pl.BlockSpec((tile, width), lambda j, m: (j, at(m)))
    in_specs = fronts + backs + [pl.BlockSpec((count, width), lambda j, m: (0, at(m)))]
    operands = [meta, *own, *sib, panels]
    alias = {}
    if not first:
        in_specs += [acc_spec]
        alias = {len(operands): 0}
        operands += [acc]
        if store:
            in_specs += [pl.BlockSpec(memory_space=pl.ANY)]
            alias[len(operands)] = 2 if last else 1
            operands += [full]
    full_shape = sds((2 * rows, columns), BF16)
    acc_shape = sds((count, 2 * rows), F32)
    out_specs, out_shape = [acc_spec, full_spec], [acc_shape, full_shape]
    if last:
        depth = extra.shape[1]
        in_specs += [
            pl.BlockSpec((depth, tile), lambda j, m: (0, jnp.minimum(j, half - 1))),
            pl.BlockSpec((depth, tile), lambda j, m: (0, jnp.maximum(j - half, 0))),
            pl.BlockSpec((count, depth), lambda j, m: (0, 0)),
        ]
        operands += [*hots, extra]
        out_specs = [acc_spec, pl.BlockSpec((8, tile), lambda j, m: (0, j)), full_spec]
        out_shape = [acc_shape, sds((8, 2 * rows), F32), full_shape]
    elif not store:
        out_specs, out_shape = acc_spec, acc_shape
    return call(
        functools.partial(score_body, parts, used, first, last),
        (2 * half,),
        in_specs,
        out_specs,
        out_shape,
        alias=alias,
        room=16,
        flops=2 * count * 2 * rows * width,
        moved=8 * count * 2 * rows + 8 * rows * width,
    )(*operands)


def merge_body(meta, mine_ref, other_ref, out_ref):
    rows = mine_ref.shape[1] // 2
    other = other_ref[...]
    other = jnp.concatenate([other[:, rows:], other[:, :rows]], axis=1)
    mine = mine_ref[...]
    peak = jnp.maximum(mine[0:1], other[0:1])
    mass = mine[1:2] * jnp.exp(mine[0:1] - peak) + other[1:2] * jnp.exp(other[0:1] - peak)
    which = lax.broadcasted_iota(I32, out_ref.shape, 0)
    out_ref[...] = jnp.where(which == 0, peak, mass)


def add_body(meta, mine_ref, other_ref, out_ref):
    out_ref[...] = (mine_ref[...].astype(F32) + other_ref[...].astype(F32)).astype(BF16)


def pairwise(body, meta, mine, other):
    spec = pl.BlockSpec(mine.shape, lambda j, m: (0, 0))
    return call(body, (1,), [spec, spec], spec, sds(mine.shape, mine.dtype), room=4)(
        meta, mine, other
    )


merge = functools.partial(pairwise, merge_body)
add_pair = functools.partial(pairwise, add_body)


def class_body(kind, steps, meta, *refs):
    if kind == "first":
        (shifted_ref, stat_ref), four = refs[:2], refs[2:6]
        hot_own, hot_sib, full_ref = refs[6:9]
        outs, (post_ref, log_ref, mass_ref) = refs[9 : 9 + steps], refs[9 + steps :]

        @pl.when(pl.program_id(0) == 0)
        def _():
            stats = [ref[...] for ref in four]
            peaks = [s[0:1] for s in stats]
            peak = jnp.maximum(jnp.maximum(peaks[0], peaks[1]), jnp.maximum(peaks[2], peaks[3]))
            parts = [s[1:2] * jnp.exp(p - peak) for s, p in zip(stats, peaks)]
            mass = (parts[0] + parts[1]) + (parts[2] + parts[3])
            factor = jnp.exp(stat_ref[0:1] - peak) / mass
            post_ref[...] = (shifted_ref[...] * factor).astype(BF16)
            log_ref[...] = (peak + jnp.log(mass))[:, : log_ref.shape[1]]
            bins, rows = mass_ref.shape[0], hot_own.shape[1]
            weights = mm(hot_own[:bins, :], post_ref[:, :rows], NT)
            weights = weights + mm(hot_sib[:bins, :], post_ref[:, rows:], NT)
            mass_ref[...] = weights.astype(BF16)

    else:
        (post_ref, full_ref), outs = refs[:2], refs[2:]
    for step, out_ref in enumerate(outs):

        @pl.when(pl.program_id(0) == step)
        def _():
            out_ref[...] = mm(post_ref[...], full_ref[...], NN).astype(out_ref.dtype)


def class_part(meta, kind, offset, steps, full, post=None, shifted=None, stats=None, hots=None, bins=0):
    rows, columns = full.shape
    width = columns // 8
    count = (shifted if post is None else post).shape[0]
    whole = lambda shape: pl.BlockSpec(shape, lambda j, m: (0, 0))
    full_spec = pl.BlockSpec((rows, width), lambda j, m: (0, m[offset + j]))
    out_specs = [whole((count, width))] * steps
    kept = steps // 2 if kind == "rest" else 0
    types = [BF16] * (steps - kept) + [F32] * kept
    out_shape = [sds((count, width), dtype) for dtype in types]
    if kind == "first":
        operands = [shifted, *stats, *hots, full]
        in_specs = [whole(shifted.shape)] + [whole(stats[0].shape)] * 5
        in_specs += [whole(hots[0].shape)] * 2 + [full_spec]
        out_specs += [whole((count, rows)), whole((1, rows // 2)), whole((bins, count))]
        out_shape += [sds((count, rows), BF16), sds((1, rows // 2), F32), sds((bins, count), BF16)]
    else:
        operands = [post, full]
        in_specs = [whole(post.shape), full_spec]
    return call(
        functools.partial(class_body, kind, steps),
        (steps,),
        in_specs,
        out_specs,
        out_shape,
        room=22 if kind == "first" else 28,
        flops=2 * count * rows * width * steps,
        moved=2 * rows * width * steps + 4 * count * (rows + width * steps),
    )(meta, *operands)


def half_body(tile, meta, *refs):
    rows = pl.ds(pl.multiple_of(pl.program_id(0) * tile, tile), tile)
    first, second, third = [ref[rows, :].astype(F32) for ref in refs[:3]]
    refs[-1][...] = first + second + third


def half_sums(meta, terms, sums=None):
    count, width = terms[0].shape
    parts = 3
    tile = count // parts
    own = sums is None

    def place(j, m):
        core = lax.rem(m[0], 2)
        return (core if own else 1 - core) * parts + j, 0

    return call(
        functools.partial(half_body, tile),
        (parts,),
        [pl.BlockSpec(memory_space=pltpu.VMEM)] * 3
        + ([] if own else [pl.BlockSpec(memory_space=pl.ANY)]),
        pl.BlockSpec((tile, width), place),
        sds((2 * count, width), F32),
        alias=None if own else {4: 0},
        room=8,
    )(meta, *terms, *([] if own else [sums]))


def two_by_two(raw_images, defocus_bin, dest_row, ctf_table, inv_noise, panels):
    dom, turns = lax.axis_size("dom"), lax.axis_size("rot")
    device, plane = lax.axis_index("dom"), lax.axis_index("rot")
    bins = ctf_table.shape[0]
    columns = raw_images.shape[1]
    chip, core = device // 2, device % 2

    def block(apart, half):
        return (chip ^ apart) * 2 + half

    x_first, y_second = block(1, 0), block(2, 1)
    x_second, y_first = block(1, 1), block(2, 0)
    even = core == 0
    order = [
        device,
        plane,
        block(3, 0),
        block(3, 1),
        jnp.where(even, x_first, y_second),
        jnp.where(even, y_second, x_first),
        block(0, 1 - core),
        jnp.where(even, y_first, x_second),
        jnp.where(even, x_second, y_first),
        block(0, core),
    ]
    meta = jnp.stack(order).astype(I32)
    inv = inv_noise[None, :]

    def across(value, apart):
        return lax.ppermute(value, "dom", [(i, i ^ apart) for i in range(dom)])

    def by_core(value, when_even, when_odd):
        pairs = [(i, i ^ (when_odd if i % 2 else when_even)) for i in range(dom)]
        return lax.ppermute(value, "dom", pairs)

    def onward(value):
        return lax.ppermute(value, "rot", [(i, (i + 1) % turns) for i in range(turns)])

    width = columns // turns
    cut = width * 3 // 8
    chunk_a, chunk_b = (0, cut), (cut, width - cut)

    def exchange(blocks):
        far_first = [across(blocks[apart], apart) for apart in (6, 7, 4, 2, 5, 3, 1)]
        return far_first + [blocks[0]]

    slot = jnp.where(dest_row >= 0, dest_row * bins + defocus_bin, -1)
    *send_a, place = pack_first(meta, raw_images, slot, bins, dom, width, chunk_a)
    recv_a = exchange(send_a)
    swapped, place = lax.optimization_barrier((across(panels, 1), place))
    send_b = pack_next(meta, raw_images, place, dom, width, chunk_b)
    together = lax.optimization_barrier

    count = panels.shape[0] // 2
    mine = lax.dynamic_slice_in_dim(panels, core * count, count, 0)
    other = lax.dynamic_slice_in_dim(swapped, core * count, count, 0)
    near = jnp.concatenate([mine, other], axis=1)

    recv_a, send_b, near = together((recv_a, send_b, near))
    share_a, hot, pick, wide = unpack_first(meta, recv_a, ctf_table, inv, width, chunk_a)
    share_a, send_b = together((share_a, send_b))
    a1, recv_b = onward(share_a), exchange(send_b)
    a1, recv_b[:2] = together((a1, recv_b[:2]))
    a2 = onward(a1)
    a2, recv_b, near = together((a2, recv_b, near))
    share_b = unpack_next(meta, pick, wide, recv_b, ctf_table, inv, width, chunk_b)
    by_x, by_y = across(near, 2), across(near, 4)
    a3, b1 = onward(a2), onward(share_b)
    sib0, hots = [across(share_a, 1), across(share_b, 1)], [hot, across(hot, 1)]
    sib1, sib2 = [across(a1, 1), across(b1, 1)], [across(a2, 1)]
    piece = near.shape[1] // 2
    far_y, far_x = across(by_x[:, :piece], 4), across(by_y[:, piece:], 2)
    b2 = onward(b1)
    panel_full, extra = energy(meta, [near, by_x, by_y, far_y, far_x], ctf_table, inv)
    a3, b2, panel_full, hots = together((a3, b2, panel_full, hots))
    b3 = onward(b2)
    sib2 = sib2 + [across(b2, 1)]

    def share(turn):
        return lambda m: lax.rem(m[1] + turns - turn, turns)

    acc, full = score(meta, share(0), [share_a, share_b], sib0, panel_full, width)
    acc, full = score(meta, share(1), [a1, b1], sib1, panel_full, width, acc, full)
    acc, full = score(meta, share(2), [a2, b2], sib2, panel_full, width, acc, full)
    final = share(turns - 1)
    a3_sib = across(a3, 1)
    acc = score(meta, final, [a3], [a3_sib], panel_full, width, acc, used=chunk_a)
    b3, acc = together((b3, acc))
    shifted, stat, full = score(
        meta,
        final,
        [a3, b3],
        [a3_sib, across(b3, 1)],
        panel_full,
        width,
        acc,
        full,
        hots,
        extra,
        chunk_b,
    )

    pair = merge(meta, stat, across(stat, 1))
    others = [
        lax.ppermute(pair, "rot", [(i, i ^ apart) for i in range(turns)]) for apart in (1, 2, 3)
    ]
    to_x, to_y, post, log_evidence, mass = class_part(
        meta, "first", 2, 2, full, None, shifted, [stat, pair, *others], hots, bins
    )
    mass_x = across(mass, 2)
    got_x, got_y = across(to_x, 2), across(to_y, 4)
    six = class_part(meta, "rest", 4, 6, full, post)
    got_x, got_y, six, mass_x = together((got_x, got_y, six, mass_x))
    send_c, send_d, give, a_sum, b_sum, keep = six
    mass = add_pair(meta, mass, mass_x)
    mass_y = across(mass, 4)
    got_c, got_d = by_core(send_c, 2, 4), by_core(send_d, 5, 3)
    down, left = got_x.astype(F32), got_y.astype(F32)
    message_a = (a_sum + jnp.where(even, down, left)).astype(BF16)
    message_b = (b_sum + jnp.where(even, left, down)).astype(BF16)
    got_a, got_b = by_core(message_a, 4, 2), by_core(message_b, 3, 5)
    got_self = across(give, 1)
    mass_y, got_a, got_c = together((mass_y, got_a, got_c))
    mass = mass.astype(F32) + mass_y.astype(F32)
    mass_other = across(mass, 1)
    bin_weights = jnp.where(
        even,
        jnp.concatenate([mass, mass_other], axis=1),
        jnp.concatenate([mass_other, mass], axis=1),
    )
    sums = half_sums(meta, [keep, got_c, got_a])
    bin_weights, got_b = together((bin_weights, got_b))
    class_sums = half_sums(meta, [got_self, got_d, got_b], sums).T
    return class_sums, bin_weights, log_evidence.reshape(-1)


def energy_block(gain_block, panel_piece):
    widened = panel_piece.astype(jnp.float32)
    return lax.dot_general(
        gain_block, widened * widened, (((1,), (1,)), ((), ())), precision=lax.Precision.HIGHEST
    )


def on_device(raw_images, defocus_bin, dest_row, ctf_table, inv_noise, panels):
    dom_count = lax.axis_size("dom")
    bin_count = ctf_table.shape[0]
    columns = raw_images.shape[1]
    hold_rows = raw_images.shape[0]
    shard_rows = hold_rows // 2
    capacity = 2 * shard_rows // dom_count
    is_live = dest_row >= 0
    target = jnp.where(is_live, dest_row // shard_rows, dom_count)
    local_row = dest_row % shard_rows
    marks = (target[:, None] == jnp.arange(dom_count, dtype=jnp.int32)[None, :]).astype(jnp.int32)
    slot_rank = jnp.sum((jnp.cumsum(marks, axis=0) - marks) * marks, axis=1)
    row_code = jnp.where(is_live, local_row * bin_count + defocus_bin, -1)
    padded_images = jnp.concatenate([raw_images, jnp.zeros((1, columns), raw_images.dtype)], axis=0)
    padded_code = jnp.concatenate([row_code, jnp.full((1,), -1, jnp.int32)], axis=0)
    position = jnp.where(is_live, target * capacity + slot_rank, dom_count * capacity)
    slot_count = dom_count * capacity
    source = (
        jnp.full((slot_count,), hold_rows, jnp.int32)
        .at[position]
        .set(jnp.arange(hold_rows, dtype=jnp.int32), mode="drop")
    )
    send_images = padded_images[source].reshape(dom_count, capacity, columns)
    send_code = padded_code[source].reshape(dom_count, capacity)
    recv_images, recv_code = (
        lax.all_to_all(send_images, "dom", split_axis=0, concat_axis=0, tiled=True),
        lax.all_to_all(send_code, "dom", split_axis=0, concat_axis=0, tiled=True),
    )
    flat_images = recv_images.reshape(-1, columns)
    flat_code = recv_code.reshape(-1)
    arrived = flat_code >= 0
    row_of = jnp.where(arrived, flat_code // bin_count, shard_rows)
    row_order = (
        jnp.zeros((shard_rows,), jnp.int32)
        .at[row_of]
        .set(jnp.arange(flat_code.shape[0], dtype=jnp.int32), mode="drop")
    )
    images = flat_images[row_order]
    bin_ids = flat_code[row_order] % bin_count
    bin_table = (bin_ids[:, None] == jnp.arange(bin_count, dtype=jnp.int32)[None, :]).astype(
        jnp.float32
    )
    ctf_rows = jnp.dot(bin_table, ctf_table, precision=lax.Precision.HIGHEST)
    factor = ctf_rows * inv_noise[None, :]
    weighted = (images.astype(jnp.float32) * jnp.concatenate([factor, factor], axis=1)).astype(
        jnp.bfloat16
    )
    gain_half = ctf_table * ctf_table * inv_noise[None, :]
    gain_full = jnp.concatenate([gain_half, gain_half], axis=1)
    panel_piece = lax.all_gather(panels, "dom", axis=1, tiled=True)
    col_block = weighted
    cross_term = lax.dot_general(
        col_block, panel_piece, (((1,), (1,)), ((), ())), preferred_element_type=jnp.float32
    )
    energy = energy_block(gain_full, panel_piece)
    scores = cross_term - 0.5 * jnp.dot(bin_table, energy, precision=lax.Precision.HIGHEST)
    local_peak = jnp.max(scores, axis=1)
    row_peak = lax.pmax(local_peak, "rot")
    shifted = jnp.exp(scores - row_peak[:, None])
    row_total = lax.psum(jnp.sum(shifted, axis=1), "rot")
    posterior = (shifted / row_total[:, None]).astype(jnp.bfloat16)
    log_evidence = row_peak + jnp.log(row_total)
    col_block = weighted
    class_sums = lax.psum_scatter(
        lax.dot_general(
            col_block, posterior, (((0,), (0,)), ((), ())), preferred_element_type=jnp.float32
        ).astype(jnp.bfloat16),
        "dom",
        scatter_dimension=0,
        tiled=True,
    ).astype(jnp.float32)
    local_mass = lax.dot_general(
        bin_table.astype(jnp.bfloat16),
        posterior,
        (((0,), (0,)), ((), ())),
        preferred_element_type=jnp.float32,
    )
    bin_weights = lax.psum(local_mass.astype(jnp.bfloat16), "dom").astype(jnp.float32)
    return (class_sums, bin_weights, log_evidence)


def solution(mesh):
    small = mesh.shape["dom"] == 8 and mesh.shape["rot"] == 4
    return jax.shard_map(
        two_by_two if small else on_device,
        mesh=mesh,
        in_specs=(P("dom", None), P("dom"), P("dom"), P(), P(), P("rot", "dom")),
        out_specs=(P("dom", "rot"), P(None, "rot"), P("dom")),
        check_vma=False,
    )
```

```python
import functools

import jax
import jax.numpy as jnp
from jax import lax
from jax.experimental import pallas as pl
from jax.experimental.pallas import tpu as pltpu
from jax.sharding import PartitionSpec as P

NN = (((1,), (0,)), ((), ()))
NT = (((1,), (1,)), ((), ()))
F32, BF16, I32 = jnp.float32, jnp.bfloat16, jnp.int32
CODE = 16
LANES = 128
MIB = 1024 * 1024


def mm(a, b, dims):
    return lax.dot_general(a, b, dims, preferred_element_type=F32)


def split3(x):
    hi = x.astype(BF16)
    rest = x - hi.astype(F32)
    mid = rest.astype(BF16)
    low = (rest - mid.astype(F32)).astype(BF16)
    return hi, mid, low


def call(body, grid, in_specs, out_specs, out_shape, scratch=(), alias=None, flops=0, moved=0, room=24):
    return pl.pallas_call(
        body,
        grid_spec=pltpu.PrefetchScalarGridSpec(
            num_scalar_prefetch=1,
            grid=grid,
            in_specs=in_specs,
            out_specs=out_specs,
            scratch_shapes=list(scratch),
        ),
        out_shape=out_shape,
        input_output_aliases=alias or {},
        compiler_params=pltpu.CompilerParams(vmem_limit_bytes=room * MIB),
        cost_estimate=pl.CostEstimate(
            flops=flops // 16, bytes_accessed=moved // 16, transcendentals=0
        ),
    )


def sds(shape, dtype):
    return jax.ShapeDtypeStruct(shape, dtype)


def one_hot_rows(out_ref, wanted):
    rows, width = out_ref.shape
    short = wanted.astype(jnp.int16)
    one, zero = jnp.ones((), BF16), jnp.zeros((), BF16)
    step = 256 if rows % 256 == 0 else rows
    for start in range(0, rows, step):
        index = lax.broadcasted_iota(jnp.int16, (step, width), 0) + jnp.int16(start)
        out_ref[start : start + step, :] = jnp.where(index == short, one, zero)


def places_of(dest, shard_rows, cap, dom, device):
    hold = dest.shape[1]
    low = lax.broadcasted_iota(I32, (dom, hold), 0) * shard_rows
    inside = jnp.logical_and(dest >= low, dest < low + shard_rows)
    marks = jnp.where(inside, 1.0, 0.0)
    local = dest - jnp.sum(jnp.where(inside, low, 0), axis=0, keepdims=True)
    lanes = 128
    before = lax.broadcasted_iota(I32, (lanes, lanes), 0) < lax.broadcasted_iota(
        I32, (lanes, lanes), 1
    )
    upper = jnp.where(before, 1.0, 0.0).astype(BF16)
    apart = lax.broadcasted_iota(I32, (dom, 1), 0) ^ device
    carry = apart.astype(F32) * cap + 1.0
    found = []
    for start in range(0, hold, lanes):
        part = marks[:, start : start + lanes]
        rank = mm(part.astype(BF16), upper, NN) + carry
        found.append(jnp.sum(jnp.where(part > 0, rank, 0.0), axis=0, keepdims=True))
        carry = carry + jnp.sum(part, axis=1, keepdims=True)
    return jnp.concatenate(found, axis=1).astype(I32) - 1, local


def joined(refs):
    return jnp.concatenate([ref[...] for ref in refs], axis=1)


def pack_first_body(dom, shard_rows, cap, bins, meta, slot_ref, *refs):
    raw, outs, (place_ref, pick) = refs[: -dom - 2], refs[-dom - 2 : -2], refs[-2:]
    slot = slot_ref[...].reshape(1, slot_ref.shape[0])
    dest, slot_bin = slot >> (bins.bit_length() - 1), slot & (bins - 1)
    place, local = places_of(dest, shard_rows, cap, dom, meta[0])
    place_ref[...] = place
    one_hot_rows(pick, place)
    which = lax.broadcasted_iota(I32, (CODE, dest.shape[1]), 0)
    digits = jnp.where(
        which == 0,
        local >> 4,
        jnp.where(which == 1, local & 15, jnp.where(which == 2, slot_bin, jnp.where(which == 3, 1, 0))),
    )
    digits = jnp.where(dest >= 0, digits, 0).astype(F32).astype(BF16)
    codes = mm(digits, pick[...], NT)
    packed = mm(pick[...], joined(raw), NN).astype(BF16)
    for index, out_ref in enumerate(outs):
        block = slice(index * cap, (index + 1) * cap)
        out_ref[:cap, :] = packed[block]
        out_ref[cap:, :] = jnp.zeros((CODE, out_ref.shape[1]), BF16)
        out_ref[cap:, :cap] = codes[:, block].astype(BF16)


def pack_next_body(cap, dom, meta, place_ref, *refs):
    raw, outs, pick = refs[: -dom - 1], refs[-dom - 1 : -1], refs[-1]
    one_hot_rows(pick, place_ref[...])
    packed = mm(pick[...], joined(raw), NN).astype(BF16)
    for index, out_ref in enumerate(outs):
        out_ref[...] = packed[index * cap : (index + 1) * cap]


def raw_specs(hold, share, chunk):
    first, width = chunk
    at = lambda k: lambda j, m: (0, m[1] * (share // LANES) + first // LANES + k)
    return [pl.BlockSpec((hold, LANES), at(k)) for k in range(width // LANES)]


def pack_first(meta, raw_images, slot, bins, dom, share, chunk):
    hold, _ = raw_images.shape
    width = chunk[1]
    cap = hold // dom
    slots = dom * cap
    specs = raw_specs(hold, share, chunk)
    return call(
        functools.partial(pack_first_body, dom, hold // 2, cap, bins),
        (1,),
        [pl.BlockSpec((hold,), lambda j, m: (0,))] + specs,
        [pl.BlockSpec((cap + CODE, width), lambda j, m: (0, 0))] * dom
        + [pl.BlockSpec((1, hold), lambda j, m: (0, 0))],
        [sds((cap + CODE, width), BF16)] * dom + [sds((1, hold), I32)],
        scratch=[pltpu.VMEM((slots, hold), BF16)],
        room=51,
        flops=2 * slots * hold * width,
        moved=4 * hold * width,
    )(meta, slot, *[raw_images] * len(specs))


def pack_next(meta, raw_images, place, dom, share, chunk):
    hold, _ = raw_images.shape
    width = chunk[1]
    cap = hold // dom
    slots = dom * cap
    specs = raw_specs(hold, share, chunk)
    return call(
        functools.partial(pack_next_body, cap, dom),
        (1,),
        [pl.BlockSpec((1, hold), lambda j, m: (0, 0))] + specs,
        [pl.BlockSpec((cap, width), lambda j, m: (0, 0))] * dom,
        [sds((cap, width), BF16)] * dom,
        scratch=[pltpu.VMEM((slots, hold), BF16)],
        room=51,
        flops=2 * slots * hold * width,
        moved=4 * hold * width,
    )(meta, place, *[raw_images] * len(specs))


def weigh(first, share, pick, wide, recv, meta, ctf_ref, inv_ref, out_ref):
    width = out_ref.shape[1]
    start = lax.rem(meta[1] * share, ctf_ref.shape[1]) + first
    columns = pl.ds(pl.multiple_of(start, LANES), width)
    table = jnp.concatenate(split3(ctf_ref[:, columns] * inv_ref[:, columns]), axis=0)
    out_ref[...] = (mm(pick, recv, NN) * mm(wide, table, NN)).astype(BF16)


def gather(pieces, whole, rows):
    for index, piece in enumerate(pieces):
        whole[index * rows : (index + 1) * rows, :] = piece[:rows, :]


def unpack_first_body(dom, bins, share, first, meta, *refs):
    pieces, recv_ref = refs[:dom], refs[-1]
    cap = pieces[0].shape[0] - CODE
    gather(pieces, recv_ref, cap)
    ctf_ref, inv_ref, out_ref, hot_ref, pick, wide = refs[dom:-1]
    shard_rows = out_ref.shape[0]
    got = jnp.concatenate([piece[cap:, :cap].astype(F32) for piece in pieces], axis=1)
    row = got[0:1] * 16.0 + got[1:2] + got[3:4] * 1024.0 - 1024.0
    one_hot_rows(pick, row.astype(I32))
    slot_bins = jnp.broadcast_to(got[2:3].astype(BF16), (8, got.shape[1]))
    down = mm(pick[...], slot_bins, NT)[:, 0:1].astype(I32)
    across = mm(slot_bins, pick[...], NT)[0:1].astype(I32)
    lane = lax.broadcasted_iota(I32, (shard_rows, 3 * bins), 1)
    wide[...] = jnp.where((lane & (bins - 1)) == down, 1.0, 0.0).astype(BF16)
    deep = lax.broadcasted_iota(I32, (3 * bins, shard_rows), 0)
    hot_ref[...] = jnp.where((deep & (bins - 1)) == across, 1.0, 0.0).astype(BF16)
    weigh(first, share, pick[...], wide[...], recv_ref[...], meta, ctf_ref, inv_ref, out_ref)


def unpack_next_body(dom, share, first, meta, *refs):
    recv_ref = refs[-1]
    gather(refs[:dom], recv_ref, refs[0].shape[0])
    pick_ref, wide_ref, ctf_ref, inv_ref, out_ref = refs[dom:-1]
    weigh(first, share, pick_ref[...], wide_ref[...], recv_ref[...], meta, ctf_ref, inv_ref, out_ref)


def unpack_first(meta, recv, ctf, inv, share, chunk):
    first, width = chunk
    dom = len(recv)
    slots = dom * (recv[0].shape[0] - CODE)
    rows = slots // 2
    bins, pix = ctf.shape
    whole = lambda shape: pl.BlockSpec(shape, lambda j, m: (0, 0))
    shapes = [(rows, width), (3 * bins, rows), (rows, slots), (rows, 3 * bins)]
    return call(
        functools.partial(unpack_first_body, dom, bins, share, first),
        (1,),
        [whole(recv[0].shape)] * dom + [whole(ctf.shape), whole(inv.shape)],
        [whole(s) for s in shapes],
        [sds(s, BF16) for s in shapes],
        scratch=[pltpu.VMEM((slots, width), BF16)],
        room=28,
        flops=2 * slots * rows * width,
        moved=2 * slots * width,
    )(meta, *recv, ctf, inv)


def unpack_next(meta, pick, wide, recv, ctf, inv, share, chunk):
    first, width = chunk
    dom = len(recv)
    slots = dom * recv[0].shape[0]
    rows = slots // 2
    whole = lambda shape: pl.BlockSpec(shape, lambda j, m: (0, 0))
    return call(
        functools.partial(unpack_next_body, dom, share, first),
        (1,),
        [whole(recv[0].shape)] * dom
        + [whole(pick.shape), whole(wide.shape), whole(ctf.shape), whole(inv.shape)],
        whole((rows, width)),
        sds((rows, width), BF16),
        scratch=[pltpu.VMEM((slots, width), BF16)],
        room=28,
        flops=2 * slots * rows * width,
        moved=2 * slots * width,
    )(meta, *recv, pick, wide, ctf, inv)


def energy_body(bins, count, meta, *refs):
    pieces, (ctf_ref, inv_ref, panel_ref, extra_ref, total) = refs[:-5], refs[-5:]
    width = panel_ref.shape[1]
    blocks = []
    for piece in pieces:
        for start in range(0, piece.shape[1], width):
            blocks.append((piece, start))
    step = pl.program_id(0)

    @pl.when(step == 0)
    def _():
        total[...] = jnp.zeros_like(total)

    gain = ctf_ref[...] * ctf_ref[...] * inv_ref[...]
    gain3 = jnp.concatenate(split3(gain), axis=0)
    for index, (piece, start) in enumerate(blocks):

        @pl.when(step == index)
        def _():
            panel = piece[:, start : start + width]
            panel_ref[...] = panel
            wide = panel.astype(F32)
            square = wide * wide
            high = square.astype(BF16)
            low = (square - high.astype(F32)).astype(BF16)
            total[...] += mm(high, gain3, NT) + mm(low, gain3, NT)

    @pl.when(step == count - 1)
    def _():
        whole = total[:, :bins] + total[:, bins : 2 * bins] + total[:, 2 * bins :]
        extra_ref[...] = jnp.concatenate(split3(-0.5 * whole), axis=1)


def energy(meta, pieces, ctf, inv):
    rows, width = pieces[-1].shape
    count = sum(piece.shape[1] for piece in pieces) // width
    bins, pix = ctf.shape
    wrap = pix // width
    return call(
        functools.partial(energy_body, bins, count),
        (count,),
        [pl.BlockSpec(piece.shape, lambda j, m: (0, 0)) for piece in pieces]
        + [
            pl.BlockSpec((bins, width), lambda j, m: (0, lax.rem(m[0] ^ j, wrap))),
            pl.BlockSpec((1, width), lambda j, m: (0, lax.rem(m[0] ^ j, wrap))),
        ],
        [
            pl.BlockSpec((rows, width), lambda j, m: (0, m[0] ^ j)),
            pl.BlockSpec((rows, 3 * bins), lambda j, m: (0, 0)),
        ],
        [sds((rows, count * width), BF16), sds((rows, 3 * bins), BF16)],
        scratch=[pltpu.VMEM((rows, 3 * bins), F32)],
        flops=2 * 4 * rows * bins * count * width * 3,
        moved=4 * rows * count * width,
    )(meta, *pieces, ctf, inv)


def score_body(parts, used, first, last, meta, *refs):
    own, sib, panel_ref, refs = (
        refs[:parts],
        refs[parts : 2 * parts],
        refs[2 * parts],
        refs[2 * parts + 1 :],
    )
    hot_own = hot_sib = None
    if first:
        acc_out, full_ref = refs
    elif last:
        acc_ref, _, shifted_ref, stat_ref, full_ref = refs
    elif used is None:
        acc_ref, _, acc_out, full_ref = refs
    else:
        acc_ref, hot_own, hot_sib, extra_ref, acc_out = refs
    half = pl.num_programs(0) // 2

    def tile(sources, hot):
        block = jnp.concatenate([source[...] for source in sources], axis=1)
        if used is None or last:
            full_ref[...] = block
        if last:
            block = block[:, used[0] : used[0] + used[1]]
        panel = panel_ref[...] if used is None else panel_ref[:, used[0] : used[0] + used[1]]
        total = mm(panel, block, NT)
        if not first:
            total = acc_ref[...] + total
        if hot is not None:
            total = total + mm(extra_ref[...], hot[...], NN)
        if not last:
            acc_out[...] = total
            return
        peak = jnp.max(total, axis=0, keepdims=True)
        shifted = jnp.exp(total - peak)
        shifted_ref[...] = shifted
        mass = jnp.sum(shifted, axis=0, keepdims=True)
        which = lax.broadcasted_iota(I32, stat_ref.shape, 0)
        stat_ref[...] = jnp.where(which == 0, peak, mass)

    @pl.when(pl.program_id(0) < half)
    def _():
        tile(own, hot_own)

    @pl.when(pl.program_id(0) >= half)
    def _():
        tile(sib, hot_sib)


def score(meta, at, own, sib, panels, width, acc=None, full=None, used=None, hots=None, extra=None):
    rows = own[0].shape[0]
    parts = len(own)
    tile = 256
    half = rows // tile
    count, columns = panels.shape
    first, last = acc is None, used is not None and hots is None
    store = used is None or last
    fronts = [pl.BlockSpec((tile, v.shape[1]), lambda j, m: (jnp.minimum(j, half - 1), 0)) for v in own]
    backs = [pl.BlockSpec((tile, v.shape[1]), lambda j, m: (jnp.maximum(j - half, 0), 0)) for v in own]
    acc_spec = pl.BlockSpec((count, tile), lambda j, m: (0, j))
    full_spec = pl.BlockSpec((tile, width), lambda j, m: (j, at(m)))
    in_specs = fronts + backs + [pl.BlockSpec((count, width), lambda j, m: (0, at(m)))]
    operands = [meta, *own, *sib, panels]
    alias = {}
    if not first:
        in_specs += [acc_spec]
        alias = {len(operands): 0}
        operands += [acc]
        if store:
            in_specs += [pl.BlockSpec(memory_space=pl.ANY)]
            alias[len(operands)] = 2 if last else 1
            operands += [full]
    full_shape = sds((2 * rows, columns), BF16)
    acc_shape = sds((count, 2 * rows), F32)
    out_specs, out_shape = [acc_spec, full_spec], [acc_shape, full_shape]
    if last:
        out_specs = [acc_spec, pl.BlockSpec((8, tile), lambda j, m: (0, j)), full_spec]
        out_shape = [acc_shape, sds((8, 2 * rows), F32), full_shape]
    elif not store:
        depth = extra.shape[1]
        in_specs += [
            pl.BlockSpec((depth, tile), lambda j, m: (0, jnp.minimum(j, half - 1))),
            pl.BlockSpec((depth, tile), lambda j, m: (0, jnp.maximum(j - half, 0))),
            pl.BlockSpec((count, depth), lambda j, m: (0, 0)),
        ]
        operands += [*hots, extra]
        out_specs, out_shape = acc_spec, acc_shape
    return call(
        functools.partial(score_body, parts, used, first, last),
        (2 * half,),
        in_specs,
        out_specs,
        out_shape,
        alias=alias,
        room=16,
        flops=2 * count * 2 * rows * width,
        moved=8 * count * 2 * rows + 8 * rows * width,
    )(*operands)


def merge_body(meta, mine_ref, other_ref, out_ref):
    rows = mine_ref.shape[1] // 2
    other = other_ref[...]
    other = jnp.concatenate([other[:, rows:], other[:, :rows]], axis=1)
    mine = mine_ref[...]
    peak = jnp.maximum(mine[0:1], other[0:1])
    mass = mine[1:2] * jnp.exp(mine[0:1] - peak) + other[1:2] * jnp.exp(other[0:1] - peak)
    which = lax.broadcasted_iota(I32, out_ref.shape, 0)
    out_ref[...] = jnp.where(which == 0, peak, mass)


def add_body(meta, mine_ref, other_ref, out_ref):
    out_ref[...] = (mine_ref[...].astype(F32) + other_ref[...].astype(F32)).astype(BF16)


def pairwise(body, meta, mine, other):
    spec = pl.BlockSpec(mine.shape, lambda j, m: (0, 0))
    return call(body, (1,), [spec, spec], spec, sds(mine.shape, mine.dtype), room=4)(
        meta, mine, other
    )


merge = functools.partial(pairwise, merge_body)
add_pair = functools.partial(pairwise, add_body)


def class_body(kind, steps, meta, *refs):
    if kind == "first":
        (shifted_ref, stat_ref), four = refs[:2], refs[2:6]
        hot_own, hot_sib, full_ref = refs[6:9]
        outs, (post_ref, log_ref, mass_ref) = refs[9 : 9 + steps], refs[9 + steps :]

        @pl.when(pl.program_id(0) == 0)
        def _():
            stats = [ref[...] for ref in four]
            peaks = [s[0:1] for s in stats]
            peak = jnp.maximum(jnp.maximum(peaks[0], peaks[1]), jnp.maximum(peaks[2], peaks[3]))
            parts = [s[1:2] * jnp.exp(p - peak) for s, p in zip(stats, peaks)]
            mass = (parts[0] + parts[1]) + (parts[2] + parts[3])
            factor = jnp.exp(stat_ref[0:1] - peak) / mass
            post_ref[...] = (shifted_ref[...] * factor).astype(BF16)
            log_ref[...] = (peak + jnp.log(mass))[:, : log_ref.shape[1]]
            bins, rows = mass_ref.shape[0], hot_own.shape[1]
            weights = mm(hot_own[:bins, :], post_ref[:, :rows], NT)
            weights = weights + mm(hot_sib[:bins, :], post_ref[:, rows:], NT)
            mass_ref[...] = weights.astype(BF16)

    else:
        (post_ref, full_ref), outs = refs[:2], refs[2:]
    for step, out_ref in enumerate(outs):

        @pl.when(pl.program_id(0) == step)
        def _():
            out_ref[...] = mm(post_ref[...], full_ref[...], NN).astype(out_ref.dtype)


def class_part(meta, kind, offset, steps, full, post=None, shifted=None, stats=None, hots=None, bins=0):
    rows, columns = full.shape
    width = columns // 8
    count = (shifted if post is None else post).shape[0]
    whole = lambda shape: pl.BlockSpec(shape, lambda j, m: (0, 0))
    full_spec = pl.BlockSpec((rows, width), lambda j, m: (0, m[offset + j]))
    out_specs = [whole((count, width))] * steps
    kept = steps // 2 if kind == "rest" else 0
    types = [BF16] * (steps - kept) + [F32] * kept
    out_shape = [sds((count, width), dtype) for dtype in types]
    if kind == "first":
        operands = [shifted, *stats, *hots, full]
        in_specs = [whole(shifted.shape)] + [whole(stats[0].shape)] * 5
        in_specs += [whole(hots[0].shape)] * 2 + [full_spec]
        out_specs += [whole((count, rows)), whole((1, rows // 2)), whole((bins, count))]
        out_shape += [sds((count, rows), BF16), sds((1, rows // 2), F32), sds((bins, count), BF16)]
    else:
        operands = [post, full]
        in_specs = [whole(post.shape), full_spec]
    return call(
        functools.partial(class_body, kind, steps),
        (steps,),
        in_specs,
        out_specs,
        out_shape,
        room=22 if kind == "first" else 28,
        flops=2 * count * rows * width * steps,
        moved=2 * rows * width * steps + 4 * count * (rows + width * steps),
    )(meta, *operands)


def own_half_body(tile, meta, keep_ref, c_ref, a_ref, out_ref):
    rows = pl.ds(pl.multiple_of(pl.program_id(0) * tile, tile), tile)
    out_ref[...] = keep_ref[rows, :] + c_ref[rows, :].astype(F32) + a_ref[rows, :].astype(F32)


def own_half(meta, keep, got_c, got_a):
    count, width = keep.shape
    parts = 3
    tile = count // parts
    return call(
        functools.partial(own_half_body, tile),
        (parts,),
        [pl.BlockSpec(memory_space=pltpu.VMEM)] * 3,
        pl.BlockSpec((tile, width), lambda j, m: (lax.rem(m[0], 2) * parts + j, 0)),
        sds((2 * count, width), F32),
        room=8,
    )(meta, keep, got_c, got_a)


def two_by_two(raw_images, defocus_bin, dest_row, ctf_table, inv_noise, panels):
    dom, turns = lax.axis_size("dom"), lax.axis_size("rot")
    device, plane = lax.axis_index("dom"), lax.axis_index("rot")
    bins = ctf_table.shape[0]
    columns = raw_images.shape[1]
    chip, core = device // 2, device % 2

    def block(apart, half):
        return (chip ^ apart) * 2 + half

    x_first, y_second = block(1, 0), block(2, 1)
    x_second, y_first = block(1, 1), block(2, 0)
    even = core == 0
    order = [
        device,
        plane,
        block(3, 0),
        block(3, 1),
        jnp.where(even, x_first, y_second),
        jnp.where(even, y_second, x_first),
        block(0, 1 - core),
        jnp.where(even, y_first, x_second),
        jnp.where(even, x_second, y_first),
        block(0, core),
    ]
    meta = jnp.stack(order).astype(I32)
    inv = inv_noise[None, :]

    def across(value, apart):
        return lax.ppermute(value, "dom", [(i, i ^ apart) for i in range(dom)])

    def by_core(value, when_even, when_odd):
        pairs = [(i, i ^ (when_odd if i % 2 else when_even)) for i in range(dom)]
        return lax.ppermute(value, "dom", pairs)

    def onward(value):
        return lax.ppermute(value, "rot", [(i, (i + 1) % turns) for i in range(turns)])

    width = columns // turns
    cut = width * 3 // 8
    chunk_a, chunk_b = (0, cut), (cut, width - cut)

    def exchange(blocks):
        far_first = [across(blocks[apart], apart) for apart in (6, 7, 4, 2, 5, 3, 1)]
        return far_first + [blocks[0]]

    slot = jnp.where(dest_row >= 0, dest_row * bins + defocus_bin, -1)
    *send_a, place = pack_first(meta, raw_images, slot, bins, dom, width, chunk_a)
    recv_a = exchange(send_a)
    swapped, place = lax.optimization_barrier((across(panels, 1), place))
    send_b = pack_next(meta, raw_images, place, dom, width, chunk_b)
    together = lax.optimization_barrier

    count = panels.shape[0] // 2
    mine = lax.dynamic_slice_in_dim(panels, core * count, count, 0)
    other = lax.dynamic_slice_in_dim(swapped, core * count, count, 0)
    near = jnp.concatenate([mine, other], axis=1)

    recv_a, send_b, near = together((recv_a, send_b, near))
    share_a, hot, pick, wide = unpack_first(meta, recv_a, ctf_table, inv, width, chunk_a)
    share_a, send_b = together((share_a, send_b))
    a1, recv_b = onward(share_a), exchange(send_b)
    a1, recv_b[:2] = together((a1, recv_b[:2]))
    a2 = onward(a1)
    share_b = unpack_next(meta, pick, wide, recv_b, ctf_table, inv, width, chunk_b)
    a2, share_b, near = together((a2, share_b, near))
    by_x, by_y = across(near, 2), across(near, 4)
    a3, b1 = onward(a2), onward(share_b)
    sib0, hots = [across(share_a, 1), across(share_b, 1)], [hot, across(hot, 1)]
    sib1, sib2 = [across(a1, 1), across(b1, 1)], [across(a2, 1)]
    piece = near.shape[1] // 2
    far_y, far_x = across(by_x[:, :piece], 4), across(by_y[:, piece:], 2)
    b2 = onward(b1)
    panel_full, extra = energy(meta, [near, by_x, by_y, far_y, far_x], ctf_table, inv)
    a3, b2, panel_full, hots = together((a3, b2, panel_full, hots))
    b3 = onward(b2)
    sib2 = sib2 + [across(b2, 1)]

    def share(turn):
        return lambda m: lax.rem(m[1] + turns - turn, turns)

    acc, full = score(meta, share(0), [share_a, share_b], sib0, panel_full, width)
    acc, full = score(meta, share(1), [a1, b1], sib1, panel_full, width, acc, full)
    acc, full = score(meta, share(2), [a2, b2], sib2, panel_full, width, acc, full)
    final = share(turns - 1)
    a3_sib = across(a3, 1)
    acc = score(
        meta, final, [a3], [a3_sib], panel_full, width, acc, None, chunk_a, hots, extra
    )
    b3, acc = together((b3, acc))
    shifted, stat, full = score(
        meta,
        final,
        [a3, b3],
        [a3_sib, across(b3, 1)],
        panel_full,
        width,
        acc,
        full,
        chunk_b,
    )

    pair = merge(meta, stat, across(stat, 1))
    others = [
        lax.ppermute(pair, "rot", [(i, i ^ apart) for i in range(turns)]) for apart in (1, 2, 3)
    ]
    to_x, to_y, post, log_evidence, mass = class_part(
        meta, "first", 2, 2, full, None, shifted, [stat, pair, *others], hots, bins
    )
    mass_x = across(mass, 2)
    got_x, got_y = across(to_x, 2), across(to_y, 4)
    six = class_part(meta, "rest", 4, 6, full, post)
    got_x, got_y, six, mass_x = together((got_x, got_y, six, mass_x))
    send_c, send_d, give, a_sum, b_sum, keep = six
    mass = add_pair(meta, mass, mass_x)
    mass_y = across(mass, 4)
    got_c, got_d = by_core(send_c, 2, 4), by_core(send_d, 5, 3)
    down, left = got_x.astype(F32), got_y.astype(F32)
    message_a = (a_sum + jnp.where(even, down, left)).astype(BF16)
    message_b = (b_sum + jnp.where(even, left, down)).astype(BF16)
    got_a, got_b = by_core(message_a, 4, 2), by_core(message_b, 3, 5)
    got_self = across(give, 1)
    mass_y, got_a, got_c = together((mass_y, got_a, got_c))
    mass = mass.astype(F32) + mass_y.astype(F32)
    mass_other = across(mass, 1)
    bin_weights = jnp.where(
        even,
        jnp.concatenate([mass, mass_other], axis=1),
        jnp.concatenate([mass_other, mass], axis=1),
    )
    sums = own_half(meta, keep, got_c, got_a)
    bin_weights, got_b = together((bin_weights, got_b))
    other_half = got_self.astype(F32) + got_d.astype(F32) + got_b.astype(F32)
    class_sums = lax.dynamic_update_slice_in_dim(sums, other_half, (1 - core) * count, 0).T
    return class_sums, bin_weights, log_evidence.reshape(-1)


def energy_block(gain_block, panel_piece):
    widened = panel_piece.astype(jnp.float32)
    return lax.dot_general(
        gain_block, widened * widened, (((1,), (1,)), ((), ())), precision=lax.Precision.HIGHEST
    )


def on_device(raw_images, defocus_bin, dest_row, ctf_table, inv_noise, panels):
    dom_count = lax.axis_size("dom")
    bin_count = ctf_table.shape[0]
    columns = raw_images.shape[1]
    hold_rows = raw_images.shape[0]
    shard_rows = hold_rows // 2
    capacity = 2 * shard_rows // dom_count
    is_live = dest_row >= 0
    target = jnp.where(is_live, dest_row // shard_rows, dom_count)
    local_row = dest_row % shard_rows
    marks = (target[:, None] == jnp.arange(dom_count, dtype=jnp.int32)[None, :]).astype(jnp.int32)
    slot_rank = jnp.sum((jnp.cumsum(marks, axis=0) - marks) * marks, axis=1)
    row_code = jnp.where(is_live, local_row * bin_count + defocus_bin, -1)
    padded_images = jnp.concatenate([raw_images, jnp.zeros((1, columns), raw_images.dtype)], axis=0)
    padded_code = jnp.concatenate([row_code, jnp.full((1,), -1, jnp.int32)], axis=0)
    position = jnp.where(is_live, target * capacity + slot_rank, dom_count * capacity)
    slot_count = dom_count * capacity
    source = (
        jnp.full((slot_count,), hold_rows, jnp.int32)
        .at[position]
        .set(jnp.arange(hold_rows, dtype=jnp.int32), mode="drop")
    )
    send_images = padded_images[source].reshape(dom_count, capacity, columns)
    send_code = padded_code[source].reshape(dom_count, capacity)
    recv_images, recv_code = (
        lax.all_to_all(send_images, "dom", split_axis=0, concat_axis=0, tiled=True),
        lax.all_to_all(send_code, "dom", split_axis=0, concat_axis=0, tiled=True),
    )
    flat_images = recv_images.reshape(-1, columns)
    flat_code = recv_code.reshape(-1)
    arrived = flat_code >= 0
    row_of = jnp.where(arrived, flat_code // bin_count, shard_rows)
    row_order = (
        jnp.zeros((shard_rows,), jnp.int32)
        .at[row_of]
        .set(jnp.arange(flat_code.shape[0], dtype=jnp.int32), mode="drop")
    )
    images = flat_images[row_order]
    bin_ids = flat_code[row_order] % bin_count
    bin_table = (bin_ids[:, None] == jnp.arange(bin_count, dtype=jnp.int32)[None, :]).astype(
        jnp.float32
    )
    ctf_rows = jnp.dot(bin_table, ctf_table, precision=lax.Precision.HIGHEST)
    factor = ctf_rows * inv_noise[None, :]
    weighted = (images.astype(jnp.float32) * jnp.concatenate([factor, factor], axis=1)).astype(
        jnp.bfloat16
    )
    gain_half = ctf_table * ctf_table * inv_noise[None, :]
    gain_full = jnp.concatenate([gain_half, gain_half], axis=1)
    panel_piece = lax.all_gather(panels, "dom", axis=1, tiled=True)
    col_block = weighted
    cross_term = lax.dot_general(
        col_block, panel_piece, (((1,), (1,)), ((), ())), preferred_element_type=jnp.float32
    )
    energy = energy_block(gain_full, panel_piece)
    scores = cross_term - 0.5 * jnp.dot(bin_table, energy, precision=lax.Precision.HIGHEST)
    local_peak = jnp.max(scores, axis=1)
    row_peak = lax.pmax(local_peak, "rot")
    shifted = jnp.exp(scores - row_peak[:, None])
    row_total = lax.psum(jnp.sum(shifted, axis=1), "rot")
    posterior = (shifted / row_total[:, None]).astype(jnp.bfloat16)
    log_evidence = row_peak + jnp.log(row_total)
    col_block = weighted
    class_sums = lax.psum_scatter(
        lax.dot_general(
            col_block, posterior, (((0,), (0,)), ((), ())), preferred_element_type=jnp.float32
        ).astype(jnp.bfloat16),
        "dom",
        scatter_dimension=0,
        tiled=True,
    ).astype(jnp.float32)
    local_mass = lax.dot_general(
        bin_table.astype(jnp.bfloat16),
        posterior,
        (((0,), (0,)), ((), ())),
        preferred_element_type=jnp.float32,
    )
    bin_weights = lax.psum(local_mass.astype(jnp.bfloat16), "dom").astype(jnp.float32)
    return (class_sums, bin_weights, log_evidence)


def solution(mesh):
    small = mesh.shape["dom"] == 8 and mesh.shape["rot"] == 4
    return jax.shard_map(
        two_by_two if small else on_device,
        mesh=mesh,
        in_specs=(P("dom", None), P("dom"), P("dom"), P(), P(), P("rot", "dom")),
        out_specs=(P("dom", "rot"), P(None, "rot"), P("dom")),
        check_vma=False,
    )
```

```python
import functools

import jax
import jax.numpy as jnp
from jax import lax
from jax.experimental import pallas as pl
from jax.experimental.pallas import tpu as pltpu
from jax.sharding import PartitionSpec as P

NN = (((1,), (0,)), ((), ()))
NT = (((1,), (1,)), ((), ()))
F32, BF16, I32 = jnp.float32, jnp.bfloat16, jnp.int32
CODE = 16
LANES = 128
MIB = 1024 * 1024


def mm(a, b, dims):
    return lax.dot_general(a, b, dims, preferred_element_type=F32)


def split3(x):
    hi = x.astype(BF16)
    rest = x - hi.astype(F32)
    mid = rest.astype(BF16)
    low = (rest - mid.astype(F32)).astype(BF16)
    return hi, mid, low


def call(body, grid, in_specs, out_specs, out_shape, scratch=(), alias=None, flops=0, moved=0, room=24):
    return pl.pallas_call(
        body,
        grid_spec=pltpu.PrefetchScalarGridSpec(
            num_scalar_prefetch=1,
            grid=grid,
            in_specs=in_specs,
            out_specs=out_specs,
            scratch_shapes=list(scratch),
        ),
        out_shape=out_shape,
        input_output_aliases=alias or {},
        compiler_params=pltpu.CompilerParams(vmem_limit_bytes=room * MIB),
        cost_estimate=pl.CostEstimate(
            flops=flops // 16, bytes_accessed=moved // 16, transcendentals=0
        ),
    )


def sds(shape, dtype):
    return jax.ShapeDtypeStruct(shape, dtype)


def one_hot_rows(out_ref, wanted):
    rows, width = out_ref.shape
    short = wanted.astype(jnp.int16)
    one, zero = jnp.ones((), BF16), jnp.zeros((), BF16)
    step = 256 if rows % 256 == 0 else rows
    for start in range(0, rows, step):
        index = lax.broadcasted_iota(jnp.int16, (step, width), 0) + jnp.int16(start)
        out_ref[start : start + step, :] = jnp.where(index == short, one, zero)


def places_of(dest, shard_rows, cap, dom, device):
    hold = dest.shape[1]
    low = lax.broadcasted_iota(I32, (dom, hold), 0) * shard_rows
    inside = jnp.logical_and(dest >= low, dest < low + shard_rows)
    marks = jnp.where(inside, 1.0, 0.0)
    local = dest - jnp.sum(jnp.where(inside, low, 0), axis=0, keepdims=True)
    lanes = 128
    before = lax.broadcasted_iota(I32, (lanes, lanes), 0) < lax.broadcasted_iota(
        I32, (lanes, lanes), 1
    )
    upper = jnp.where(before, 1.0, 0.0).astype(BF16)
    apart = lax.broadcasted_iota(I32, (dom, 1), 0) ^ device
    carry = apart.astype(F32) * cap + 1.0
    found = []
    for start in range(0, hold, lanes):
        part = marks[:, start : start + lanes]
        rank = mm(part.astype(BF16), upper, NN) + carry
        found.append(jnp.sum(jnp.where(part > 0, rank, 0.0), axis=0, keepdims=True))
        carry = carry + jnp.sum(part, axis=1, keepdims=True)
    return jnp.concatenate(found, axis=1).astype(I32) - 1, local


def joined(refs):
    return jnp.concatenate([ref[...] for ref in refs], axis=1)


def pack_first_body(dom, shard_rows, cap, bins, meta, slot_ref, *refs):
    raw, outs, (place_ref, pick) = refs[: -dom - 2], refs[-dom - 2 : -2], refs[-2:]
    slot = slot_ref[...].reshape(1, slot_ref.shape[0])
    dest, slot_bin = slot >> (bins.bit_length() - 1), slot & (bins - 1)
    place, local = places_of(dest, shard_rows, cap, dom, meta[0])
    place_ref[...] = place
    one_hot_rows(pick, place)
    which = lax.broadcasted_iota(I32, (CODE, dest.shape[1]), 0)
    digits = jnp.where(
        which == 0,
        local >> 4,
        jnp.where(which == 1, local & 15, jnp.where(which == 2, slot_bin, jnp.where(which == 3, 1, 0))),
    )
    digits = jnp.where(dest >= 0, digits, 0).astype(F32).astype(BF16)
    codes = mm(digits, pick[...], NT)
    packed = mm(pick[...], joined(raw), NN).astype(BF16)
    for index, out_ref in enumerate(outs):
        block = slice(index * cap, (index + 1) * cap)
        out_ref[:cap, :] = packed[block]
        out_ref[cap:, :] = jnp.zeros((CODE, out_ref.shape[1]), BF16)
        out_ref[cap:, :cap] = codes[:, block].astype(BF16)


def pack_next_body(cap, dom, meta, place_ref, *refs):
    raw, outs, pick = refs[: -dom - 1], refs[-dom - 1 : -1], refs[-1]
    one_hot_rows(pick, place_ref[...])
    packed = mm(pick[...], joined(raw), NN).astype(BF16)
    for index, out_ref in enumerate(outs):
        out_ref[...] = packed[index * cap : (index + 1) * cap]


def raw_specs(hold, share, chunk):
    first, width = chunk
    at = lambda k: lambda j, m: (0, m[1] * (share // LANES) + first // LANES + k)
    return [pl.BlockSpec((hold, LANES), at(k)) for k in range(width // LANES)]


def pack_first(meta, raw_images, slot, bins, dom, share, chunk):
    hold, _ = raw_images.shape
    width = chunk[1]
    cap = hold // dom
    slots = dom * cap
    specs = raw_specs(hold, share, chunk)
    return call(
        functools.partial(pack_first_body, dom, hold // 2, cap, bins),
        (1,),
        [pl.BlockSpec((hold,), lambda j, m: (0,))] + specs,
        [pl.BlockSpec((cap + CODE, width), lambda j, m: (0, 0))] * dom
        + [pl.BlockSpec((1, hold), lambda j, m: (0, 0))],
        [sds((cap + CODE, width), BF16)] * dom + [sds((1, hold), I32)],
        scratch=[pltpu.VMEM((slots, hold), BF16)],
        room=51,
        flops=2 * slots * hold * width,
        moved=4 * hold * width,
    )(meta, slot, *[raw_images] * len(specs))


def pack_next(meta, raw_images, place, dom, share, chunk):
    hold, _ = raw_images.shape
    width = chunk[1]
    cap = hold // dom
    slots = dom * cap
    specs = raw_specs(hold, share, chunk)
    return call(
        functools.partial(pack_next_body, cap, dom),
        (1,),
        [pl.BlockSpec((1, hold), lambda j, m: (0, 0))] + specs,
        [pl.BlockSpec((cap, width), lambda j, m: (0, 0))] * dom,
        [sds((cap, width), BF16)] * dom,
        scratch=[pltpu.VMEM((slots, hold), BF16)],
        room=51,
        flops=2 * slots * hold * width,
        moved=4 * hold * width,
    )(meta, place, *[raw_images] * len(specs))


def weigh(first, share, pick, wide, recv, meta, ctf_ref, inv_ref, out_ref):
    width = out_ref.shape[1]
    start = lax.rem(meta[1] * share, ctf_ref.shape[1]) + first
    columns = pl.ds(pl.multiple_of(start, LANES), width)
    table = jnp.concatenate(split3(ctf_ref[:, columns] * inv_ref[:, columns]), axis=0)
    out_ref[...] = (mm(pick, recv, NN) * mm(wide, table, NN)).astype(BF16)


def gather(pieces, whole, rows):
    for index, piece in enumerate(pieces):
        whole[index * rows : (index + 1) * rows, :] = piece[:rows, :]


def unpack_first_body(dom, bins, share, first, meta, *refs):
    pieces, recv_ref = refs[:dom], refs[-1]
    cap = pieces[0].shape[0] - CODE
    gather(pieces, recv_ref, cap)
    ctf_ref, inv_ref, out_ref, hot_ref, pick, wide = refs[dom:-1]
    shard_rows = out_ref.shape[0]
    got = jnp.concatenate([piece[cap:, :cap].astype(F32) for piece in pieces], axis=1)
    row = got[0:1] * 16.0 + got[1:2] + got[3:4] * 1024.0 - 1024.0
    one_hot_rows(pick, row.astype(I32))
    slot_bins = jnp.broadcast_to(got[2:3].astype(BF16), (8, got.shape[1]))
    down = mm(pick[...], slot_bins, NT)[:, 0:1].astype(I32)
    across = mm(slot_bins, pick[...], NT)[0:1].astype(I32)
    lane = lax.broadcasted_iota(I32, (shard_rows, 3 * bins), 1)
    wide[...] = jnp.where((lane & (bins - 1)) == down, 1.0, 0.0).astype(BF16)
    deep = lax.broadcasted_iota(I32, (3 * bins, shard_rows), 0)
    hot_ref[...] = jnp.where((deep & (bins - 1)) == across, 1.0, 0.0).astype(BF16)
    weigh(first, share, pick[...], wide[...], recv_ref[...], meta, ctf_ref, inv_ref, out_ref)


def unpack_next_body(dom, share, first, meta, *refs):
    recv_ref = refs[-1]
    gather(refs[:dom], recv_ref, refs[0].shape[0])
    pick_ref, wide_ref, ctf_ref, inv_ref, out_ref = refs[dom:-1]
    weigh(first, share, pick_ref[...], wide_ref[...], recv_ref[...], meta, ctf_ref, inv_ref, out_ref)


def unpack_first(meta, recv, ctf, inv, share, chunk):
    first, width = chunk
    dom = len(recv)
    slots = dom * (recv[0].shape[0] - CODE)
    rows = slots // 2
    bins, pix = ctf.shape
    whole = lambda shape: pl.BlockSpec(shape, lambda j, m: (0, 0))
    shapes = [(rows, width), (3 * bins, rows), (rows, slots), (rows, 3 * bins)]
    return call(
        functools.partial(unpack_first_body, dom, bins, share, first),
        (1,),
        [whole(recv[0].shape)] * dom + [whole(ctf.shape), whole(inv.shape)],
        [whole(s) for s in shapes],
        [sds(s, BF16) for s in shapes],
        scratch=[pltpu.VMEM((slots, width), BF16)],
        room=28,
        flops=2 * slots * rows * width,
        moved=2 * slots * width,
    )(meta, *recv, ctf, inv)


def unpack_next(meta, pick, wide, recv, ctf, inv, share, chunk):
    first, width = chunk
    dom = len(recv)
    slots = dom * recv[0].shape[0]
    rows = slots // 2
    whole = lambda shape: pl.BlockSpec(shape, lambda j, m: (0, 0))
    return call(
        functools.partial(unpack_next_body, dom, share, first),
        (1,),
        [whole(recv[0].shape)] * dom
        + [whole(pick.shape), whole(wide.shape), whole(ctf.shape), whole(inv.shape)],
        whole((rows, width)),
        sds((rows, width), BF16),
        scratch=[pltpu.VMEM((slots, width), BF16)],
        room=28,
        flops=2 * slots * rows * width,
        moved=2 * slots * width,
    )(meta, *recv, pick, wide, ctf, inv)


def energy_body(bins, count, last, meta, *refs):
    if last:
        pieces, refs = refs[:-6], refs[-6:]
        ctf_ref, inv_ref, _, _, panel_ref, _ = refs
    else:
        pieces, (ctf_ref, inv_ref, panel_ref, _) = refs[:-4], refs[-4:]
    width = panel_ref.shape[1]
    blocks = []
    for piece in pieces:
        for start in range(0, piece.shape[1], width):
            blocks.append((piece, start))
    step = pl.program_id(0)
    gain = ctf_ref[...] * ctf_ref[...] * inv_ref[...]
    gain3 = jnp.concatenate(split3(gain), axis=0)
    return step, blocks, gain3, width


def add_energy(panel, gain3):
    wide = panel.astype(F32)
    square = wide * wide
    high = square.astype(BF16)
    low = (square - high.astype(F32)).astype(BF16)
    return mm(high, gain3, NT) + mm(low, gain3, NT)


def near_energy_body(bins, count, meta, *refs):
    step, blocks, gain3, width = energy_body(bins, count, False, meta, *refs)
    panel_ref, total = refs[-2:]

    @pl.when(step == 0)
    def _():
        total[...] = jnp.zeros_like(total)

    for index, (piece, start) in enumerate(blocks):

        @pl.when(step == index)
        def _():
            panel = piece[:, start : start + width]
            panel_ref[...] = panel
            total[...] += add_energy(panel, gain3)


def far_energy_body(bins, count, meta, *refs):
    refs, total = refs[:-1], refs[-1]
    step, blocks, gain3, width = energy_body(bins, count, True, meta, *refs)
    before_ref, _, panel_ref, extra_ref = refs[-4:]

    @pl.when(step == 0)
    def _():
        total[...] = before_ref[...]

    for index, (piece, start) in enumerate(blocks):

        @pl.when(step == index)
        def _():
            panel = piece[:, start : start + width]
            panel_ref[...] = panel
            total[...] += add_energy(panel, gain3)

    @pl.when(step == count - 1)
    def _():
        whole = total[:, :bins] + total[:, bins : 2 * bins] + total[:, 2 * bins :]
        extra_ref[...] = jnp.concatenate(split3(-0.5 * whole), axis=1)


def energy(meta, pieces, ctf, inv, width, first, before=None, panels=None):
    rows = pieces[0].shape[0]
    count = sum(piece.shape[1] for piece in pieces) // width
    bins, pix = ctf.shape
    wrap = pix // width
    last = before is not None
    whole = lambda shape: pl.BlockSpec(shape, lambda j, m: (0, 0))
    table = lambda height: pl.BlockSpec(
        (height, width), lambda j, m: (0, lax.rem(m[0] ^ (first + j), wrap))
    )
    in_specs = [whole(piece.shape) for piece in pieces] + [table(bins), table(1)]
    operands = [meta, *pieces, ctf, inv]
    alias = None
    if last:
        in_specs += [whole(before.shape), pl.BlockSpec(memory_space=pl.ANY)]
        alias = {len(operands) + 1: 0}
        operands += [before, panels]
    sums = sds((rows, 3 * bins), BF16 if last else F32)
    return call(
        functools.partial(far_energy_body if last else near_energy_body, bins, count),
        (count,),
        in_specs,
        [pl.BlockSpec((rows, width), lambda j, m: (0, m[0] ^ (first + j))), whole(sums.shape)],
        [sds((rows, 2 * pix), BF16), sums],
        scratch=[pltpu.VMEM((rows, 3 * bins), F32)] if last else [],
        alias=alias,
        flops=2 * 4 * rows * bins * count * width * 3,
        moved=4 * rows * count * width,
    )(*operands)


def score_body(parts, used, first, last, meta, *refs):
    own, sib, panel_ref, refs = (
        refs[:parts],
        refs[parts : 2 * parts],
        refs[2 * parts],
        refs[2 * parts + 1 :],
    )
    hot_own = hot_sib = None
    if first:
        acc_out, full_ref = refs
    elif last:
        acc_ref, _, shifted_ref, stat_ref, full_ref = refs
    elif used is None:
        acc_ref, _, acc_out, full_ref = refs
    else:
        acc_ref, hot_own, hot_sib, extra_ref, acc_out = refs
    half = pl.num_programs(0) // 2

    def tile(sources, hot):
        block = jnp.concatenate([source[...] for source in sources], axis=1)
        if used is None or last:
            full_ref[...] = block
        if last:
            block = block[:, used[0] : used[0] + used[1]]
        panel = panel_ref[...] if used is None else panel_ref[:, used[0] : used[0] + used[1]]
        total = mm(panel, block, NT)
        if not first:
            total = acc_ref[...] + total
        if hot is not None:
            total = total + mm(extra_ref[...], hot[...], NN)
        if not last:
            acc_out[...] = total
            return
        peak = jnp.max(total, axis=0, keepdims=True)
        shifted = jnp.exp(total - peak)
        shifted_ref[...] = shifted
        mass = jnp.sum(shifted, axis=0, keepdims=True)
        which = lax.broadcasted_iota(I32, stat_ref.shape, 0)
        stat_ref[...] = jnp.where(which == 0, peak, mass)

    @pl.when(pl.program_id(0) < half)
    def _():
        tile(own, hot_own)

    @pl.when(pl.program_id(0) >= half)
    def _():
        tile(sib, hot_sib)


def score(meta, at, own, sib, panels, width, acc=None, full=None, used=None, hots=None, extra=None):
    rows = own[0].shape[0]
    parts = len(own)
    tile = 256
    half = rows // tile
    count, columns = panels.shape
    first, last = acc is None, used is not None and hots is None
    store = used is None or last
    fronts = [pl.BlockSpec((tile, v.shape[1]), lambda j, m: (jnp.minimum(j, half - 1), 0)) for v in own]
    backs = [pl.BlockSpec((tile, v.shape[1]), lambda j, m: (jnp.maximum(j - half, 0), 0)) for v in own]
    acc_spec = pl.BlockSpec((count, tile), lambda j, m: (0, j))
    full_spec = pl.BlockSpec((tile, width), lambda j, m: (j, at(m)))
    in_specs = fronts + backs + [pl.BlockSpec((count, width), lambda j, m: (0, at(m)))]
    operands = [meta, *own, *sib, panels]
    alias = {}
    if not first:
        in_specs += [acc_spec]
        alias = {len(operands): 0}
        operands += [acc]
        if store:
            in_specs += [pl.BlockSpec(memory_space=pl.ANY)]
            alias[len(operands)] = 2 if last else 1
            operands += [full]
    full_shape = sds((2 * rows, columns), BF16)
    acc_shape = sds((count, 2 * rows), F32)
    out_specs, out_shape = [acc_spec, full_spec], [acc_shape, full_shape]
    if last:
        out_specs = [acc_spec, pl.BlockSpec((8, tile), lambda j, m: (0, j)), full_spec]
        out_shape = [acc_shape, sds((8, 2 * rows), F32), full_shape]
    elif not store:
        depth = extra.shape[1]
        in_specs += [
            pl.BlockSpec((depth, tile), lambda j, m: (0, jnp.minimum(j, half - 1))),
            pl.BlockSpec((depth, tile), lambda j, m: (0, jnp.maximum(j - half, 0))),
            pl.BlockSpec((count, depth), lambda j, m: (0, 0)),
        ]
        operands += [*hots, extra]
        out_specs, out_shape = acc_spec, acc_shape
    return call(
        functools.partial(score_body, parts, used, first, last),
        (2 * half,),
        in_specs,
        out_specs,
        out_shape,
        alias=alias,
        room=16,
        flops=2 * count * 2 * rows * width,
        moved=8 * count * 2 * rows + 8 * rows * width,
    )(*operands)


def merge_body(meta, mine_ref, other_ref, out_ref):
    rows = mine_ref.shape[1] // 2
    other = other_ref[...]
    other = jnp.concatenate([other[:, rows:], other[:, :rows]], axis=1)
    mine = mine_ref[...]
    peak = jnp.maximum(mine[0:1], other[0:1])
    mass = mine[1:2] * jnp.exp(mine[0:1] - peak) + other[1:2] * jnp.exp(other[0:1] - peak)
    which = lax.broadcasted_iota(I32, out_ref.shape, 0)
    out_ref[...] = jnp.where(which == 0, peak, mass)


def add_body(meta, mine_ref, other_ref, out_ref):
    out_ref[...] = (mine_ref[...].astype(F32) + other_ref[...].astype(F32)).astype(BF16)


def pairwise(body, meta, mine, other):
    spec = pl.BlockSpec(mine.shape, lambda j, m: (0, 0))
    return call(body, (1,), [spec, spec], spec, sds(mine.shape, mine.dtype), room=4)(
        meta, mine, other
    )


merge = functools.partial(pairwise, merge_body)
add_pair = functools.partial(pairwise, add_body)


def class_body(kind, steps, meta, *refs):
    if kind == "first":
        (shifted_ref, stat_ref), four = refs[:2], refs[2:6]
        hot_own, hot_sib, full_ref = refs[6:9]
        outs, (post_ref, log_ref, mass_ref) = refs[9 : 9 + steps], refs[9 + steps :]

        @pl.when(pl.program_id(0) == 0)
        def _():
            stats = [ref[...] for ref in four]
            peaks = [s[0:1] for s in stats]
            peak = jnp.maximum(jnp.maximum(peaks[0], peaks[1]), jnp.maximum(peaks[2], peaks[3]))
            parts = [s[1:2] * jnp.exp(p - peak) for s, p in zip(stats, peaks)]
            mass = (parts[0] + parts[1]) + (parts[2] + parts[3])
            factor = jnp.exp(stat_ref[0:1] - peak) / mass
            post_ref[...] = (shifted_ref[...] * factor).astype(BF16)
            log_ref[...] = (peak + jnp.log(mass))[:, : log_ref.shape[1]]
            bins, rows = mass_ref.shape[0], hot_own.shape[1]
            weights = mm(hot_own[:bins, :], post_ref[:, :rows], NT)
            weights = weights + mm(hot_sib[:bins, :], post_ref[:, rows:], NT)
            mass_ref[...] = weights.astype(BF16)

    else:
        (post_ref, full_ref), outs = refs[:2], refs[2:]
    for step, out_ref in enumerate(outs):

        @pl.when(pl.program_id(0) == step)
        def _():
            out_ref[...] = mm(post_ref[...], full_ref[...], NN).astype(out_ref.dtype)


def class_part(meta, kind, offset, steps, full, post=None, shifted=None, stats=None, hots=None, bins=0):
    rows, columns = full.shape
    width = columns // 8
    count = (shifted if post is None else post).shape[0]
    whole = lambda shape: pl.BlockSpec(shape, lambda j, m: (0, 0))
    full_spec = pl.BlockSpec((rows, width), lambda j, m: (0, m[offset + j]))
    out_specs = [whole((count, width))] * steps
    kept = steps // 2 if kind == "rest" else 0
    types = [BF16] * (steps - kept) + [F32] * kept
    out_shape = [sds((count, width), dtype) for dtype in types]
    if kind == "first":
        operands = [shifted, *stats, *hots, full]
        in_specs = [whole(shifted.shape)] + [whole(stats[0].shape)] * 5
        in_specs += [whole(hots[0].shape)] * 2 + [full_spec]
        out_specs += [whole((count, rows)), whole((1, rows // 2)), whole((bins, count))]
        out_shape += [sds((count, rows), BF16), sds((1, rows // 2), F32), sds((bins, count), BF16)]
    else:
        operands = [post, full]
        in_specs = [whole(post.shape), full_spec]
    return call(
        functools.partial(class_body, kind, steps),
        (steps,),
        in_specs,
        out_specs,
        out_shape,
        room=22 if kind == "first" else 28,
        flops=2 * count * rows * width * steps,
        moved=2 * rows * width * steps + 4 * count * (rows + width * steps),
    )(meta, *operands)


def own_half_body(tile, meta, keep_ref, c_ref, a_ref, out_ref):
    rows = pl.ds(pl.multiple_of(pl.program_id(0) * tile, tile), tile)
    out_ref[...] = keep_ref[rows, :] + c_ref[rows, :].astype(F32) + a_ref[rows, :].astype(F32)


def own_half(meta, keep, got_c, got_a):
    count, width = keep.shape
    parts = 3
    tile = count // parts
    return call(
        functools.partial(own_half_body, tile),
        (parts,),
        [pl.BlockSpec(memory_space=pltpu.VMEM)] * 3,
        pl.BlockSpec((tile, width), lambda j, m: (lax.rem(m[0], 2) * parts + j, 0)),
        sds((2 * count, width), F32),
        room=8,
    )(meta, keep, got_c, got_a)


def two_by_two(raw_images, defocus_bin, dest_row, ctf_table, inv_noise, panels):
    dom, turns = lax.axis_size("dom"), lax.axis_size("rot")
    device, plane = lax.axis_index("dom"), lax.axis_index("rot")
    bins = ctf_table.shape[0]
    columns = raw_images.shape[1]
    chip, core = device // 2, device % 2

    def block(apart, half):
        return (chip ^ apart) * 2 + half

    x_first, y_second = block(1, 0), block(2, 1)
    x_second, y_first = block(1, 1), block(2, 0)
    even = core == 0
    order = [
        device,
        plane,
        block(3, 0),
        block(3, 1),
        jnp.where(even, x_first, y_second),
        jnp.where(even, y_second, x_first),
        block(0, 1 - core),
        jnp.where(even, y_first, x_second),
        jnp.where(even, x_second, y_first),
        block(0, core),
    ]
    meta = jnp.stack(order).astype(I32)
    inv = inv_noise[None, :]

    def across(value, apart):
        return lax.ppermute(value, "dom", [(i, i ^ apart) for i in range(dom)])

    def by_core(value, when_even, when_odd):
        pairs = [(i, i ^ (when_odd if i % 2 else when_even)) for i in range(dom)]
        return lax.ppermute(value, "dom", pairs)

    def onward(value):
        return lax.ppermute(value, "rot", [(i, (i + 1) % turns) for i in range(turns)])

    width = columns // turns
    cut = width * 3 // 8
    chunk_a, chunk_b = (0, cut), (cut, width - cut)

    def exchange(blocks):
        far_first = [across(blocks[apart], apart) for apart in (6, 7, 4, 2, 5, 3, 1)]
        return far_first + [blocks[0]]

    slot = jnp.where(dest_row >= 0, dest_row * bins + defocus_bin, -1)
    *send_a, place = pack_first(meta, raw_images, slot, bins, dom, width, chunk_a)
    recv_a = exchange(send_a)
    swapped, place = lax.optimization_barrier((across(panels, 1), place))
    send_b = pack_next(meta, raw_images, place, dom, width, chunk_b)
    together = lax.optimization_barrier

    count = panels.shape[0] // 2
    mine = lax.dynamic_slice_in_dim(panels, core * count, count, 0)
    other = lax.dynamic_slice_in_dim(swapped, core * count, count, 0)
    near = jnp.concatenate([mine, other], axis=1)

    recv_a, send_b, near = together((recv_a, send_b, near))
    share_a, hot, pick, wide = unpack_first(meta, recv_a, ctf_table, inv, width, chunk_a)
    share_a, send_b = together((share_a, send_b))
    a1, recv_b = onward(share_a), exchange(send_b)
    piece = near.shape[1] // 2
    panel_full, energies = energy(meta, [near], ctf_table, inv, piece, 0)
    a1, recv_b[:2], panel_full, energies = together((a1, recv_b[:2], panel_full, energies))
    a2 = onward(a1)
    share_b = unpack_next(meta, pick, wide, recv_b, ctf_table, inv, width, chunk_b)
    a2, share_b, near = together((a2, share_b, near))
    by_x, by_y = across(near, 2), across(near, 4)
    a3, b1 = onward(a2), onward(share_b)
    sib0, hots = [across(share_a, 1), across(share_b, 1)], [hot, across(hot, 1)]
    sib1, sib2 = [across(a1, 1), across(b1, 1)], [across(a2, 1)]
    piece = near.shape[1] // 2
    far_y, far_x = across(by_x[:, :piece], 4), across(by_y[:, piece:], 2)
    b2 = onward(b1)
    panel_full, extra = energy(
        meta, [by_x, by_y, far_y, far_x], ctf_table, inv, piece, 2, energies, panel_full
    )
    a3, b2, panel_full, hots = together((a3, b2, panel_full, hots))
    b3 = onward(b2)
    sib2 = sib2 + [across(b2, 1)]

    def share(turn):
        return lambda m: lax.rem(m[1] + turns - turn, turns)

    acc, full = score(meta, share(0), [share_a, share_b], sib0, panel_full, width)
    acc, full = score(meta, share(1), [a1, b1], sib1, panel_full, width, acc, full)
    acc, full = score(meta, share(2), [a2, b2], sib2, panel_full, width, acc, full)
    final = share(turns - 1)
    a3_sib = across(a3, 1)
    acc = score(
        meta, final, [a3], [a3_sib], panel_full, width, acc, None, chunk_a, hots, extra
    )
    b3, acc = together((b3, acc))
    shifted, stat, full = score(
        meta,
        final,
        [a3, b3],
        [a3_sib, across(b3, 1)],
        panel_full,
        width,
        acc,
        full,
        chunk_b,
    )

    pair = merge(meta, stat, across(stat, 1))
    others = [
        lax.ppermute(pair, "rot", [(i, i ^ apart) for i in range(turns)]) for apart in (1, 2, 3)
    ]
    to_x, to_y, post, log_evidence, mass = class_part(
        meta, "first", 2, 2, full, None, shifted, [stat, pair, *others], hots, bins
    )
    mass_x = across(mass, 2)
    got_x, got_y = across(to_x, 2), across(to_y, 4)
    six = class_part(meta, "rest", 4, 6, full, post)
    got_x, got_y, six, mass_x = together((got_x, got_y, six, mass_x))
    send_c, send_d, give, a_sum, b_sum, keep = six
    mass = add_pair(meta, mass, mass_x)
    mass_y = across(mass, 4)
    got_c, got_d = by_core(send_c, 2, 4), by_core(send_d, 5, 3)
    down, left = got_x.astype(F32), got_y.astype(F32)
    message_a = (a_sum + jnp.where(even, down, left)).astype(BF16)
    message_b = (b_sum + jnp.where(even, left, down)).astype(BF16)
    got_a, got_b = by_core(message_a, 4, 2), by_core(message_b, 3, 5)
    got_self = across(give, 1)
    mass_y, got_a, got_c = together((mass_y, got_a, got_c))
    mass = mass.astype(F32) + mass_y.astype(F32)
    mass_other = across(mass, 1)
    bin_weights = jnp.where(
        even,
        jnp.concatenate([mass, mass_other], axis=1),
        jnp.concatenate([mass_other, mass], axis=1),
    )
    sums = own_half(meta, keep, got_c, got_a)
    bin_weights, got_b = together((bin_weights, got_b))
    other_half = got_self.astype(F32) + got_d.astype(F32) + got_b.astype(F32)
    class_sums = lax.dynamic_update_slice_in_dim(sums, other_half, (1 - core) * count, 0).T
    return class_sums, bin_weights, log_evidence.reshape(-1)


def energy_block(gain_block, panel_piece):
    widened = panel_piece.astype(jnp.float32)
    return lax.dot_general(
        gain_block, widened * widened, (((1,), (1,)), ((), ())), precision=lax.Precision.HIGHEST
    )


def on_device(raw_images, defocus_bin, dest_row, ctf_table, inv_noise, panels):
    dom_count = lax.axis_size("dom")
    bin_count = ctf_table.shape[0]
    columns = raw_images.shape[1]
    hold_rows = raw_images.shape[0]
    shard_rows = hold_rows // 2
    capacity = 2 * shard_rows // dom_count
    is_live = dest_row >= 0
    target = jnp.where(is_live, dest_row // shard_rows, dom_count)
    local_row = dest_row % shard_rows
    marks = (target[:, None] == jnp.arange(dom_count, dtype=jnp.int32)[None, :]).astype(jnp.int32)
    slot_rank = jnp.sum((jnp.cumsum(marks, axis=0) - marks) * marks, axis=1)
    row_code = jnp.where(is_live, local_row * bin_count + defocus_bin, -1)
    padded_images = jnp.concatenate([raw_images, jnp.zeros((1, columns), raw_images.dtype)], axis=0)
    padded_code = jnp.concatenate([row_code, jnp.full((1,), -1, jnp.int32)], axis=0)
    position = jnp.where(is_live, target * capacity + slot_rank, dom_count * capacity)
    slot_count = dom_count * capacity
    source = (
        jnp.full((slot_count,), hold_rows, jnp.int32)
        .at[position]
        .set(jnp.arange(hold_rows, dtype=jnp.int32), mode="drop")
    )
    send_images = padded_images[source].reshape(dom_count, capacity, columns)
    send_code = padded_code[source].reshape(dom_count, capacity)
    recv_images, recv_code = (
        lax.all_to_all(send_images, "dom", split_axis=0, concat_axis=0, tiled=True),
        lax.all_to_all(send_code, "dom", split_axis=0, concat_axis=0, tiled=True),
    )
    flat_images = recv_images.reshape(-1, columns)
    flat_code = recv_code.reshape(-1)
    arrived = flat_code >= 0
    row_of = jnp.where(arrived, flat_code // bin_count, shard_rows)
    row_order = (
        jnp.zeros((shard_rows,), jnp.int32)
        .at[row_of]
        .set(jnp.arange(flat_code.shape[0], dtype=jnp.int32), mode="drop")
    )
    images = flat_images[row_order]
    bin_ids = flat_code[row_order] % bin_count
    bin_table = (bin_ids[:, None] == jnp.arange(bin_count, dtype=jnp.int32)[None, :]).astype(
        jnp.float32
    )
    ctf_rows = jnp.dot(bin_table, ctf_table, precision=lax.Precision.HIGHEST)
    factor = ctf_rows * inv_noise[None, :]
    weighted = (images.astype(jnp.float32) * jnp.concatenate([factor, factor], axis=1)).astype(
        jnp.bfloat16
    )
    gain_half = ctf_table * ctf_table * inv_noise[None, :]
    gain_full = jnp.concatenate([gain_half, gain_half], axis=1)
    panel_piece = lax.all_gather(panels, "dom", axis=1, tiled=True)
    col_block = weighted
    cross_term = lax.dot_general(
        col_block, panel_piece, (((1,), (1,)), ((), ())), preferred_element_type=jnp.float32
    )
    energy = energy_block(gain_full, panel_piece)
    scores = cross_term - 0.5 * jnp.dot(bin_table, energy, precision=lax.Precision.HIGHEST)
    local_peak = jnp.max(scores, axis=1)
    row_peak = lax.pmax(local_peak, "rot")
    shifted = jnp.exp(scores - row_peak[:, None])
    row_total = lax.psum(jnp.sum(shifted, axis=1), "rot")
    posterior = (shifted / row_total[:, None]).astype(jnp.bfloat16)
    log_evidence = row_peak + jnp.log(row_total)
    col_block = weighted
    class_sums = lax.psum_scatter(
        lax.dot_general(
            col_block, posterior, (((0,), (0,)), ((), ())), preferred_element_type=jnp.float32
        ).astype(jnp.bfloat16),
        "dom",
        scatter_dimension=0,
        tiled=True,
    ).astype(jnp.float32)
    local_mass = lax.dot_general(
        bin_table.astype(jnp.bfloat16),
        posterior,
        (((0,), (0,)), ((), ())),
        preferred_element_type=jnp.float32,
    )
    bin_weights = lax.psum(local_mass.astype(jnp.bfloat16), "dom").astype(jnp.float32)
    return (class_sums, bin_weights, log_evidence)


def solution(mesh):
    small = mesh.shape["dom"] == 8 and mesh.shape["rot"] == 4
    return jax.shard_map(
        two_by_two if small else on_device,
        mesh=mesh,
        in_specs=(P("dom", None), P("dom"), P("dom"), P(), P(), P("rot", "dom")),
        out_specs=(P("dom", "rot"), P(None, "rot"), P("dom")),
        check_vma=False,
    )
```

```python
import functools

import jax
import jax.numpy as jnp
from jax import lax
from jax.experimental import pallas as pl
from jax.experimental.pallas import tpu as pltpu
from jax.sharding import PartitionSpec as P

NN = (((1,), (0,)), ((), ()))
NT = (((1,), (1,)), ((), ()))
F32, BF16, I32 = jnp.float32, jnp.bfloat16, jnp.int32
CODE = 16
LANES = 128
MIB = 1024 * 1024


def mm(a, b, dims):
    return lax.dot_general(a, b, dims, preferred_element_type=F32)


def split3(x):
    hi = x.astype(BF16)
    rest = x - hi.astype(F32)
    mid = rest.astype(BF16)
    low = (rest - mid.astype(F32)).astype(BF16)
    return hi, mid, low


def call(body, grid, in_specs, out_specs, out_shape, scratch=(), alias=None, flops=0, moved=0, room=24):
    return pl.pallas_call(
        body,
        grid_spec=pltpu.PrefetchScalarGridSpec(
            num_scalar_prefetch=1,
            grid=grid,
            in_specs=in_specs,
            out_specs=out_specs,
            scratch_shapes=list(scratch),
        ),
        out_shape=out_shape,
        input_output_aliases=alias or {},
        compiler_params=pltpu.CompilerParams(vmem_limit_bytes=room * MIB),
        cost_estimate=pl.CostEstimate(
            flops=flops // 16, bytes_accessed=moved // 16, transcendentals=0
        ),
    )


def sds(shape, dtype):
    return jax.ShapeDtypeStruct(shape, dtype)


def one_hot_rows(out_ref, wanted):
    rows, width = out_ref.shape
    short = wanted.astype(jnp.int16)
    one, zero = jnp.ones((), BF16), jnp.zeros((), BF16)
    step = 256 if rows % 256 == 0 else rows
    for start in range(0, rows, step):
        index = lax.broadcasted_iota(jnp.int16, (step, width), 0) + jnp.int16(start)
        out_ref[start : start + step, :] = jnp.where(index == short, one, zero)


def places_of(dest, shard_rows, cap, dom, device):
    hold = dest.shape[1]
    low = lax.broadcasted_iota(I32, (dom, hold), 0) * shard_rows
    inside = jnp.logical_and(dest >= low, dest < low + shard_rows)
    marks = jnp.where(inside, 1.0, 0.0)
    local = dest - jnp.sum(jnp.where(inside, low, 0), axis=0, keepdims=True)
    lanes = 128
    before = lax.broadcasted_iota(I32, (lanes, lanes), 0) < lax.broadcasted_iota(
        I32, (lanes, lanes), 1
    )
    upper = jnp.where(before, 1.0, 0.0).astype(BF16)
    apart = lax.broadcasted_iota(I32, (dom, 1), 0) ^ device
    carry = apart.astype(F32) * cap + 1.0
    found = []
    for start in range(0, hold, lanes):
        part = marks[:, start : start + lanes]
        rank = mm(part.astype(BF16), upper, NN) + carry
        found.append(jnp.sum(jnp.where(part > 0, rank, 0.0), axis=0, keepdims=True))
        carry = carry + jnp.sum(part, axis=1, keepdims=True)
    return jnp.concatenate(found, axis=1).astype(I32) - 1, local


def joined(refs):
    return jnp.concatenate([ref[...] for ref in refs], axis=1)


def pack_first_body(dom, shard_rows, cap, bins, meta, slot_ref, *refs):
    raw, outs, (place_ref, pick) = refs[: -dom - 2], refs[-dom - 2 : -2], refs[-2:]
    slot = slot_ref[...].reshape(1, slot_ref.shape[0])
    dest, slot_bin = slot >> (bins.bit_length() - 1), slot & (bins - 1)
    place, local = places_of(dest, shard_rows, cap, dom, meta[0])
    place_ref[...] = place
    one_hot_rows(pick, place)
    which = lax.broadcasted_iota(I32, (CODE, dest.shape[1]), 0)
    digits = jnp.where(
        which == 0,
        local >> 4,
        jnp.where(which == 1, local & 15, jnp.where(which == 2, slot_bin, jnp.where(which == 3, 1, 0))),
    )
    digits = jnp.where(dest >= 0, digits, 0).astype(F32).astype(BF16)
    codes = mm(digits, pick[...], NT)
    packed = mm(pick[...], joined(raw), NN).astype(BF16)
    for index, out_ref in enumerate(outs):
        block = slice(index * cap, (index + 1) * cap)
        out_ref[:cap, :] = packed[block]
        out_ref[cap:, :] = jnp.zeros((CODE, out_ref.shape[1]), BF16)
        out_ref[cap:, :cap] = codes[:, block].astype(BF16)


def pack_next_body(cap, dom, meta, place_ref, *refs):
    raw, outs, pick = refs[: -dom - 1], refs[-dom - 1 : -1], refs[-1]
    one_hot_rows(pick, place_ref[...])
    packed = mm(pick[...], joined(raw), NN).astype(BF16)
    for index, out_ref in enumerate(outs):
        out_ref[...] = packed[index * cap : (index + 1) * cap]


def raw_specs(hold, share, chunk):
    first, width = chunk
    at = lambda k: lambda j, m: (0, m[1] * (share // LANES) + first // LANES + k)
    return [pl.BlockSpec((hold, LANES), at(k)) for k in range(width // LANES)]


def pack_first(meta, raw_images, slot, bins, dom, share, chunk):
    hold, _ = raw_images.shape
    width = chunk[1]
    cap = hold // dom
    slots = dom * cap
    specs = raw_specs(hold, share, chunk)
    return call(
        functools.partial(pack_first_body, dom, hold // 2, cap, bins),
        (1,),
        [pl.BlockSpec((hold,), lambda j, m: (0,))] + specs,
        [pl.BlockSpec((cap + CODE, width), lambda j, m: (0, 0))] * dom
        + [pl.BlockSpec((1, hold), lambda j, m: (0, 0))],
        [sds((cap + CODE, width), BF16)] * dom + [sds((1, hold), I32)],
        scratch=[pltpu.VMEM((slots, hold), BF16)],
        room=51,
        flops=2 * slots * hold * width,
        moved=4 * hold * width,
    )(meta, slot, *[raw_images] * len(specs))


def pack_next(meta, raw_images, place, dom, share, chunk):
    hold, _ = raw_images.shape
    width = chunk[1]
    cap = hold // dom
    slots = dom * cap
    specs = raw_specs(hold, share, chunk)
    return call(
        functools.partial(pack_next_body, cap, dom),
        (1,),
        [pl.BlockSpec((1, hold), lambda j, m: (0, 0))] + specs,
        [pl.BlockSpec((cap, width), lambda j, m: (0, 0))] * dom,
        [sds((cap, width), BF16)] * dom,
        scratch=[pltpu.VMEM((slots, hold), BF16)],
        room=51,
        flops=2 * slots * hold * width,
        moved=4 * hold * width,
    )(meta, place, *[raw_images] * len(specs))


def weigh(first, share, pick, wide, recv, meta, ctf_ref, inv_ref, out_ref):
    width = out_ref.shape[1]
    start = lax.rem(meta[1] * share, ctf_ref.shape[1]) + first
    columns = pl.ds(pl.multiple_of(start, LANES), width)
    table = jnp.concatenate(split3(ctf_ref[:, columns] * inv_ref[:, columns]), axis=0)
    out_ref[...] = (mm(pick, recv, NN) * mm(wide, table, NN)).astype(BF16)


def gather(pieces, whole, rows):
    for index, piece in enumerate(pieces):
        whole[index * rows : (index + 1) * rows, :] = piece[:rows, :]


def unpack_first_body(dom, bins, share, first, meta, *refs):
    pieces, recv_ref = refs[:dom], refs[-1]
    cap = pieces[0].shape[0] - CODE
    gather(pieces, recv_ref, cap)
    ctf_ref, inv_ref, out_ref, hot_ref, pick, wide = refs[dom:-1]
    shard_rows = out_ref.shape[0]
    got = jnp.concatenate([piece[cap:, :cap].astype(F32) for piece in pieces], axis=1)
    row = got[0:1] * 16.0 + got[1:2] + got[3:4] * 1024.0 - 1024.0
    one_hot_rows(pick, row.astype(I32))
    slot_bins = jnp.broadcast_to(got[2:3].astype(BF16), (8, got.shape[1]))
    down = mm(pick[...], slot_bins, NT)[:, 0:1].astype(I32)
    across = mm(slot_bins, pick[...], NT)[0:1].astype(I32)
    lane = lax.broadcasted_iota(I32, (shard_rows, 3 * bins), 1)
    wide[...] = jnp.where((lane & (bins - 1)) == down, 1.0, 0.0).astype(BF16)
    deep = lax.broadcasted_iota(I32, (3 * bins, shard_rows), 0)
    hot_ref[...] = jnp.where((deep & (bins - 1)) == across, 1.0, 0.0).astype(BF16)
    weigh(first, share, pick[...], wide[...], recv_ref[...], meta, ctf_ref, inv_ref, out_ref)


def unpack_next_body(dom, share, first, meta, *refs):
    recv_ref = refs[-1]
    gather(refs[:dom], recv_ref, refs[0].shape[0])
    pick_ref, wide_ref, ctf_ref, inv_ref, out_ref = refs[dom:-1]
    weigh(first, share, pick_ref[...], wide_ref[...], recv_ref[...], meta, ctf_ref, inv_ref, out_ref)


def unpack_first(meta, recv, ctf, inv, share, chunk):
    first, width = chunk
    dom = len(recv)
    slots = dom * (recv[0].shape[0] - CODE)
    rows = slots // 2
    bins, pix = ctf.shape
    whole = lambda shape: pl.BlockSpec(shape, lambda j, m: (0, 0))
    shapes = [(rows, width), (3 * bins, rows), (rows, slots), (rows, 3 * bins)]
    return call(
        functools.partial(unpack_first_body, dom, bins, share, first),
        (1,),
        [whole(recv[0].shape)] * dom + [whole(ctf.shape), whole(inv.shape)],
        [whole(s) for s in shapes],
        [sds(s, BF16) for s in shapes],
        scratch=[pltpu.VMEM((slots, width), BF16)],
        room=28,
        flops=2 * slots * rows * width,
        moved=2 * slots * width,
    )(meta, *recv, ctf, inv)


def unpack_next(meta, pick, wide, recv, ctf, inv, share, chunk):
    first, width = chunk
    dom = len(recv)
    slots = dom * recv[0].shape[0]
    rows = slots // 2
    whole = lambda shape: pl.BlockSpec(shape, lambda j, m: (0, 0))
    return call(
        functools.partial(unpack_next_body, dom, share, first),
        (1,),
        [whole(recv[0].shape)] * dom
        + [whole(pick.shape), whole(wide.shape), whole(ctf.shape), whole(inv.shape)],
        whole((rows, width)),
        sds((rows, width), BF16),
        scratch=[pltpu.VMEM((slots, width), BF16)],
        room=28,
        flops=2 * slots * rows * width,
        moved=2 * slots * width,
    )(meta, *recv, pick, wide, ctf, inv)


def energy_body(bins, count, last, meta, *refs):
    if last:
        pieces, refs = refs[:-6], refs[-6:]
        ctf_ref, inv_ref, _, _, panel_ref, _ = refs
    else:
        pieces, (ctf_ref, inv_ref, panel_ref, _) = refs[:-4], refs[-4:]
    width = panel_ref.shape[1]
    blocks = []
    for piece in pieces:
        for start in range(0, piece.shape[1], width):
            blocks.append((piece, start))
    step = pl.program_id(0)
    gain = ctf_ref[...] * ctf_ref[...] * inv_ref[...]
    gain3 = jnp.concatenate(split3(gain), axis=0)
    return step, blocks, gain3, width


def add_energy(panel, gain3):
    wide = panel.astype(F32)
    square = wide * wide
    high = square.astype(BF16)
    low = (square - high.astype(F32)).astype(BF16)
    return mm(high, gain3, NT) + mm(low, gain3, NT)


def near_energy_body(bins, count, meta, *refs):
    step, blocks, gain3, width = energy_body(bins, count, False, meta, *refs)
    panel_ref, total = refs[-2:]

    @pl.when(step == 0)
    def _():
        total[...] = jnp.zeros_like(total)

    for index, (piece, start) in enumerate(blocks):

        @pl.when(step == index)
        def _():
            panel = piece[:, start : start + width]
            panel_ref[...] = panel
            total[...] += add_energy(panel, gain3)


def far_energy_body(bins, count, meta, *refs):
    refs, total = refs[:-1], refs[-1]
    step, blocks, gain3, width = energy_body(bins, count, True, meta, *refs)
    before_ref, _, panel_ref, extra_ref = refs[-4:]

    @pl.when(step == 0)
    def _():
        total[...] = before_ref[...]

    for index, (piece, start) in enumerate(blocks):

        @pl.when(step == index)
        def _():
            panel = piece[:, start : start + width]
            panel_ref[...] = panel
            total[...] += add_energy(panel, gain3)

    @pl.when(step == count - 1)
    def _():
        whole = total[:, :bins] + total[:, bins : 2 * bins] + total[:, 2 * bins :]
        extra_ref[...] = jnp.concatenate(split3(-0.5 * whole), axis=1)


def energy(meta, pieces, ctf, inv, width, first, before=None, panels=None):
    rows = pieces[0].shape[0]
    count = sum(piece.shape[1] for piece in pieces) // width
    bins, pix = ctf.shape
    wrap = pix // width
    last = before is not None
    whole = lambda shape: pl.BlockSpec(shape, lambda j, m: (0, 0))
    table = lambda height: pl.BlockSpec(
        (height, width), lambda j, m: (0, lax.rem(m[0] ^ (first + j), wrap))
    )
    in_specs = [whole(piece.shape) for piece in pieces] + [table(bins), table(1)]
    operands = [meta, *pieces, ctf, inv]
    alias = None
    if last:
        in_specs += [whole(before.shape), pl.BlockSpec(memory_space=pl.ANY)]
        alias = {len(operands) + 1: 0}
        operands += [before, panels]
    sums = sds((rows, 3 * bins), BF16 if last else F32)
    return call(
        functools.partial(far_energy_body if last else near_energy_body, bins, count),
        (count,),
        in_specs,
        [pl.BlockSpec((rows, width), lambda j, m: (0, m[0] ^ (first + j))), whole(sums.shape)],
        [sds((rows, 2 * pix), BF16), sums],
        scratch=[pltpu.VMEM((rows, 3 * bins), F32)] if last else [],
        alias=alias,
        flops=2 * 4 * rows * bins * count * width * 3,
        moved=4 * rows * count * width,
    )(*operands)


def score_body(parts, used, first, last, meta, *refs):
    own, sib, panel_ref, refs = (
        refs[:parts],
        refs[parts : 2 * parts],
        refs[2 * parts],
        refs[2 * parts + 1 :],
    )
    hot_own = hot_sib = None
    if first:
        acc_out, full_ref = refs
    elif last:
        acc_ref, _, shifted_ref, stat_ref, full_ref = refs
    elif used is None:
        acc_ref, _, acc_out, full_ref = refs
    else:
        acc_ref, hot_own, hot_sib, extra_ref, acc_out = refs
    half = pl.num_programs(0) // 2

    def tile(sources, hot):
        block = jnp.concatenate([source[...] for source in sources], axis=1)
        if used is None or last:
            full_ref[...] = block
        if last:
            block = block[:, used[0] : used[0] + used[1]]
        panel = panel_ref[...] if used is None else panel_ref[:, used[0] : used[0] + used[1]]
        total = mm(panel, block, NT)
        if not first:
            total = acc_ref[...] + total
        if hot is not None:
            total = total + mm(extra_ref[...], hot[...], NN)
        if not last:
            acc_out[...] = total
            return
        peak = jnp.max(total, axis=0, keepdims=True)
        shifted = jnp.exp(total - peak)
        shifted_ref[...] = shifted
        mass = jnp.sum(shifted, axis=0, keepdims=True)
        which = lax.broadcasted_iota(I32, stat_ref.shape, 0)
        stat_ref[...] = jnp.where(which == 0, peak, mass)

    @pl.when(pl.program_id(0) < half)
    def _():
        tile(own, hot_own)

    @pl.when(pl.program_id(0) >= half)
    def _():
        tile(sib, hot_sib)


def score(meta, at, own, sib, panels, width, acc=None, full=None, used=None, hots=None, extra=None):
    rows = own[0].shape[0]
    parts = len(own)
    tile = 256
    half = rows // tile
    count, columns = panels.shape
    first, last = acc is None, used is not None and hots is None
    store = used is None or last
    fronts = [pl.BlockSpec((tile, v.shape[1]), lambda j, m: (jnp.minimum(j, half - 1), 0)) for v in own]
    backs = [pl.BlockSpec((tile, v.shape[1]), lambda j, m: (jnp.maximum(j - half, 0), 0)) for v in own]
    acc_spec = pl.BlockSpec((count, tile), lambda j, m: (0, j))
    full_spec = pl.BlockSpec((tile, width), lambda j, m: (j, at(m)))
    in_specs = fronts + backs + [pl.BlockSpec((count, width), lambda j, m: (0, at(m)))]
    operands = [meta, *own, *sib, panels]
    alias = {}
    if not first:
        in_specs += [acc_spec]
        alias = {len(operands): 0}
        operands += [acc]
        if store:
            in_specs += [pl.BlockSpec(memory_space=pl.ANY)]
            alias[len(operands)] = 2 if last else 1
            operands += [full]
    full_shape = sds((2 * rows, columns), BF16)
    acc_shape = sds((count, 2 * rows), F32)
    out_specs, out_shape = [acc_spec, full_spec], [acc_shape, full_shape]
    if last:
        out_specs = [acc_spec, pl.BlockSpec((8, tile), lambda j, m: (0, j)), full_spec]
        out_shape = [acc_shape, sds((8, 2 * rows), F32), full_shape]
    elif not store:
        depth = extra.shape[1]
        in_specs += [
            pl.BlockSpec((depth, tile), lambda j, m: (0, jnp.minimum(j, half - 1))),
            pl.BlockSpec((depth, tile), lambda j, m: (0, jnp.maximum(j - half, 0))),
            pl.BlockSpec((count, depth), lambda j, m: (0, 0)),
        ]
        operands += [*hots, extra]
        out_specs, out_shape = acc_spec, acc_shape
    return call(
        functools.partial(score_body, parts, used, first, last),
        (2 * half,),
        in_specs,
        out_specs,
        out_shape,
        alias=alias,
        room=16,
        flops=2 * count * 2 * rows * width,
        moved=8 * count * 2 * rows + 8 * rows * width,
    )(*operands)


def merge_body(meta, mine_ref, other_ref, out_ref):
    rows = mine_ref.shape[1] // 2
    other = other_ref[...]
    other = jnp.concatenate([other[:, rows:], other[:, :rows]], axis=1)
    mine = mine_ref[...]
    peak = jnp.maximum(mine[0:1], other[0:1])
    mass = mine[1:2] * jnp.exp(mine[0:1] - peak) + other[1:2] * jnp.exp(other[0:1] - peak)
    which = lax.broadcasted_iota(I32, out_ref.shape, 0)
    out_ref[...] = jnp.where(which == 0, peak, mass)


def add_body(meta, mine_ref, other_ref, out_ref):
    out_ref[...] = (mine_ref[...].astype(F32) + other_ref[...].astype(F32)).astype(BF16)


def pairwise(body, meta, mine, other):
    spec = pl.BlockSpec(mine.shape, lambda j, m: (0, 0))
    return call(body, (1,), [spec, spec], spec, sds(mine.shape, mine.dtype), room=4)(
        meta, mine, other
    )


merge = functools.partial(pairwise, merge_body)
add_pair = functools.partial(pairwise, add_body)


def class_body(kind, steps, meta, *refs):
    if kind == "first":
        (shifted_ref, stat_ref), four = refs[:2], refs[2:6]
        hot_own, hot_sib, full_ref = refs[6:9]
        outs, (post_ref, log_ref, mass_ref) = refs[9 : 9 + steps], refs[9 + steps :]

        @pl.when(pl.program_id(0) == 0)
        def _():
            stats = [ref[...] for ref in four]
            peaks = [s[0:1] for s in stats]
            peak = jnp.maximum(jnp.maximum(peaks[0], peaks[1]), jnp.maximum(peaks[2], peaks[3]))
            parts = [s[1:2] * jnp.exp(p - peak) for s, p in zip(stats, peaks)]
            mass = (parts[0] + parts[1]) + (parts[2] + parts[3])
            factor = jnp.exp(stat_ref[0:1] - peak) / mass
            post_ref[...] = (shifted_ref[...] * factor).astype(BF16)
            log_ref[...] = (peak + jnp.log(mass))[:, : log_ref.shape[1]]
            bins, rows = mass_ref.shape[0], hot_own.shape[1]
            weights = mm(hot_own[:bins, :], post_ref[:, :rows], NT)
            weights = weights + mm(hot_sib[:bins, :], post_ref[:, rows:], NT)
            mass_ref[...] = weights.astype(BF16)

    else:
        (post_ref, full_ref), outs = refs[:2], refs[2:]
    for step, out_ref in enumerate(outs):

        @pl.when(pl.program_id(0) == step)
        def _():
            out_ref[...] = mm(post_ref[...], full_ref[...], NN).astype(out_ref.dtype)


def class_part(meta, kind, offset, steps, full, post=None, shifted=None, stats=None, hots=None, bins=0):
    rows, columns = full.shape
    width = columns // 8
    count = (shifted if post is None else post).shape[0]
    whole = lambda shape: pl.BlockSpec(shape, lambda j, m: (0, 0))
    full_spec = pl.BlockSpec((rows, width), lambda j, m: (0, m[offset + j]))
    out_specs = [whole((count, width))] * steps
    kept = steps // 2 if kind == "rest" else 0
    types = [BF16] * (steps - kept) + [F32] * kept
    out_shape = [sds((count, width), dtype) for dtype in types]
    if kind == "first":
        operands = [shifted, *stats, *hots, full]
        in_specs = [whole(shifted.shape)] + [whole(stats[0].shape)] * 5
        in_specs += [whole(hots[0].shape)] * 2 + [full_spec]
        out_specs += [whole((count, rows)), whole((1, rows // 2)), whole((bins, count))]
        out_shape += [sds((count, rows), BF16), sds((1, rows // 2), F32), sds((bins, count), BF16)]
    else:
        operands = [post, full]
        in_specs = [whole(post.shape), full_spec]
    return call(
        functools.partial(class_body, kind, steps),
        (steps,),
        in_specs,
        out_specs,
        out_shape,
        room=22 if kind == "first" else 28,
        flops=2 * count * rows * width * steps,
        moved=2 * rows * width * steps + 4 * count * (rows + width * steps),
    )(meta, *operands)


def own_half_body(tile, meta, keep_ref, c_ref, a_ref, out_ref):
    rows = pl.ds(pl.multiple_of(pl.program_id(0) * tile, tile), tile)
    out_ref[...] = keep_ref[rows, :] + c_ref[rows, :].astype(F32) + a_ref[rows, :].astype(F32)


def own_half(meta, keep, got_c, got_a):
    count, width = keep.shape
    parts = 3
    tile = count // parts
    return call(
        functools.partial(own_half_body, tile),
        (parts,),
        [pl.BlockSpec(memory_space=pltpu.VMEM)] * 3,
        pl.BlockSpec((tile, width), lambda j, m: (lax.rem(m[0], 2) * parts + j, 0)),
        sds((2 * count, width), F32),
        room=8,
    )(meta, keep, got_c, got_a)


def two_by_two(raw_images, defocus_bin, dest_row, ctf_table, inv_noise, panels):
    dom, turns = lax.axis_size("dom"), lax.axis_size("rot")
    device, plane = lax.axis_index("dom"), lax.axis_index("rot")
    bins = ctf_table.shape[0]
    columns = raw_images.shape[1]
    chip, core = device // 2, device % 2

    def block(apart, half):
        return (chip ^ apart) * 2 + half

    x_first, y_second = block(1, 0), block(2, 1)
    x_second, y_first = block(1, 1), block(2, 0)
    even = core == 0
    order = [
        device,
        plane,
        block(3, 0),
        block(3, 1),
        jnp.where(even, x_first, y_second),
        jnp.where(even, y_second, x_first),
        block(0, 1 - core),
        jnp.where(even, y_first, x_second),
        jnp.where(even, x_second, y_first),
        block(0, core),
    ]
    meta = jnp.stack(order).astype(I32)
    inv = inv_noise[None, :]

    def across(value, apart):
        return lax.ppermute(value, "dom", [(i, i ^ apart) for i in range(dom)])

    def by_core(value, when_even, when_odd):
        pairs = [(i, i ^ (when_odd if i % 2 else when_even)) for i in range(dom)]
        return lax.ppermute(value, "dom", pairs)

    def onward(value):
        return lax.ppermute(value, "rot", [(i, (i + 1) % turns) for i in range(turns)])

    width = columns // turns
    cut = width * 3 // 8
    chunk_a, chunk_b = (0, cut), (cut, width - cut)

    def exchange(blocks):
        far_first = [across(blocks[apart], apart) for apart in (6, 7, 4, 2, 5, 3, 1)]
        return far_first + [blocks[0]]

    slot = jnp.where(dest_row >= 0, dest_row * bins + defocus_bin, -1)
    *send_a, place = pack_first(meta, raw_images, slot, bins, dom, width, chunk_a)
    recv_a = exchange(send_a)
    swapped, place = lax.optimization_barrier((across(panels, 1), place))
    send_b = pack_next(meta, raw_images, place, dom, width, chunk_b)
    together = lax.optimization_barrier

    count = panels.shape[0] // 2
    mine = lax.dynamic_slice_in_dim(panels, core * count, count, 0)
    other = lax.dynamic_slice_in_dim(swapped, core * count, count, 0)
    near = jnp.concatenate([mine, other], axis=1)

    recv_a, send_b, near = together((recv_a, send_b, near))
    share_a, hot, pick, wide = unpack_first(meta, recv_a, ctf_table, inv, width, chunk_a)
    share_a, send_b = together((share_a, send_b))
    a1, recv_b = onward(share_a), exchange(send_b)
    piece = near.shape[1] // 2
    panel_full, energies = energy(meta, [near], ctf_table, inv, piece, 0)
    a1, recv_b[:2], panel_full, energies = together((a1, recv_b[:2], panel_full, energies))
    a2 = onward(a1)
    recv_b, near = together((recv_b, near))
    share_b = unpack_next(meta, pick, wide, recv_b, ctf_table, inv, width, chunk_b)
    a2, share_b = together((a2, share_b))
    by_x, by_y = across(near, 2), across(near, 4)
    a3, b1 = onward(a2), onward(share_b)
    sib0, hots = [across(share_a, 1), across(share_b, 1)], [hot, across(hot, 1)]
    sib1, sib2 = [across(a1, 1), across(b1, 1)], [across(a2, 1)]
    piece = near.shape[1] // 2
    far_y, far_x = across(by_x[:, :piece], 4), across(by_y[:, piece:], 2)
    b2 = onward(b1)
    panel_full, extra = energy(
        meta, [by_x, by_y, far_y, far_x], ctf_table, inv, piece, 2, energies, panel_full
    )
    a3, b2, panel_full, hots = together((a3, b2, panel_full, hots))
    b3 = onward(b2)
    sib2 = sib2 + [across(b2, 1)]

    def share(turn):
        return lambda m: lax.rem(m[1] + turns - turn, turns)

    acc, full = score(meta, share(0), [share_a, share_b], sib0, panel_full, width)
    acc, full = score(meta, share(1), [a1, b1], sib1, panel_full, width, acc, full)
    acc, full = score(meta, share(2), [a2, b2], sib2, panel_full, width, acc, full)
    final = share(turns - 1)
    a3_sib = across(a3, 1)
    acc = score(
        meta, final, [a3], [a3_sib], panel_full, width, acc, None, chunk_a, hots, extra
    )
    b3, acc = together((b3, acc))
    shifted, stat, full = score(
        meta,
        final,
        [a3, b3],
        [a3_sib, across(b3, 1)],
        panel_full,
        width,
        acc,
        full,
        chunk_b,
    )

    pair = merge(meta, stat, across(stat, 1))
    others = [
        lax.ppermute(pair, "rot", [(i, i ^ apart) for i in range(turns)]) for apart in (1, 2, 3)
    ]
    to_x, to_y, post, log_evidence, mass = class_part(
        meta, "first", 2, 2, full, None, shifted, [stat, pair, *others], hots, bins
    )
    mass_x = across(mass, 2)
    got_x, got_y = across(to_x, 2), across(to_y, 4)
    six = class_part(meta, "rest", 4, 6, full, post)
    got_x, got_y, six, mass_x = together((got_x, got_y, six, mass_x))
    send_c, send_d, give, a_sum, b_sum, keep = six
    mass = add_pair(meta, mass, mass_x)
    mass_y = across(mass, 4)
    got_c, got_d = by_core(send_c, 2, 4), by_core(send_d, 5, 3)
    down, left = got_x.astype(F32), got_y.astype(F32)
    message_a = (a_sum + jnp.where(even, down, left)).astype(BF16)
    message_b = (b_sum + jnp.where(even, left, down)).astype(BF16)
    got_a, got_b = by_core(message_a, 4, 2), by_core(message_b, 3, 5)
    got_self = across(give, 1)
    mass_y, got_a, got_c = together((mass_y, got_a, got_c))
    mass = mass.astype(F32) + mass_y.astype(F32)
    mass_other = across(mass, 1)
    bin_weights = jnp.where(
        even,
        jnp.concatenate([mass, mass_other], axis=1),
        jnp.concatenate([mass_other, mass], axis=1),
    )
    sums = own_half(meta, keep, got_c, got_a)
    bin_weights, got_b = together((bin_weights, got_b))
    other_half = got_self.astype(F32) + got_d.astype(F32) + got_b.astype(F32)
    class_sums = lax.dynamic_update_slice_in_dim(sums, other_half, (1 - core) * count, 0).T
    return class_sums, bin_weights, log_evidence.reshape(-1)


def energy_block(gain_block, panel_piece):
    widened = panel_piece.astype(jnp.float32)
    return lax.dot_general(
        gain_block, widened * widened, (((1,), (1,)), ((), ())), precision=lax.Precision.HIGHEST
    )


def on_device(raw_images, defocus_bin, dest_row, ctf_table, inv_noise, panels):
    dom_count = lax.axis_size("dom")
    bin_count = ctf_table.shape[0]
    columns = raw_images.shape[1]
    hold_rows = raw_images.shape[0]
    shard_rows = hold_rows // 2
    capacity = 2 * shard_rows // dom_count
    is_live = dest_row >= 0
    target = jnp.where(is_live, dest_row // shard_rows, dom_count)
    local_row = dest_row % shard_rows
    marks = (target[:, None] == jnp.arange(dom_count, dtype=jnp.int32)[None, :]).astype(jnp.int32)
    slot_rank = jnp.sum((jnp.cumsum(marks, axis=0) - marks) * marks, axis=1)
    row_code = jnp.where(is_live, local_row * bin_count + defocus_bin, -1)
    padded_images = jnp.concatenate([raw_images, jnp.zeros((1, columns), raw_images.dtype)], axis=0)
    padded_code = jnp.concatenate([row_code, jnp.full((1,), -1, jnp.int32)], axis=0)
    position = jnp.where(is_live, target * capacity + slot_rank, dom_count * capacity)
    slot_count = dom_count * capacity
    source = (
        jnp.full((slot_count,), hold_rows, jnp.int32)
        .at[position]
        .set(jnp.arange(hold_rows, dtype=jnp.int32), mode="drop")
    )
    send_images = padded_images[source].reshape(dom_count, capacity, columns)
    send_code = padded_code[source].reshape(dom_count, capacity)
    recv_images, recv_code = (
        lax.all_to_all(send_images, "dom", split_axis=0, concat_axis=0, tiled=True),
        lax.all_to_all(send_code, "dom", split_axis=0, concat_axis=0, tiled=True),
    )
    flat_images = recv_images.reshape(-1, columns)
    flat_code = recv_code.reshape(-1)
    arrived = flat_code >= 0
    row_of = jnp.where(arrived, flat_code // bin_count, shard_rows)
    row_order = (
        jnp.zeros((shard_rows,), jnp.int32)
        .at[row_of]
        .set(jnp.arange(flat_code.shape[0], dtype=jnp.int32), mode="drop")
    )
    images = flat_images[row_order]
    bin_ids = flat_code[row_order] % bin_count
    bin_table = (bin_ids[:, None] == jnp.arange(bin_count, dtype=jnp.int32)[None, :]).astype(
        jnp.float32
    )
    ctf_rows = jnp.dot(bin_table, ctf_table, precision=lax.Precision.HIGHEST)
    factor = ctf_rows * inv_noise[None, :]
    weighted = (images.astype(jnp.float32) * jnp.concatenate([factor, factor], axis=1)).astype(
        jnp.bfloat16
    )
    gain_half = ctf_table * ctf_table * inv_noise[None, :]
    gain_full = jnp.concatenate([gain_half, gain_half], axis=1)
    panel_piece = lax.all_gather(panels, "dom", axis=1, tiled=True)
    col_block = weighted
    cross_term = lax.dot_general(
        col_block, panel_piece, (((1,), (1,)), ((), ())), preferred_element_type=jnp.float32
    )
    energy = energy_block(gain_full, panel_piece)
    scores = cross_term - 0.5 * jnp.dot(bin_table, energy, precision=lax.Precision.HIGHEST)
    local_peak = jnp.max(scores, axis=1)
    row_peak = lax.pmax(local_peak, "rot")
    shifted = jnp.exp(scores - row_peak[:, None])
    row_total = lax.psum(jnp.sum(shifted, axis=1), "rot")
    posterior = (shifted / row_total[:, None]).astype(jnp.bfloat16)
    log_evidence = row_peak + jnp.log(row_total)
    col_block = weighted
    class_sums = lax.psum_scatter(
        lax.dot_general(
            col_block, posterior, (((0,), (0,)), ((), ())), preferred_element_type=jnp.float32
        ).astype(jnp.bfloat16),
        "dom",
        scatter_dimension=0,
        tiled=True,
    ).astype(jnp.float32)
    local_mass = lax.dot_general(
        bin_table.astype(jnp.bfloat16),
        posterior,
        (((0,), (0,)), ((), ())),
        preferred_element_type=jnp.float32,
    )
    bin_weights = lax.psum(local_mass.astype(jnp.bfloat16), "dom").astype(jnp.float32)
    return (class_sums, bin_weights, log_evidence)


def solution(mesh):
    small = mesh.shape["dom"] == 8 and mesh.shape["rot"] == 4
    return jax.shard_map(
        two_by_two if small else on_device,
        mesh=mesh,
        in_specs=(P("dom", None), P("dom"), P("dom"), P(), P(), P("rot", "dom")),
        out_specs=(P("dom", "rot"), P(None, "rot"), P("dom")),
        check_vma=False,
    )
```

```python
import functools

import jax
import jax.numpy as jnp
from jax import lax
from jax.experimental import pallas as pl
from jax.experimental.pallas import tpu as pltpu
from jax.sharding import PartitionSpec as P

NN = (((1,), (0,)), ((), ()))
NT = (((1,), (1,)), ((), ()))
F32, BF16, I32 = jnp.float32, jnp.bfloat16, jnp.int32
CODE = 16
LANES = 128
MIB = 1024 * 1024


def mm(a, b, dims):
    return lax.dot_general(a, b, dims, preferred_element_type=F32)


def split3(x):
    hi = x.astype(BF16)
    rest = x - hi.astype(F32)
    mid = rest.astype(BF16)
    low = (rest - mid.astype(F32)).astype(BF16)
    return hi, mid, low


def call(body, grid, in_specs, out_specs, out_shape, scratch=(), alias=None, flops=0, moved=0, room=24):
    return pl.pallas_call(
        body,
        grid_spec=pltpu.PrefetchScalarGridSpec(
            num_scalar_prefetch=1,
            grid=grid,
            in_specs=in_specs,
            out_specs=out_specs,
            scratch_shapes=list(scratch),
        ),
        out_shape=out_shape,
        input_output_aliases=alias or {},
        compiler_params=pltpu.CompilerParams(vmem_limit_bytes=room * MIB),
        cost_estimate=pl.CostEstimate(
            flops=flops // 16, bytes_accessed=moved // 16, transcendentals=0
        ),
    )


def sds(shape, dtype):
    return jax.ShapeDtypeStruct(shape, dtype)


def one_hot_rows(out_ref, wanted):
    rows, width = out_ref.shape
    short = wanted.astype(jnp.int16)
    one, zero = jnp.ones((), BF16), jnp.zeros((), BF16)
    step = 256 if rows % 256 == 0 else rows
    for start in range(0, rows, step):
        index = lax.broadcasted_iota(jnp.int16, (step, width), 0) + jnp.int16(start)
        out_ref[start : start + step, :] = jnp.where(index == short, one, zero)


def places_of(dest, shard_rows, cap, dom, device):
    hold = dest.shape[1]
    low = lax.broadcasted_iota(I32, (dom, hold), 0) * shard_rows
    inside = jnp.logical_and(dest >= low, dest < low + shard_rows)
    marks = jnp.where(inside, 1.0, 0.0)
    local = dest - jnp.sum(jnp.where(inside, low, 0), axis=0, keepdims=True)
    lanes = 128
    before = lax.broadcasted_iota(I32, (lanes, lanes), 0) < lax.broadcasted_iota(
        I32, (lanes, lanes), 1
    )
    upper = jnp.where(before, 1.0, 0.0).astype(BF16)
    apart = lax.broadcasted_iota(I32, (dom, 1), 0) ^ device
    carry = apart.astype(F32) * cap + 1.0
    found = []
    for start in range(0, hold, lanes):
        part = marks[:, start : start + lanes]
        rank = mm(part.astype(BF16), upper, NN) + carry
        found.append(jnp.sum(jnp.where(part > 0, rank, 0.0), axis=0, keepdims=True))
        carry = carry + jnp.sum(part, axis=1, keepdims=True)
    return jnp.concatenate(found, axis=1).astype(I32) - 1, local


def joined(refs):
    return jnp.concatenate([ref[...] for ref in refs], axis=1)


def pack_first_body(dom, shard_rows, cap, bins, meta, slot_ref, *refs):
    raw, outs, (place_ref, pick) = refs[: -dom - 2], refs[-dom - 2 : -2], refs[-2:]
    slot = slot_ref[...].reshape(1, slot_ref.shape[0])
    dest, slot_bin = slot >> (bins.bit_length() - 1), slot & (bins - 1)
    place, local = places_of(dest, shard_rows, cap, dom, meta[0])
    place_ref[...] = place
    one_hot_rows(pick, place)
    which = lax.broadcasted_iota(I32, (CODE, dest.shape[1]), 0)
    digits = jnp.where(
        which == 0,
        local >> 4,
        jnp.where(which == 1, local & 15, jnp.where(which == 2, slot_bin, jnp.where(which == 3, 1, 0))),
    )
    digits = jnp.where(dest >= 0, digits, 0).astype(F32).astype(BF16)
    codes = mm(digits, pick[...], NT)
    packed = mm(pick[...], joined(raw), NN).astype(BF16)
    for index, out_ref in enumerate(outs):
        block = slice(index * cap, (index + 1) * cap)
        out_ref[:cap, :] = packed[block]
        out_ref[cap:, :] = jnp.zeros((CODE, out_ref.shape[1]), BF16)
        out_ref[cap:, :cap] = codes[:, block].astype(BF16)


def pack_next_body(cap, dom, meta, place_ref, *refs):
    raw, outs, pick = refs[: -dom - 1], refs[-dom - 1 : -1], refs[-1]
    one_hot_rows(pick, place_ref[...])
    packed = mm(pick[...], joined(raw), NN).astype(BF16)
    for index, out_ref in enumerate(outs):
        out_ref[...] = packed[index * cap : (index + 1) * cap]


def raw_specs(hold, share, chunk):
    first, width = chunk
    at = lambda k: lambda j, m: (0, m[1] * (share // LANES) + first // LANES + k)
    return [pl.BlockSpec((hold, LANES), at(k)) for k in range(width // LANES)]


def pack_first(meta, raw_images, slot, bins, dom, share, chunk):
    hold, _ = raw_images.shape
    width = chunk[1]
    cap = hold // dom
    slots = dom * cap
    specs = raw_specs(hold, share, chunk)
    return call(
        functools.partial(pack_first_body, dom, hold // 2, cap, bins),
        (1,),
        [pl.BlockSpec((hold,), lambda j, m: (0,))] + specs,
        [pl.BlockSpec((cap + CODE, width), lambda j, m: (0, 0))] * dom
        + [pl.BlockSpec((1, hold), lambda j, m: (0, 0))],
        [sds((cap + CODE, width), BF16)] * dom + [sds((1, hold), I32)],
        scratch=[pltpu.VMEM((slots, hold), BF16)],
        room=51,
        flops=2 * slots * hold * width,
        moved=4 * hold * width,
    )(meta, slot, *[raw_images] * len(specs))


def pack_next(meta, raw_images, place, dom, share, chunk):
    hold, _ = raw_images.shape
    width = chunk[1]
    cap = hold // dom
    slots = dom * cap
    specs = raw_specs(hold, share, chunk)
    return call(
        functools.partial(pack_next_body, cap, dom),
        (1,),
        [pl.BlockSpec((1, hold), lambda j, m: (0, 0))] + specs,
        [pl.BlockSpec((cap, width), lambda j, m: (0, 0))] * dom,
        [sds((cap, width), BF16)] * dom,
        scratch=[pltpu.VMEM((slots, hold), BF16)],
        room=51,
        flops=2 * slots * hold * width,
        moved=4 * hold * width,
    )(meta, place, *[raw_images] * len(specs))


def weigh(first, share, pick, wide, recv, meta, ctf_ref, inv_ref, out_ref):
    width = out_ref.shape[1]
    start = lax.rem(meta[1] * share, ctf_ref.shape[1]) + first
    columns = pl.ds(pl.multiple_of(start, LANES), width)
    table = jnp.concatenate(split3(ctf_ref[:, columns] * inv_ref[:, columns]), axis=0)
    out_ref[...] = (mm(pick, recv, NN) * mm(wide, table, NN)).astype(BF16)


def gather(pieces, whole, rows):
    for index, piece in enumerate(pieces):
        whole[index * rows : (index + 1) * rows, :] = piece[:rows, :]


def unpack_first_body(dom, bins, share, first, meta, *refs):
    pieces, recv_ref = refs[:dom], refs[-1]
    cap = pieces[0].shape[0] - CODE
    gather(pieces, recv_ref, cap)
    ctf_ref, inv_ref, out_ref, hot_ref, pick, wide = refs[dom:-1]
    shard_rows = out_ref.shape[0]
    got = jnp.concatenate([piece[cap:, :cap].astype(F32) for piece in pieces], axis=1)
    row = got[0:1] * 16.0 + got[1:2] + got[3:4] * 1024.0 - 1024.0
    one_hot_rows(pick, row.astype(I32))
    slot_bins = jnp.broadcast_to(got[2:3].astype(BF16), (8, got.shape[1]))
    down = mm(pick[...], slot_bins, NT)[:, 0:1].astype(I32)
    across = mm(slot_bins, pick[...], NT)[0:1].astype(I32)
    lane = lax.broadcasted_iota(I32, (shard_rows, 3 * bins), 1)
    wide[...] = jnp.where((lane & (bins - 1)) == down, 1.0, 0.0).astype(BF16)
    deep = lax.broadcasted_iota(I32, (3 * bins, shard_rows), 0)
    hot_ref[...] = jnp.where((deep & (bins - 1)) == across, 1.0, 0.0).astype(BF16)
    weigh(first, share, pick[...], wide[...], recv_ref[...], meta, ctf_ref, inv_ref, out_ref)


def unpack_next_body(dom, share, first, meta, *refs):
    recv_ref = refs[-1]
    gather(refs[:dom], recv_ref, refs[0].shape[0])
    pick_ref, wide_ref, ctf_ref, inv_ref, out_ref = refs[dom:-1]
    weigh(first, share, pick_ref[...], wide_ref[...], recv_ref[...], meta, ctf_ref, inv_ref, out_ref)


def unpack_first(meta, recv, ctf, inv, share, chunk):
    first, width = chunk
    dom = len(recv)
    slots = dom * (recv[0].shape[0] - CODE)
    rows = slots // 2
    bins, pix = ctf.shape
    whole = lambda shape: pl.BlockSpec(shape, lambda j, m: (0, 0))
    shapes = [(rows, width), (3 * bins, rows), (rows, slots), (rows, 3 * bins)]
    return call(
        functools.partial(unpack_first_body, dom, bins, share, first),
        (1,),
        [whole(recv[0].shape)] * dom + [whole(ctf.shape), whole(inv.shape)],
        [whole(s) for s in shapes],
        [sds(s, BF16) for s in shapes],
        scratch=[pltpu.VMEM((slots, width), BF16)],
        room=28,
        flops=2 * slots * rows * width,
        moved=2 * slots * width,
    )(meta, *recv, ctf, inv)


def unpack_next(meta, pick, wide, recv, ctf, inv, share, chunk):
    first, width = chunk
    dom = len(recv)
    slots = dom * recv[0].shape[0]
    rows = slots // 2
    whole = lambda shape: pl.BlockSpec(shape, lambda j, m: (0, 0))
    return call(
        functools.partial(unpack_next_body, dom, share, first),
        (1,),
        [whole(recv[0].shape)] * dom
        + [whole(pick.shape), whole(wide.shape), whole(ctf.shape), whole(inv.shape)],
        whole((rows, width)),
        sds((rows, width), BF16),
        scratch=[pltpu.VMEM((slots, width), BF16)],
        room=28,
        flops=2 * slots * rows * width,
        moved=2 * slots * width,
    )(meta, *recv, pick, wide, ctf, inv)


def energy_body(bins, count, last, meta, *refs):
    if last:
        pieces, refs = refs[:-6], refs[-6:]
        ctf_ref, inv_ref, _, _, panel_ref, _ = refs
    else:
        pieces, (ctf_ref, inv_ref, panel_ref, _) = refs[:-4], refs[-4:]
    width = panel_ref.shape[1]
    blocks = []
    for piece in pieces:
        for start in range(0, piece.shape[1], width):
            blocks.append((piece, start))
    step = pl.program_id(0)
    gain = ctf_ref[...] * ctf_ref[...] * inv_ref[...]
    gain3 = jnp.concatenate(split3(gain), axis=0)
    return step, blocks, gain3, width


def add_energy(panel, gain3):
    wide = panel.astype(F32)
    square = wide * wide
    high = square.astype(BF16)
    low = (square - high.astype(F32)).astype(BF16)
    return mm(high, gain3, NT) + mm(low, gain3, NT)


def near_energy_body(bins, count, meta, *refs):
    step, blocks, gain3, width = energy_body(bins, count, False, meta, *refs)
    panel_ref, total = refs[-2:]

    @pl.when(step == 0)
    def _():
        total[...] = jnp.zeros_like(total)

    for index, (piece, start) in enumerate(blocks):

        @pl.when(step == index)
        def _():
            panel = piece[:, start : start + width]
            panel_ref[...] = panel
            total[...] += add_energy(panel, gain3)


def far_energy_body(bins, count, meta, *refs):
    refs, total = refs[:-1], refs[-1]
    step, blocks, gain3, width = energy_body(bins, count, True, meta, *refs)
    before_ref, _, panel_ref, extra_ref = refs[-4:]

    @pl.when(step == 0)
    def _():
        total[...] = before_ref[...]

    for index, (piece, start) in enumerate(blocks):

        @pl.when(step == index)
        def _():
            panel = piece[:, start : start + width]
            panel_ref[...] = panel
            total[...] += add_energy(panel, gain3)

    @pl.when(step == count - 1)
    def _():
        whole = total[:, :bins] + total[:, bins : 2 * bins] + total[:, 2 * bins :]
        extra_ref[...] = jnp.concatenate(split3(-0.5 * whole), axis=1)


def energy(meta, pieces, ctf, inv, width, first, before=None, panels=None):
    rows = pieces[0].shape[0]
    count = sum(piece.shape[1] for piece in pieces) // width
    bins, pix = ctf.shape
    wrap = pix // width
    last = before is not None
    whole = lambda shape: pl.BlockSpec(shape, lambda j, m: (0, 0))
    table = lambda height: pl.BlockSpec(
        (height, width), lambda j, m: (0, lax.rem(m[0] ^ (first + j), wrap))
    )
    in_specs = [whole(piece.shape) for piece in pieces] + [table(bins), table(1)]
    operands = [meta, *pieces, ctf, inv]
    alias = None
    if last:
        in_specs += [whole(before.shape), pl.BlockSpec(memory_space=pl.ANY)]
        alias = {len(operands) + 1: 0}
        operands += [before, panels]
    sums = sds((rows, 3 * bins), BF16 if last else F32)
    return call(
        functools.partial(far_energy_body if last else near_energy_body, bins, count),
        (count,),
        in_specs,
        [pl.BlockSpec((rows, width), lambda j, m: (0, m[0] ^ (first + j))), whole(sums.shape)],
        [sds((rows, 2 * pix), BF16), sums],
        scratch=[pltpu.VMEM((rows, 3 * bins), F32)] if last else [],
        alias=alias,
        flops=2 * 4 * rows * bins * count * width * 3,
        moved=4 * rows * count * width,
    )(*operands)


def score_body(parts, used, first, last, meta, *refs):
    own, sib, panel_ref, refs = (
        refs[:parts],
        refs[parts : 2 * parts],
        refs[2 * parts],
        refs[2 * parts + 1 :],
    )
    hot_own = hot_sib = None
    if first:
        acc_out, full_ref = refs
    elif last:
        acc_ref, _, shifted_ref, stat_ref, full_ref = refs
    elif used is None:
        acc_ref, _, acc_out, full_ref = refs
    else:
        acc_ref, hot_own, hot_sib, extra_ref, acc_out = refs
    half = pl.num_programs(0) // 2

    def tile(sources, hot):
        block = jnp.concatenate([source[...] for source in sources], axis=1)
        if used is None or last:
            full_ref[...] = block
        if last:
            block = block[:, used[0] : used[0] + used[1]]
        panel = panel_ref[...] if used is None else panel_ref[:, used[0] : used[0] + used[1]]
        total = mm(panel, block, NT)
        if not first:
            total = acc_ref[...] + total
        if hot is not None:
            total = total + mm(extra_ref[...], hot[...], NN)
        if not last:
            acc_out[...] = total
            return
        peak = jnp.max(total, axis=0, keepdims=True)
        shifted = jnp.exp(total - peak)
        shifted_ref[...] = shifted
        mass = jnp.sum(shifted, axis=0, keepdims=True)
        which = lax.broadcasted_iota(I32, stat_ref.shape, 0)
        stat_ref[...] = jnp.where(which == 0, peak, mass)

    @pl.when(pl.program_id(0) < half)
    def _():
        tile(own, hot_own)

    @pl.when(pl.program_id(0) >= half)
    def _():
        tile(sib, hot_sib)


def score(meta, at, own, sib, panels, width, acc=None, full=None, used=None, hots=None, extra=None):
    rows = own[0].shape[0]
    parts = len(own)
    tile = 384
    half = rows // tile
    count, columns = panels.shape
    first, last = acc is None, used is not None and hots is None
    store = used is None or last
    fronts = [pl.BlockSpec((tile, v.shape[1]), lambda j, m: (jnp.minimum(j, half - 1), 0)) for v in own]
    backs = [pl.BlockSpec((tile, v.shape[1]), lambda j, m: (jnp.maximum(j - half, 0), 0)) for v in own]
    acc_spec = pl.BlockSpec((count, tile), lambda j, m: (0, j))
    full_spec = pl.BlockSpec((tile, width), lambda j, m: (j, at(m)))
    in_specs = fronts + backs + [pl.BlockSpec((count, width), lambda j, m: (0, at(m)))]
    operands = [meta, *own, *sib, panels]
    alias = {}
    if not first:
        in_specs += [acc_spec]
        alias = {len(operands): 0}
        operands += [acc]
        if store:
            in_specs += [pl.BlockSpec(memory_space=pl.ANY)]
            alias[len(operands)] = 2 if last else 1
            operands += [full]
    full_shape = sds((2 * rows, columns), BF16)
    acc_shape = sds((count, 2 * rows), F32)
    out_specs, out_shape = [acc_spec, full_spec], [acc_shape, full_shape]
    if last:
        out_specs = [acc_spec, pl.BlockSpec((8, tile), lambda j, m: (0, j)), full_spec]
        out_shape = [acc_shape, sds((8, 2 * rows), F32), full_shape]
    elif not store:
        depth = extra.shape[1]
        in_specs += [
            pl.BlockSpec((depth, tile), lambda j, m: (0, jnp.minimum(j, half - 1))),
            pl.BlockSpec((depth, tile), lambda j, m: (0, jnp.maximum(j - half, 0))),
            pl.BlockSpec((count, depth), lambda j, m: (0, 0)),
        ]
        operands += [*hots, extra]
        out_specs, out_shape = acc_spec, acc_shape
    return call(
        functools.partial(score_body, parts, used, first, last),
        (2 * half,),
        in_specs,
        out_specs,
        out_shape,
        alias=alias,
        room=24,
        flops=2 * count * 2 * rows * width,
        moved=8 * count * 2 * rows + 8 * rows * width,
    )(*operands)


def merge_body(meta, mine_ref, other_ref, out_ref):
    rows = mine_ref.shape[1] // 2
    other = other_ref[...]
    other = jnp.concatenate([other[:, rows:], other[:, :rows]], axis=1)
    mine = mine_ref[...]
    peak = jnp.maximum(mine[0:1], other[0:1])
    mass = mine[1:2] * jnp.exp(mine[0:1] - peak) + other[1:2] * jnp.exp(other[0:1] - peak)
    which = lax.broadcasted_iota(I32, out_ref.shape, 0)
    out_ref[...] = jnp.where(which == 0, peak, mass)


def add_body(meta, mine_ref, other_ref, out_ref):
    out_ref[...] = (mine_ref[...].astype(F32) + other_ref[...].astype(F32)).astype(BF16)


def pairwise(body, meta, mine, other):
    spec = pl.BlockSpec(mine.shape, lambda j, m: (0, 0))
    return call(body, (1,), [spec, spec], spec, sds(mine.shape, mine.dtype), room=4)(
        meta, mine, other
    )


merge = functools.partial(pairwise, merge_body)
add_pair = functools.partial(pairwise, add_body)


def class_body(kind, steps, meta, *refs):
    if kind == "first":
        (shifted_ref, stat_ref), four = refs[:2], refs[2:6]
        hot_own, hot_sib, full_ref = refs[6:9]
        outs, (post_ref, log_ref, mass_ref) = refs[9 : 9 + steps], refs[9 + steps :]

        @pl.when(pl.program_id(0) == 0)
        def _():
            stats = [ref[...] for ref in four]
            peaks = [s[0:1] for s in stats]
            peak = jnp.maximum(jnp.maximum(peaks[0], peaks[1]), jnp.maximum(peaks[2], peaks[3]))
            parts = [s[1:2] * jnp.exp(p - peak) for s, p in zip(stats, peaks)]
            mass = (parts[0] + parts[1]) + (parts[2] + parts[3])
            factor = jnp.exp(stat_ref[0:1] - peak) / mass
            post_ref[...] = (shifted_ref[...] * factor).astype(BF16)
            log_ref[...] = (peak + jnp.log(mass))[:, : log_ref.shape[1]]
            bins, rows = mass_ref.shape[0], hot_own.shape[1]
            weights = mm(hot_own[:bins, :], post_ref[:, :rows], NT)
            weights = weights + mm(hot_sib[:bins, :], post_ref[:, rows:], NT)
            mass_ref[...] = weights.astype(BF16)

    else:
        (post_ref, full_ref), outs = refs[:2], refs[2:]
    for step, out_ref in enumerate(outs):

        @pl.when(pl.program_id(0) == step)
        def _():
            out_ref[...] = mm(post_ref[...], full_ref[...], NN).astype(out_ref.dtype)


def class_part(meta, kind, offset, steps, full, post=None, shifted=None, stats=None, hots=None, bins=0):
    rows, columns = full.shape
    width = columns // 8
    count = (shifted if post is None else post).shape[0]
    whole = lambda shape: pl.BlockSpec(shape, lambda j, m: (0, 0))
    full_spec = pl.BlockSpec((rows, width), lambda j, m: (0, m[offset + j]))
    out_specs = [whole((count, width))] * steps
    kept = steps // 2 if kind == "rest" else 0
    types = [BF16] * (steps - kept) + [F32] * kept
    out_shape = [sds((count, width), dtype) for dtype in types]
    if kind == "first":
        operands = [shifted, *stats, *hots, full]
        in_specs = [whole(shifted.shape)] + [whole(stats[0].shape)] * 5
        in_specs += [whole(hots[0].shape)] * 2 + [full_spec]
        out_specs += [whole((count, rows)), whole((1, rows // 2)), whole((bins, count))]
        out_shape += [sds((count, rows), BF16), sds((1, rows // 2), F32), sds((bins, count), BF16)]
    else:
        operands = [post, full]
        in_specs = [whole(post.shape), full_spec]
    return call(
        functools.partial(class_body, kind, steps),
        (steps,),
        in_specs,
        out_specs,
        out_shape,
        room=22 if kind == "first" else 28,
        flops=2 * count * rows * width * steps,
        moved=2 * rows * width * steps + 4 * count * (rows + width * steps),
    )(meta, *operands)


def own_half_body(tile, meta, keep_ref, c_ref, a_ref, out_ref):
    rows = pl.ds(pl.multiple_of(pl.program_id(0) * tile, tile), tile)
    out_ref[...] = keep_ref[rows, :] + c_ref[rows, :].astype(F32) + a_ref[rows, :].astype(F32)


def own_half(meta, keep, got_c, got_a):
    count, width = keep.shape
    parts = 3
    tile = count // parts
    return call(
        functools.partial(own_half_body, tile),
        (parts,),
        [pl.BlockSpec(memory_space=pltpu.VMEM)] * 3,
        pl.BlockSpec((tile, width), lambda j, m: (lax.rem(m[0], 2) * parts + j, 0)),
        sds((2 * count, width), F32),
        room=8,
    )(meta, keep, got_c, got_a)


def two_by_two(raw_images, defocus_bin, dest_row, ctf_table, inv_noise, panels):
    dom, turns = lax.axis_size("dom"), lax.axis_size("rot")
    device, plane = lax.axis_index("dom"), lax.axis_index("rot")
    bins = ctf_table.shape[0]
    columns = raw_images.shape[1]
    chip, core = device // 2, device % 2

    def block(apart, half):
        return (chip ^ apart) * 2 + half

    x_first, y_second = block(1, 0), block(2, 1)
    x_second, y_first = block(1, 1), block(2, 0)
    even = core == 0
    order = [
        device,
        plane,
        block(3, 0),
        block(3, 1),
        jnp.where(even, x_first, y_second),
        jnp.where(even, y_second, x_first),
        block(0, 1 - core),
        jnp.where(even, y_first, x_second),
        jnp.where(even, x_second, y_first),
        block(0, core),
    ]
    meta = jnp.stack(order).astype(I32)
    inv = inv_noise[None, :]

    def across(value, apart):
        return lax.ppermute(value, "dom", [(i, i ^ apart) for i in range(dom)])

    def by_core(value, when_even, when_odd):
        pairs = [(i, i ^ (when_odd if i % 2 else when_even)) for i in range(dom)]
        return lax.ppermute(value, "dom", pairs)

    def onward(value):
        return lax.ppermute(value, "rot", [(i, (i + 1) % turns) for i in range(turns)])

    width = columns // turns
    cut = width * 3 // 8
    chunk_a, chunk_b = (0, cut), (cut, width - cut)

    def exchange(blocks):
        far_first = [across(blocks[apart], apart) for apart in (6, 7, 4, 2, 5, 3, 1)]
        return far_first + [blocks[0]]

    slot = jnp.where(dest_row >= 0, dest_row * bins + defocus_bin, -1)
    *send_a, place = pack_first(meta, raw_images, slot, bins, dom, width, chunk_a)
    recv_a = exchange(send_a)
    swapped, place = lax.optimization_barrier((across(panels, 1), place))
    send_b = pack_next(meta, raw_images, place, dom, width, chunk_b)
    together = lax.optimization_barrier

    count = panels.shape[0] // 2
    mine = lax.dynamic_slice_in_dim(panels, core * count, count, 0)
    other = lax.dynamic_slice_in_dim(swapped, core * count, count, 0)
    near = jnp.concatenate([mine, other], axis=1)

    recv_a, send_b, near = together((recv_a, send_b, near))
    share_a, hot, pick, wide = unpack_first(meta, recv_a, ctf_table, inv, width, chunk_a)
    share_a, send_b = together((share_a, send_b))
    a1, recv_b = onward(share_a), exchange(send_b)
    piece = near.shape[1] // 2
    panel_full, energies = energy(meta, [near], ctf_table, inv, piece, 0)
    a1, recv_b[:2], panel_full, energies = together((a1, recv_b[:2], panel_full, energies))
    a2 = onward(a1)
    share_b = unpack_next(meta, pick, wide, recv_b, ctf_table, inv, width, chunk_b)
    a2, share_b, near = together((a2, share_b, near))
    by_x, by_y = across(near, 2), across(near, 4)
    a3, b1 = onward(a2), onward(share_b)
    sib0, hots = [across(share_a, 1), across(share_b, 1)], [hot, across(hot, 1)]
    sib1, sib2 = [across(a1, 1), across(b1, 1)], [across(a2, 1)]
    piece = near.shape[1] // 2
    far_y, far_x = across(by_x[:, :piece], 4), across(by_y[:, piece:], 2)
    b2 = onward(b1)
    panel_full, extra = energy(
        meta, [by_x, by_y, far_y, far_x], ctf_table, inv, piece, 2, energies, panel_full
    )
    a3, b2, panel_full, hots = together((a3, b2, panel_full, hots))
    b3 = onward(b2)
    sib2 = sib2 + [across(b2, 1)]

    def share(turn):
        return lambda m: lax.rem(m[1] + turns - turn, turns)

    acc, full = score(meta, share(0), [share_a, share_b], sib0, panel_full, width)
    acc, full = score(meta, share(1), [a1, b1], sib1, panel_full, width, acc, full)
    acc, full = score(meta, share(2), [a2, b2], sib2, panel_full, width, acc, full)
    final = share(turns - 1)
    a3_sib = across(a3, 1)
    acc = score(
        meta, final, [a3], [a3_sib], panel_full, width, acc, None, chunk_a, hots, extra
    )
    b3, acc = together((b3, acc))
    shifted, stat, full = score(
        meta,
        final,
        [a3, b3],
        [a3_sib, across(b3, 1)],
        panel_full,
        width,
        acc,
        full,
        chunk_b,
    )

    pair = merge(meta, stat, across(stat, 1))
    others = [
        lax.ppermute(pair, "rot", [(i, i ^ apart) for i in range(turns)]) for apart in (1, 2, 3)
    ]
    to_x, to_y, post, log_evidence, mass = class_part(
        meta, "first", 2, 2, full, None, shifted, [stat, pair, *others], hots, bins
    )
    mass_x = across(mass, 2)
    got_x, got_y = across(to_x, 2), across(to_y, 4)
    six = class_part(meta, "rest", 4, 6, full, post)
    got_x, got_y, six, mass_x = together((got_x, got_y, six, mass_x))
    send_c, send_d, give, a_sum, b_sum, keep = six
    mass = add_pair(meta, mass, mass_x)
    mass_y = across(mass, 4)
    got_c, got_d = by_core(send_c, 2, 4), by_core(send_d, 5, 3)
    down, left = got_x.astype(F32), got_y.astype(F32)
    message_a = (a_sum + jnp.where(even, down, left)).astype(BF16)
    message_b = (b_sum + jnp.where(even, left, down)).astype(BF16)
    got_a, got_b = by_core(message_a, 4, 2), by_core(message_b, 3, 5)
    got_self = across(give, 1)
    mass_y, got_a, got_c = together((mass_y, got_a, got_c))
    mass = mass.astype(F32) + mass_y.astype(F32)
    mass_other = across(mass, 1)
    bin_weights = jnp.where(
        even,
        jnp.concatenate([mass, mass_other], axis=1),
        jnp.concatenate([mass_other, mass], axis=1),
    )
    sums = own_half(meta, keep, got_c, got_a)
    bin_weights, got_b = together((bin_weights, got_b))
    other_half = got_self.astype(F32) + got_d.astype(F32) + got_b.astype(F32)
    class_sums = lax.dynamic_update_slice_in_dim(sums, other_half, (1 - core) * count, 0).T
    return class_sums, bin_weights, log_evidence.reshape(-1)


def energy_block(gain_block, panel_piece):
    widened = panel_piece.astype(jnp.float32)
    return lax.dot_general(
        gain_block, widened * widened, (((1,), (1,)), ((), ())), precision=lax.Precision.HIGHEST
    )


def on_device(raw_images, defocus_bin, dest_row, ctf_table, inv_noise, panels):
    dom_count = lax.axis_size("dom")
    bin_count = ctf_table.shape[0]
    columns = raw_images.shape[1]
    hold_rows = raw_images.shape[0]
    shard_rows = hold_rows // 2
    capacity = 2 * shard_rows // dom_count
    is_live = dest_row >= 0
    target = jnp.where(is_live, dest_row // shard_rows, dom_count)
    local_row = dest_row % shard_rows
    marks = (target[:, None] == jnp.arange(dom_count, dtype=jnp.int32)[None, :]).astype(jnp.int32)
    slot_rank = jnp.sum((jnp.cumsum(marks, axis=0) - marks) * marks, axis=1)
    row_code = jnp.where(is_live, local_row * bin_count + defocus_bin, -1)
    padded_images = jnp.concatenate([raw_images, jnp.zeros((1, columns), raw_images.dtype)], axis=0)
    padded_code = jnp.concatenate([row_code, jnp.full((1,), -1, jnp.int32)], axis=0)
    position = jnp.where(is_live, target * capacity + slot_rank, dom_count * capacity)
    slot_count = dom_count * capacity
    source = (
        jnp.full((slot_count,), hold_rows, jnp.int32)
        .at[position]
        .set(jnp.arange(hold_rows, dtype=jnp.int32), mode="drop")
    )
    send_images = padded_images[source].reshape(dom_count, capacity, columns)
    send_code = padded_code[source].reshape(dom_count, capacity)
    recv_images, recv_code = (
        lax.all_to_all(send_images, "dom", split_axis=0, concat_axis=0, tiled=True),
        lax.all_to_all(send_code, "dom", split_axis=0, concat_axis=0, tiled=True),
    )
    flat_images = recv_images.reshape(-1, columns)
    flat_code = recv_code.reshape(-1)
    arrived = flat_code >= 0
    row_of = jnp.where(arrived, flat_code // bin_count, shard_rows)
    row_order = (
        jnp.zeros((shard_rows,), jnp.int32)
        .at[row_of]
        .set(jnp.arange(flat_code.shape[0], dtype=jnp.int32), mode="drop")
    )
    images = flat_images[row_order]
    bin_ids = flat_code[row_order] % bin_count
    bin_table = (bin_ids[:, None] == jnp.arange(bin_count, dtype=jnp.int32)[None, :]).astype(
        jnp.float32
    )
    ctf_rows = jnp.dot(bin_table, ctf_table, precision=lax.Precision.HIGHEST)
    factor = ctf_rows * inv_noise[None, :]
    weighted = (images.astype(jnp.float32) * jnp.concatenate([factor, factor], axis=1)).astype(
        jnp.bfloat16
    )
    gain_half = ctf_table * ctf_table * inv_noise[None, :]
    gain_full = jnp.concatenate([gain_half, gain_half], axis=1)
    panel_piece = lax.all_gather(panels, "dom", axis=1, tiled=True)
    col_block = weighted
    cross_term = lax.dot_general(
        col_block, panel_piece, (((1,), (1,)), ((), ())), preferred_element_type=jnp.float32
    )
    energy = energy_block(gain_full, panel_piece)
    scores = cross_term - 0.5 * jnp.dot(bin_table, energy, precision=lax.Precision.HIGHEST)
    local_peak = jnp.max(scores, axis=1)
    row_peak = lax.pmax(local_peak, "rot")
    shifted = jnp.exp(scores - row_peak[:, None])
    row_total = lax.psum(jnp.sum(shifted, axis=1), "rot")
    posterior = (shifted / row_total[:, None]).astype(jnp.bfloat16)
    log_evidence = row_peak + jnp.log(row_total)
    col_block = weighted
    class_sums = lax.psum_scatter(
        lax.dot_general(
            col_block, posterior, (((0,), (0,)), ((), ())), preferred_element_type=jnp.float32
        ).astype(jnp.bfloat16),
        "dom",
        scatter_dimension=0,
        tiled=True,
    ).astype(jnp.float32)
    local_mass = lax.dot_general(
        bin_table.astype(jnp.bfloat16),
        posterior,
        (((0,), (0,)), ((), ())),
        preferred_element_type=jnp.float32,
    )
    bin_weights = lax.psum(local_mass.astype(jnp.bfloat16), "dom").astype(jnp.float32)
    return (class_sums, bin_weights, log_evidence)


def solution(mesh):
    small = mesh.shape["dom"] == 8 and mesh.shape["rot"] == 4
    return jax.shard_map(
        two_by_two if small else on_device,
        mesh=mesh,
        in_specs=(P("dom", None), P("dom"), P("dom"), P(), P(), P("rot", "dom")),
        out_specs=(P("dom", "rot"), P(None, "rot"), P("dom")),
        check_vma=False,
    )
```
